128 devices in a mesh: section: 4 (over z), shard: 32 (over y, x, core).
Axes of the slice: x: 4, y: 4, z: 4, core: 2. Of those that a mesh axis runs over, the one named last changes fastest.
Arguments:
- saved: bfloat16 [4, 4, 1024, 8, 1024], P('section', None, 'shard'), may hold values from -6 to 6
- pooled: bfloat16 [4, 1024, 8, 1024], P('section', 'shard'), may hold values from -6 to 6
- grad_top: bfloat16 [4, 1024, 8, 1024], P(None, 'shard'), may hold values from -6 to 6
- w_in: bfloat16 [4, 1024, 1024], P('section'), may hold values from -0.1875 to 0.1875
- w_out: bfloat16 [4, 1024, 1024], P('section'), may hold values from -0.1875 to 0.1875
- feature_ids: int32 [4, 1024, 8], P(None, 'shard'), may hold values from 0 to 131071, as said below
- holder_order: int32 [4], replicated, may hold values from 0 to 3, each once
Outputs:
- grad_w_in: float32 [4, 1024, 1024], P('section', 'shard')
- grad_w_out: float32 [4, 1024, 1024], P('section', 'shard')
- table_grad: float32 [131072, 1024], P(('section', 'shard'))
The draws below stay inside these ranges and needn't reach their ends.
Inputs may be any that keep to these rules, and one draw needn't show every extreme that they name: `feature_ids`: feature k names a row of table k, rows k * 16384 to (k + 1) * 16384 - 1. Row i belongs to owner i // 1024. In each micro-batch, the rows j * 32 to (j + 1) * 32 - 1 name exactly 2 rows of every owner.
All inputs are finite; a program needn't handle non-finite values.
Results may differ from the reference program's by a relative error of at most 0.0095.
Values may be sent and summed in bfloat16 or wider, within the bound.
A program may use at most 192 MiB of HBM per device.

```python
import jax
import jax.numpy as jnp

D = 1024
FEAT = 8
BROWS_DEV = 32
ROWS_OWN = 1024
MB = 4
SECTIONS = 4
BROWS = 1024
TABLE_ROWS = 131072


def draw_feature_ids(key, part):
    key = jax.random.fold_in(key, 11)
    key_perm, key_rows = jax.random.split(key)
    per_table = TABLE_ROWS // ROWS_OWN // FEAT
    shard_count = BROWS // BROWS_DEV
    blocks = MB * shard_count * FEAT
    block_keys = jax.random.split(key_perm, blocks)
    shuffled = jax.vmap(lambda sub_key: jax.random.permutation(sub_key, BROWS_DEV))(block_keys)
    shuffled = shuffled.reshape(MB, shard_count, FEAT, BROWS_DEV)
    shuffled = jnp.transpose(shuffled, (0, 1, 3, 2)).reshape(MB, BROWS, FEAT).astype(jnp.int32)
    local_owner = shuffled % per_table
    within = jax.random.randint(key_rows, (MB, BROWS, FEAT), 0, ROWS_OWN).astype(jnp.int32)
    feat_index = jnp.arange(FEAT, dtype=jnp.int32)[None, None, :]
    top_mark = (shuffled == per_table - 1) & (feat_index == FEAT - 1)
    low_mark = (shuffled == 0) & (feat_index == 0)
    within = jnp.where(top_mark, ROWS_OWN - 1, within)
    within = jnp.where(low_mark, 0, within)
    return ((feat_index * per_table + local_owner) * ROWS_OWN + within).astype(jnp.int32)


def spiked(array, own_key, source, target, parts, factor):
    def block_of(position):
        return (jnp.arange(array.shape[position]) // (array.shape[position] // parts)).reshape((-1,) + (1,) * (array.ndim - 1 - position))

    near = jax.random.permutation(own_key, parts)[block_of(target)]
    far = (block_of(target) + parts // 2) % parts
    return jnp.where((block_of(source) == near) | (block_of(source) == far), factor * array, array)


def shard_levels(own_key, shape, cuts, least, top_value):
    loudness, own = 1.0, jax.random.fold_in(own_key, 6)
    for position, blocks in cuts:
        heights = jnp.exp(jax.random.uniform(jax.random.fold_in(own, position), (blocks,), jnp.float32, least / len(cuts), top_value / len(cuts)))
        loudness = loudness * jnp.repeat(heights, shape[position] // blocks).reshape([-1 if axis == position else 1 for axis in range(len(shape))])
    return loudness


def normal_values(key, dims, deviation, most, pieces=(), kind=jnp.bfloat16):
    drawn = deviation * jax.random.normal(key, dims, jnp.float32)
    if pieces:
        drawn = drawn * shard_levels(key, dims, pieces, -0.22, 0.18)
    return jnp.clip(drawn, -most, most).astype(kind)


def heavy_noise(stream_key, extent, spread, reach, pieces, heavy, kind=jnp.bfloat16):
    values = spread * jax.random.normal(stream_key, extent, jnp.float32)
    if pieces:
        values = values * shard_levels(stream_key, extent, pieces, -0.22, 0.18)
    return jnp.clip(spiked(values, jax.random.fold_in(stream_key, 3), *heavy), -reach, reach).astype(kind)


def setup_inputs(seed: int = 0) -> dict:
    arg_keys = jax.random.split(jax.random.key(seed), 8)
    saved = heavy_noise(arg_keys[0], (SECTIONS, MB, BROWS, FEAT, D), 1.0, 6.0, ((0, 4), (2, 32)), (2, 4, 32, 2.75))
    pooled = normal_values(arg_keys[1], (MB, BROWS, FEAT, D), 1.0, 6.0, ((0, 4), (1, 32)))
    grad_top = normal_values(arg_keys[2], (MB, BROWS, FEAT, D), 1.0, 6.0, ((1, 32),))
    w_in = normal_values(arg_keys[3], (SECTIONS, D, D), D ** -0.5, 0.1875, ((0, 4),))
    w_out = normal_values(arg_keys[4], (SECTIONS, D, D), D ** -0.5, 0.1875, ((0, 4),))
    feature_ids = draw_feature_ids(jax.random.fold_in(arg_keys[7], 71), 0)
    holder_order = jax.random.permutation(arg_keys[6], MB).astype(jnp.int32)
    return dict(saved=saved, pooled=pooled, grad_top=grad_top, w_in=w_in, w_out=w_out, feature_ids=feature_ids, holder_order=holder_order)


def silu_parts(pre_act):
    sigmoid_val = jax.nn.sigmoid(pre_act)
    return pre_act * sigmoid_val, sigmoid_val * (1.0 + pre_act * (1.0 - sigmoid_val))


def reference(saved, pooled, grad_top, w_in, w_out, feature_ids, holder_order):
    inverse = jnp.zeros((MB,), jnp.int32).at[holder_order].set(jnp.arange(MB, dtype=jnp.int32))
    grads_in = [jnp.zeros((D, D), jnp.float32) for layer_id in range(SECTIONS)]
    grads_out = [jnp.zeros((D, D), jnp.float32) for layer_id in range(SECTIONS)]
    pooled_grads = []
    for micro_id in range(MB):
        grad_now = grad_top[micro_id].reshape(-1, D)
        for layer_id in reversed(range(SECTIONS)):
            if layer_id == 0:
                pooled_now = pooled[inverse[micro_id]].reshape(-1, D).astype(jnp.float32)
                layer_input = (saved[0, micro_id].reshape(-1, D).astype(jnp.float32) + pooled_now).astype(jnp.bfloat16)
            else:
                layer_input = saved[layer_id, micro_id].reshape(-1, D)
            pre_act = jnp.dot(layer_input, w_in[layer_id], preferred_element_type=jnp.float32)
            act_val, slope_val = silu_parts(pre_act)
            activ = act_val.astype(jnp.bfloat16)
            grad_act = jnp.dot(grad_now, w_out[layer_id].T, preferred_element_type=jnp.float32)
            grad_pre = (grad_act * slope_val).astype(jnp.bfloat16)
            grads_out[layer_id] = grads_out[layer_id] + jnp.dot(activ.T, grad_now, preferred_element_type=jnp.float32)
            grads_in[layer_id] = grads_in[layer_id] + jnp.dot(layer_input.T, grad_pre, preferred_element_type=jnp.float32)
            back_term = jnp.dot(grad_pre, w_in[layer_id].T, preferred_element_type=jnp.float32)
            grad_now = (grad_now.astype(jnp.float32) + back_term).astype(jnp.bfloat16)
        pooled_grads.append(grad_now)
    all_grads = jnp.concatenate(pooled_grads, axis=0).astype(jnp.float32)
    row_ids = feature_ids.reshape(-1).astype(jnp.int32)
    table_grad = jax.ops.segment_sum(all_grads, row_ids, num_segments=TABLE_ROWS)
    return jnp.stack(grads_in), jnp.stack(grads_out), table_grad
```

```python
import jax
import jax.numpy as jnp
from jax import lax
from jax.experimental import pallas as pl
from jax.experimental.pallas import tpu as pltpu
from jax.sharding import PartitionSpec as P

ROWS_OWN = 1024
MESH = pl.DeviceIdType.MESH
F32 = jnp.float32
BF16 = jnp.bfloat16

SECTIONS = 4
SHARDS = 32
SIDE = 4
MICRO = 4
TOK = 256
CHUNK = 128
WIDTH = 1024
SHARE = WIDTH // SHARDS
PER_PLANE = TOK // SECTIONS
TILE = 256
CHUNKS = TOK // CHUNK


def dot_nt(a, b):
    return lax.dot_general(a, b, (((1,), (1,)), ((), ())), preferred_element_type=F32)


def dot_tn(a, b):
    return lax.dot_general(a, b, (((0,), (0,)), ((), ())), preferred_element_type=F32)


def kernel(
    inverse,
    saved,
    pooled,
    grad_top,
    w_in,
    w_out,
    rank,
    out_in,
    out_out,
    out_rows,
    win,
    wout,
    xbuf,
    gbuf,
    nbuf,
    pbuf,
    act,
    slope,
    dz,
    acc,
    sorted_rows,
    routed,
    spread,
    send_a,
    recv_a,
    send_b,
    recv_b,
    own_b,
    send_c,
    recv_c,
    load_sem,
    top_sem,
    pool_send,
    pool_recv,
    relay_send,
    relay_recv,
    route_send,
    route_recv,
    spread_send,
    spread_recv,
    a_send,
    a_recv,
    b_send,
    b_recv,
    c_send,
    c_recv,
):
    sec = lax.axis_index("section")
    sh = lax.axis_index("shard")
    core = sh % 2
    px = (sh // 2) % SIDE
    py = sh // (2 * SIDE)
    first = sec == 0
    last = sec == SECTIONS - 1

    def at(y, x, c):
        return (sec, (y * SIDE + x) * 2 + c)

    def micro_rows(m):
        return pl.ds(pl.multiple_of(m * TOK, TOK), TOK)

    def chunk_rows(c):
        return pl.ds(pl.multiple_of(c * CHUNK, CHUNK), CHUNK)

    def load_x(m):
        rows = micro_rows(m)
        return pltpu.make_async_copy(saved.at[rows], xbuf.at[rows], load_sem.at[2 + m])

    def load_top(m):
        rows = micro_rows(m)
        return pltpu.make_async_copy(grad_top.at[rows], gbuf.at[rows], top_sem.at[m])

    load_win = pltpu.make_async_copy(w_in, win, load_sem.at[0])
    load_wout = pltpu.make_async_copy(w_out, wout, load_sem.at[1])
    load_pool = pltpu.make_async_copy(pooled, pbuf.at[0], load_sem.at[2 + MICRO])

    load_win.start()
    load_x(0).start()
    load_wout.start()

    @pl.when(last)
    def _():
        for m in range(MICRO):
            load_top(m).start()

    for m in range(1, MICRO):
        load_x(m).start()

    @pl.when(first)
    def _():
        load_pool.start()

    barrier = pltpu.get_barrier_semaphore()

    def greet(k, carry):
        pl.semaphore_signal(
            barrier, inc=1, device_id=(sec, (sh + k) % SHARDS), device_id_type=MESH
        )
        return carry

    lax.fori_loop(1, SHARDS, greet, 0)
    for k in range(1, SECTIONS):
        pl.semaphore_signal(
            barrier, inc=1, device_id=((sec + k) % SECTIONS, sh), device_id_type=MESH
        )
    pl.semaphore_wait(barrier, SHARDS - 1 + SECTIONS - 1)

    def pool_copy(s):
        return pltpu.make_async_remote_copy(
            src_ref=pooled,
            dst_ref=pbuf.at[s],
            send_sem=pool_send,
            recv_sem=pool_recv.at[s],
            device_id=(0, sh),
            device_id_type=MESH,
        )

    def relay_copy(c):
        rows = chunk_rows(c)
        return pltpu.make_async_remote_copy(
            src_ref=nbuf.at[rows],
            dst_ref=gbuf.at[rows],
            send_sem=relay_send.at[c],
            recv_sem=relay_recv.at[c],
            device_id=(jnp.maximum(sec - 1, 0), sh),
            device_id_type=MESH,
        )

    def route_copy(m, p):
        return pltpu.make_async_remote_copy(
            src_ref=sorted_rows.at[m, pl.ds(p * PER_PLANE, PER_PLANE)],
            dst_ref=routed.at[pl.ds(pl.multiple_of(m * PER_PLANE, PER_PLANE), PER_PLANE)],
            send_sem=route_send.at[m, p],
            recv_sem=route_recv.at[m],
            device_id=(p, sh),
            device_id_type=MESH,
        )

    @pl.when(jnp.logical_not(first))
    def _():
        pool_copy(sec).start()

    def clear(i, carry):
        rows = pl.ds(pl.multiple_of(i * 64, 64), 64)
        for mat in range(2):
            acc[mat, rows, :] = jnp.zeros((64, WIDTH), F32)
        return carry

    lax.fori_loop(0, WIDTH // 64, clear, 0)

    load_win.wait()

    def micro_step(m, carry):
        rows = micro_rows(m)
        load_x(m).wait()

        @pl.when(first)
        def _():
            @pl.when(m == 0)
            def _():
                load_pool.wait()
                for s in range(1, SECTIONS):
                    pool_copy(s).wait_recv()

            extra = pbuf[inverse[m]]
            xbuf[rows, :] = (xbuf[rows, :].astype(F32) + extra.astype(F32)).astype(BF16)

        for j in range(WIDTH // TILE):
            cols = pl.ds(j * TILE, TILE)
            z = jnp.dot(xbuf[rows, :], win[:, cols], preferred_element_type=F32)
            sig = jax.nn.sigmoid(z)
            act[:, cols] = (z * sig).astype(BF16)
            slope[:, cols] = sig * (1.0 + z * (1.0 - sig))

        @pl.when(m == 0)
        def _():
            load_wout.wait()

        @pl.when(last)
        def _():
            load_top(m).wait()

        for k in range(CHUNKS):
            c = m * CHUNKS + k
            crows = chunk_rows(c)
            krows = pl.ds(k * CHUNK, CHUNK)

            @pl.when(jnp.logical_not(last))
            def _():
                relay_copy(c).wait_recv()

            g = gbuf[crows, :]
            for j in range(WIDTH // TILE):
                cols = pl.ds(j * TILE, TILE)
                ga = dot_nt(g, wout[cols, :])
                dz[krows, cols] = (ga * slope[krows, cols]).astype(BF16)
            for j in range(WIDTH // TILE):
                cols = pl.ds(j * TILE, TILE)
                back = dot_nt(dz[krows, :], win[cols, :])
                nbuf[crows, cols] = (gbuf[crows, cols].astype(F32) + back).astype(BF16)

            @pl.when(jnp.logical_not(first))
            def _():
                relay_copy(c).start()

        @pl.when(first)
        def _():
            target = lax.broadcasted_iota(jnp.int32, (TOK, TOK), 0)
            pick = jnp.where(target == rank[m], 1.0, 0.0).astype(BF16)
            ordered = jnp.dot(pick, nbuf[rows, :], preferred_element_type=F32).astype(BF16)
            sorted_rows[m] = ordered
            for p in range(1, SECTIONS):
                route_copy(m, p).start()
            routed[pl.ds(pl.multiple_of(m * PER_PLANE, PER_PLANE), PER_PLANE), :] = ordered[
                :PER_PLANE, :
            ]

        def weight_tile(i, inner):
            cols = pl.ds(pl.multiple_of(i * TILE, TILE), TILE)
            acc[0, cols, :] += dot_tn(xbuf[rows, cols], dz[...])
            acc[1, cols, :] += dot_tn(act[:, cols], gbuf[rows, :])
            return inner

        lax.fori_loop(0, WIDTH // TILE, weight_tile, 0)
        return carry

    lax.fori_loop(0, MICRO, micro_step, 0)

    def mine(mat):
        return px if mat == 0 else py

    def acc_rows(mat, t, o, c):
        block = (o * SIDE + t) if mat == 0 else (t * SIDE + o)
        return pl.ds(pl.multiple_of(block * 2 * SHARE + c * SHARE, SHARE), SHARE)

    def a_copy(mat, t):
        return pltpu.make_async_remote_copy(
            src_ref=send_a.at[mat, t],
            dst_ref=recv_a.at[mat, t],
            send_sem=a_send.at[mat, t],
            recv_sem=a_recv.at[mat, t],
            device_id=at(py, px, 1 - core),
            device_id_type=MESH,
        )

    def b_copy(mat, d):
        t = (mine(mat) + d) % SIDE
        return pltpu.make_async_remote_copy(
            src_ref=send_b.at[mat, d - 1],
            dst_ref=recv_b.at[mat, d - 1],
            send_sem=b_send.at[mat, d - 1],
            recv_sem=b_recv.at[mat, d - 1],
            device_id=at(py, t, core) if mat == 0 else at(t, px, core),
            device_id_type=MESH,
        )

    def c_copy(mat, d):
        t = (mine(1 - mat) + d) % SIDE
        return pltpu.make_async_remote_copy(
            src_ref=send_c.at[mat, d - 1],
            dst_ref=recv_c.at[mat, d - 1],
            send_sem=c_send.at[mat, d - 1],
            recv_sem=c_recv.at[mat, d - 1],
            device_id=at(t, px, core) if mat == 0 else at(py, t, core),
            device_id_type=MESH,
        )

    order = (2, 1, 3, 0)
    for d in order:
        for mat in range(2):
            t = (mine(mat) + d) % SIDE

            def fill_a(o, carry, mat=mat, t=t):
                send_a[mat, t, o] = acc[mat, acc_rows(mat, t, o, 1 - core), :].astype(BF16)
                return carry

            lax.fori_loop(0, SIDE, fill_a, 0)
            a_copy(mat, t).start()

    for d in order:
        for mat in range(2):
            t = (mine(mat) + d) % SIDE
            a_copy(mat, t).wait_recv()

            def add_a(o, carry, mat=mat, t=t, d=d):
                both = acc[mat, acc_rows(mat, t, o, core), :] + recv_a[mat, t, o].astype(F32)
                if d == 0:
                    own_b[mat, o] = both
                else:
                    send_b[mat, d - 1, o] = both.astype(BF16)
                return carry

            lax.fori_loop(0, SIDE, add_a, 0)
            if d != 0:
                b_copy(mat, d).start()

    @pl.when(jnp.logical_not(first))
    def _():
        for m in range(MICRO):
            route_copy(m, 1).wait_recv()

    row = lax.broadcasted_iota(jnp.int32, (TOK, TOK), 0)
    col = lax.broadcasted_iota(jnp.int32, (TOK, TOK), 1)
    source = ((row >> 1) & 3) * PER_PLANE + (row >> 3) * 2 + (row & 1)
    regroup = jnp.where(source == col, 1.0, 0.0).astype(BF16)
    by_owner = jnp.dot(regroup, routed[...], preferred_element_type=F32)
    spread[...] = by_owner.reshape(SHARDS, 2 * MICRO, WIDTH).astype(BF16)

    def spread_copy(k, to, came):
        return pltpu.make_async_remote_copy(
            src_ref=spread.at[to],
            dst_ref=out_rows.at[came],
            send_sem=spread_send.at[k],
            recv_sem=spread_recv.at[k],
            device_id=(sec, to),
            device_id_type=MESH,
        )

    def hand_out(k, carry):
        spread_copy(k, (sh + k) % SHARDS, sh).start()
        return carry

    lax.fori_loop(1, SHARDS, hand_out, 0)
    out_rows[sh] = spread[sh]

    for d in range(1, SIDE):
        for mat in range(2):
            b_copy(mat, d).wait_recv()
    for mat in range(2):

        def add_b(o, carry, mat=mat):
            total = own_b[mat, o]
            for d in range(1, SIDE):
                total = total + recv_b[mat, d - 1, o].astype(F32)
            own_b[mat, o] = total
            return carry

        lax.fori_loop(0, SIDE, add_b, 0)
        for d in (2, 1, 3):
            t = (mine(1 - mat) + d) % SIDE
            send_c[mat, d - 1] = own_b[mat, t].astype(BF16)
            c_copy(mat, d).start()

    for mat, out in ((0, out_in), (1, out_out)):
        total = own_b[mat, mine(1 - mat)]
        for d in range(1, SIDE):
            c_copy(mat, d).wait_recv()
            total = total + recv_c[mat, d - 1].astype(F32)
        out[...] = total

    def collect(k, carry):
        spread_copy(k, (sh + k) % SHARDS, (sh + SHARDS - k) % SHARDS).wait_recv()
        return carry

    lax.fori_loop(1, SHARDS, collect, 0)

    @pl.when(jnp.logical_not(first))
    def _():
        pool_copy(sec).wait_send()

        def left(c, carry):
            relay_copy(c).wait_send()
            return carry

        lax.fori_loop(0, MICRO * CHUNKS, left, 0)

    @pl.when(first)
    def _():
        for m in range(MICRO):
            for p in range(1, SECTIONS):
                route_copy(m, p).wait_send()

    def spread_left(k, carry):
        spread_copy(k, (sh + k) % SHARDS, sh).wait_send()
        return carry

    lax.fori_loop(1, SHARDS, spread_left, 0)
    for mat in range(2):
        for t in range(SIDE):
            a_copy(mat, t).wait_send()
        for d in range(1, SIDE):
            b_copy(mat, d).wait_send()
            c_copy(mat, d).wait_send()


def relay(inverse, saved, pooled, grad_top, w_in, w_out, rank):
    vmem = pl.BlockSpec(memory_space=pltpu.VMEM)
    anywhere = pl.BlockSpec(memory_space=pl.ANY)
    dma = pltpu.SemaphoreType.DMA
    tokens = MICRO * TOK
    return pl.pallas_call(
        kernel,
        out_shape=(
            jax.ShapeDtypeStruct((SHARE, WIDTH), F32),
            jax.ShapeDtypeStruct((SHARE, WIDTH), F32),
            jax.ShapeDtypeStruct((SHARDS, 2 * MICRO, WIDTH), BF16),
        ),
        in_specs=[pl.BlockSpec(memory_space=pltpu.SMEM)] + [anywhere] * 5 + [vmem],
        out_specs=(vmem, vmem, vmem),
        scratch_shapes=[
            pltpu.VMEM((WIDTH, WIDTH), BF16),
            pltpu.VMEM((WIDTH, WIDTH), BF16),
            pltpu.VMEM((tokens, WIDTH), BF16),
            pltpu.VMEM((tokens, WIDTH), BF16),
            pltpu.VMEM((tokens, WIDTH), BF16),
            pltpu.VMEM((SECTIONS, TOK, WIDTH), BF16),
            pltpu.VMEM((TOK, WIDTH), BF16),
            pltpu.VMEM((TOK, WIDTH), F32),
            pltpu.VMEM((TOK, WIDTH), BF16),
            pltpu.VMEM((2, WIDTH, WIDTH), F32),
            pltpu.VMEM((MICRO, TOK, WIDTH), BF16),
            pltpu.VMEM((TOK, WIDTH), BF16),
            pltpu.VMEM((SHARDS, 2 * MICRO, WIDTH), BF16),
            pltpu.VMEM((2, SIDE, SIDE, SHARE, WIDTH), BF16),
            pltpu.VMEM((2, SIDE, SIDE, SHARE, WIDTH), BF16),
            pltpu.VMEM((2, SIDE - 1, SIDE, SHARE, WIDTH), BF16),
            pltpu.VMEM((2, SIDE - 1, SIDE, SHARE, WIDTH), BF16),
            pltpu.VMEM((2, SIDE, SHARE, WIDTH), F32),
            pltpu.VMEM((2, SIDE - 1, SHARE, WIDTH), BF16),
            pltpu.VMEM((2, SIDE - 1, SHARE, WIDTH), BF16),
            dma((3 + MICRO,)),
            dma((MICRO,)),
            dma,
            dma((SECTIONS,)),
            dma((MICRO * CHUNKS,)),
            dma((MICRO * CHUNKS,)),
            dma((MICRO, SECTIONS)),
            dma((MICRO,)),
            dma((SHARDS,)),
            dma((SHARDS,)),
            dma((2, SIDE)),
            dma((2, SIDE)),
            dma((2, SIDE - 1)),
            dma((2, SIDE - 1)),
            dma((2, SIDE - 1)),
            dma((2, SIDE - 1)),
        ],
        compiler_params=pltpu.CompilerParams(
            collective_id=0, has_side_effects=True, vmem_limit_bytes=56 * 1024 * 1024
        ),
        cost_estimate=pl.CostEstimate(
            flops=10 * tokens * WIDTH * WIDTH, bytes_accessed=9 * 2**20, transcendentals=tokens * WIDTH
        ),
        name="relay",
    )(inverse, saved, pooled, grad_top, w_in, w_out, rank)


def local(saved, pooled, grad_top, w_in, w_out, feature_ids, holder_order):
    section_id = lax.axis_index("section")
    shard_id = lax.axis_index("shard")
    tokens = MICRO * TOK
    micro_range = jnp.arange(MICRO, dtype=jnp.int32)
    inverse = jnp.sum(
        jnp.where(holder_order[None, :] == micro_range[:, None], micro_range[None, :], 0), axis=1
    )
    ids = feature_ids.reshape(MICRO, TOK)
    owner = ids // ROWS_OWN
    position = jnp.arange(TOK, dtype=jnp.int32)
    earlier = (owner[:, :, None] == owner[:, None, :]) & (position[None, :] < position[:, None])
    rank = 2 * owner + jnp.sum(earlier.astype(jnp.int32), axis=2)
    out_in, out_out, rows = relay(
        inverse,
        saved.reshape(tokens, WIDTH),
        pooled.reshape(TOK, WIDTH),
        grad_top.reshape(tokens, WIDTH),
        w_in[0],
        w_out[0],
        rank.reshape(MICRO, 1, TOK),
    )
    all_ids = lax.all_gather(ids, "shard", axis=0)
    own = section_id * SHARDS + shard_id
    key = position * ROWS_OWN + all_ids % ROWS_OWN
    named = all_ids // ROWS_OWN == own
    low = jnp.min(jnp.where(named, key, TOK * ROWS_OWN), axis=2)
    high = jnp.max(jnp.where(named, key, -1), axis=2)
    row_of = (jnp.stack([low, high], axis=2) % ROWS_OWN).reshape(-1)
    one_hot = (jnp.arange(ROWS_OWN, dtype=jnp.int32)[:, None] == row_of[None, :]).astype(BF16)
    table_grad = jnp.dot(one_hot, rows.reshape(-1, WIDTH), preferred_element_type=F32)
    return (out_in[None], out_out[None], table_grad)


def solution(mesh):
    return jax.shard_map(
        local,
        mesh=mesh,
        in_specs=(
            P("section", None, "shard", None, None),
            P("section", "shard", None, None),
            P(None, "shard", None, None),
            P("section", None, None),
            P("section", None, None),
            P(None, "shard", None),
            P(),
        ),
        out_specs=(
            P("section", "shard", None),
            P("section", "shard", None),
            P(("section", "shard"), None),
        ),
        check_vma=False,
    )
```

```python
import jax
import jax.numpy as jnp
from jax import lax
from jax.experimental import pallas as pl
from jax.experimental.pallas import tpu as pltpu
from jax.sharding import PartitionSpec as P

ROWS_OWN = 1024
MESH = pl.DeviceIdType.MESH
F32 = jnp.float32
BF16 = jnp.bfloat16

SECTIONS = 4
SHARDS = 32
SIDE = 4
MICRO = 4
TOK = 256
CHUNK = 64
WIDTH = 1024
SHARE = WIDTH // SHARDS
PER_PLANE = TOK // SECTIONS
TILE = 256
WIDE = 512
CHUNKS = TOK // CHUNK


def dot_tn(a, b):
    return lax.dot_general(a, b, (((0,), (0,)), ((), ())), preferred_element_type=F32)


def kernel(
    holder,
    saved,
    pooled,
    grad_top,
    w_in,
    w_out,
    ids,
    out_in,
    out_out,
    out_rows,
    out_named,
    win,
    wout,
    win_t,
    wout_t,
    xbuf,
    gbuf,
    nbuf,
    pbuf,
    act,
    slope,
    dz,
    acc,
    rank,
    all_ids,
    sorted_rows,
    routed,
    spread,
    send_a,
    recv_a,
    send_b,
    recv_b,
    own_b,
    send_c,
    recv_c,
    load_sem,
    top_sem,
    pool_send,
    pool_recv,
    relay_send,
    relay_recv,
    route_send,
    route_recv,
    spread_send,
    spread_recv,
    ids_send,
    ids_recv,
    a_send,
    a_recv,
    b_send,
    b_recv,
    c_send,
    c_recv,
):
    sec = lax.axis_index("section")
    sh = lax.axis_index("shard")
    core = sh % 2
    px = (sh // 2) % SIDE
    py = sh // (2 * SIDE)
    first = sec == 0
    last = sec == SECTIONS - 1

    def at(y, x, c):
        return (sec, (y * SIDE + x) * 2 + c)

    def micro_rows(m):
        return pl.ds(pl.multiple_of(m * TOK, TOK), TOK)

    def chunk_rows(c):
        return pl.ds(pl.multiple_of(c * CHUNK, CHUNK), CHUNK)

    def load_x(m):
        rows = micro_rows(m)
        return pltpu.make_async_copy(saved.at[rows], xbuf.at[rows], load_sem.at[2 + m])

    def load_top(m):
        rows = micro_rows(m)
        return pltpu.make_async_copy(grad_top.at[rows], gbuf.at[rows], top_sem.at[m])

    load_win = pltpu.make_async_copy(w_in, win, load_sem.at[0])
    load_wout = pltpu.make_async_copy(w_out, wout, load_sem.at[1])
    load_pool = pltpu.make_async_copy(pooled, pbuf.at[0], load_sem.at[2 + MICRO])

    load_win.start()
    load_x(0).start()
    load_wout.start()

    @pl.when(last)
    def _():
        for m in range(MICRO):
            load_top(m).start()

    for m in range(1, MICRO):
        load_x(m).start()

    @pl.when(first)
    def _():
        load_pool.start()

    barrier = pltpu.get_barrier_semaphore()

    def greet(k, carry):
        pl.semaphore_signal(
            barrier, inc=1, device_id=(sec, (sh + k) % SHARDS), device_id_type=MESH
        )
        return carry

    lax.fori_loop(1, SHARDS, greet, 0)
    for k in range(1, SECTIONS):
        pl.semaphore_signal(
            barrier, inc=1, device_id=((sec + k) % SECTIONS, sh), device_id_type=MESH
        )

    def pool_copy(s):
        return pltpu.make_async_remote_copy(
            src_ref=pooled,
            dst_ref=pbuf.at[s],
            send_sem=pool_send,
            recv_sem=pool_recv.at[s],
            device_id=(0, sh),
            device_id_type=MESH,
        )

    def relay_copy(c):
        rows = chunk_rows(c)
        return pltpu.make_async_remote_copy(
            src_ref=nbuf.at[rows],
            dst_ref=gbuf.at[rows],
            send_sem=relay_send.at[c],
            recv_sem=relay_recv.at[c],
            device_id=(jnp.maximum(sec - 1, 0), sh),
            device_id_type=MESH,
        )

    def route_copy(m, p):
        return pltpu.make_async_remote_copy(
            src_ref=sorted_rows.at[m, pl.ds(p * PER_PLANE, PER_PLANE)],
            dst_ref=routed.at[pl.ds(pl.multiple_of(m * PER_PLANE, PER_PLANE), PER_PLANE)],
            send_sem=route_send.at[m, p],
            recv_sem=route_recv.at[m],
            device_id=(p, sh),
            device_id_type=MESH,
        )

    def ids_copy(k, to, came):
        return pltpu.make_async_remote_copy(
            src_ref=ids,
            dst_ref=all_ids.at[came],
            send_sem=ids_send.at[k],
            recv_sem=ids_recv.at[k],
            device_id=(sec, to),
            device_id_type=MESH,
        )

    def forward(m):
        rows = micro_rows(m)
        load_x(m).wait()

        @pl.when(first)
        def _():
            slot = 0
            for j in range(1, MICRO):
                slot = jnp.where(holder[j] == m, j, slot)
            extra = pbuf[slot]
            xbuf[rows, :] = (xbuf[rows, :].astype(F32) + extra.astype(F32)).astype(BF16)

        for j in range(WIDTH // TILE):
            cols = pl.ds(j * TILE, TILE)
            z = jnp.dot(xbuf[rows, :], win[:, cols], preferred_element_type=F32)
            sig = jax.nn.sigmoid(z)
            act[:, cols] = (z * sig).astype(BF16)
            slope[:, cols] = sig * (1.0 + z * (1.0 - sig))

    def backward(c, k):
        crows = chunk_rows(c)
        krows = pl.ds(k * CHUNK, CHUNK)
        for j in range(WIDTH // WIDE):
            cols = pl.ds(j * WIDE, WIDE)
            ga = jnp.dot(gbuf[crows, :], wout_t[:, cols], preferred_element_type=F32)
            dz[krows, cols] = (ga * slope[krows, cols]).astype(BF16)
        for j in range(WIDTH // WIDE):
            cols = pl.ds(j * WIDE, WIDE)
            back = jnp.dot(dz[krows, :], win_t[:, cols], preferred_element_type=F32)
            nbuf[crows, cols] = (gbuf[crows, cols].astype(F32) + back).astype(BF16)

    def weight_grads(m):
        rows = micro_rows(m)
        for i in range(WIDTH // TILE):
            cols = pl.ds(i * TILE, TILE)
            acc[0, cols, :] += dot_tn(xbuf[rows, cols], dz[...])
            acc[1, cols, :] += dot_tn(act[:, cols], gbuf[rows, :])

    load_win.wait()
    for j in range(WIDTH // TILE):
        cols = pl.ds(j * TILE, TILE)
        win_t[:, cols] = win[cols, :].T

    @pl.when(jnp.logical_not(first))
    def _():
        forward(0)

    load_wout.wait()
    for j in range(WIDTH // TILE):
        cols = pl.ds(j * TILE, TILE)
        wout_t[:, cols] = wout[cols, :].T

    pl.semaphore_wait(barrier, SHARDS - 1 + SECTIONS - 1)

    @pl.when(jnp.logical_not(first))
    def _():
        pool_copy(sec).start()

    def clear(i, carry):
        rows = pl.ds(pl.multiple_of(i * 64, 64), 64)
        for mat in range(2):
            acc[mat, rows, :] = jnp.zeros((64, WIDTH), F32)
        return carry

    def tell_ids(k, carry):
        ids_copy(k, (sh + k) % SHARDS, sh).start()
        return carry

    @pl.when(first)
    def _():
        lax.fori_loop(0, WIDTH // 64, clear, 0)
        lax.fori_loop(1, SHARDS, tell_ids, 0)
        row = lax.broadcasted_iota(jnp.int32, (TOK, TOK), 0)
        col = lax.broadcasted_iota(jnp.int32, (TOK, TOK), 1)
        feat = ids.shape[1]
        lane = lax.broadcasted_iota(jnp.int32, (ids.shape[2], TOK), 1)
        lead = lax.broadcasted_iota(jnp.int32, (ids.shape[2], TOK), 0)
        widen = jnp.where(lane >> 3 == lead, 1.0, 0.0).astype(BF16)
        for m in range(MICRO):
            owner = (ids[m] >> 10).astype(F32).astype(BF16)
            wide = jnp.dot(owner, widen, preferred_element_type=F32)
            inner = lax.broadcasted_iota(jnp.int32, (feat, TOK), 1) & 7
            outer = lax.broadcasted_iota(jnp.int32, (feat, TOK), 0)
            across = jnp.sum(jnp.where(inner == outer, wide, 0.0), axis=0, keepdims=True)
            down = jnp.sum(jnp.where(row == col, across, 0.0), axis=1, keepdims=True)
            earlier = jnp.where((down == across) & (row < col), 1.0, 0.0)
            rank[m] = 2.0 * across + jnp.sum(earlier, axis=0, keepdims=True)
        load_pool.wait()
        for s in range(1, SECTIONS):
            pool_copy(s).wait_recv()
        forward(0)

    @pl.when(last)
    def _():
        load_top(0).wait()
        for k in range(CHUNKS):
            backward(k, k)
            relay_copy(k).start()

    @pl.when(jnp.logical_not(first))
    def _():
        lax.fori_loop(0, WIDTH // 64, clear, 0)
        lax.fori_loop(1, SHARDS, tell_ids, 0)

    all_ids[sh] = ids[...]

    def micro_step(m, carry):
        rows = micro_rows(m)

        @pl.when(jnp.logical_not(last & (m == 0)))
        def _():
            @pl.when(last)
            def _():
                load_top(m).wait()

            for k in range(CHUNKS):
                c = m * CHUNKS + k

                @pl.when(jnp.logical_not(last))
                def _():
                    relay_copy(c).wait_recv()

                backward(c, k)

                @pl.when(jnp.logical_not(first))
                def _():
                    relay_copy(c).start()

        @pl.when(first)
        def _():
            target = lax.broadcasted_iota(jnp.int32, (TOK, TOK), 0).astype(F32)
            pick = jnp.where(target == rank[m], 1.0, 0.0).astype(BF16)
            ordered = jnp.dot(pick, nbuf[rows, :], preferred_element_type=F32).astype(BF16)
            sorted_rows[m] = ordered
            for p in range(1, SECTIONS):
                route_copy(m, p).start()
            routed[pl.ds(pl.multiple_of(m * PER_PLANE, PER_PLANE), PER_PLANE), :] = ordered[
                :PER_PLANE, :
            ]

        weight_grads(m)

        @pl.when(m < MICRO - 1)
        def _():
            forward(m + 1)

        return carry

    lax.fori_loop(0, MICRO, micro_step, 0)

    def mine(mat):
        return px if mat == 0 else py

    def acc_rows(mat, t, o, c):
        block = (o * SIDE + t) if mat == 0 else (t * SIDE + o)
        return pl.ds(pl.multiple_of(block * 2 * SHARE + c * SHARE, SHARE), SHARE)

    def a_copy(mat, t):
        return pltpu.make_async_remote_copy(
            src_ref=send_a.at[mat, t],
            dst_ref=recv_a.at[mat, t],
            send_sem=a_send.at[mat, t],
            recv_sem=a_recv.at[mat, t],
            device_id=at(py, px, 1 - core),
            device_id_type=MESH,
        )

    def b_copy(mat, d):
        t = (mine(mat) + d) % SIDE
        return pltpu.make_async_remote_copy(
            src_ref=send_b.at[mat, d - 1],
            dst_ref=recv_b.at[mat, d - 1],
            send_sem=b_send.at[mat, d - 1],
            recv_sem=b_recv.at[mat, d - 1],
            device_id=at(py, t, core) if mat == 0 else at(t, px, core),
            device_id_type=MESH,
        )

    def c_copy(mat, d):
        t = (mine(1 - mat) + d) % SIDE
        return pltpu.make_async_remote_copy(
            src_ref=send_c.at[mat, d - 1],
            dst_ref=recv_c.at[mat, d - 1],
            send_sem=c_send.at[mat, d - 1],
            recv_sem=c_recv.at[mat, d - 1],
            device_id=at(t, px, core) if mat == 0 else at(py, t, core),
            device_id_type=MESH,
        )

    order = (2, 1, 3, 0)
    for d in order:
        for mat in range(2):
            t = (mine(mat) + d) % SIDE

            def fill_a(o, carry, mat=mat, t=t):
                send_a[mat, t, o] = acc[mat, acc_rows(mat, t, o, 1 - core), :].astype(BF16)
                return carry

            lax.fori_loop(0, SIDE, fill_a, 0)
            a_copy(mat, t).start()

    for d in order:
        for mat in range(2):
            t = (mine(mat) + d) % SIDE
            a_copy(mat, t).wait_recv()

            def add_a(o, carry, mat=mat, t=t, d=d):
                both = acc[mat, acc_rows(mat, t, o, core), :] + recv_a[mat, t, o].astype(F32)
                if d == 0:
                    own_b[mat, o] = both
                else:
                    send_b[mat, d - 1, o] = both.astype(BF16)
                return carry

            lax.fori_loop(0, SIDE, add_a, 0)
            if d != 0:
                b_copy(mat, d).start()

    @pl.when(jnp.logical_not(first))
    def _():
        for m in range(MICRO):
            route_copy(m, 1).wait_recv()

    row = lax.broadcasted_iota(jnp.int32, (TOK, TOK), 0)
    col = lax.broadcasted_iota(jnp.int32, (TOK, TOK), 1)
    source = ((row >> 1) & 3) * PER_PLANE + (row >> 3) * 2 + (row & 1)
    regroup = jnp.where(source == col, 1.0, 0.0).astype(BF16)
    by_owner = jnp.dot(regroup, routed[...], preferred_element_type=F32)
    spread[...] = by_owner.reshape(SHARDS, 2 * MICRO, WIDTH).astype(BF16)

    def spread_copy(k, to, came):
        return pltpu.make_async_remote_copy(
            src_ref=spread.at[to],
            dst_ref=out_rows.at[came],
            send_sem=spread_send.at[k],
            recv_sem=spread_recv.at[k],
            device_id=(sec, to),
            device_id_type=MESH,
        )

    def hand_out(k, carry):
        spread_copy(k, (sh + k) % SHARDS, sh).start()
        return carry

    lax.fori_loop(1, SHARDS, hand_out, 0)
    out_rows[sh] = spread[sh]

    def hear_ids(k, carry):
        ids_copy(k, (sh + k) % SHARDS, (sh + SHARDS - k) % SHARDS).wait_recv()
        return carry

    lax.fori_loop(1, SHARDS, hear_ids, 0)
    own = sec * SHARDS + sh
    feature = own // (SECTIONS * SHARDS // ids.shape[1])
    heard = all_ids[:, :, feature, :].reshape(SHARDS * MICRO, ids.shape[2])
    place = lax.broadcasted_iota(jnp.int32, heard.shape, 1) * ROWS_OWN + (heard & (ROWS_OWN - 1))
    ours = heard >> 10 == own
    low = jnp.min(jnp.where(ours, place, 1 << 20), axis=1, keepdims=True) & (ROWS_OWN - 1)
    high = jnp.max(jnp.where(ours, place, -1), axis=1, keepdims=True) & (ROWS_OWN - 1)
    at_lane = lax.broadcasted_iota(jnp.int32, (SHARDS * MICRO, 128), 1)
    parts = jnp.where(
        at_lane == 0,
        low >> 5,
        jnp.where(at_lane == 1, low & 31, jnp.where(at_lane == 2, high >> 5, high & 31)),
    )
    half = lax.broadcasted_iota(jnp.int32, (TOK, SHARDS * MICRO), 0) >> 1
    twice = jnp.where(
        half == lax.broadcasted_iota(jnp.int32, (TOK, SHARDS * MICRO), 1), 1.0, 0.0
    ).astype(BF16)
    both = jnp.dot(twice, parts.astype(F32).astype(BF16), preferred_element_type=F32)
    odd = lax.broadcasted_iota(jnp.int32, (TOK, 1), 0) & 1
    row_of = jnp.where(
        odd == 0, both[:, 0:1] * 32.0 + both[:, 1:2], both[:, 2:3] * 32.0 + both[:, 3:4]
    )
    out_named[...] = jnp.broadcast_to(row_of.astype(jnp.int32), (TOK, 128))

    for d in range(1, SIDE):
        for mat in range(2):
            b_copy(mat, d).wait_recv()
    for mat in range(2):

        def add_b(o, carry, mat=mat):
            total = own_b[mat, o]
            for d in range(1, SIDE):
                total = total + recv_b[mat, d - 1, o].astype(F32)
            own_b[mat, o] = total
            return carry

        lax.fori_loop(0, SIDE, add_b, 0)
        for d in (2, 1, 3):
            t = (mine(1 - mat) + d) % SIDE
            send_c[mat, d - 1] = own_b[mat, t].astype(BF16)
            c_copy(mat, d).start()

    for mat, out in ((0, out_in), (1, out_out)):
        total = own_b[mat, mine(1 - mat)]
        for d in range(1, SIDE):
            c_copy(mat, d).wait_recv()
            total = total + recv_c[mat, d - 1].astype(F32)
        out[...] = total

    def collect(k, carry):
        spread_copy(k, (sh + k) % SHARDS, (sh + SHARDS - k) % SHARDS).wait_recv()
        return carry

    lax.fori_loop(1, SHARDS, collect, 0)

    @pl.when(jnp.logical_not(first))
    def _():
        pool_copy(sec).wait_send()

        def left(c, carry):
            relay_copy(c).wait_send()
            return carry

        lax.fori_loop(0, MICRO * CHUNKS, left, 0)

    @pl.when(first)
    def _():
        for m in range(MICRO):
            for p in range(1, SECTIONS):
                route_copy(m, p).wait_send()

    def spread_left(k, carry):
        spread_copy(k, (sh + k) % SHARDS, sh).wait_send()
        return carry

    lax.fori_loop(1, SHARDS, spread_left, 0)

    def ids_left(k, carry):
        ids_copy(k, (sh + k) % SHARDS, sh).wait_send()
        return carry

    lax.fori_loop(1, SHARDS, ids_left, 0)
    for mat in range(2):
        for t in range(SIDE):
            a_copy(mat, t).wait_send()
        for d in range(1, SIDE):
            b_copy(mat, d).wait_send()
            c_copy(mat, d).wait_send()


def relay(holder, saved, pooled, grad_top, w_in, w_out, ids):
    vmem = pl.BlockSpec(memory_space=pltpu.VMEM)
    anywhere = pl.BlockSpec(memory_space=pl.ANY)
    dma = pltpu.SemaphoreType.DMA
    tokens = MICRO * TOK
    return pl.pallas_call(
        kernel,
        out_shape=(
            jax.ShapeDtypeStruct((SHARE, WIDTH), F32),
            jax.ShapeDtypeStruct((SHARE, WIDTH), F32),
            jax.ShapeDtypeStruct((SHARDS, 2 * MICRO, WIDTH), BF16),
            jax.ShapeDtypeStruct((TOK, 128), jnp.int32),
        ),
        in_specs=[pl.BlockSpec(memory_space=pltpu.SMEM)] + [anywhere] * 5 + [vmem],
        out_specs=(vmem, vmem, vmem, vmem),
        scratch_shapes=[
            pltpu.VMEM((WIDTH, WIDTH), BF16),
            pltpu.VMEM((WIDTH, WIDTH), BF16),
            pltpu.VMEM((WIDTH, WIDTH), BF16),
            pltpu.VMEM((WIDTH, WIDTH), BF16),
            pltpu.VMEM((tokens, WIDTH), BF16),
            pltpu.VMEM((tokens, WIDTH), BF16),
            pltpu.VMEM((tokens, WIDTH), BF16),
            pltpu.VMEM((SECTIONS, TOK, WIDTH), BF16),
            pltpu.VMEM((TOK, WIDTH), BF16),
            pltpu.VMEM((TOK, WIDTH), F32),
            pltpu.VMEM((TOK, WIDTH), BF16),
            pltpu.VMEM((2, WIDTH, WIDTH), F32),
            pltpu.VMEM((MICRO, 1, TOK), F32),
            pltpu.VMEM((SHARDS,) + ids.shape, jnp.int32),
            pltpu.VMEM((MICRO, TOK, WIDTH), BF16),
            pltpu.VMEM((TOK, WIDTH), BF16),
            pltpu.VMEM((SHARDS, 2 * MICRO, WIDTH), BF16),
            pltpu.VMEM((2, SIDE, SIDE, SHARE, WIDTH), BF16),
            pltpu.VMEM((2, SIDE, SIDE, SHARE, WIDTH), BF16),
            pltpu.VMEM((2, SIDE - 1, SIDE, SHARE, WIDTH), BF16),
            pltpu.VMEM((2, SIDE - 1, SIDE, SHARE, WIDTH), BF16),
            pltpu.VMEM((2, SIDE, SHARE, WIDTH), F32),
            pltpu.VMEM((2, SIDE - 1, SHARE, WIDTH), BF16),
            pltpu.VMEM((2, SIDE - 1, SHARE, WIDTH), BF16),
            dma((3 + MICRO,)),
            dma((MICRO,)),
            dma,
            dma((SECTIONS,)),
            dma((MICRO * CHUNKS,)),
            dma((MICRO * CHUNKS,)),
            dma((MICRO, SECTIONS)),
            dma((MICRO,)),
            dma((SHARDS,)),
            dma((SHARDS,)),
            dma((SHARDS,)),
            dma((SHARDS,)),
            dma((2, SIDE)),
            dma((2, SIDE)),
            dma((2, SIDE - 1)),
            dma((2, SIDE - 1)),
            dma((2, SIDE - 1)),
            dma((2, SIDE - 1)),
        ],
        compiler_params=pltpu.CompilerParams(
            collective_id=0, has_side_effects=True, vmem_limit_bytes=56 * 1024 * 1024
        ),
        cost_estimate=pl.CostEstimate(
            flops=10 * tokens * WIDTH * WIDTH, bytes_accessed=9 * 2**20, transcendentals=tokens * WIDTH
        ),
        name="relay",
    )(holder, saved, pooled, grad_top, w_in, w_out, ids)


def table_kernel(named, rows, grad_in, grad_out, table, out_in, out_out):
    block = pl.program_id(0)
    lane = lax.broadcasted_iota(jnp.int32, (TOK, TILE), 1) + block * TILE
    hit = jnp.where(lane == named[:, 0:1], 1.0, 0.0).astype(BF16)
    table[...] = dot_tn(hit, rows[...])

    @pl.when(block == 0)
    def _():
        out_in[...] = grad_in[...]
        out_out[...] = grad_out[...]


def owner_sums(named, rows, grad_in, grad_out):
    def whole(array):
        return pl.BlockSpec(array.shape, lambda b: (0, 0))

    return pl.pallas_call(
        table_kernel,
        grid=(ROWS_OWN // TILE,),
        out_shape=(
            jax.ShapeDtypeStruct((ROWS_OWN, WIDTH), F32),
            jax.ShapeDtypeStruct(grad_in.shape, F32),
            jax.ShapeDtypeStruct(grad_out.shape, F32),
        ),
        in_specs=[whole(named), whole(rows), whole(grad_in), whole(grad_out)],
        out_specs=(
            pl.BlockSpec((TILE, WIDTH), lambda b: (b, 0)),
            whole(grad_in),
            whole(grad_out),
        ),
        cost_estimate=pl.CostEstimate(
            flops=2 * ROWS_OWN * TOK * WIDTH, bytes_accessed=5 * 2**20, transcendentals=0
        ),
        name="owner_sums",
    )(named, rows, grad_in, grad_out)


def local(saved, pooled, grad_top, w_in, w_out, feature_ids, holder_order):
    tokens = MICRO * TOK
    out_in, out_out, rows, named = relay(
        holder_order,
        saved.reshape(tokens, WIDTH),
        pooled.reshape(TOK, WIDTH),
        grad_top.reshape(tokens, WIDTH),
        w_in[0],
        w_out[0],
        jnp.transpose(feature_ids, (0, 2, 1)),
    )
    table_grad, grad_in, grad_out = owner_sums(named, rows.reshape(TOK, WIDTH), out_in, out_out)
    return (grad_in[None], grad_out[None], table_grad)


def solution(mesh):
    return jax.shard_map(
        local,
        mesh=mesh,
        in_specs=(
            P("section", None, "shard", None, None),
            P("section", "shard", None, None),
            P(None, "shard", None, None),
            P("section", None, None),
            P("section", None, None),
            P(None, "shard", None),
            P(),
        ),
        out_specs=(
            P("section", "shard", None),
            P("section", "shard", None),
            P(("section", "shard"), None),
        ),
        check_vma=False,
    )
```

```python
import jax
import jax.numpy as jnp
from jax import lax
from jax.experimental import pallas as pl
from jax.experimental.pallas import tpu as pltpu
from jax.sharding import PartitionSpec as P

ROWS_OWN = 1024
MESH = pl.DeviceIdType.MESH
F32 = jnp.float32
BF16 = jnp.bfloat16

SECTIONS = 4
SHARDS = 32
SIDE = 4
MICRO = 4
TOK = 256
CHUNK = 64
LATE = 32
WIDTH = 1024
SHARE = WIDTH // SHARDS
PER_PLANE = TOK // SECTIONS
TILE = 256
WIDE = 512
CHUNKS = TOK // CHUNK
EARLY = (MICRO - 1) * CHUNKS
LATES = TOK // LATE
PIECES = EARLY + LATES
HALF = WIDTH // 2
BLOCK = 2 * SHARE


def dot_tn(a, b):
    return lax.dot_general(a, b, (((0,), (0,)), ((), ())), preferred_element_type=F32)


def kernel(
    holder,
    saved,
    pooled,
    grad_top,
    w_in,
    w_out,
    ids,
    out_in,
    out_out,
    out_rows,
    out_named,
    win,
    wout,
    win_t,
    wout_t,
    xbuf,
    gbuf,
    nbuf,
    pbuf,
    act,
    slope,
    dz,
    acc,
    rank,
    all_ids,
    sorted_rows,
    routed,
    spread,
    peer_l,
    peer_r,
    send_x,
    recv_x,
    send_y,
    recv_y,
    own_c,
    send_c,
    recv_c,
    load_sem,
    top_sem,
    pool_send,
    pool_recv,
    relay_send,
    relay_recv,
    route_send,
    route_recv,
    spread_send,
    spread_recv,
    ids_send,
    ids_recv,
    l_send,
    l_recv,
    r_send,
    r_recv,
    x_send,
    x_recv,
    y_send,
    y_recv,
    c_send,
    c_recv,
):
    sec = lax.axis_index("section")
    sh = lax.axis_index("shard")
    core = sh % 2
    px = (sh // 2) % SIDE
    py = sh // (2 * SIDE)
    first = sec == 0
    last = sec == SECTIONS - 1

    def at(y, x, c):
        return (sec, (y * SIDE + x) * 2 + c)

    def micro_rows(m):
        return pl.ds(pl.multiple_of(m * TOK, TOK), TOK)

    def chunk_rows(c, size):
        start = c * CHUNK if size == CHUNK else EARLY * CHUNK + (c - EARLY) * LATE
        return pl.ds(pl.multiple_of(start, size), size)

    def load_x(m):
        rows = micro_rows(m)
        return pltpu.make_async_copy(saved.at[rows], xbuf.at[rows], load_sem.at[2 + m])

    def load_top(m):
        rows = micro_rows(m)
        return pltpu.make_async_copy(grad_top.at[rows], gbuf.at[rows], top_sem.at[m])

    load_win = pltpu.make_async_copy(w_in, win, load_sem.at[0])
    load_wout = pltpu.make_async_copy(w_out, wout, load_sem.at[1])
    load_pool = pltpu.make_async_copy(pooled, pbuf.at[0], load_sem.at[2 + MICRO])

    load_win.start()
    load_x(0).start()
    load_wout.start()

    @pl.when(last)
    def _():
        for m in range(MICRO):
            load_top(m).start()

    for m in range(1, MICRO):
        load_x(m).start()

    @pl.when(first)
    def _():
        load_pool.start()

    barrier = pltpu.get_barrier_semaphore()

    def greet(k, carry):
        pl.semaphore_signal(
            barrier, inc=1, device_id=(sec, (sh + k) % SHARDS), device_id_type=MESH
        )
        return carry

    lax.fori_loop(1, SHARDS, greet, 0)
    for k in range(1, SECTIONS):
        pl.semaphore_signal(
            barrier, inc=1, device_id=((sec + k) % SECTIONS, sh), device_id_type=MESH
        )

    def pool_copy(s):
        return pltpu.make_async_remote_copy(
            src_ref=pooled,
            dst_ref=pbuf.at[s],
            send_sem=pool_send,
            recv_sem=pool_recv.at[s],
            device_id=(0, sh),
            device_id_type=MESH,
        )

    def relay_copy(c, size):
        rows = chunk_rows(c, size)
        return pltpu.make_async_remote_copy(
            src_ref=nbuf.at[rows],
            dst_ref=gbuf.at[rows],
            send_sem=relay_send.at[c],
            recv_sem=relay_recv.at[c],
            device_id=(jnp.maximum(sec - 1, 0), sh),
            device_id_type=MESH,
        )

    def route_copy(m, p):
        return pltpu.make_async_remote_copy(
            src_ref=sorted_rows.at[m, pl.ds(p * PER_PLANE, PER_PLANE)],
            dst_ref=routed.at[pl.ds(pl.multiple_of(m * PER_PLANE, PER_PLANE), PER_PLANE)],
            send_sem=route_send.at[m, p],
            recv_sem=route_recv.at[m],
            device_id=(p, sh),
            device_id_type=MESH,
        )

    def ids_copy(k, to, came):
        return pltpu.make_async_remote_copy(
            src_ref=ids,
            dst_ref=all_ids.at[came],
            send_sem=ids_send.at[k],
            recv_sem=ids_recv.at[k],
            device_id=(sec, to),
            device_id_type=MESH,
        )

    def left_copy(m, source):
        rows = micro_rows(m)
        return pltpu.make_async_remote_copy(
            src_ref=source.at[rows],
            dst_ref=peer_l.at[rows],
            send_sem=l_send.at[m],
            recv_sem=l_recv.at[m],
            device_id=at(py, px, 1 - core),
            device_id_type=MESH,
        )

    def right_copy(n, source, start, size):
        rows = pl.ds(pl.multiple_of(start, 64), size)
        return pltpu.make_async_remote_copy(
            src_ref=source.at[rows],
            dst_ref=peer_r.at[rows],
            send_sem=r_send.at[n],
            recv_sem=r_recv.at[n],
            device_id=at(py, px, 1 - core),
            device_id_type=MESH,
        )

    def send_left(m):
        @pl.when(core == 0)
        def _():
            left_copy(m, act).start()

        @pl.when(core == 1)
        def _():
            left_copy(m, xbuf).start()

    def send_right(n, start, size):
        @pl.when(core == 0)
        def _():
            right_copy(n, gbuf, start, size).start()

        @pl.when(core == 1)
        def _():
            right_copy(n, dz, start, size).start()

    def forward(m):
        rows = micro_rows(m)
        load_x(m).wait()

        @pl.when(first)
        def _():
            slot = 0
            for j in range(1, MICRO):
                slot = jnp.where(holder[j] == m, j, slot)
            extra = pbuf[slot]
            xbuf[rows, :] = (xbuf[rows, :].astype(F32) + extra.astype(F32)).astype(BF16)

        for j in range(WIDTH // TILE):
            cols = pl.ds(j * TILE, TILE)
            z = jnp.dot(xbuf[rows, :], win[:, cols], preferred_element_type=F32)
            sig = jax.nn.sigmoid(z)
            act[rows, cols] = (z * sig).astype(BF16)
            slope[:, cols] = sig * (1.0 + z * (1.0 - sig))

    def backward(c, k, size):
        crows = chunk_rows(c, size)
        krows = pl.ds(k * size, size)
        for j in range(WIDTH // WIDE):
            cols = pl.ds(j * WIDE, WIDE)
            ga = jnp.dot(gbuf[crows, :], wout_t[:, cols], preferred_element_type=F32)
            dz[crows, cols] = (ga * slope[krows, cols]).astype(BF16)
        for j in range(WIDTH // WIDE):
            cols = pl.ds(j * WIDE, WIDE)
            back = jnp.dot(dz[crows, :], win_t[:, cols], preferred_element_type=F32)
            nbuf[crows, cols] = (gbuf[crows, cols].astype(F32) + back).astype(BF16)

    def own_grads(m, and_peer):
        rows = micro_rows(m)
        for kind, left, right in ((0, xbuf, dz), (1, act, gbuf)):

            @pl.when(core == kind)
            def _(left=left, right=right):
                for i in range(WIDTH // TILE):
                    cols = pl.ds(i * TILE, TILE)
                    total = acc[cols, :] + dot_tn(left[rows, cols], right[rows, :])
                    if and_peer:
                        total = total + dot_tn(peer_l[rows, cols], peer_r[rows, :])
                    acc[cols, :] = total

    def weight_grads(m):
        left_copy(m, act).wait_recv()
        right_copy(m, dz, m * TOK, TOK).wait_recv()
        own_grads(m, True)

    load_win.wait()
    for j in range(WIDTH // TILE):
        cols = pl.ds(j * TILE, TILE)
        win_t[:, cols] = win[cols, :].T

    @pl.when(jnp.logical_not(first))
    def _():
        forward(0)

    load_wout.wait()
    for j in range(WIDTH // TILE):
        cols = pl.ds(j * TILE, TILE)
        wout_t[:, cols] = wout[cols, :].T

    pl.semaphore_wait(barrier, SHARDS - 1 + SECTIONS - 1)

    @pl.when(jnp.logical_not(first))
    def _():
        pool_copy(sec).start()

    def clear(i, carry):
        rows = pl.ds(pl.multiple_of(i * 64, 64), 64)
        acc[rows, :] = jnp.zeros((64, WIDTH), F32)
        return carry

    def tell_ids(k, carry):
        ids_copy(k, (sh + k) % SHARDS, sh).start()
        return carry

    @pl.when(first)
    def _():
        lax.fori_loop(0, WIDTH // 64, clear, 0)
        lax.fori_loop(1, SHARDS, tell_ids, 0)
        row = lax.broadcasted_iota(jnp.int32, (TOK, TOK), 0)
        col = lax.broadcasted_iota(jnp.int32, (TOK, TOK), 1)
        feat = ids.shape[1]
        lane = lax.broadcasted_iota(jnp.int32, (ids.shape[2], TOK), 1)
        lead = lax.broadcasted_iota(jnp.int32, (ids.shape[2], TOK), 0)
        widen = jnp.where(lane >> 3 == lead, 1.0, 0.0).astype(BF16)
        for m in range(MICRO):
            owner = (ids[m] >> 10).astype(F32).astype(BF16)
            wide = jnp.dot(owner, widen, preferred_element_type=F32)
            inner = lax.broadcasted_iota(jnp.int32, (feat, TOK), 1) & 7
            outer = lax.broadcasted_iota(jnp.int32, (feat, TOK), 0)
            across = jnp.sum(jnp.where(inner == outer, wide, 0.0), axis=0, keepdims=True)
            down = jnp.sum(jnp.where(row == col, across, 0.0), axis=1, keepdims=True)
            earlier = jnp.where((down == across) & (row < col), 1.0, 0.0)
            rank[m] = 2.0 * across + jnp.sum(earlier, axis=0, keepdims=True)
        load_pool.wait()
        for s in range(1, SECTIONS):
            pool_copy(s).wait_recv()
        forward(0)

    @pl.when(last)
    def _():
        load_top(0).wait()
        for k in range(CHUNKS):
            backward(k, k, CHUNK)
            relay_copy(k, CHUNK).start()

    @pl.when(jnp.logical_not(first))
    def _():
        lax.fori_loop(0, WIDTH // 64, clear, 0)
        lax.fori_loop(1, SHARDS, tell_ids, 0)

    all_ids[sh] = ids[...]
    send_left(0)

    def step(c, k, size):
        @pl.when(jnp.logical_not(last))
        def _():
            relay_copy(c, size).wait_recv()

        backward(c, k, size)

        @pl.when(jnp.logical_not(first))
        def _():
            relay_copy(c, size).start()

    def route(m):
        rows = micro_rows(m)

        @pl.when(first)
        def _():
            target = lax.broadcasted_iota(jnp.int32, (TOK, TOK), 0).astype(F32)
            pick = jnp.where(target == rank[m], 1.0, 0.0).astype(BF16)
            ordered = jnp.dot(pick, nbuf[rows, :], preferred_element_type=F32).astype(BF16)
            sorted_rows[m] = ordered
            for p in range(1, SECTIONS):
                route_copy(m, p).start()
            routed[pl.ds(pl.multiple_of(m * PER_PLANE, PER_PLANE), PER_PLANE), :] = ordered[
                :PER_PLANE, :
            ]

    def micro_step(m, carry):
        @pl.when(jnp.logical_not(last & (m == 0)))
        def _():
            @pl.when(last)
            def _():
                load_top(m).wait()

            for k in range(CHUNKS):
                step(m * CHUNKS + k, k, CHUNK)
                if k == 0:

                    @pl.when(m > 0)
                    def _():
                        weight_grads(m - 1)

        send_right(m, m * TOK, TOK)
        route(m)
        forward(m + 1)
        send_left(m + 1)
        return carry

    lax.fori_loop(0, MICRO - 1, micro_step, 0)

    final = MICRO - 1
    tail = TOK - 2 * LATE

    @pl.when(last)
    def _():
        load_top(final).wait()

    for k in range(LATES):
        step(EARLY + k, k, LATE)
        if k == 0:
            weight_grads(final - 1)
        if k == LATES - 3:
            send_right(final, final * TOK, tail)
    send_right(final + 1, final * TOK + tail, TOK - tail)
    route(final)
    own_grads(final, False)

    def block_rows(y, x):
        return pl.ds(pl.multiple_of((y * SIDE + x) * BLOCK, BLOCK), BLOCK)

    left_half = pl.ds(0, HALF)
    right_half = pl.ds(HALF, HALF)

    def x_copy(d, y):
        to = (px + d) % SIDE
        return pltpu.make_async_remote_copy(
            src_ref=send_x.at[y, pl.ds(pl.multiple_of(to * BLOCK, BLOCK), BLOCK)],
            dst_ref=recv_x.at[d - 1, y],
            send_sem=x_send.at[d - 1, y],
            recv_sem=x_recv.at[d - 1, y],
            device_id=at(py, to, core),
            device_id_type=MESH,
        )

    def y_copy(d):
        return pltpu.make_async_remote_copy(
            src_ref=send_y.at[d - 1],
            dst_ref=recv_y.at[d - 1],
            send_sem=y_send.at[d - 1],
            recv_sem=y_recv.at[d - 1],
            device_id=at((py + d) % SIDE, px, core),
            device_id_type=MESH,
        )

    def c_copy(h, e, c, kind):
        there = (py + e) % SIDE if h == 0 else (px + e) % SIDE
        return pltpu.make_async_remote_copy(
            src_ref=send_c.at[h, e, c],
            dst_ref=recv_c.at[kind, h, e],
            send_sem=c_send.at[h, e, c],
            recv_sem=c_recv.at[kind, h, e],
            device_id=at(there, px, c) if h == 0 else at(py, there, c),
            device_id_type=MESH,
        )

    order = (2, 1, 3, 0)
    frows = micro_rows(final)
    left_copy(final, act).wait_recv()
    right_copy(final, dz, final * TOK, tail).wait_recv()
    right_copy(final + 1, dz, final * TOK + tail, TOK - tail).wait_recv()
    for d in order:
        y = (py + d) % SIDE
        cols = pl.ds(pl.multiple_of(y * TILE, TILE), TILE)
        total = acc[cols, :] + dot_tn(peer_l[frows, cols], peer_r[frows, :])
        acc[cols, :] = total
        send_x[y] = total[:, :HALF].astype(BF16)
        for dx in (2, 1, 3):
            x_copy(dx, y).start()
        if d != 0:
            send_y[d - 1] = total[:, HALF:].astype(BF16)
            y_copy(d).start()

    @pl.when(jnp.logical_not(first))
    def _():
        for m in range(MICRO):
            route_copy(m, 1).wait_recv()

    row = lax.broadcasted_iota(jnp.int32, (TOK, TOK), 0)
    col = lax.broadcasted_iota(jnp.int32, (TOK, TOK), 1)
    source = ((row >> 1) & 3) * PER_PLANE + (row >> 3) * 2 + (row & 1)
    regroup = jnp.where(source == col, 1.0, 0.0).astype(BF16)
    by_owner = jnp.dot(regroup, routed[...], preferred_element_type=F32)
    spread[...] = by_owner.reshape(SHARDS, 2 * MICRO, WIDTH).astype(BF16)

    def spread_copy(k, to, came):
        return pltpu.make_async_remote_copy(
            src_ref=spread.at[to],
            dst_ref=out_rows.at[came],
            send_sem=spread_send.at[k],
            recv_sem=spread_recv.at[k],
            device_id=(sec, to),
            device_id_type=MESH,
        )

    def hand_out(k, carry):
        spread_copy(k, (sh + k) % SHARDS, sh).start()
        return carry

    lax.fori_loop(1, SHARDS, hand_out, 0)
    out_rows[sh] = spread[sh]

    def hear_ids(k, carry):
        ids_copy(k, (sh + k) % SHARDS, (sh + SHARDS - k) % SHARDS).wait_recv()
        return carry

    lax.fori_loop(1, SHARDS, hear_ids, 0)
    own = sec * SHARDS + sh
    feature = own // (SECTIONS * SHARDS // ids.shape[1])
    heard = all_ids[:, :, feature, :].reshape(SHARDS * MICRO, ids.shape[2])
    place = lax.broadcasted_iota(jnp.int32, heard.shape, 1) * ROWS_OWN + (heard & (ROWS_OWN - 1))
    ours = heard >> 10 == own
    low = jnp.min(jnp.where(ours, place, 1 << 20), axis=1, keepdims=True) & (ROWS_OWN - 1)
    high = jnp.max(jnp.where(ours, place, -1), axis=1, keepdims=True) & (ROWS_OWN - 1)
    at_lane = lax.broadcasted_iota(jnp.int32, (SHARDS * MICRO, 128), 1)
    parts = jnp.where(
        at_lane == 0,
        low >> 5,
        jnp.where(at_lane == 1, low & 31, jnp.where(at_lane == 2, high >> 5, high & 31)),
    )
    half = lax.broadcasted_iota(jnp.int32, (TOK, SHARDS * MICRO), 0) >> 1
    twice = jnp.where(
        half == lax.broadcasted_iota(jnp.int32, (TOK, SHARDS * MICRO), 1), 1.0, 0.0
    ).astype(BF16)
    both = jnp.dot(twice, parts.astype(F32).astype(BF16), preferred_element_type=F32)
    odd = lax.broadcasted_iota(jnp.int32, (TOK, 1), 0) & 1
    row_of = jnp.where(
        odd == 0, both[:, 0:1] * 32.0 + both[:, 1:2], both[:, 2:3] * 32.0 + both[:, 3:4]
    )
    out_named[...] = jnp.broadcast_to(row_of.astype(jnp.int32), (TOK, 128))

    for d in range(1, SIDE):
        y_copy(d).wait_recv()
    for e in order:
        y = (py + e) % SIDE
        for d in range(1, SIDE):
            x_copy(d, y).wait_recv()
        x = (px + e) % SIDE
        total = acc[block_rows(y, px), left_half]
        other = acc[block_rows(py, x), right_half]
        for d in range(1, SIDE):
            total = total + recv_x[d - 1, y].astype(F32)
            xrows = pl.ds(pl.multiple_of(x * BLOCK, BLOCK), BLOCK)
            other = other + recv_y[d - 1, xrows, :].astype(F32)
        for h, part in ((0, total), (1, other)):
            for c in range(2):
                send_c[h, e, c] = part[c * SHARE : (c + 1) * SHARE, :].astype(BF16)
                if e == 0:

                    @pl.when(core == c)
                    def _(h=h, c=c, part=part):
                        own_c[h] = part[c * SHARE : (c + 1) * SHARE, :]

                    @pl.when(core != c)
                    def _(h=h, c=c):
                        c_copy(h, 0, c, core).start()
                else:
                    c_copy(h, e, c, core).start()

    for kind, out in ((0, out_in), (1, out_out)):
        for h, cols in ((0, left_half), (1, right_half)):

            @pl.when(core == kind)
            def _(h=h, out=out, cols=cols):
                out[:, cols] = own_c[h]

            @pl.when(core != kind)
            def _(h=h, out=out, cols=cols, kind=kind):
                c_copy(h, 0, 1 - kind, kind).wait_recv()
                out[:, cols] = recv_c[kind, h, 0].astype(F32)

            total = out[:, cols]
            for e in range(1, SIDE):
                c_copy(h, e, 0, kind).wait_recv()
                total = total + recv_c[kind, h, e].astype(F32)
            out[:, cols] = total

    def collect(k, carry):
        spread_copy(k, (sh + k) % SHARDS, (sh + SHARDS - k) % SHARDS).wait_recv()
        return carry

    lax.fori_loop(1, SHARDS, collect, 0)

    @pl.when(jnp.logical_not(first))
    def _():
        pool_copy(sec).wait_send()

        def left(c, carry):
            relay_copy(c, CHUNK).wait_send()
            return carry

        lax.fori_loop(0, EARLY, left, 0)

        def left_late(c, carry):
            relay_copy(c, LATE).wait_send()
            return carry

        lax.fori_loop(EARLY, PIECES, left_late, 0)

    @pl.when(first)
    def _():
        for m in range(MICRO):
            for p in range(1, SECTIONS):
                route_copy(m, p).wait_send()

    def spread_left(k, carry):
        spread_copy(k, (sh + k) % SHARDS, sh).wait_send()
        return carry

    lax.fori_loop(1, SHARDS, spread_left, 0)

    def ids_left(k, carry):
        ids_copy(k, (sh + k) % SHARDS, sh).wait_send()
        return carry

    lax.fori_loop(1, SHARDS, ids_left, 0)
    for m in range(MICRO):
        left_copy(m, act).wait_send()
    for m in range(final):
        right_copy(m, dz, m * TOK, TOK).wait_send()
    right_copy(final, dz, final * TOK, tail).wait_send()
    right_copy(final + 1, dz, final * TOK + tail, TOK - tail).wait_send()
    for d in range(1, SIDE):
        y_copy(d).wait_send()
        for y in range(SIDE):
            x_copy(d, y).wait_send()
        for h in range(2):
            for c in range(2):
                c_copy(h, d, c, core).wait_send()
    for h in range(2):
        c_copy(h, 0, 1 - core, core).wait_send()


def relay(holder, saved, pooled, grad_top, w_in, w_out, ids):
    vmem = pl.BlockSpec(memory_space=pltpu.VMEM)
    anywhere = pl.BlockSpec(memory_space=pl.ANY)
    dma = pltpu.SemaphoreType.DMA
    tokens = MICRO * TOK
    return pl.pallas_call(
        kernel,
        out_shape=(
            jax.ShapeDtypeStruct((SHARE, WIDTH), F32),
            jax.ShapeDtypeStruct((SHARE, WIDTH), F32),
            jax.ShapeDtypeStruct((SHARDS, 2 * MICRO, WIDTH), BF16),
            jax.ShapeDtypeStruct((TOK, 128), jnp.int32),
        ),
        in_specs=[pl.BlockSpec(memory_space=pltpu.SMEM)] + [anywhere] * 5 + [vmem],
        out_specs=(vmem, vmem, vmem, vmem),
        scratch_shapes=[
            pltpu.VMEM((WIDTH, WIDTH), BF16),
            pltpu.VMEM((WIDTH, WIDTH), BF16),
            pltpu.VMEM((WIDTH, WIDTH), BF16),
            pltpu.VMEM((WIDTH, WIDTH), BF16),
            pltpu.VMEM((tokens, WIDTH), BF16),
            pltpu.VMEM((tokens, WIDTH), BF16),
            pltpu.VMEM((tokens, WIDTH), BF16),
            pltpu.VMEM((SECTIONS, TOK, WIDTH), BF16),
            pltpu.VMEM((tokens, WIDTH), BF16),
            pltpu.VMEM((TOK, WIDTH), F32),
            pltpu.VMEM((tokens, WIDTH), BF16),
            pltpu.VMEM((WIDTH, WIDTH), F32),
            pltpu.VMEM((MICRO, 1, TOK), F32),
            pltpu.VMEM((SHARDS,) + ids.shape, jnp.int32),
            pltpu.VMEM((MICRO, TOK, WIDTH), BF16),
            pltpu.VMEM((TOK, WIDTH), BF16),
            pltpu.VMEM((SHARDS, 2 * MICRO, WIDTH), BF16),
            pltpu.VMEM((tokens, WIDTH), BF16),
            pltpu.VMEM((tokens, WIDTH), BF16),
            pltpu.VMEM((SIDE, SIDE * BLOCK, HALF), BF16),
            pltpu.VMEM((SIDE - 1, SIDE, BLOCK, HALF), BF16),
            pltpu.VMEM((SIDE - 1, SIDE * BLOCK, HALF), BF16),
            pltpu.VMEM((SIDE - 1, SIDE * BLOCK, HALF), BF16),
            pltpu.VMEM((2, SHARE, HALF), F32),
            pltpu.VMEM((2, SIDE, 2, SHARE, HALF), BF16),
            pltpu.VMEM((2, 2, SIDE, SHARE, HALF), BF16),
            dma((3 + MICRO,)),
            dma((MICRO,)),
            dma,
            dma((SECTIONS,)),
            dma((PIECES,)),
            dma((PIECES,)),
            dma((MICRO, SECTIONS)),
            dma((MICRO,)),
            dma((SHARDS,)),
            dma((SHARDS,)),
            dma((SHARDS,)),
            dma((SHARDS,)),
            dma((MICRO,)),
            dma((MICRO,)),
            dma((MICRO + 1,)),
            dma((MICRO + 1,)),
            dma((SIDE - 1, SIDE)),
            dma((SIDE - 1, SIDE)),
            dma((SIDE - 1,)),
            dma((SIDE - 1,)),
            dma((2, SIDE, 2)),
            dma((2, 2, SIDE)),
        ],
        compiler_params=pltpu.CompilerParams(
            collective_id=0, has_side_effects=True, vmem_limit_bytes=56 * 1024 * 1024
        ),
        cost_estimate=pl.CostEstimate(
            flops=10 * tokens * WIDTH * WIDTH, bytes_accessed=9 * 2**20, transcendentals=tokens * WIDTH
        ),
        name="relay",
    )(holder, saved, pooled, grad_top, w_in, w_out, ids)


def table_kernel(named, rows, grad_in, grad_out, table, out_in, out_out):
    block = pl.program_id(0)
    lane = lax.broadcasted_iota(jnp.int32, (TOK, TILE), 1) + block * TILE
    hit = jnp.where(lane == named[:, 0:1], 1.0, 0.0).astype(BF16)
    table[...] = dot_tn(hit, rows[...])

    @pl.when(block == 0)
    def _():
        out_in[...] = grad_in[...]
        out_out[...] = grad_out[...]


def owner_sums(named, rows, grad_in, grad_out):
    def whole(array):
        return pl.BlockSpec(array.shape, lambda b: (0, 0))

    return pl.pallas_call(
        table_kernel,
        grid=(ROWS_OWN // TILE,),
        out_shape=(
            jax.ShapeDtypeStruct((ROWS_OWN, WIDTH), F32),
            jax.ShapeDtypeStruct(grad_in.shape, F32),
            jax.ShapeDtypeStruct(grad_out.shape, F32),
        ),
        in_specs=[whole(named), whole(rows), whole(grad_in), whole(grad_out)],
        out_specs=(
            pl.BlockSpec((TILE, WIDTH), lambda b: (b, 0)),
            whole(grad_in),
            whole(grad_out),
        ),
        cost_estimate=pl.CostEstimate(
            flops=2 * ROWS_OWN * TOK * WIDTH, bytes_accessed=5 * 2**20, transcendentals=0
        ),
        name="owner_sums",
    )(named, rows, grad_in, grad_out)


def local(saved, pooled, grad_top, w_in, w_out, feature_ids, holder_order):
    tokens = MICRO * TOK
    out_in, out_out, rows, named = relay(
        holder_order,
        saved.reshape(tokens, WIDTH),
        pooled.reshape(TOK, WIDTH),
        grad_top.reshape(tokens, WIDTH),
        w_in[0],
        w_out[0],
        jnp.transpose(feature_ids, (0, 2, 1)),
    )
    table_grad, grad_in, grad_out = owner_sums(named, rows.reshape(TOK, WIDTH), out_in, out_out)
    return (grad_in[None], grad_out[None], table_grad)


def solution(mesh):
    return jax.shard_map(
        local,
        mesh=mesh,
        in_specs=(
            P("section", None, "shard", None, None),
            P("section", "shard", None, None),
            P(None, "shard", None, None),
            P("section", None, None),
            P("section", None, None),
            P(None, "shard", None),
            P(),
        ),
        out_specs=(
            P("section", "shard", None),
            P("section", "shard", None),
            P(("section", "shard"), None),
        ),
        check_vma=False,
    )
```

```python
import jax
import jax.numpy as jnp
from jax import lax
from jax.experimental import pallas as pl
from jax.experimental.pallas import tpu as pltpu
from jax.sharding import PartitionSpec as P

ROWS_OWN = 1024
MESH = pl.DeviceIdType.MESH
F32 = jnp.float32
BF16 = jnp.bfloat16

SECTIONS = 4
SHARDS = 32
SIDE = 4
MICRO = 4
TOK = 256
CHUNK = 64
LATE = 32
WIDTH = 1024
SHARE = WIDTH // SHARDS
PER_PLANE = TOK // SECTIONS
TILE = 256
WIDE = 512
CHUNKS = TOK // CHUNK
EARLY = MICRO * CHUNKS - 1
PIECES = EARLY + CHUNK // LATE
SOON = (MICRO - 1) * PER_PLANE
HALF = WIDTH // 2
BLOCK = 2 * SHARE


def dot_tn(a, b):
    return lax.dot_general(a, b, (((0,), (0,)), ((), ())), preferred_element_type=F32)


def kernel(
    holder,
    saved,
    pooled,
    grad_top,
    w_in,
    w_out,
    ids,
    out_in,
    out_out,
    out_rows,
    out_named,
    win,
    wout,
    win_t,
    wout_t,
    xbuf,
    gbuf,
    nbuf,
    pbuf,
    act,
    slope,
    dz,
    acc,
    rank,
    all_ids,
    sorted_rows,
    routed,
    soon,
    got_soon,
    late,
    got_late,
    flat,
    peer_l,
    peer_r,
    send_x,
    recv_x,
    send_y,
    recv_y,
    own_c,
    send_c,
    recv_c,
    load_sem,
    top_sem,
    pool_send,
    pool_recv,
    relay_send,
    relay_recv,
    route_send,
    route_recv,
    soon_send,
    soon_recv,
    late_send,
    late_recv,
    ready,
    ids_send,
    ids_recv,
    l_send,
    l_recv,
    r_send,
    r_recv,
    x_send,
    x_recv,
    y_send,
    y_recv,
    c_send,
    c_recv,
):
    sec = lax.axis_index("section")
    sh = lax.axis_index("shard")
    core = sh % 2
    px = (sh // 2) % SIDE
    py = sh // (2 * SIDE)
    first = sec == 0
    last = sec == SECTIONS - 1

    def at(y, x, c):
        return (sec, (y * SIDE + x) * 2 + c)

    def micro_rows(m):
        return pl.ds(pl.multiple_of(m * TOK, TOK), TOK)

    def chunk_rows(c, size):
        start = c * CHUNK if size == CHUNK else EARLY * CHUNK + (c - EARLY) * LATE
        return pl.ds(pl.multiple_of(start, size), size)

    def load_x(m):
        rows = micro_rows(m)
        return pltpu.make_async_copy(saved.at[rows], xbuf.at[rows], load_sem.at[2 + m])

    def load_top(m):
        rows = micro_rows(m)
        return pltpu.make_async_copy(grad_top.at[rows], gbuf.at[rows], top_sem.at[m])

    load_win = pltpu.make_async_copy(w_in, win, load_sem.at[0])
    load_wout = pltpu.make_async_copy(w_out, wout, load_sem.at[1])
    load_pool = pltpu.make_async_copy(pooled, pbuf.at[0], load_sem.at[2 + MICRO])

    load_win.start()
    load_x(0).start()
    load_wout.start()

    @pl.when(last)
    def _():
        for m in range(MICRO):
            load_top(m).start()

    for m in range(1, MICRO):
        load_x(m).start()

    @pl.when(first)
    def _():
        load_pool.start()

    barrier = pltpu.get_barrier_semaphore()

    def greet(y, x, c):
        pl.semaphore_signal(barrier, inc=1, device_id=at(y, x, c), device_id_type=MESH)

    for k in range(1, SECTIONS):
        pl.semaphore_signal(
            barrier, inc=1, device_id=((sec + k) % SECTIONS, sh), device_id_type=MESH
        )
    for k in range(1, SIDE):
        greet(py, (px + k) % SIDE, core)
        greet((py + k) % SIDE, px, core)
    greet(py, px, 1 - core)

    def tell_row():
        for k in range(1, SIDE):
            to = at(py, (px + k) % SIDE, core)
            pl.semaphore_signal(ready.at[0], inc=1, device_id=to, device_id_type=MESH)

    def tell_plane():
        pl.semaphore_wait(ready.at[0], SIDE - 1)
        for k in range(1, SIDE):
            to = at((py + k) % SIDE, px, core)
            pl.semaphore_signal(ready.at[1], inc=1, device_id=to, device_id_type=MESH)

    def tell_all():
        pl.semaphore_wait(ready.at[1], SIDE - 1)
        lax.fori_loop(1, SHARDS, tell_ids, 0)

    def pool_copy(s):
        return pltpu.make_async_remote_copy(
            src_ref=pooled,
            dst_ref=pbuf.at[s],
            send_sem=pool_send,
            recv_sem=pool_recv.at[s],
            device_id=(0, sh),
            device_id_type=MESH,
        )

    def relay_copy(c, size):
        rows = chunk_rows(c, size)
        return pltpu.make_async_remote_copy(
            src_ref=nbuf.at[rows],
            dst_ref=gbuf.at[rows],
            send_sem=relay_send.at[c],
            recv_sem=relay_recv.at[c],
            device_id=(jnp.maximum(sec - 1, 0), sh),
            device_id_type=MESH,
        )

    def route_copy(m, p):
        return pltpu.make_async_remote_copy(
            src_ref=sorted_rows.at[m, pl.ds(p * PER_PLANE, PER_PLANE)],
            dst_ref=routed.at[pl.ds(pl.multiple_of(m * PER_PLANE, PER_PLANE), PER_PLANE)],
            send_sem=route_send.at[m, p],
            recv_sem=route_recv.at[m],
            device_id=(p, sh),
            device_id_type=MESH,
        )

    def ids_copy(k, to, came):
        return pltpu.make_async_remote_copy(
            src_ref=ids,
            dst_ref=all_ids.at[came],
            send_sem=ids_send.at[k],
            recv_sem=ids_recv.at[k],
            device_id=(sec, to),
            device_id_type=MESH,
        )

    def left_copy(m, source):
        rows = micro_rows(m)
        return pltpu.make_async_remote_copy(
            src_ref=source.at[rows],
            dst_ref=peer_l.at[rows],
            send_sem=l_send.at[m],
            recv_sem=l_recv.at[m],
            device_id=at(py, px, 1 - core),
            device_id_type=MESH,
        )

    def right_copy(n, source, start, size):
        rows = pl.ds(pl.multiple_of(start, 64), size)
        return pltpu.make_async_remote_copy(
            src_ref=source.at[rows],
            dst_ref=peer_r.at[rows],
            send_sem=r_send.at[n],
            recv_sem=r_recv.at[n],
            device_id=at(py, px, 1 - core),
            device_id_type=MESH,
        )

    def send_left(m):
        @pl.when(core == 0)
        def _():
            left_copy(m, act).start()

        @pl.when(core == 1)
        def _():
            left_copy(m, xbuf).start()

    def send_right(n, start, size):
        @pl.when(core == 0)
        def _():
            right_copy(n, gbuf, start, size).start()

        @pl.when(core == 1)
        def _():
            right_copy(n, dz, start, size).start()

    def forward(m):
        rows = micro_rows(m)
        load_x(m).wait()

        @pl.when(first)
        def _():
            slot = 0
            for j in range(1, MICRO):
                slot = jnp.where(holder[j] == m, j, slot)
            extra = pbuf[slot]
            xbuf[rows, :] = (xbuf[rows, :].astype(F32) + extra.astype(F32)).astype(BF16)

        for j in range(WIDTH // TILE):
            cols = pl.ds(j * TILE, TILE)
            z = jnp.dot(xbuf[rows, :], win[:, cols], preferred_element_type=F32)
            sig = jax.nn.sigmoid(z)
            act[rows, cols] = (z * sig).astype(BF16)
            slope[:, cols] = sig * (1.0 + z * (1.0 - sig))

    def backward(c, start, size):
        crows = chunk_rows(c, size)
        krows = pl.ds(start, size)
        for j in range(WIDTH // WIDE):
            cols = pl.ds(j * WIDE, WIDE)
            ga = jnp.dot(gbuf[crows, :], wout_t[:, cols], preferred_element_type=F32)
            dz[crows, cols] = (ga * slope[krows, cols]).astype(BF16)
        for j in range(WIDTH // WIDE):
            cols = pl.ds(j * WIDE, WIDE)
            back = jnp.dot(dz[crows, :], win_t[:, cols], preferred_element_type=F32)
            nbuf[crows, cols] = (gbuf[crows, cols].astype(F32) + back).astype(BF16)

    def own_grads(m, and_peer):
        rows = micro_rows(m)
        for kind, left, right in ((0, xbuf, dz), (1, act, gbuf)):

            @pl.when(core == kind)
            def _(left=left, right=right):
                for i in range(WIDTH // TILE):
                    cols = pl.ds(i * TILE, TILE)
                    total = acc[cols, :] + dot_tn(left[rows, cols], right[rows, :])
                    if and_peer:
                        total = total + dot_tn(peer_l[rows, cols], peer_r[rows, :])
                    acc[cols, :] = total

    def weight_grads(m):
        left_copy(m, act).wait_recv()
        right_copy(m, dz, m * TOK, TOK).wait_recv()
        own_grads(m, True)

    load_win.wait()
    for j in range(WIDTH // TILE):
        cols = pl.ds(j * TILE, TILE)
        win_t[:, cols] = win[cols, :].T

    @pl.when(jnp.logical_not(first))
    def _():
        forward(0)

    load_wout.wait()
    for j in range(WIDTH // TILE):
        cols = pl.ds(j * TILE, TILE)
        wout_t[:, cols] = wout[cols, :].T

    pl.semaphore_wait(barrier, SECTIONS - 1 + 2 * (SIDE - 1) + 1)
    tell_row()

    @pl.when(jnp.logical_not(first))
    def _():
        pool_copy(sec).start()

    def clear(i, carry):
        rows = pl.ds(pl.multiple_of(i * 64, 64), 64)
        acc[rows, :] = jnp.zeros((64, WIDTH), F32)
        return carry

    def tell_ids(k, carry):
        ids_copy(k, (sh + k) % SHARDS, sh).start()
        return carry

    @pl.when(first)
    def _():
        lax.fori_loop(0, WIDTH // 64, clear, 0)
        tell_plane()
        row = lax.broadcasted_iota(jnp.int32, (TOK, TOK), 0)
        col = lax.broadcasted_iota(jnp.int32, (TOK, TOK), 1)
        feat = ids.shape[1]
        lane = lax.broadcasted_iota(jnp.int32, (ids.shape[2], TOK), 1)
        lead = lax.broadcasted_iota(jnp.int32, (ids.shape[2], TOK), 0)
        widen = jnp.where(lane >> 3 == lead, 1.0, 0.0).astype(BF16)
        for m in range(MICRO):
            owner = (ids[m] >> 10).astype(F32).astype(BF16)
            wide = jnp.dot(owner, widen, preferred_element_type=F32)
            inner = lax.broadcasted_iota(jnp.int32, (feat, TOK), 1) & 7
            outer = lax.broadcasted_iota(jnp.int32, (feat, TOK), 0)
            across = jnp.sum(jnp.where(inner == outer, wide, 0.0), axis=0, keepdims=True)
            down = jnp.sum(jnp.where(row == col, across, 0.0), axis=1, keepdims=True)
            earlier = jnp.where((down == across) & (row < col), 1.0, 0.0)
            rank[m] = 2.0 * across + jnp.sum(earlier, axis=0, keepdims=True)
        tell_all()
        load_pool.wait()
        for s in range(1, SECTIONS):
            pool_copy(s).wait_recv()
        forward(0)

    @pl.when(last)
    def _():
        load_top(0).wait()
        for k in range(CHUNKS):
            backward(k, k * CHUNK, CHUNK)
            relay_copy(k, CHUNK).start()

    @pl.when(jnp.logical_not(first))
    def _():
        tell_plane()
        lax.fori_loop(0, WIDTH // 64, clear, 0)
        tell_all()

    all_ids[sh] = ids[...]
    send_left(0)

    def step(c, start, size):
        @pl.when(jnp.logical_not(last))
        def _():
            relay_copy(c, size).wait_recv()

        backward(c, start, size)

        @pl.when(jnp.logical_not(first))
        def _():
            relay_copy(c, size).start()

    def route(m):
        rows = micro_rows(m)

        @pl.when(first)
        def _():
            target = lax.broadcasted_iota(jnp.int32, (TOK, TOK), 0).astype(F32)
            pick = jnp.where(target == rank[m], 1.0, 0.0).astype(BF16)
            ordered = jnp.dot(pick, nbuf[rows, :], preferred_element_type=F32).astype(BF16)
            sorted_rows[m] = ordered
            for p in range(1, SECTIONS):
                route_copy(m, p).start()
            routed[pl.ds(pl.multiple_of(m * PER_PLANE, PER_PLANE), PER_PLANE), :] = ordered[
                :PER_PLANE, :
            ]

    def micro_step(m, carry):
        @pl.when(jnp.logical_not(last & (m == 0)))
        def _():
            @pl.when(last)
            def _():
                load_top(m).wait()

            for k in range(CHUNKS):
                step(m * CHUNKS + k, k * CHUNK, CHUNK)
                if k == 0:

                    @pl.when(m > 0)
                    def _():
                        weight_grads(m - 1)

        send_right(m, m * TOK, TOK)
        route(m)
        forward(m + 1)
        send_left(m + 1)
        return carry

    lax.fori_loop(0, MICRO - 1, micro_step, 0)

    final = MICRO - 1
    tail = TOK - CHUNK

    def unit_copy(source, target, send, recv, k, to, came):
        return pltpu.make_async_remote_copy(
            src_ref=source.at[to],
            dst_ref=target.at[came],
            send_sem=send.at[k],
            recv_sem=recv.at[k],
            device_id=(sec, to),
            device_id_type=MESH,
        )

    def soon_copy(k, to, came):
        return unit_copy(soon, got_soon, soon_send, soon_recv, k, to, came)

    def late_copy(k, to, came):
        return unit_copy(late, got_late, late_send, late_recv, k, to, came)

    def hand_soon(k, carry):
        soon_copy(k, (sh + k) % SHARDS, sh).start()
        return carry

    def hand_late(k, carry):
        late_copy(k, (sh + k) % SHARDS, sh).start()
        return carry

    def soon_units():
        row = lax.broadcasted_iota(jnp.int32, (SOON, SOON), 0)
        col = lax.broadcasted_iota(jnp.int32, (SOON, SOON), 1)
        target = ((col >> 1) & (SHARDS - 1)) * (2 * (MICRO - 1)) + (col >> 6) * 2 + (col & 1)
        regroup = jnp.where(row == target, 1.0, 0.0).astype(BF16)
        by_owner = jnp.dot(regroup, routed[pl.ds(0, SOON), :], preferred_element_type=F32)
        for b in range(8):
            flat[pl.ds(b, SOON, stride=8), :] = by_owner[:, b * 128 : (b + 1) * 128]
        soon[...] = flat[...].reshape(soon.shape).astype(BF16)
        got_soon[sh] = soon[sh]

    def late_units():
        by_owner = routed[pl.ds(SOON, PER_PLANE), :].astype(F32)
        for b in range(8):
            flat[pl.ds(b, PER_PLANE, stride=8), :] = by_owner[:, b * 128 : (b + 1) * 128]
        late[...] = flat[pl.ds(0, PER_PLANE * 8), :].reshape(late.shape).astype(BF16)
        got_late[sh] = late[sh]

    def to_rows(got, start, count):
        flat[pl.ds(0, count * 8), :] = got[...].astype(F32).reshape(count * 8, 128)
        for b in range(8):
            out_rows[pl.ds(start, count), pl.ds(b * 128, 128)] = flat[
                pl.ds(b, count, stride=8), :
            ].astype(BF16)

    @pl.when(last)
    def _():
        load_top(final).wait()

    for k in range(CHUNKS - 1):
        step(final * CHUNKS + k, k * CHUNK, CHUNK)
        if k == 0:
            weight_grads(final - 1)

            @pl.when(first)
            def _():
                soon_units()
        if k == 1:

            @pl.when(first)
            def _():
                lax.fori_loop(1, SHARDS // 2, hand_soon, 0)
        if k == 2:
            send_right(final, final * TOK, tail)

            @pl.when(first)
            def _():
                lax.fori_loop(SHARDS // 2, SHARDS, hand_soon, 0)

    for k in range(CHUNK // LATE):
        step(EARLY + k, tail + k * LATE, LATE)
    send_right(final + 1, final * TOK + tail, TOK - tail)
    own_grads(final, False)

    def block_rows(y, x):
        return pl.ds(pl.multiple_of((y * SIDE + x) * BLOCK, BLOCK), BLOCK)

    left_half = pl.ds(0, HALF)
    right_half = pl.ds(HALF, HALF)

    def x_copy(d, y):
        to = (px + d) % SIDE
        return pltpu.make_async_remote_copy(
            src_ref=send_x.at[y, pl.ds(pl.multiple_of(to * BLOCK, BLOCK), BLOCK)],
            dst_ref=recv_x.at[d - 1, y],
            send_sem=x_send.at[d - 1, y],
            recv_sem=x_recv.at[d - 1, y],
            device_id=at(py, to, core),
            device_id_type=MESH,
        )

    def y_copy(d, x):
        rows = pl.ds(pl.multiple_of(x * BLOCK, BLOCK), BLOCK)
        return pltpu.make_async_remote_copy(
            src_ref=send_y.at[d - 1, rows],
            dst_ref=recv_y.at[d - 1, rows],
            send_sem=y_send.at[d - 1, x],
            recv_sem=y_recv.at[d - 1, x],
            device_id=at((py + d) % SIDE, px, core),
            device_id_type=MESH,
        )

    def c_copy(h, e, c, kind):
        there = (py + e) % SIDE if h == 0 else (px + e) % SIDE
        return pltpu.make_async_remote_copy(
            src_ref=send_c.at[h, e, c],
            dst_ref=recv_c.at[kind, h, e],
            send_sem=c_send.at[h, e, c],
            recv_sem=c_recv.at[kind, h, e],
            device_id=at(there, px, c) if h == 0 else at(py, there, c),
            device_id_type=MESH,
        )

    order = (2, 1, 3, 0)
    frows = micro_rows(final)
    left_copy(final, act).wait_recv()
    right_copy(final, dz, final * TOK, tail).wait_recv()
    right_copy(final + 1, dz, final * TOK + tail, TOK - tail).wait_recv()
    for d in order:
        y = (py + d) % SIDE
        cols = pl.ds(pl.multiple_of(y * TILE, TILE), TILE)
        total = acc[cols, :] + dot_tn(peer_l[frows, cols], peer_r[frows, :])
        acc[cols, :] = total
        send_x[y] = total[:, :HALF].astype(BF16)
        for dx in (2, 1, 3):
            x_copy(dx, y).start()
        if d != 0:
            send_y[d - 1] = total[:, HALF:].astype(BF16)
    for e in order:
        for d in (2, 1, 3):
            y_copy(d, (px + e) % SIDE).start()
    route(final)

    @pl.when(jnp.logical_not(first))
    def _():
        for m in range(MICRO - 1):
            route_copy(m, 1).wait_recv()
        soon_units()
        lax.fori_loop(1, SHARDS, hand_soon, 0)
        route_copy(final, 1).wait_recv()

    late_units()
    lax.fori_loop(1, SHARDS, hand_late, 0)

    def hear_ids(k, carry):
        ids_copy(k, (sh + k) % SHARDS, (sh + SHARDS - k) % SHARDS).wait_recv()
        return carry

    lax.fori_loop(1, SHARDS, hear_ids, 0)
    own = sec * SHARDS + sh
    feature = own // (SECTIONS * SHARDS // ids.shape[1])
    heard = all_ids[:, :, feature, :].reshape(SHARDS * MICRO, ids.shape[2])
    place = lax.broadcasted_iota(jnp.int32, heard.shape, 1) * ROWS_OWN + (heard & (ROWS_OWN - 1))
    ours = heard >> 10 == own
    low = jnp.min(jnp.where(ours, place, 1 << 20), axis=1, keepdims=True) & (ROWS_OWN - 1)
    high = jnp.max(jnp.where(ours, place, -1), axis=1, keepdims=True) & (ROWS_OWN - 1)
    at_lane = lax.broadcasted_iota(jnp.int32, (SHARDS * MICRO, 128), 1)
    parts = jnp.where(
        at_lane == 0,
        low >> 5,
        jnp.where(at_lane == 1, low & 31, jnp.where(at_lane == 2, high >> 5, high & 31)),
    )
    half = lax.broadcasted_iota(jnp.int32, (TOK, SHARDS * MICRO), 0) >> 1
    pair = lax.broadcasted_iota(jnp.int32, (TOK, SHARDS * MICRO), 1)
    came, micro = pair >> 2, pair & (MICRO - 1)
    place_of = jnp.where(
        micro < final, came * (MICRO - 1) + micro, SHARDS * (MICRO - 1) + came
    )
    twice = jnp.where(half == place_of, 1.0, 0.0).astype(BF16)
    both = jnp.dot(twice, parts.astype(F32).astype(BF16), preferred_element_type=F32)
    odd = lax.broadcasted_iota(jnp.int32, (TOK, 1), 0) & 1
    row_of = jnp.where(
        odd == 0, both[:, 0:1] * 32.0 + both[:, 1:2], both[:, 2:3] * 32.0 + both[:, 3:4]
    )
    out_named[...] = jnp.broadcast_to(row_of.astype(jnp.int32), (TOK, 128))

    for e in order:
        y = (py + e) % SIDE
        x = (px + e) % SIDE
        for d in range(1, SIDE):
            x_copy(d, y).wait_recv()
            y_copy(d, x).wait_recv()
        total = acc[block_rows(y, px), left_half]
        other = acc[block_rows(py, x), right_half]
        for d in range(1, SIDE):
            total = total + recv_x[d - 1, y].astype(F32)
            xrows = pl.ds(pl.multiple_of(x * BLOCK, BLOCK), BLOCK)
            other = other + recv_y[d - 1, xrows, :].astype(F32)
        for h, part in ((0, total), (1, other)):
            for c in range(2):
                send_c[h, e, c] = part[c * SHARE : (c + 1) * SHARE, :].astype(BF16)
                if e == 0:

                    @pl.when(core == c)
                    def _(h=h, c=c, part=part):
                        own_c[h] = part[c * SHARE : (c + 1) * SHARE, :]

                    @pl.when(core != c)
                    def _(h=h, c=c):
                        c_copy(h, 0, c, core).start()
                else:
                    c_copy(h, e, c, core).start()

    for kind, out in ((0, out_in), (1, out_out)):
        for h, cols in ((0, left_half), (1, right_half)):

            @pl.when(core == kind)
            def _(h=h, out=out, cols=cols):
                out[:, cols] = own_c[h]

            @pl.when(core != kind)
            def _(h=h, out=out, cols=cols, kind=kind):
                c_copy(h, 0, 1 - kind, kind).wait_recv()
                out[:, cols] = recv_c[kind, h, 0].astype(F32)

            total = out[:, cols]
            for e in range(1, SIDE):
                c_copy(h, e, 0, kind).wait_recv()
                total = total + recv_c[kind, h, e].astype(F32)
            out[:, cols] = total

    def collect_soon(k, carry):
        soon_copy(k, (sh + k) % SHARDS, (sh + SHARDS - k) % SHARDS).wait_recv()
        return carry

    def collect_late(k, carry):
        late_copy(k, (sh + k) % SHARDS, (sh + SHARDS - k) % SHARDS).wait_recv()
        return carry

    lax.fori_loop(1, SHARDS, collect_soon, 0)
    to_rows(got_soon, 0, SOON)
    lax.fori_loop(1, SHARDS, collect_late, 0)
    to_rows(got_late, SOON, PER_PLANE)

    @pl.when(jnp.logical_not(first))
    def _():
        pool_copy(sec).wait_send()

        def left(c, carry):
            relay_copy(c, CHUNK).wait_send()
            return carry

        lax.fori_loop(0, EARLY, left, 0)

        def left_late(c, carry):
            relay_copy(c, LATE).wait_send()
            return carry

        lax.fori_loop(EARLY, PIECES, left_late, 0)

    @pl.when(first)
    def _():
        for m in range(MICRO):
            for p in range(1, SECTIONS):
                route_copy(m, p).wait_send()

    def units_left(k, carry):
        soon_copy(k, (sh + k) % SHARDS, sh).wait_send()
        late_copy(k, (sh + k) % SHARDS, sh).wait_send()
        return carry

    lax.fori_loop(1, SHARDS, units_left, 0)

    def ids_left(k, carry):
        ids_copy(k, (sh + k) % SHARDS, sh).wait_send()
        return carry

    lax.fori_loop(1, SHARDS, ids_left, 0)
    for m in range(MICRO):
        left_copy(m, act).wait_send()
    for m in range(final):
        right_copy(m, dz, m * TOK, TOK).wait_send()
    right_copy(final, dz, final * TOK, tail).wait_send()
    right_copy(final + 1, dz, final * TOK + tail, TOK - tail).wait_send()
    for d in range(1, SIDE):
        for y in range(SIDE):
            x_copy(d, y).wait_send()
            y_copy(d, y).wait_send()
        for h in range(2):
            for c in range(2):
                c_copy(h, d, c, core).wait_send()
    for h in range(2):
        c_copy(h, 0, 1 - core, core).wait_send()


def relay(holder, saved, pooled, grad_top, w_in, w_out, ids):
    vmem = pl.BlockSpec(memory_space=pltpu.VMEM)
    anywhere = pl.BlockSpec(memory_space=pl.ANY)
    dma = pltpu.SemaphoreType.DMA
    tokens = MICRO * TOK
    return pl.pallas_call(
        kernel,
        out_shape=(
            jax.ShapeDtypeStruct((SHARE, WIDTH), F32),
            jax.ShapeDtypeStruct((SHARE, WIDTH), F32),
            jax.ShapeDtypeStruct((TOK, WIDTH), BF16),
            jax.ShapeDtypeStruct((TOK, 128), jnp.int32),
        ),
        in_specs=[pl.BlockSpec(memory_space=pltpu.SMEM)] + [anywhere] * 5 + [vmem],
        out_specs=(vmem, vmem, vmem, vmem),
        scratch_shapes=[
            pltpu.VMEM((WIDTH, WIDTH), BF16),
            pltpu.VMEM((WIDTH, WIDTH), BF16),
            pltpu.VMEM((WIDTH, WIDTH), BF16),
            pltpu.VMEM((WIDTH, WIDTH), BF16),
            pltpu.VMEM((tokens, WIDTH), BF16),
            pltpu.VMEM((tokens, WIDTH), BF16),
            pltpu.VMEM((tokens, WIDTH), BF16),
            pltpu.VMEM((SECTIONS, TOK, WIDTH), BF16),
            pltpu.VMEM((tokens, WIDTH), BF16),
            pltpu.VMEM((TOK, WIDTH), F32),
            pltpu.VMEM((tokens, WIDTH), BF16),
            pltpu.VMEM((WIDTH, WIDTH), F32),
            pltpu.VMEM((MICRO, 1, TOK), F32),
            pltpu.VMEM((SHARDS,) + ids.shape, jnp.int32),
            pltpu.VMEM((MICRO, TOK, WIDTH), BF16),
            pltpu.VMEM((TOK, WIDTH), BF16),
            pltpu.VMEM((SHARDS, 16 * (MICRO - 1), 128), BF16),
            pltpu.VMEM((SHARDS, 16 * (MICRO - 1), 128), BF16),
            pltpu.VMEM((SHARDS, 16, 128), BF16),
            pltpu.VMEM((SHARDS, 16, 128), BF16),
            pltpu.VMEM((SOON * 8, 128), F32),
            pltpu.VMEM((tokens, WIDTH), BF16),
            pltpu.VMEM((tokens, WIDTH), BF16),
            pltpu.VMEM((SIDE, SIDE * BLOCK, HALF), BF16),
            pltpu.VMEM((SIDE - 1, SIDE, BLOCK, HALF), BF16),
            pltpu.VMEM((SIDE - 1, SIDE * BLOCK, HALF), BF16),
            pltpu.VMEM((SIDE - 1, SIDE * BLOCK, HALF), BF16),
            pltpu.VMEM((2, SHARE, HALF), F32),
            pltpu.VMEM((2, SIDE, 2, SHARE, HALF), BF16),
            pltpu.VMEM((2, 2, SIDE, SHARE, HALF), BF16),
            dma((3 + MICRO,)),
            dma((MICRO,)),
            dma,
            dma((SECTIONS,)),
            dma((PIECES,)),
            dma((PIECES,)),
            dma((MICRO, SECTIONS)),
            dma((MICRO,)),
            dma((SHARDS,)),
            dma((SHARDS,)),
            dma((SHARDS,)),
            dma((SHARDS,)),
            pltpu.SemaphoreType.REGULAR((2,)),
            dma((SHARDS,)),
            dma((SHARDS,)),
            dma((MICRO,)),
            dma((MICRO,)),
            dma((MICRO + 1,)),
            dma((MICRO + 1,)),
            dma((SIDE - 1, SIDE)),
            dma((SIDE - 1, SIDE)),
            dma((SIDE - 1, SIDE)),
            dma((SIDE - 1, SIDE)),
            dma((2, SIDE, 2)),
            dma((2, 2, SIDE)),
        ],
        compiler_params=pltpu.CompilerParams(
            collective_id=0, has_side_effects=True, vmem_limit_bytes=56 * 1024 * 1024
        ),
        cost_estimate=pl.CostEstimate(
            flops=10 * tokens * WIDTH * WIDTH, bytes_accessed=9 * 2**20, transcendentals=tokens * WIDTH
        ),
        name="relay",
    )(holder, saved, pooled, grad_top, w_in, w_out, ids)


def table_kernel(named, rows, grad_in, grad_out, table, out_in, out_out):
    block = pl.program_id(0)
    lane = lax.broadcasted_iota(jnp.int32, (TOK, TILE), 1) + block * TILE
    hit = jnp.where(lane == named[:, 0:1], 1.0, 0.0).astype(BF16)
    table[...] = dot_tn(hit, rows[...])

    @pl.when(block == 0)
    def _():
        out_in[...] = grad_in[...]
        out_out[...] = grad_out[...]


def owner_sums(named, rows, grad_in, grad_out):
    def whole(array):
        return pl.BlockSpec(array.shape, lambda b: (0, 0))

    return pl.pallas_call(
        table_kernel,
        grid=(ROWS_OWN // TILE,),
        out_shape=(
            jax.ShapeDtypeStruct((ROWS_OWN, WIDTH), F32),
            jax.ShapeDtypeStruct(grad_in.shape, F32),
            jax.ShapeDtypeStruct(grad_out.shape, F32),
        ),
        in_specs=[whole(named), whole(rows), whole(grad_in), whole(grad_out)],
        out_specs=(
            pl.BlockSpec((TILE, WIDTH), lambda b: (b, 0)),
            whole(grad_in),
            whole(grad_out),
        ),
        cost_estimate=pl.CostEstimate(
            flops=2 * ROWS_OWN * TOK * WIDTH, bytes_accessed=5 * 2**20, transcendentals=0
        ),
        name="owner_sums",
    )(named, rows, grad_in, grad_out)


def local(saved, pooled, grad_top, w_in, w_out, feature_ids, holder_order):
    tokens = MICRO * TOK
    out_in, out_out, rows, named = relay(
        holder_order,
        saved.reshape(tokens, WIDTH),
        pooled.reshape(TOK, WIDTH),
        grad_top.reshape(tokens, WIDTH),
        w_in[0],
        w_out[0],
        jnp.transpose(feature_ids, (0, 2, 1)),
    )
    table_grad, grad_in, grad_out = owner_sums(named, rows, out_in, out_out)
    return (grad_in[None], grad_out[None], table_grad)


def solution(mesh):
    return jax.shard_map(
        local,
        mesh=mesh,
        in_specs=(
            P("section", None, "shard", None, None),
            P("section", "shard", None, None),
            P(None, "shard", None, None),
            P("section", None, None),
            P("section", None, None),
            P(None, "shard", None),
            P(),
        ),
        out_specs=(
            P("section", "shard", None),
            P("section", "shard", None),
            P(("section", "shard"), None),
        ),
        check_vma=False,
    )
```

```python
import jax
import jax.numpy as jnp
from jax import lax
from jax.experimental import pallas as pl
from jax.experimental.pallas import tpu as pltpu
from jax.sharding import PartitionSpec as P

ROWS_OWN = 1024
MESH = pl.DeviceIdType.MESH
F32 = jnp.float32
BF16 = jnp.bfloat16

SECTIONS = 4
SHARDS = 32
SIDE = 4
MICRO = 4
TOK = 256
CHUNK = 64
LATE = 32
WIDTH = 1024
SHARE = WIDTH // SHARDS
PER_PLANE = TOK // SECTIONS
TILE = 256
WIDE = 512
CHUNKS = TOK // CHUNK
EARLY = MICRO * CHUNKS - 1
PIECES = EARLY + CHUNK // LATE
SOON = (MICRO - 1) * PER_PLANE
HALF = WIDTH // 2
BLOCK = 2 * SHARE


def dot_tn(a, b):
    return lax.dot_general(a, b, (((0,), (0,)), ((), ())), preferred_element_type=F32)


def kernel(
    holder,
    saved,
    pooled,
    grad_top,
    w_in,
    w_out,
    ids,
    out_in,
    out_out,
    out_rows,
    out_named,
    win,
    wout,
    win_t,
    wout_t,
    xbuf,
    gbuf,
    nbuf,
    pbuf,
    act,
    slope,
    dz,
    acc,
    rank,
    all_ids,
    sorted_rows,
    routed,
    soon,
    got_soon,
    late,
    got_late,
    flat,
    named,
    rows_buf,
    grads,
    transit,
    peer_l,
    peer_r,
    send_x,
    recv_x,
    send_y,
    recv_y,
    own_c,
    send_c,
    recv_c,
    load_sem,
    top_sem,
    pool_send,
    pool_recv,
    relay_send,
    relay_recv,
    route_send,
    route_recv,
    soon_send,
    soon_recv,
    late_send,
    late_recv,
    ready,
    hop_send,
    hop_recv,
    pass_send,
    pass_recv,
    out_sem,
    ids_send,
    ids_recv,
    l_send,
    l_recv,
    r_send,
    r_recv,
    x_send,
    x_recv,
    y_send,
    y_recv,
    c_send,
    c_recv,
):
    sec = lax.axis_index("section")
    sh = lax.axis_index("shard")
    core = sh % 2
    px = (sh // 2) % SIDE
    py = sh // (2 * SIDE)
    first = sec == 0
    last = sec == SECTIONS - 1

    def at(y, x, c):
        return (sec, (y * SIDE + x) * 2 + c)

    def micro_rows(m):
        return pl.ds(pl.multiple_of(m * TOK, TOK), TOK)

    def chunk_rows(c, size):
        start = c * CHUNK if size == CHUNK else EARLY * CHUNK + (c - EARLY) * LATE
        return pl.ds(pl.multiple_of(start, size), size)

    def load_x(m):
        rows = micro_rows(m)
        return pltpu.make_async_copy(saved.at[rows], xbuf.at[rows], load_sem.at[2 + m])

    def load_top(m):
        rows = micro_rows(m)
        return pltpu.make_async_copy(grad_top.at[rows], gbuf.at[rows], top_sem.at[m])

    load_win = pltpu.make_async_copy(w_in, win, load_sem.at[0])
    load_wout = pltpu.make_async_copy(w_out, wout, load_sem.at[1])
    load_pool = pltpu.make_async_copy(pooled, pbuf.at[0], load_sem.at[2 + MICRO])

    load_win.start()
    load_x(0).start()
    load_wout.start()

    @pl.when(last)
    def _():
        for m in range(MICRO):
            load_top(m).start()

    for m in range(1, MICRO):
        load_x(m).start()

    @pl.when(first)
    def _():
        load_pool.start()

    barrier = pltpu.get_barrier_semaphore()

    def greet(y, x, c):
        pl.semaphore_signal(barrier, inc=1, device_id=at(y, x, c), device_id_type=MESH)

    for k in range(1, SECTIONS):
        pl.semaphore_signal(
            barrier, inc=1, device_id=((sec + k) % SECTIONS, sh), device_id_type=MESH
        )
    for k in range(1, SIDE):
        greet(py, (px + k) % SIDE, core)
        greet((py + k) % SIDE, px, core)
    greet(py, px, 1 - core)

    def tell_row():
        for k in range(1, SIDE):
            to = at(py, (px + k) % SIDE, core)
            pl.semaphore_signal(ready.at[0], inc=1, device_id=to, device_id_type=MESH)

    def tell_plane():
        pl.semaphore_wait(ready.at[0], SIDE - 1)
        for k in range(1, SIDE):
            to = at((py + k) % SIDE, px, core)
            pl.semaphore_signal(ready.at[1], inc=1, device_id=to, device_id_type=MESH)

    def tell_all():
        pl.semaphore_wait(ready.at[1], SIDE - 1)
        lax.fori_loop(1, SHARDS, tell_ids, 0)

    def pool_copy(s):
        return pltpu.make_async_remote_copy(
            src_ref=pooled,
            dst_ref=pbuf.at[s],
            send_sem=pool_send,
            recv_sem=pool_recv.at[s],
            device_id=(0, sh),
            device_id_type=MESH,
        )

    def pool_rows(h):
        return pl.ds(h * (TOK // 2), TOK // 2)

    def hop_copy(h):
        return pltpu.make_async_remote_copy(
            src_ref=pooled.at[pool_rows(h)],
            dst_ref=transit.at[pool_rows(h)],
            send_sem=hop_send.at[h],
            recv_sem=hop_recv.at[h],
            device_id=(SECTIONS - 1, sh),
            device_id_type=MESH,
        )

    def pass_copy(h):
        return pltpu.make_async_remote_copy(
            src_ref=transit.at[pool_rows(h)],
            dst_ref=pbuf.at[2, pool_rows(h)],
            send_sem=pass_send.at[h],
            recv_sem=pass_recv.at[h],
            device_id=(0, sh),
            device_id_type=MESH,
        )

    def pass_pool(h):
        hop_copy(h).wait_recv()
        pass_copy(h).start()

    def relay_copy(c, size):
        rows = chunk_rows(c, size)
        return pltpu.make_async_remote_copy(
            src_ref=nbuf.at[rows],
            dst_ref=gbuf.at[rows],
            send_sem=relay_send.at[c],
            recv_sem=relay_recv.at[c],
            device_id=(jnp.maximum(sec - 1, 0), sh),
            device_id_type=MESH,
        )

    def route_copy(m, p):
        return pltpu.make_async_remote_copy(
            src_ref=sorted_rows.at[m, pl.ds(p * PER_PLANE, PER_PLANE)],
            dst_ref=routed.at[pl.ds(pl.multiple_of(m * PER_PLANE, PER_PLANE), PER_PLANE)],
            send_sem=route_send.at[m, p],
            recv_sem=route_recv.at[m],
            device_id=(p, sh),
            device_id_type=MESH,
        )

    def ids_copy(to, came):
        return pltpu.make_async_remote_copy(
            src_ref=ids,
            dst_ref=all_ids.at[came],
            send_sem=ids_send,
            recv_sem=ids_recv,
            device_id=(sec, to),
            device_id_type=MESH,
        )

    def left_copy(m, source):
        rows = micro_rows(m)
        return pltpu.make_async_remote_copy(
            src_ref=source.at[rows],
            dst_ref=peer_l.at[rows],
            send_sem=l_send.at[m],
            recv_sem=l_recv.at[m],
            device_id=at(py, px, 1 - core),
            device_id_type=MESH,
        )

    def right_copy(n, source, start, size):
        rows = pl.ds(pl.multiple_of(start, 64), size)
        return pltpu.make_async_remote_copy(
            src_ref=source.at[rows],
            dst_ref=peer_r.at[rows],
            send_sem=r_send.at[n],
            recv_sem=r_recv.at[n],
            device_id=at(py, px, 1 - core),
            device_id_type=MESH,
        )

    def send_left(m):
        @pl.when(core == 0)
        def _():
            left_copy(m, act).start()

        @pl.when(core == 1)
        def _():
            left_copy(m, xbuf).start()

    def send_right(n, start, size):
        @pl.when(core == 0)
        def _():
            right_copy(n, gbuf, start, size).start()

        @pl.when(core == 1)
        def _():
            right_copy(n, dz, start, size).start()

    def forward_open(m):
        rows = micro_rows(m)
        load_x(m).wait()

        @pl.when(first)
        def _():
            slot = 0
            for j in range(1, MICRO):
                slot = jnp.where(holder[j] == m, j, slot)
            extra = pbuf[slot]
            xbuf[rows, :] = (xbuf[rows, :].astype(F32) + extra.astype(F32)).astype(BF16)

    def forward_tile(m, j):
        rows = micro_rows(m)
        cols = pl.ds(j * TILE, TILE)
        z = jnp.dot(xbuf[rows, :], win[:, cols], preferred_element_type=F32)
        sig = jax.nn.sigmoid(z)
        act[rows, cols] = (z * sig).astype(BF16)
        slope[m % 2, :, cols] = sig * (1.0 + z * (1.0 - sig))

    def forward(m):
        forward_open(m)
        for j in range(WIDTH // TILE):
            forward_tile(m, j)

    def backward(m, c, start, size):
        crows = chunk_rows(c, size)
        krows = pl.ds(start, size)
        for j in range(WIDTH // WIDE):
            cols = pl.ds(j * WIDE, WIDE)
            ga = jnp.dot(gbuf[crows, :], wout_t[:, cols], preferred_element_type=F32)
            dz[crows, cols] = (ga * slope[m % 2, krows, cols]).astype(BF16)
        for j in range(WIDTH // WIDE):
            cols = pl.ds(j * WIDE, WIDE)
            back = jnp.dot(dz[crows, :], win_t[:, cols], preferred_element_type=F32)
            nbuf[crows, cols] = (gbuf[crows, cols].astype(F32) + back).astype(BF16)

    def grad_tiles(m, tiles, and_peer):
        rows = micro_rows(m)
        for kind, left, right in ((0, xbuf, dz), (1, act, gbuf)):

            @pl.when(core == kind)
            def _(left=left, right=right):
                for i in tiles:
                    cols = pl.ds(i * TILE, TILE)
                    total = acc[cols, :] + dot_tn(left[rows, cols], right[rows, :])
                    if and_peer:
                        total = total + dot_tn(peer_l[rows, cols], peer_r[rows, :])
                    acc[cols, :] = total

    def hear_peer(m):
        left_copy(m, act).wait_recv()
        right_copy(m, dz, m * TOK, TOK).wait_recv()

    load_win.wait()
    for j in range(WIDTH // TILE):
        cols = pl.ds(j * TILE, TILE)
        win_t[:, cols] = win[cols, :].T

    @pl.when(jnp.logical_not(first))
    def _():
        forward(0)

    load_wout.wait()
    for j in range(WIDTH // TILE):
        cols = pl.ds(j * TILE, TILE)
        wout_t[:, cols] = wout[cols, :].T

    pl.semaphore_wait(barrier, SECTIONS - 1 + 2 * (SIDE - 1) + 1)
    tell_row()

    @pl.when((sec == 1) | last)
    def _():
        pool_copy(sec).start()

    @pl.when(sec == 2)
    def _():
        hop_copy(0).start()
        hop_copy(1).start()

    def clear(i, carry):
        rows = pl.ds(pl.multiple_of(i * 64, 64), 64)
        acc[rows, :] = jnp.zeros((64, WIDTH), F32)
        return carry

    def tell_ids(k, carry):
        ids_copy((sh + k) % SHARDS, sh).start()
        return carry

    @pl.when(first)
    def _():
        lax.fori_loop(0, WIDTH // 64, clear, 0)
        tell_plane()
        row = lax.broadcasted_iota(jnp.int32, (TOK, TOK), 0)
        col = lax.broadcasted_iota(jnp.int32, (TOK, TOK), 1)
        feat = ids.shape[1]
        lane = lax.broadcasted_iota(jnp.int32, (ids.shape[2], TOK), 1)
        lead = lax.broadcasted_iota(jnp.int32, (ids.shape[2], TOK), 0)
        widen = jnp.where(lane >> 3 == lead, 1.0, 0.0).astype(BF16)
        for m in range(MICRO):
            owner = (ids[m] >> 10).astype(F32).astype(BF16)
            wide = jnp.dot(owner, widen, preferred_element_type=F32)
            inner = lax.broadcasted_iota(jnp.int32, (feat, TOK), 1) & 7
            outer = lax.broadcasted_iota(jnp.int32, (feat, TOK), 0)
            across = jnp.sum(jnp.where(inner == outer, wide, 0.0), axis=0, keepdims=True)
            down = jnp.sum(jnp.where(row == col, across, 0.0), axis=1, keepdims=True)
            earlier = jnp.where((down == across) & (row < col), 1.0, 0.0)
            rank[m] = 2.0 * across + jnp.sum(earlier, axis=0, keepdims=True)
        tell_all()
        load_pool.wait()
        for s in (1, SECTIONS - 1):
            pool_copy(s).wait_recv()
        for h in range(2):
            pass_copy(h).wait_recv()
        forward(0)

    @pl.when(last)
    def _():
        load_top(0).wait()
        for k in range(CHUNKS):
            backward(0, k, k * CHUNK, CHUNK)
            relay_copy(k, CHUNK).start()

    @pl.when(jnp.logical_not(first))
    def _():
        tell_plane()
        lax.fori_loop(0, WIDTH // 64, clear, 0)
        tell_all()

    @pl.when(last)
    def _():
        pass_pool(0)

    all_ids[sh] = ids[...]
    send_left(0)

    def step(m, c, start, size):
        @pl.when(jnp.logical_not(last))
        def _():
            relay_copy(c, size).wait_recv()

        backward(m, c, start, size)

        @pl.when(jnp.logical_not(first))
        def _():
            relay_copy(c, size).start()

    def route(m):
        rows = micro_rows(m)

        @pl.when(first)
        def _():
            target = lax.broadcasted_iota(jnp.int32, (TOK, TOK), 0).astype(F32)
            pick = jnp.where(target == rank[m], 1.0, 0.0).astype(BF16)
            ordered = jnp.dot(pick, nbuf[rows, :], preferred_element_type=F32).astype(BF16)
            sorted_rows[m] = ordered
            for p in range(1, SECTIONS):
                route_copy(m, p).start()
            routed[pl.ds(pl.multiple_of(m * PER_PLANE, PER_PLANE), PER_PLANE), :] = ordered[
                :PER_PLANE, :
            ]

    def micro_step(m, carry):
        @pl.when(last & (m == 1))
        def _():
            pass_pool(1)

        for k in range(CHUNKS):

            @pl.when(jnp.logical_not(last & (m == 0)))
            def _(k=k):
                if k == 0:

                    @pl.when(last)
                    def _():
                        load_top(m).wait()

                step(m, m * CHUNKS + k, k * CHUNK, CHUNK)

            if k == 0:
                forward_open(m + 1)
                forward_tile(m + 1, 0)
                forward_tile(m + 1, 1)
            if k == 1:
                forward_tile(m + 1, 2)
                forward_tile(m + 1, 3)
                send_left(m + 1)
            if k > 0:

                @pl.when(m > 0)
                def _(k=k):
                    if k == 1:
                        hear_peer(m - 1)
                    grad_tiles(m - 1, ((0,), (1, 2), (3,))[k - 1], True)

        send_right(m, m * TOK, TOK)
        route(m)
        return carry

    lax.fori_loop(0, MICRO - 1, micro_step, 0)

    final = MICRO - 1
    tail = TOK - CHUNK

    def unit_copy(source, target, send, recv, to, came):
        return pltpu.make_async_remote_copy(
            src_ref=source.at[to],
            dst_ref=target.at[came],
            send_sem=send,
            recv_sem=recv,
            device_id=(sec, to),
            device_id_type=MESH,
        )

    def hand_soon(k, carry):
        to = (sh + k) % SHARDS
        unit_copy(soon, got_soon, soon_send, soon_recv, to, sh).start()
        return carry

    def hand_late(k, carry):
        to = (sh + k) % SHARDS
        unit_copy(late, got_late, late_send, late_recv, to, sh).start()
        return carry

    def wait_all(ref, semaphore):
        others = ref.at[pl.ds(0, SHARDS - 1)]
        pltpu.make_async_copy(others, others, semaphore).wait()

    def soon_units():
        row = lax.broadcasted_iota(jnp.int32, (SOON, SOON), 0)
        col = lax.broadcasted_iota(jnp.int32, (SOON, SOON), 1)
        target = ((col >> 1) & (SHARDS - 1)) * (2 * (MICRO - 1)) + (col >> 6) * 2 + (col & 1)
        regroup = jnp.where(row == target, 1.0, 0.0).astype(BF16)
        by_owner = jnp.dot(regroup, routed[pl.ds(0, SOON), :], preferred_element_type=F32)
        for b in range(8):
            flat[pl.ds(b, SOON, stride=8), :] = by_owner[:, b * 128 : (b + 1) * 128]
        soon[...] = flat[...].reshape(soon.shape).astype(BF16)
        got_soon[sh] = soon[sh]

    def late_units():
        by_owner = routed[pl.ds(SOON, PER_PLANE), :].astype(F32)
        for b in range(8):
            flat[pl.ds(b, PER_PLANE, stride=8), :] = by_owner[:, b * 128 : (b + 1) * 128]
        late[...] = flat[pl.ds(0, PER_PLANE * 8), :].reshape(late.shape).astype(BF16)
        got_late[sh] = late[sh]

    def to_rows(got, start, count):
        flat[pl.ds(0, count * 8), :] = got[...].astype(F32).reshape(count * 8, 128)
        for b in range(8):
            rows_buf[pl.ds(start, count), pl.ds(b * 128, 128)] = flat[
                pl.ds(b, count, stride=8), :
            ].astype(BF16)

    @pl.when(last)
    def _():
        load_top(final).wait()

    for k in range(CHUNKS - 1):
        step(final, final * CHUNKS + k, k * CHUNK, CHUNK)
        if k == 0:

            @pl.when(first)
            def _():
                soon_units()
        if k == 1:
            hear_peer(final - 1)
            grad_tiles(final - 1, (0, 1), True)

            @pl.when(first)
            def _():
                lax.fori_loop(1, SHARDS // 2, hand_soon, 0)
        if k == 2:
            send_right(final, final * TOK, tail)
            grad_tiles(final - 1, (2, 3), True)

            @pl.when(first)
            def _():
                lax.fori_loop(SHARDS // 2, SHARDS, hand_soon, 0)

    for k in range(CHUNK // LATE):
        step(final, EARLY + k, tail + k * LATE, LATE)
    send_right(final + 1, final * TOK + tail, TOK - tail)
    grad_tiles(final, (0, 1, 2, 3), False)

    def block_rows(y, x):
        return pl.ds(pl.multiple_of((y * SIDE + x) * BLOCK, BLOCK), BLOCK)

    left_half = pl.ds(0, HALF)
    right_half = pl.ds(HALF, HALF)

    def x_copy(d, y):
        to = (px + d) % SIDE
        return pltpu.make_async_remote_copy(
            src_ref=send_x.at[y, pl.ds(pl.multiple_of(to * BLOCK, BLOCK), BLOCK)],
            dst_ref=recv_x.at[d - 1, y],
            send_sem=x_send.at[d - 1, y],
            recv_sem=x_recv.at[d - 1, y],
            device_id=at(py, to, core),
            device_id_type=MESH,
        )

    def y_copy(d, x):
        rows = pl.ds(pl.multiple_of(x * BLOCK, BLOCK), BLOCK)
        return pltpu.make_async_remote_copy(
            src_ref=send_y.at[d - 1, rows],
            dst_ref=recv_y.at[d - 1, rows],
            send_sem=y_send.at[d - 1, x],
            recv_sem=y_recv.at[d - 1, x],
            device_id=at((py + d) % SIDE, px, core),
            device_id_type=MESH,
        )

    def c_copy(h, e, c, kind):
        there = (py + e) % SIDE if h == 0 else (px + e) % SIDE
        return pltpu.make_async_remote_copy(
            src_ref=send_c.at[h, e, c],
            dst_ref=recv_c.at[kind, h, e],
            send_sem=c_send.at[h, e, c],
            recv_sem=c_recv.at[kind, h, e],
            device_id=at(there, px, c) if h == 0 else at(py, there, c),
            device_id_type=MESH,
        )

    order = (2, 1, 3, 0)
    frows = micro_rows(final)
    left_copy(final, act).wait_recv()
    right_copy(final, dz, final * TOK, tail).wait_recv()
    right_copy(final + 1, dz, final * TOK + tail, TOK - tail).wait_recv()
    for d in order:
        y = (py + d) % SIDE
        cols = pl.ds(pl.multiple_of(y * TILE, TILE), TILE)
        total = acc[cols, :] + dot_tn(peer_l[frows, cols], peer_r[frows, :])
        acc[cols, :] = total
        send_x[y] = total[:, :HALF].astype(BF16)
        for dx in (2, 1, 3):
            x_copy(dx, y).start()
        if d != 0:
            send_y[d - 1] = total[:, HALF:].astype(BF16)
    for e in order:
        for d in (2, 1, 3):
            y_copy(d, (px + e) % SIDE).start()
    route(final)

    @pl.when(jnp.logical_not(first))
    def _():
        for m in range(MICRO - 1):
            route_copy(m, 1).wait_recv()
        soon_units()
        lax.fori_loop(1, SHARDS, hand_soon, 0)
        route_copy(final, 1).wait_recv()

    late_units()
    lax.fori_loop(1, SHARDS, hand_late, 0)

    wait_all(all_ids, ids_recv)
    own = sec * SHARDS + sh
    feature = own // (SECTIONS * SHARDS // ids.shape[1])
    heard = all_ids[:, :, feature, :].reshape(SHARDS * MICRO, ids.shape[2])
    place = lax.broadcasted_iota(jnp.int32, heard.shape, 1) * ROWS_OWN + (heard & (ROWS_OWN - 1))
    ours = heard >> 10 == own
    low = jnp.min(jnp.where(ours, place, 1 << 20), axis=1, keepdims=True) & (ROWS_OWN - 1)
    high = jnp.max(jnp.where(ours, place, -1), axis=1, keepdims=True) & (ROWS_OWN - 1)
    at_lane = lax.broadcasted_iota(jnp.int32, (SHARDS * MICRO, 128), 1)
    parts = jnp.where(
        at_lane == 0,
        low >> 5,
        jnp.where(at_lane == 1, low & 31, jnp.where(at_lane == 2, high >> 5, high & 31)),
    )
    half = lax.broadcasted_iota(jnp.int32, (TOK, SHARDS * MICRO), 0) >> 1
    pair = lax.broadcasted_iota(jnp.int32, (TOK, SHARDS * MICRO), 1)
    came, micro = pair >> 2, pair & (MICRO - 1)
    place_of = jnp.where(
        micro < final, came * (MICRO - 1) + micro, SHARDS * (MICRO - 1) + came
    )
    twice = jnp.where(half == place_of, 1.0, 0.0).astype(BF16)
    both = jnp.dot(twice, parts.astype(F32).astype(BF16), preferred_element_type=F32)
    odd = lax.broadcasted_iota(jnp.int32, (TOK, 1), 0) & 1
    row_of = jnp.where(
        odd == 0, both[:, 0:1] * 32.0 + both[:, 1:2], both[:, 2:3] * 32.0 + both[:, 3:4]
    )
    named[...] = jnp.broadcast_to(row_of.astype(jnp.int32), (TOK, 128))
    put_named = pltpu.make_async_copy(named, out_named, out_sem.at[0])
    put_named.start()

    wait_all(all_ids, ids_send)
    wait_all(soon, soon_send)

    @pl.when((sec == 1) | last)
    def _():
        pool_copy(sec).wait_send()

    @pl.when(sec == 2)
    def _():
        hop_copy(0).wait_send()
        hop_copy(1).wait_send()

    @pl.when(last)
    def _():
        pass_copy(0).wait_send()
        pass_copy(1).wait_send()

    @pl.when(jnp.logical_not(first))
    def _():
        def left(c, carry):
            relay_copy(c, CHUNK).wait_send()
            return carry

        lax.fori_loop(0, EARLY, left, 0)
        for c in range(EARLY, PIECES):
            relay_copy(c, LATE).wait_send()

    @pl.when(first)
    def _():
        for m in range(MICRO):
            for p in range(1, SECTIONS):
                route_copy(m, p).wait_send()

    for m in range(MICRO):
        left_copy(m, act).wait_send()
    for m in range(final):
        right_copy(m, dz, m * TOK, TOK).wait_send()
    right_copy(final, dz, final * TOK, tail).wait_send()
    right_copy(final + 1, dz, final * TOK + tail, TOK - tail).wait_send()

    for e in order:
        y = (py + e) % SIDE
        x = (px + e) % SIDE
        for d in range(1, SIDE):
            x_copy(d, y).wait_recv()
            y_copy(d, x).wait_recv()
        total = acc[block_rows(y, px), left_half]
        other = acc[block_rows(py, x), right_half]
        for d in range(1, SIDE):
            total = total + recv_x[d - 1, y].astype(F32)
            xrows = pl.ds(pl.multiple_of(x * BLOCK, BLOCK), BLOCK)
            other = other + recv_y[d - 1, xrows, :].astype(F32)
        for h, part in ((0, total), (1, other)):
            for c in range(2):
                send_c[h, e, c] = part[c * SHARE : (c + 1) * SHARE, :].astype(BF16)
                if e == 0:

                    @pl.when(core == c)
                    def _(h=h, c=c, part=part):
                        own_c[h] = part[c * SHARE : (c + 1) * SHARE, :]

                    @pl.when(core != c)
                    def _(h=h, c=c):
                        c_copy(h, 0, c, core).start()
                else:
                    c_copy(h, e, c, core).start()

    wait_all(got_soon, soon_recv)
    to_rows(got_soon, 0, SOON)
    wait_all(got_late, late_recv)
    to_rows(got_late, SOON, PER_PLANE)
    put_rows = pltpu.make_async_copy(rows_buf, out_rows, out_sem.at[1])
    put_rows.start()
    wait_all(late, late_send)
    for d in range(1, SIDE):
        for y in range(SIDE):
            x_copy(d, y).wait_send()
            y_copy(d, y).wait_send()

    put_grads = []
    for kind, out in ((0, out_in), (1, out_out)):
        for h, cols in ((0, left_half), (1, right_half)):

            @pl.when(core == kind)
            def _(h=h, cols=cols, kind=kind):
                grads[kind, :, cols] = own_c[h]

            @pl.when(core != kind)
            def _(h=h, cols=cols, kind=kind):
                c_copy(h, 0, 1 - kind, kind).wait_recv()
                grads[kind, :, cols] = recv_c[kind, h, 0].astype(F32)

            total = grads[kind, :, cols]
            for e in range(1, SIDE):
                c_copy(h, e, 0, kind).wait_recv()
                total = total + recv_c[kind, h, e].astype(F32)
            grads[kind, :, cols] = total
        put = pltpu.make_async_copy(grads.at[kind], out, out_sem.at[2 + kind])
        put.start()
        put_grads.append(put)

    for h in range(2):
        for d in range(1, SIDE):
            for c in range(2):
                c_copy(h, d, c, core).wait_send()
        c_copy(h, 0, 1 - core, core).wait_send()
    for put in (put_named, put_rows, *put_grads):
        put.wait()


def relay(holder, saved, pooled, grad_top, w_in, w_out, ids):
    vmem = pl.BlockSpec(memory_space=pltpu.VMEM)
    anywhere = pl.BlockSpec(memory_space=pl.ANY)
    dma = pltpu.SemaphoreType.DMA
    tokens = MICRO * TOK
    return pl.pallas_call(
        kernel,
        out_shape=(
            jax.ShapeDtypeStruct((SHARE, WIDTH), F32),
            jax.ShapeDtypeStruct((SHARE, WIDTH), F32),
            jax.ShapeDtypeStruct((TOK, WIDTH), BF16),
            jax.ShapeDtypeStruct((TOK, 128), jnp.int32),
        ),
        in_specs=[pl.BlockSpec(memory_space=pltpu.SMEM)] + [anywhere] * 5 + [vmem],
        out_specs=(anywhere, anywhere, anywhere, anywhere),
        scratch_shapes=[
            pltpu.VMEM((WIDTH, WIDTH), BF16),
            pltpu.VMEM((WIDTH, WIDTH), BF16),
            pltpu.VMEM((WIDTH, WIDTH), BF16),
            pltpu.VMEM((WIDTH, WIDTH), BF16),
            pltpu.VMEM((tokens, WIDTH), BF16),
            pltpu.VMEM((tokens, WIDTH), BF16),
            pltpu.VMEM((tokens, WIDTH), BF16),
            pltpu.VMEM((SECTIONS, TOK, WIDTH), BF16),
            pltpu.VMEM((tokens, WIDTH), BF16),
            pltpu.VMEM((2, TOK, WIDTH), F32),
            pltpu.VMEM((tokens, WIDTH), BF16),
            pltpu.VMEM((WIDTH, WIDTH), F32),
            pltpu.VMEM((MICRO, 1, TOK), F32),
            pltpu.VMEM((SHARDS,) + ids.shape, jnp.int32),
            pltpu.VMEM((MICRO, TOK, WIDTH), BF16),
            pltpu.VMEM((TOK, WIDTH), BF16),
            pltpu.VMEM((SHARDS, 16 * (MICRO - 1), 128), BF16),
            pltpu.VMEM((SHARDS, 16 * (MICRO - 1), 128), BF16),
            pltpu.VMEM((SHARDS, 16, 128), BF16),
            pltpu.VMEM((SHARDS, 16, 128), BF16),
            pltpu.VMEM((SOON * 8, 128), F32),
            pltpu.VMEM((TOK, 128), jnp.int32),
            pltpu.VMEM((TOK, WIDTH), BF16),
            pltpu.VMEM((2, SHARE, WIDTH), F32),
            pltpu.VMEM((TOK, WIDTH), BF16),
            pltpu.VMEM((tokens, WIDTH), BF16),
            pltpu.VMEM((tokens, WIDTH), BF16),
            pltpu.VMEM((SIDE, SIDE * BLOCK, HALF), BF16),
            pltpu.VMEM((SIDE - 1, SIDE, BLOCK, HALF), BF16),
            pltpu.VMEM((SIDE - 1, SIDE * BLOCK, HALF), BF16),
            pltpu.VMEM((SIDE - 1, SIDE * BLOCK, HALF), BF16),
            pltpu.VMEM((2, SHARE, HALF), F32),
            pltpu.VMEM((2, SIDE, 2, SHARE, HALF), BF16),
            pltpu.VMEM((2, 2, SIDE, SHARE, HALF), BF16),
            dma((3 + MICRO,)),
            dma((MICRO,)),
            dma,
            dma((SECTIONS,)),
            dma((PIECES,)),
            dma((PIECES,)),
            dma((MICRO, SECTIONS)),
            dma((MICRO,)),
            dma,
            dma,
            dma,
            dma,
            pltpu.SemaphoreType.REGULAR((2,)),
            dma((2,)),
            dma((2,)),
            dma((2,)),
            dma((2,)),
            dma((4,)),
            dma,
            dma,
            dma((MICRO,)),
            dma((MICRO,)),
            dma((MICRO + 1,)),
            dma((MICRO + 1,)),
            dma((SIDE - 1, SIDE)),
            dma((SIDE - 1, SIDE)),
            dma((SIDE - 1, SIDE)),
            dma((SIDE - 1, SIDE)),
            dma((2, SIDE, 2)),
            dma((2, 2, SIDE)),
        ],
        compiler_params=pltpu.CompilerParams(
            collective_id=0, has_side_effects=True, vmem_limit_bytes=56 * 1024 * 1024
        ),
        cost_estimate=pl.CostEstimate(
            flops=10 * tokens * WIDTH * WIDTH, bytes_accessed=9 * 2**20, transcendentals=tokens * WIDTH
        ),
        name="relay",
    )(holder, saved, pooled, grad_top, w_in, w_out, ids)


def table_kernel(named, rows, grad_in, grad_out, table, out_in, out_out):
    block = pl.program_id(0)
    lane = lax.broadcasted_iota(jnp.int32, (TOK, WIDE), 1) + block * WIDE
    hit = jnp.where(lane == named[:, 0:1], 1.0, 0.0).astype(BF16)
    table[...] = dot_tn(hit, rows[...])

    @pl.when(block == 0)
    def _():
        out_in[...] = grad_in[...]
        out_out[...] = grad_out[...]


def owner_sums(named, rows, grad_in, grad_out):
    def whole(array):
        return pl.BlockSpec(array.shape, lambda b: (0, 0))

    return pl.pallas_call(
        table_kernel,
        grid=(ROWS_OWN // WIDE,),
        out_shape=(
            jax.ShapeDtypeStruct((ROWS_OWN, WIDTH), F32),
            jax.ShapeDtypeStruct(grad_in.shape, F32),
            jax.ShapeDtypeStruct(grad_out.shape, F32),
        ),
        in_specs=[whole(named), whole(rows), whole(grad_in), whole(grad_out)],
        out_specs=(
            pl.BlockSpec((WIDE, WIDTH), lambda b: (b, 0)),
            whole(grad_in),
            whole(grad_out),
        ),
        compiler_params=pltpu.CompilerParams(vmem_limit_bytes=32 * 1024 * 1024),
        cost_estimate=pl.CostEstimate(
            flops=2 * ROWS_OWN * TOK * WIDTH, bytes_accessed=5 * 2**20, transcendentals=0
        ),
        name="owner_sums",
    )(named, rows, grad_in, grad_out)


def local(saved, pooled, grad_top, w_in, w_out, feature_ids, holder_order):
    tokens = MICRO * TOK
    out_in, out_out, rows, named = relay(
        holder_order,
        saved.reshape(tokens, WIDTH),
        pooled.reshape(TOK, WIDTH),
        grad_top.reshape(tokens, WIDTH),
        w_in[0],
        w_out[0],
        jnp.transpose(feature_ids, (0, 2, 1)),
    )
    table_grad, grad_in, grad_out = owner_sums(named, rows, out_in, out_out)
    return (grad_in[None], grad_out[None], table_grad)


def solution(mesh):
    return jax.shard_map(
        local,
        mesh=mesh,
        in_specs=(
            P("section", None, "shard", None, None),
            P("section", "shard", None, None),
            P(None, "shard", None, None),
            P("section", None, None),
            P("section", None, None),
            P(None, "shard", None),
            P(),
        ),
        out_specs=(
            P("section", "shard", None),
            P("section", "shard", None),
            P(("section", "shard"), None),
        ),
        check_vma=False,
    )
```

```python
import jax
import jax.numpy as jnp
from jax import lax
from jax.experimental import pallas as pl
from jax.experimental.pallas import tpu as pltpu
from jax.sharding import PartitionSpec as P

ROWS_OWN = 1024
MESH = pl.DeviceIdType.MESH
F32 = jnp.float32
BF16 = jnp.bfloat16

SECTIONS = 4
SHARDS = 32
SIDE = 4
MICRO = 4
TOK = 256
CHUNK = 64
PIECE = 32
WIDTH = 1024
SHARE = WIDTH // SHARDS
PER_PLANE = TOK // SECTIONS
TILE = 256
WIDE = 512
CHUNKS = TOK // CHUNK
SPLIT = CHUNK // PIECE
PIECES = MICRO * TOK // PIECE
SOON = (MICRO - 1) * PER_PLANE
HALF = WIDTH // 2
BLOCK = 2 * SHARE


def dot_tn(a, b):
    return lax.dot_general(a, b, (((0,), (0,)), ((), ())), preferred_element_type=F32)


def kernel(
    holder,
    saved,
    pooled,
    grad_top,
    w_in,
    w_out,
    ids,
    out_in,
    out_out,
    out_rows,
    out_named,
    win,
    wout,
    win_t,
    wout_t,
    xbuf,
    gbuf,
    nbuf,
    pbuf,
    act,
    slope,
    dz,
    acc,
    rank,
    all_ids,
    sorted_rows,
    routed,
    soon,
    got_soon,
    late,
    got_late,
    flat,
    named,
    rows_buf,
    grads,
    transit,
    peer_l,
    peer_r,
    send_x,
    recv_x,
    send_y,
    recv_y,
    own_c,
    send_c,
    recv_c,
    load_sem,
    top_sem,
    pool_send,
    pool_recv,
    relay_send,
    relay_recv,
    route_send,
    route_recv,
    soon_send,
    soon_recv,
    late_send,
    late_recv,
    ready,
    hop_send,
    hop_recv,
    pass_send,
    pass_recv,
    out_sem,
    ids_send,
    ids_recv,
    l_send,
    l_recv,
    r_send,
    r_recv,
    x_send,
    x_recv,
    y_send,
    y_recv,
    c_send,
    c_recv,
):
    sec = lax.axis_index("section")
    sh = lax.axis_index("shard")
    core = sh % 2
    px = (sh // 2) % SIDE
    py = sh // (2 * SIDE)
    first = sec == 0
    last = sec == SECTIONS - 1

    def at(y, x, c):
        return (sec, (y * SIDE + x) * 2 + c)

    def micro_rows(m):
        return pl.ds(pl.multiple_of(m * TOK, TOK), TOK)

    def token_rows(start, size):
        return pl.ds(pl.multiple_of(start, size), size)

    def load_x(m):
        rows = micro_rows(m)
        return pltpu.make_async_copy(saved.at[rows], xbuf.at[rows], load_sem.at[2 + m])

    def load_top(m):
        rows = micro_rows(m)
        return pltpu.make_async_copy(grad_top.at[rows], gbuf.at[rows], top_sem.at[m])

    load_win = pltpu.make_async_copy(w_in, win, load_sem.at[0])
    load_wout = pltpu.make_async_copy(w_out, wout, load_sem.at[1])
    load_pool = pltpu.make_async_copy(pooled, pbuf.at[0], load_sem.at[2 + MICRO])

    load_win.start()
    load_x(0).start()
    load_wout.start()

    @pl.when(last)
    def _():
        for m in range(MICRO):
            load_top(m).start()

    for m in range(1, MICRO):
        load_x(m).start()

    @pl.when(first)
    def _():
        load_pool.start()

    barrier = pltpu.get_barrier_semaphore()

    def greet(y, x, c):
        pl.semaphore_signal(barrier, inc=1, device_id=at(y, x, c), device_id_type=MESH)

    for k in range(1, SECTIONS):
        pl.semaphore_signal(
            barrier, inc=1, device_id=((sec + k) % SECTIONS, sh), device_id_type=MESH
        )
    for k in range(1, SIDE):
        greet(py, (px + k) % SIDE, core)
        greet((py + k) % SIDE, px, core)
    greet(py, px, 1 - core)

    def tell_row():
        for k in range(1, SIDE):
            to = at(py, (px + k) % SIDE, core)
            pl.semaphore_signal(ready.at[0], inc=1, device_id=to, device_id_type=MESH)

    def tell_plane():
        pl.semaphore_wait(ready.at[0], SIDE - 1)
        for k in range(1, SIDE):
            to = at((py + k) % SIDE, px, core)
            pl.semaphore_signal(ready.at[1], inc=1, device_id=to, device_id_type=MESH)

    def tell_all():
        pl.semaphore_wait(ready.at[1], SIDE - 1)
        lax.fori_loop(1, SHARDS, tell_ids, 0)

    def pool_copy(s):
        return pltpu.make_async_remote_copy(
            src_ref=pooled,
            dst_ref=pbuf.at[s],
            send_sem=pool_send,
            recv_sem=pool_recv.at[s],
            device_id=(0, sh),
            device_id_type=MESH,
        )

    def pool_rows(h):
        return pl.ds(h * (TOK // 2), TOK // 2)

    def hop_copy(h):
        return pltpu.make_async_remote_copy(
            src_ref=pooled.at[pool_rows(h)],
            dst_ref=transit.at[pool_rows(h)],
            send_sem=hop_send.at[h],
            recv_sem=hop_recv.at[h],
            device_id=(SECTIONS - 1, sh),
            device_id_type=MESH,
        )

    def pass_copy(h):
        return pltpu.make_async_remote_copy(
            src_ref=transit.at[pool_rows(h)],
            dst_ref=pbuf.at[2, pool_rows(h)],
            send_sem=pass_send.at[h],
            recv_sem=pass_recv.at[h],
            device_id=(0, sh),
            device_id_type=MESH,
        )

    def pass_pool(h):
        hop_copy(h).wait_recv()
        pass_copy(h).start()

    def relay_copy(c):
        rows = token_rows(c * PIECE, PIECE)
        return pltpu.make_async_remote_copy(
            src_ref=nbuf.at[rows],
            dst_ref=gbuf.at[rows],
            send_sem=relay_send.at[c],
            recv_sem=relay_recv.at[c],
            device_id=(jnp.maximum(sec - 1, 0), sh),
            device_id_type=MESH,
        )

    def route_copy(m, p):
        return pltpu.make_async_remote_copy(
            src_ref=sorted_rows.at[m, pl.ds(p * PER_PLANE, PER_PLANE)],
            dst_ref=routed.at[pl.ds(pl.multiple_of(m * PER_PLANE, PER_PLANE), PER_PLANE)],
            send_sem=route_send.at[m, p],
            recv_sem=route_recv.at[m],
            device_id=(p, sh),
            device_id_type=MESH,
        )

    def ids_copy(to, came):
        return pltpu.make_async_remote_copy(
            src_ref=ids,
            dst_ref=all_ids.at[came],
            send_sem=ids_send,
            recv_sem=ids_recv,
            device_id=(sec, to),
            device_id_type=MESH,
        )

    def left_copy(m, source):
        rows = micro_rows(m)
        return pltpu.make_async_remote_copy(
            src_ref=source.at[rows],
            dst_ref=peer_l.at[rows],
            send_sem=l_send.at[m],
            recv_sem=l_recv.at[m],
            device_id=at(py, px, 1 - core),
            device_id_type=MESH,
        )

    def right_copy(n, source, start, size):
        rows = pl.ds(pl.multiple_of(start, 64), size)
        return pltpu.make_async_remote_copy(
            src_ref=source.at[rows],
            dst_ref=peer_r.at[rows],
            send_sem=r_send.at[n],
            recv_sem=r_recv.at[n],
            device_id=at(py, px, 1 - core),
            device_id_type=MESH,
        )

    def send_left(m):
        @pl.when(core == 0)
        def _():
            left_copy(m, act).start()

        @pl.when(core == 1)
        def _():
            left_copy(m, xbuf).start()

    def send_right(n, start, size):
        @pl.when(core == 0)
        def _():
            right_copy(n, gbuf, start, size).start()

        @pl.when(core == 1)
        def _():
            right_copy(n, dz, start, size).start()

    def forward_open(m):
        rows = micro_rows(m)
        load_x(m).wait()

        @pl.when(first)
        def _():
            slot = 0
            for j in range(1, MICRO):
                slot = jnp.where(holder[j] == m, j, slot)
            extra = pbuf[slot]
            xbuf[rows, :] = (xbuf[rows, :].astype(F32) + extra.astype(F32)).astype(BF16)

    def forward_tile(m, j):
        rows = micro_rows(m)
        cols = pl.ds(j * TILE, TILE)
        z = jnp.dot(xbuf[rows, :], win[:, cols], preferred_element_type=F32)
        sig = jax.nn.sigmoid(z)
        act[rows, cols] = (z * sig).astype(BF16)
        slope[m % 2, :, cols] = sig * (1.0 + z * (1.0 - sig))

    def forward(m):
        forward_open(m)
        for j in range(WIDTH // TILE):
            forward_tile(m, j)

    def backward(m, start, size):
        crows = token_rows(m * TOK + start, size)
        krows = pl.ds(start, size)
        for j in range(WIDTH // WIDE):
            cols = pl.ds(j * WIDE, WIDE)
            ga = jnp.dot(gbuf[crows, :], wout_t[:, cols], preferred_element_type=F32)
            dz[crows, cols] = (ga * slope[m % 2, krows, cols]).astype(BF16)
        for j in range(WIDTH // WIDE):
            cols = pl.ds(j * WIDE, WIDE)
            back = jnp.dot(dz[crows, :], win_t[:, cols], preferred_element_type=F32)
            nbuf[crows, cols] = (gbuf[crows, cols].astype(F32) + back).astype(BF16)

    def grad_tiles(m, tiles, and_peer):
        rows = micro_rows(m)
        for kind, left, right in ((0, xbuf, dz), (1, act, gbuf)):

            @pl.when(core == kind)
            def _(left=left, right=right):
                for i in tiles:
                    cols = pl.ds(i * TILE, TILE)
                    total = acc[cols, :] + dot_tn(left[rows, cols], right[rows, :])
                    if and_peer:
                        total = total + dot_tn(peer_l[rows, cols], peer_r[rows, :])
                    acc[cols, :] = total

    def hear_peer(m):
        left_copy(m, act).wait_recv()
        right_copy(m, dz, m * TOK, TOK).wait_recv()

    load_win.wait()
    for j in range(WIDTH // TILE):
        cols = pl.ds(j * TILE, TILE)
        win_t[:, cols] = win[cols, :].T

    @pl.when(jnp.logical_not(first))
    def _():
        forward(0)

    load_wout.wait()
    for j in range(WIDTH // TILE):
        cols = pl.ds(j * TILE, TILE)
        wout_t[:, cols] = wout[cols, :].T

    pl.semaphore_wait(barrier, SECTIONS - 1 + 2 * (SIDE - 1) + 1)
    tell_row()

    @pl.when((sec == 1) | last)
    def _():
        pool_copy(sec).start()

    @pl.when(sec == 2)
    def _():
        hop_copy(0).start()
        hop_copy(1).start()

    def clear(i, carry):
        rows = pl.ds(pl.multiple_of(i * 64, 64), 64)
        acc[rows, :] = jnp.zeros((64, WIDTH), F32)
        return carry

    def tell_ids(k, carry):
        ids_copy((sh + k) % SHARDS, sh).start()
        return carry

    @pl.when(first)
    def _():
        lax.fori_loop(0, WIDTH // 64, clear, 0)
        tell_plane()
        row = lax.broadcasted_iota(jnp.int32, (TOK, TOK), 0)
        col = lax.broadcasted_iota(jnp.int32, (TOK, TOK), 1)
        feat = ids.shape[1]
        lane = lax.broadcasted_iota(jnp.int32, (ids.shape[2], TOK), 1)
        lead = lax.broadcasted_iota(jnp.int32, (ids.shape[2], TOK), 0)
        widen = jnp.where(lane >> 3 == lead, 1.0, 0.0).astype(BF16)
        for m in range(MICRO):
            owner = (ids[m] >> 10).astype(F32).astype(BF16)
            wide = jnp.dot(owner, widen, preferred_element_type=F32)
            inner = lax.broadcasted_iota(jnp.int32, (feat, TOK), 1) & 7
            outer = lax.broadcasted_iota(jnp.int32, (feat, TOK), 0)
            across = jnp.sum(jnp.where(inner == outer, wide, 0.0), axis=0, keepdims=True)
            down = jnp.sum(jnp.where(row == col, across, 0.0), axis=1, keepdims=True)
            earlier = jnp.where((down == across) & (row < col), 1.0, 0.0)
            rank[m] = 2.0 * across + jnp.sum(earlier, axis=0, keepdims=True)
        tell_all()
        load_pool.wait()
        for s in (1, SECTIONS - 1):
            pool_copy(s).wait_recv()
        for h in range(2):
            pass_copy(h).wait_recv()
        forward(0)

    @pl.when(last)
    def _():
        load_top(0).wait()
        for k in range(CHUNKS):
            backward(0, k * CHUNK, CHUNK)
            for i in range(SPLIT):
                relay_copy(k * SPLIT + i).start()

    @pl.when(jnp.logical_not(first))
    def _():
        tell_plane()
        lax.fori_loop(0, WIDTH // 64, clear, 0)
        tell_all()

    @pl.when(last)
    def _():
        pass_pool(0)

    all_ids[sh] = ids[...]
    send_left(0)

    def step(m, start, size):
        pieces = [(m * TOK + start) // PIECE + i for i in range(size // PIECE)]

        @pl.when(jnp.logical_not(last))
        def _():
            for c in pieces:
                relay_copy(c).wait_recv()

        backward(m, start, size)

        @pl.when(jnp.logical_not(first))
        def _():
            for c in pieces:
                relay_copy(c).start()

    inner = jnp.logical_not(first | last)

    def chunks(m, slots, final_one):
        for k in range(CHUNKS):
            fine = final_one and k == CHUNKS - 1
            for i in range(SPLIT):

                def piece(k=k, i=i):
                    step(m, k * CHUNK + i * PIECE, PIECE)

                if fine:
                    piece()
                else:
                    pl.when(inner)(piece)
                if not fine and i == SPLIT - 1:

                    @pl.when(first | (last & (m > 0)))
                    def _(k=k):
                        step(m, k * CHUNK, CHUNK)

                slots[k * SPLIT + i]()

    def route(m):
        rows = micro_rows(m)

        @pl.when(first)
        def _():
            target = lax.broadcasted_iota(jnp.int32, (TOK, TOK), 0).astype(F32)
            pick = jnp.where(target == rank[m], 1.0, 0.0).astype(BF16)
            ordered = jnp.dot(pick, nbuf[rows, :], preferred_element_type=F32).astype(BF16)
            sorted_rows[m] = ordered
            for p in range(1, SECTIONS):
                route_copy(m, p).start()
            routed[pl.ds(pl.multiple_of(m * PER_PLANE, PER_PLANE), PER_PLANE), :] = ordered[
                :PER_PLANE, :
            ]

    def micro_step(m, carry):
        @pl.when(last & (m == 2))
        def _():
            pass_pool(1)

        @pl.when(last & (m > 0))
        def _():
            load_top(m).wait()

        def forward_slot(j):
            def work():
                if j == 0:
                    forward_open(m + 1)
                forward_tile(m + 1, j)
                if j == WIDTH // TILE - 1:
                    send_left(m + 1)

            return work

        def grad_slot(i):
            def work():
                @pl.when(m > 0)
                def _():
                    if i == 0:
                        hear_peer(m - 1)
                    grad_tiles(m - 1, (i,), True)

            return work

        tiles = range(WIDTH // TILE)
        chunks(m, [forward_slot(j) for j in tiles] + [grad_slot(i) for i in tiles], False)
        send_right(m, m * TOK, TOK)
        route(m)
        return carry

    lax.fori_loop(0, MICRO - 1, micro_step, 0)

    final = MICRO - 1
    tail = TOK - CHUNK

    def unit_copy(source, target, send, recv, to, came):
        return pltpu.make_async_remote_copy(
            src_ref=source.at[to],
            dst_ref=target.at[came],
            send_sem=send,
            recv_sem=recv,
            device_id=(sec, to),
            device_id_type=MESH,
        )

    def hand_soon(k, carry):
        to = (sh + k) % SHARDS
        unit_copy(soon, got_soon, soon_send, soon_recv, to, sh).start()
        return carry

    def hand_late(k, carry):
        to = (sh + k) % SHARDS
        unit_copy(late, got_late, late_send, late_recv, to, sh).start()
        return carry

    def wait_all(ref, semaphore):
        others = ref.at[pl.ds(0, SHARDS - 1)]
        pltpu.make_async_copy(others, others, semaphore).wait()

    def soon_units():
        row = lax.broadcasted_iota(jnp.int32, (SOON, SOON), 0)
        col = lax.broadcasted_iota(jnp.int32, (SOON, SOON), 1)
        target = ((col >> 1) & (SHARDS - 1)) * (2 * (MICRO - 1)) + (col >> 6) * 2 + (col & 1)
        regroup = jnp.where(row == target, 1.0, 0.0).astype(BF16)
        by_owner = jnp.dot(regroup, routed[pl.ds(0, SOON), :], preferred_element_type=F32)
        for b in range(8):
            flat[pl.ds(b, SOON, stride=8), :] = by_owner[:, b * 128 : (b + 1) * 128]
        soon[...] = flat[...].reshape(soon.shape).astype(BF16)
        got_soon[sh] = soon[sh]

    def late_units():
        by_owner = routed[pl.ds(SOON, PER_PLANE), :].astype(F32)
        for b in range(8):
            flat[pl.ds(b, PER_PLANE, stride=8), :] = by_owner[:, b * 128 : (b + 1) * 128]
        late[...] = flat[pl.ds(0, PER_PLANE * 8), :].reshape(late.shape).astype(BF16)
        got_late[sh] = late[sh]

    def to_rows(got, start, count):
        flat[pl.ds(0, count * 8), :] = got[...].astype(F32).reshape(count * 8, 128)
        for b in range(8):
            rows_buf[pl.ds(start, count), pl.ds(b * 128, 128)] = flat[
                pl.ds(b, count, stride=8), :
            ].astype(BF16)

    @pl.when(last)
    def _():
        load_top(final).wait()

    def final_slot(n):
        def work():
            if n == 1:
                hear_peer(final - 1)
            if 1 <= n <= WIDTH // TILE:
                grad_tiles(final - 1, (n - 1,), True)
            if n == 5:
                send_right(final, final * TOK, tail)

            @pl.when(first)
            def _():
                if n == 0:
                    soon_units()
                if n == 2:
                    lax.fori_loop(1, SHARDS // 2, hand_soon, 0)
                if n == 4:
                    lax.fori_loop(SHARDS // 2, SHARDS, hand_soon, 0)

        return work

    chunks(final, [final_slot(n) for n in range(CHUNKS * SPLIT)], True)
    send_right(final + 1, final * TOK + tail, TOK - tail)
    grad_tiles(final, (0, 1, 2, 3), False)

    def block_rows(y, x):
        return pl.ds(pl.multiple_of((y * SIDE + x) * BLOCK, BLOCK), BLOCK)

    left_half = pl.ds(0, HALF)
    right_half = pl.ds(HALF, HALF)

    def x_copy(d, y):
        to = (px + d) % SIDE
        return pltpu.make_async_remote_copy(
            src_ref=send_x.at[y, pl.ds(pl.multiple_of(to * BLOCK, BLOCK), BLOCK)],
            dst_ref=recv_x.at[d - 1, y],
            send_sem=x_send.at[d - 1, y],
            recv_sem=x_recv.at[d - 1, y],
            device_id=at(py, to, core),
            device_id_type=MESH,
        )

    def y_copy(d, x):
        rows = pl.ds(pl.multiple_of(x * BLOCK, BLOCK), BLOCK)
        return pltpu.make_async_remote_copy(
            src_ref=send_y.at[d - 1, rows],
            dst_ref=recv_y.at[d - 1, rows],
            send_sem=y_send.at[d - 1, x],
            recv_sem=y_recv.at[d - 1, x],
            device_id=at((py + d) % SIDE, px, core),
            device_id_type=MESH,
        )

    def c_copy(h, e, c, kind):
        there = (py + e) % SIDE if h == 0 else (px + e) % SIDE
        return pltpu.make_async_remote_copy(
            src_ref=send_c.at[h, e, c],
            dst_ref=recv_c.at[kind, h, e],
            send_sem=c_send.at[h, e, c],
            recv_sem=c_recv.at[kind, h, e],
            device_id=at(there, px, c) if h == 0 else at(py, there, c),
            device_id_type=MESH,
        )

    order = (2, 1, 3, 0)
    frows = micro_rows(final)
    left_copy(final, act).wait_recv()
    right_copy(final, dz, final * TOK, tail).wait_recv()
    right_copy(final + 1, dz, final * TOK + tail, TOK - tail).wait_recv()
    for d in order:
        y = (py + d) % SIDE
        cols = pl.ds(pl.multiple_of(y * TILE, TILE), TILE)
        total = acc[cols, :] + dot_tn(peer_l[frows, cols], peer_r[frows, :])
        acc[cols, :] = total
        send_x[y] = total[:, :HALF].astype(BF16)
        for dx in (2, 1, 3):
            x_copy(dx, y).start()
        if d != 0:
            send_y[d - 1] = total[:, HALF:].astype(BF16)
    for e in order:
        for d in (2, 1, 3):
            y_copy(d, (px + e) % SIDE).start()
    route(final)

    @pl.when(jnp.logical_not(first))
    def _():
        for m in range(MICRO - 1):
            route_copy(m, 1).wait_recv()
        soon_units()
        lax.fori_loop(1, SHARDS, hand_soon, 0)
        route_copy(final, 1).wait_recv()

    late_units()
    lax.fori_loop(1, SHARDS, hand_late, 0)

    wait_all(all_ids, ids_recv)
    own = sec * SHARDS + sh
    feature = own // (SECTIONS * SHARDS // ids.shape[1])
    heard = all_ids[:, :, feature, :].reshape(SHARDS * MICRO, ids.shape[2])
    place = lax.broadcasted_iota(jnp.int32, heard.shape, 1) * ROWS_OWN + (heard & (ROWS_OWN - 1))
    ours = heard >> 10 == own
    low = jnp.min(jnp.where(ours, place, 1 << 20), axis=1, keepdims=True) & (ROWS_OWN - 1)
    high = jnp.max(jnp.where(ours, place, -1), axis=1, keepdims=True) & (ROWS_OWN - 1)
    at_lane = lax.broadcasted_iota(jnp.int32, (SHARDS * MICRO, 128), 1)
    parts = jnp.where(
        at_lane == 0,
        low >> 5,
        jnp.where(at_lane == 1, low & 31, jnp.where(at_lane == 2, high >> 5, high & 31)),
    )
    half = lax.broadcasted_iota(jnp.int32, (TOK, SHARDS * MICRO), 0) >> 1
    pair = lax.broadcasted_iota(jnp.int32, (TOK, SHARDS * MICRO), 1)
    came, micro = pair >> 2, pair & (MICRO - 1)
    place_of = jnp.where(
        micro < final, came * (MICRO - 1) + micro, SHARDS * (MICRO - 1) + came
    )
    twice = jnp.where(half == place_of, 1.0, 0.0).astype(BF16)
    both = jnp.dot(twice, parts.astype(F32).astype(BF16), preferred_element_type=F32)
    odd = lax.broadcasted_iota(jnp.int32, (TOK, 1), 0) & 1
    row_of = jnp.where(
        odd == 0, both[:, 0:1] * 32.0 + both[:, 1:2], both[:, 2:3] * 32.0 + both[:, 3:4]
    )
    named[...] = jnp.broadcast_to(row_of.astype(jnp.int32), (TOK, 128))
    put_named = pltpu.make_async_copy(named, out_named, out_sem.at[0])
    put_named.start()

    wait_all(all_ids, ids_send)
    wait_all(soon, soon_send)

    @pl.when((sec == 1) | last)
    def _():
        pool_copy(sec).wait_send()

    @pl.when(sec == 2)
    def _():
        hop_copy(0).wait_send()
        hop_copy(1).wait_send()

    @pl.when(last)
    def _():
        pass_copy(0).wait_send()
        pass_copy(1).wait_send()

    @pl.when(jnp.logical_not(first))
    def _():
        def left(c, carry):
            relay_copy(c).wait_send()
            return carry

        lax.fori_loop(0, PIECES, left, 0)

    @pl.when(first)
    def _():
        for m in range(final):
            for p in range(1, SECTIONS):
                route_copy(m, p).wait_send()

    for m in range(MICRO):
        left_copy(m, act).wait_send()
    for m in range(final):
        right_copy(m, dz, m * TOK, TOK).wait_send()
    right_copy(final, dz, final * TOK, tail).wait_send()
    right_copy(final + 1, dz, final * TOK + tail, TOK - tail).wait_send()

    for e in order:
        y = (py + e) % SIDE
        x = (px + e) % SIDE
        for d in range(1, SIDE):
            x_copy(d, y).wait_recv()
            y_copy(d, x).wait_recv()
        total = acc[block_rows(y, px), left_half]
        other = acc[block_rows(py, x), right_half]
        for d in range(1, SIDE):
            total = total + recv_x[d - 1, y].astype(F32)
            xrows = pl.ds(pl.multiple_of(x * BLOCK, BLOCK), BLOCK)
            other = other + recv_y[d - 1, xrows, :].astype(F32)
        for h, part in ((0, total), (1, other)):
            for c in range(2):
                send_c[h, e, c] = part[c * SHARE : (c + 1) * SHARE, :].astype(BF16)
                if e == 0:

                    @pl.when(core == c)
                    def _(h=h, c=c, part=part):
                        own_c[h] = part[c * SHARE : (c + 1) * SHARE, :]

                    @pl.when(core != c)
                    def _(h=h, c=c):
                        c_copy(h, 0, c, core).start()
                else:
                    c_copy(h, e, c, core).start()

    wait_all(got_soon, soon_recv)
    to_rows(got_soon, 0, SOON)
    wait_all(got_late, late_recv)
    to_rows(got_late, SOON, PER_PLANE)
    put_rows = pltpu.make_async_copy(rows_buf, out_rows, out_sem.at[1])
    put_rows.start()
    wait_all(late, late_send)

    @pl.when(first)
    def _():
        for p in range(1, SECTIONS):
            route_copy(final, p).wait_send()

    for d in range(1, SIDE):
        for y in range(SIDE):
            x_copy(d, y).wait_send()
            y_copy(d, y).wait_send()

    put_grads = []
    for kind, out in ((0, out_in), (1, out_out)):
        for h, cols in ((0, left_half), (1, right_half)):

            @pl.when(core == kind)
            def _(h=h, cols=cols, kind=kind):
                grads[kind, :, cols] = own_c[h]

            @pl.when(core != kind)
            def _(h=h, cols=cols, kind=kind):
                c_copy(h, 0, 1 - kind, kind).wait_recv()
                grads[kind, :, cols] = recv_c[kind, h, 0].astype(F32)

            total = grads[kind, :, cols]
            for e in range(1, SIDE):
                c_copy(h, e, 0, kind).wait_recv()
                total = total + recv_c[kind, h, e].astype(F32)
            grads[kind, :, cols] = total
        put = pltpu.make_async_copy(grads.at[kind], out, out_sem.at[2 + kind])
        put.start()
        put_grads.append(put)

    for h in range(2):
        for d in range(1, SIDE):
            for c in range(2):
                c_copy(h, d, c, core).wait_send()
        c_copy(h, 0, 1 - core, core).wait_send()
    for put in (put_named, put_rows, *put_grads):
        put.wait()


def relay(holder, saved, pooled, grad_top, w_in, w_out, ids):
    vmem = pl.BlockSpec(memory_space=pltpu.VMEM)
    anywhere = pl.BlockSpec(memory_space=pl.ANY)
    dma = pltpu.SemaphoreType.DMA
    tokens = MICRO * TOK
    return pl.pallas_call(
        kernel,
        out_shape=(
            jax.ShapeDtypeStruct((SHARE, WIDTH), F32),
            jax.ShapeDtypeStruct((SHARE, WIDTH), F32),
            jax.ShapeDtypeStruct((TOK, WIDTH), BF16),
            jax.ShapeDtypeStruct((TOK, 128), jnp.int32),
        ),
        in_specs=[pl.BlockSpec(memory_space=pltpu.SMEM)] + [anywhere] * 5 + [vmem],
        out_specs=(anywhere, anywhere, anywhere, anywhere),
        scratch_shapes=[
            pltpu.VMEM((WIDTH, WIDTH), BF16),
            pltpu.VMEM((WIDTH, WIDTH), BF16),
            pltpu.VMEM((WIDTH, WIDTH), BF16),
            pltpu.VMEM((WIDTH, WIDTH), BF16),
            pltpu.VMEM((tokens, WIDTH), BF16),
            pltpu.VMEM((tokens, WIDTH), BF16),
            pltpu.VMEM((tokens, WIDTH), BF16),
            pltpu.VMEM((SECTIONS, TOK, WIDTH), BF16),
            pltpu.VMEM((tokens, WIDTH), BF16),
            pltpu.VMEM((2, TOK, WIDTH), F32),
            pltpu.VMEM((tokens, WIDTH), BF16),
            pltpu.VMEM((WIDTH, WIDTH), F32),
            pltpu.VMEM((MICRO, 1, TOK), F32),
            pltpu.VMEM((SHARDS,) + ids.shape, jnp.int32),
            pltpu.VMEM((MICRO, TOK, WIDTH), BF16),
            pltpu.VMEM((TOK, WIDTH), BF16),
            pltpu.VMEM((SHARDS, 16 * (MICRO - 1), 128), BF16),
            pltpu.VMEM((SHARDS, 16 * (MICRO - 1), 128), BF16),
            pltpu.VMEM((SHARDS, 16, 128), BF16),
            pltpu.VMEM((SHARDS, 16, 128), BF16),
            pltpu.VMEM((SOON * 8, 128), F32),
            pltpu.VMEM((TOK, 128), jnp.int32),
            pltpu.VMEM((TOK, WIDTH), BF16),
            pltpu.VMEM((2, SHARE, WIDTH), F32),
            pltpu.VMEM((TOK, WIDTH), BF16),
            pltpu.VMEM((tokens, WIDTH), BF16),
            pltpu.VMEM((tokens, WIDTH), BF16),
            pltpu.VMEM((SIDE, SIDE * BLOCK, HALF), BF16),
            pltpu.VMEM((SIDE - 1, SIDE, BLOCK, HALF), BF16),
            pltpu.VMEM((SIDE - 1, SIDE * BLOCK, HALF), BF16),
            pltpu.VMEM((SIDE - 1, SIDE * BLOCK, HALF), BF16),
            pltpu.VMEM((2, SHARE, HALF), F32),
            pltpu.VMEM((2, SIDE, 2, SHARE, HALF), BF16),
            pltpu.VMEM((2, 2, SIDE, SHARE, HALF), BF16),
            dma((3 + MICRO,)),
            dma((MICRO,)),
            dma,
            dma((SECTIONS,)),
            dma((PIECES,)),
            dma((PIECES,)),
            dma((MICRO, SECTIONS)),
            dma((MICRO,)),
            dma,
            dma,
            dma,
            dma,
            pltpu.SemaphoreType.REGULAR((2,)),
            dma((2,)),
            dma((2,)),
            dma((2,)),
            dma((2,)),
            dma((4,)),
            dma,
            dma,
            dma((MICRO,)),
            dma((MICRO,)),
            dma((MICRO + 1,)),
            dma((MICRO + 1,)),
            dma((SIDE - 1, SIDE)),
            dma((SIDE - 1, SIDE)),
            dma((SIDE - 1, SIDE)),
            dma((SIDE - 1, SIDE)),
            dma((2, SIDE, 2)),
            dma((2, 2, SIDE)),
        ],
        compiler_params=pltpu.CompilerParams(
            collective_id=0, has_side_effects=True, vmem_limit_bytes=56 * 1024 * 1024
        ),
        cost_estimate=pl.CostEstimate(
            flops=10 * tokens * WIDTH * WIDTH, bytes_accessed=9 * 2**20, transcendentals=tokens * WIDTH
        ),
        name="relay",
    )(holder, saved, pooled, grad_top, w_in, w_out, ids)


def table_kernel(named, rows, grad_in, grad_out, table, out_in, out_out):
    block = pl.program_id(0)
    lane = lax.broadcasted_iota(jnp.int32, (TOK, WIDE), 1) + block * WIDE
    hit = jnp.where(lane == named[:, 0:1], 1.0, 0.0).astype(BF16)
    table[...] = dot_tn(hit, rows[...])

    @pl.when(block == 0)
    def _():
        out_in[...] = grad_in[...]
        out_out[...] = grad_out[...]


def owner_sums(named, rows, grad_in, grad_out):
    def whole(array):
        return pl.BlockSpec(array.shape, lambda b: (0, 0))

    return pl.pallas_call(
        table_kernel,
        grid=(ROWS_OWN // WIDE,),
        out_shape=(
            jax.ShapeDtypeStruct((ROWS_OWN, WIDTH), F32),
            jax.ShapeDtypeStruct(grad_in.shape, F32),
            jax.ShapeDtypeStruct(grad_out.shape, F32),
        ),
        in_specs=[whole(named), whole(rows), whole(grad_in), whole(grad_out)],
        out_specs=(
            pl.BlockSpec((WIDE, WIDTH), lambda b: (b, 0)),
            whole(grad_in),
            whole(grad_out),
        ),
        compiler_params=pltpu.CompilerParams(vmem_limit_bytes=32 * 1024 * 1024),
        cost_estimate=pl.CostEstimate(
            flops=2 * ROWS_OWN * TOK * WIDTH, bytes_accessed=5 * 2**20, transcendentals=0
        ),
        name="owner_sums",
    )(named, rows, grad_in, grad_out)


def local(saved, pooled, grad_top, w_in, w_out, feature_ids, holder_order):
    tokens = MICRO * TOK
    out_in, out_out, rows, named = relay(
        holder_order,
        saved.reshape(tokens, WIDTH),
        pooled.reshape(TOK, WIDTH),
        grad_top.reshape(tokens, WIDTH),
        w_in[0],
        w_out[0],
        jnp.transpose(feature_ids, (0, 2, 1)),
    )
    table_grad, grad_in, grad_out = owner_sums(named, rows, out_in, out_out)
    return (grad_in[None], grad_out[None], table_grad)


def solution(mesh):
    return jax.shard_map(
        local,
        mesh=mesh,
        in_specs=(
            P("section", None, "shard", None, None),
            P("section", "shard", None, None),
            P(None, "shard", None, None),
            P("section", None, None),
            P("section", None, None),
            P(None, "shard", None),
            P(),
        ),
        out_specs=(
            P("section", "shard", None),
            P("section", "shard", None),
            P(("section", "shard"), None),
        ),
        check_vma=False,
    )
```

```python
import jax
import jax.numpy as jnp
from jax import lax
from jax.experimental import pallas as pl
from jax.experimental.pallas import tpu as pltpu
from jax.sharding import PartitionSpec as P

ROWS_OWN = 1024
MESH = pl.DeviceIdType.MESH
F32 = jnp.float32
BF16 = jnp.bfloat16

SECTIONS = 4
SHARDS = 32
SIDE = 4
MICRO = 4
TOK = 256
CHUNK = 64
PIECE = 32
WIDTH = 1024
SHARE = WIDTH // SHARDS
PER_PLANE = TOK // SECTIONS
TILE = 256
WIDE = 512
CHUNKS = TOK // CHUNK
SPLIT = CHUNK // PIECE
PIECES = MICRO * TOK // PIECE
SOON = (MICRO - 1) * PER_PLANE
HALF = WIDTH // 2
BLOCK = 2 * SHARE


def dot_tn(a, b):
    return lax.dot_general(a, b, (((0,), (0,)), ((), ())), preferred_element_type=F32)


def kernel(
    holder,
    saved,
    pooled,
    grad_top,
    w_in,
    w_out,
    ids,
    out_in,
    out_out,
    out_rows,
    out_named,
    win,
    wout,
    win_t,
    wout_t,
    xbuf,
    gbuf,
    nbuf,
    pbuf,
    act,
    slope,
    dz,
    acc,
    rank,
    all_ids,
    sorted_rows,
    routed,
    soon,
    got_soon,
    late,
    got_late,
    flat,
    named,
    rows_buf,
    grads,
    transit,
    peer_l,
    peer_r,
    send_x,
    recv_x,
    send_y,
    recv_y,
    own_c,
    send_c,
    recv_c,
    load_sem,
    top_sem,
    pool_send,
    pool_recv,
    relay_send,
    relay_recv,
    route_send,
    route_recv,
    soon_send,
    soon_recv,
    late_send,
    late_recv,
    ready,
    hop_send,
    hop_recv,
    pass_send,
    pass_recv,
    out_sem,
    ids_send,
    ids_recv,
    l_send,
    l_recv,
    r_send,
    r_recv,
    x_send,
    x_recv,
    y_send,
    y_recv,
    c_send,
    c_recv,
):
    sec = lax.axis_index("section")
    sh = lax.axis_index("shard")
    core = sh % 2
    px = (sh // 2) % SIDE
    py = sh // (2 * SIDE)
    first = sec == 0
    last = sec == SECTIONS - 1

    def at(y, x, c):
        return (sec, (y * SIDE + x) * 2 + c)

    def micro_rows(m):
        return pl.ds(pl.multiple_of(m * TOK, TOK), TOK)

    def token_rows(start, size):
        return pl.ds(pl.multiple_of(start, size), size)

    def load_x(m):
        rows = micro_rows(m)
        return pltpu.make_async_copy(saved.at[rows], xbuf.at[rows], load_sem.at[2 + m])

    def load_top(m):
        rows = micro_rows(m)
        return pltpu.make_async_copy(grad_top.at[rows], gbuf.at[rows], top_sem.at[m])

    load_win = pltpu.make_async_copy(w_in, win, load_sem.at[0])
    load_wout = pltpu.make_async_copy(w_out, wout, load_sem.at[1])
    load_pool = pltpu.make_async_copy(pooled, pbuf.at[0], load_sem.at[2 + MICRO])

    load_win.start()
    load_x(0).start()
    load_wout.start()

    @pl.when(last)
    def _():
        load_top(0).start()

    @pl.when(first)
    def _():
        load_pool.start()

    barrier = pltpu.get_barrier_semaphore()

    def greet(y, x, c):
        pl.semaphore_signal(barrier, inc=1, device_id=at(y, x, c), device_id_type=MESH)

    for k in range(1, SECTIONS):
        pl.semaphore_signal(
            barrier, inc=1, device_id=((sec + k) % SECTIONS, sh), device_id_type=MESH
        )
    for k in range(1, SIDE):
        greet(py, (px + k) % SIDE, core)
        greet((py + k) % SIDE, px, core)
    greet(py, px, 1 - core)

    def tell_row():
        for k in range(1, SIDE):
            to = at(py, (px + k) % SIDE, core)
            pl.semaphore_signal(ready.at[0], inc=1, device_id=to, device_id_type=MESH)

    def tell_plane():
        pl.semaphore_wait(ready.at[0], SIDE - 1)
        for k in range(1, SIDE):
            to = at((py + k) % SIDE, px, core)
            pl.semaphore_signal(ready.at[1], inc=1, device_id=to, device_id_type=MESH)

    def tell_all():
        pl.semaphore_wait(ready.at[1], SIDE - 1)
        lax.fori_loop(1, SHARDS, tell_ids, 0)

    def pool_copy(s):
        return pltpu.make_async_remote_copy(
            src_ref=pooled,
            dst_ref=pbuf.at[s],
            send_sem=pool_send,
            recv_sem=pool_recv.at[s],
            device_id=(0, sh),
            device_id_type=MESH,
        )

    def pool_rows(h):
        return pl.ds(h * (TOK // 2), TOK // 2)

    def hop_copy(h):
        return pltpu.make_async_remote_copy(
            src_ref=pooled.at[pool_rows(h)],
            dst_ref=transit.at[pool_rows(h)],
            send_sem=hop_send.at[h],
            recv_sem=hop_recv.at[h],
            device_id=(SECTIONS - 1, sh),
            device_id_type=MESH,
        )

    def pass_copy(h):
        return pltpu.make_async_remote_copy(
            src_ref=transit.at[pool_rows(h)],
            dst_ref=pbuf.at[2, pool_rows(h)],
            send_sem=pass_send.at[h],
            recv_sem=pass_recv.at[h],
            device_id=(0, sh),
            device_id_type=MESH,
        )

    def pass_pool(h):
        hop_copy(h).wait_recv()
        pass_copy(h).start()

    def relay_copy(c):
        rows = token_rows(c * PIECE, PIECE)
        return pltpu.make_async_remote_copy(
            src_ref=nbuf.at[rows],
            dst_ref=gbuf.at[rows],
            send_sem=relay_send.at[c],
            recv_sem=relay_recv.at[c],
            device_id=(jnp.maximum(sec - 1, 0), sh),
            device_id_type=MESH,
        )

    def route_copy(m, p):
        return pltpu.make_async_remote_copy(
            src_ref=sorted_rows.at[m, pl.ds(p * PER_PLANE, PER_PLANE)],
            dst_ref=routed.at[pl.ds(pl.multiple_of(m * PER_PLANE, PER_PLANE), PER_PLANE)],
            send_sem=route_send.at[m, p],
            recv_sem=route_recv.at[m],
            device_id=(p, sh),
            device_id_type=MESH,
        )

    def ids_copy(to, came):
        return pltpu.make_async_remote_copy(
            src_ref=ids,
            dst_ref=all_ids.at[came],
            send_sem=ids_send,
            recv_sem=ids_recv,
            device_id=(sec, to),
            device_id_type=MESH,
        )

    def left_copy(m, source):
        rows = micro_rows(m)
        return pltpu.make_async_remote_copy(
            src_ref=source.at[rows],
            dst_ref=peer_l.at[rows],
            send_sem=l_send.at[m],
            recv_sem=l_recv.at[m],
            device_id=at(py, px, 1 - core),
            device_id_type=MESH,
        )

    def right_copy(n, source, start, size):
        rows = pl.ds(pl.multiple_of(start, 64), size)
        return pltpu.make_async_remote_copy(
            src_ref=source.at[rows],
            dst_ref=peer_r.at[rows],
            send_sem=r_send.at[n],
            recv_sem=r_recv.at[n],
            device_id=at(py, px, 1 - core),
            device_id_type=MESH,
        )

    def send_left(m):
        @pl.when(core == 0)
        def _():
            left_copy(m, act).start()

        @pl.when(core == 1)
        def _():
            left_copy(m, xbuf).start()

    def send_right(n, start, size):
        @pl.when(core == 0)
        def _():
            right_copy(n, gbuf, start, size).start()

        @pl.when(core == 1)
        def _():
            right_copy(n, dz, start, size).start()

    def forward_open(m):
        rows = micro_rows(m)
        load_x(m).wait()

        @pl.when(first)
        def _():
            slot = 0
            for j in range(1, MICRO):
                slot = jnp.where(holder[j] == m, j, slot)
            extra = pbuf[slot]
            xbuf[rows, :] = (xbuf[rows, :].astype(F32) + extra.astype(F32)).astype(BF16)

    def forward_tile(m, j):
        rows = micro_rows(m)
        cols = pl.ds(j * TILE, TILE)
        z = jnp.dot(xbuf[rows, :], win[:, cols], preferred_element_type=F32)
        sig = jax.nn.sigmoid(z)
        act[rows, cols] = (z * sig).astype(BF16)
        slope[m % 2, :, cols] = sig * (1.0 + z * (1.0 - sig))

    def forward(m):
        forward_open(m)
        for j in range(WIDTH // TILE):
            forward_tile(m, j)

    def backward(m, start, size):
        crows = token_rows(m * TOK + start, size)
        krows = pl.ds(start, size)
        for j in range(WIDTH // WIDE):
            cols = pl.ds(j * WIDE, WIDE)
            ga = jnp.dot(gbuf[crows, :], wout_t[:, cols], preferred_element_type=F32)
            dz[crows, cols] = (ga * slope[m % 2, krows, cols]).astype(BF16)
        for j in range(WIDTH // WIDE):
            cols = pl.ds(j * WIDE, WIDE)
            back = jnp.dot(dz[crows, :], win_t[:, cols], preferred_element_type=F32)
            nbuf[crows, cols] = (gbuf[crows, cols].astype(F32) + back).astype(BF16)

    def grad_tiles(m, tiles, and_peer):
        rows = micro_rows(m)
        for kind, left, right in ((0, xbuf, dz), (1, act, gbuf)):

            @pl.when(core == kind)
            def _(left=left, right=right):
                for i in tiles:
                    cols = pl.ds(i * TILE, TILE)
                    total = acc[cols, :] + dot_tn(left[rows, cols], right[rows, :])
                    if and_peer:
                        total = total + dot_tn(peer_l[rows, cols], peer_r[rows, :])
                    acc[cols, :] = total

    def hear_peer(m):
        left_copy(m, act).wait_recv()
        right_copy(m, dz, m * TOK, TOK).wait_recv()

    load_win.wait()
    for j in range(WIDTH // TILE):
        cols = pl.ds(j * TILE, TILE)
        win_t[:, cols] = win[cols, :].T

    @pl.when(jnp.logical_not(first))
    def _():
        forward(0)

    load_wout.wait()
    for j in range(WIDTH // TILE):
        cols = pl.ds(j * TILE, TILE)
        wout_t[:, cols] = wout[cols, :].T

    pl.semaphore_wait(barrier, SECTIONS - 1 + 2 * (SIDE - 1) + 1)
    tell_row()

    @pl.when((sec == 1) | last)
    def _():
        pool_copy(sec).start()

    @pl.when(sec == 2)
    def _():
        hop_copy(0).start()
        hop_copy(1).start()

    @pl.when(last)
    def _():
        load_top(0).wait()
        for i in range(SPLIT):
            backward(0, i * PIECE, PIECE)
            relay_copy(i).start()
        for k in range(1, CHUNKS):
            backward(0, k * CHUNK, CHUNK)
            for i in range(SPLIT):
                relay_copy(k * SPLIT + i).start()
        for m in range(1, MICRO):
            load_top(m).start()

    for m in range(1, MICRO):
        load_x(m).start()

    def clear(i, carry):
        rows = pl.ds(pl.multiple_of(i * 64, 64), 64)
        acc[rows, :] = jnp.zeros((64, WIDTH), F32)
        return carry

    def tell_ids(k, carry):
        ids_copy((sh + k) % SHARDS, sh).start()
        return carry

    @pl.when(first)
    def _():
        lax.fori_loop(0, WIDTH // 64, clear, 0)
        tell_plane()
        row = lax.broadcasted_iota(jnp.int32, (TOK, TOK), 0)
        col = lax.broadcasted_iota(jnp.int32, (TOK, TOK), 1)
        feat = ids.shape[1]
        lane = lax.broadcasted_iota(jnp.int32, (ids.shape[2], TOK), 1)
        lead = lax.broadcasted_iota(jnp.int32, (ids.shape[2], TOK), 0)
        widen = jnp.where(lane >> 3 == lead, 1.0, 0.0).astype(BF16)
        for m in range(MICRO):
            owner = (ids[m] >> 10).astype(F32).astype(BF16)
            wide = jnp.dot(owner, widen, preferred_element_type=F32)
            inner = lax.broadcasted_iota(jnp.int32, (feat, TOK), 1) & 7
            outer = lax.broadcasted_iota(jnp.int32, (feat, TOK), 0)
            across = jnp.sum(jnp.where(inner == outer, wide, 0.0), axis=0, keepdims=True)
            down = jnp.sum(jnp.where(row == col, across, 0.0), axis=1, keepdims=True)
            earlier = jnp.where((down == across) & (row < col), 1.0, 0.0)
            rank[m] = 2.0 * across + jnp.sum(earlier, axis=0, keepdims=True)
        tell_all()
        load_pool.wait()
        for s in (1, SECTIONS - 1):
            pool_copy(s).wait_recv()
        for h in range(2):
            pass_copy(h).wait_recv()
        forward(0)

    @pl.when(jnp.logical_not(first))
    def _():
        tell_plane()
        lax.fori_loop(0, WIDTH // 64, clear, 0)
        tell_all()

    @pl.when(last)
    def _():
        pass_pool(0)

    all_ids[sh] = ids[...]
    send_left(0)

    def step(m, start, size, hook=None):
        pieces = [(m * TOK + start) // PIECE + i for i in range(size // PIECE)]

        @pl.when(jnp.logical_not(last))
        def _():
            for c in pieces:
                relay_copy(c).wait_recv()

        if hook is not None:
            hook()
        backward(m, start, size)

        @pl.when(jnp.logical_not(first))
        def _():
            for c in pieces:
                relay_copy(c).start()

    inner = jnp.logical_not(first | last)

    def chunks(m, slots, hook=None):
        for k in range(CHUNKS):
            fine = hook is not None and k == CHUNKS - 1
            for i in range(SPLIT):

                def piece(k=k, i=i):
                    at_last = hook if fine and i == SPLIT - 1 else None
                    step(m, k * CHUNK + i * PIECE, PIECE, at_last)

                if fine:
                    piece()
                else:
                    pl.when(inner)(piece)
                if not fine and i == SPLIT - 1:

                    @pl.when(first | (last & (m > 0)))
                    def _(k=k):
                        step(m, k * CHUNK, CHUNK)

                slots[k * SPLIT + i]()

    def route(m):
        rows = micro_rows(m)

        @pl.when(first)
        def _():
            target = lax.broadcasted_iota(jnp.int32, (TOK, TOK), 0).astype(F32)
            pick = jnp.where(target == rank[m], 1.0, 0.0).astype(BF16)
            ordered = jnp.dot(pick, nbuf[rows, :], preferred_element_type=F32).astype(BF16)
            sorted_rows[m] = ordered
            for p in range(1, SECTIONS):
                route_copy(m, p).start()
            routed[pl.ds(pl.multiple_of(m * PER_PLANE, PER_PLANE), PER_PLANE), :] = ordered[
                :PER_PLANE, :
            ]

    def micro_step(m, carry):
        @pl.when(last & (m == 2))
        def _():
            pass_pool(1)

        @pl.when(last & (m > 0))
        def _():
            load_top(m).wait()

        def forward_slot(j):
            def work():
                if j == 0:
                    forward_open(m + 1)
                forward_tile(m + 1, j)
                if j == WIDTH // TILE - 1:
                    send_left(m + 1)

            return work

        def grad_slot(i):
            def work():
                @pl.when(m > 0)
                def _():
                    if i == 0:
                        hear_peer(m - 1)
                    grad_tiles(m - 1, (i,), True)

            return work

        tiles = range(WIDTH // TILE)
        chunks(m, [forward_slot(j) for j in tiles] + [grad_slot(i) for i in tiles])
        send_right(m, m * TOK, TOK)
        route(m)
        return carry

    lax.fori_loop(0, MICRO - 1, micro_step, 0)

    final = MICRO - 1
    tail = TOK - CHUNK

    def unit_copy(source, target, send, recv, to, came):
        return pltpu.make_async_remote_copy(
            src_ref=source.at[to],
            dst_ref=target.at[came],
            send_sem=send,
            recv_sem=recv,
            device_id=(sec, to),
            device_id_type=MESH,
        )

    def hand_soon(k, carry):
        to = (sh + k) % SHARDS
        unit_copy(soon, got_soon, soon_send, soon_recv, to, sh).start()
        return carry

    def hand_late(k, carry):
        to = (sh + k) % SHARDS
        unit_copy(late, got_late, late_send, late_recv, to, sh).start()
        return carry

    def wait_all(ref, semaphore):
        others = ref.at[pl.ds(0, SHARDS - 1)]
        pltpu.make_async_copy(others, others, semaphore).wait()

    def soon_units():
        row = lax.broadcasted_iota(jnp.int32, (SOON, SOON), 0)
        col = lax.broadcasted_iota(jnp.int32, (SOON, SOON), 1)
        target = ((col >> 1) & (SHARDS - 1)) * (2 * (MICRO - 1)) + (col >> 6) * 2 + (col & 1)
        regroup = jnp.where(row == target, 1.0, 0.0).astype(BF16)
        by_owner = jnp.dot(regroup, routed[pl.ds(0, SOON), :], preferred_element_type=F32)
        for b in range(8):
            flat[pl.ds(b, SOON, stride=8), :] = by_owner[:, b * 128 : (b + 1) * 128]
        soon[...] = flat[...].reshape(soon.shape).astype(BF16)
        got_soon[sh] = soon[sh]

    def late_units():
        by_owner = routed[pl.ds(SOON, PER_PLANE), :].astype(F32)
        for b in range(8):
            flat[pl.ds(b, PER_PLANE, stride=8), :] = by_owner[:, b * 128 : (b + 1) * 128]
        late[...] = flat[pl.ds(0, PER_PLANE * 8), :].reshape(late.shape).astype(BF16)
        got_late[sh] = late[sh]

    def to_rows(got, start, count):
        flat[pl.ds(0, count * 8), :] = got[...].astype(F32).reshape(count * 8, 128)
        for b in range(8):
            rows_buf[pl.ds(start, count), pl.ds(b * 128, 128)] = flat[
                pl.ds(b, count, stride=8), :
            ].astype(BF16)

    @pl.when(last)
    def _():
        load_top(final).wait()

    def final_slot(n):
        def work():
            if n == 2:
                hear_peer(final - 1)
            if 2 <= n < 2 + WIDTH // TILE:
                grad_tiles(final - 1, (n - 2,), True)
            if n == 5:
                send_right(final, final * TOK, tail)

            @pl.when(first)
            def _():
                if n == 0:
                    soon_units()
                if n == 2:
                    lax.fori_loop(1, SHARDS // 2, hand_soon, 0)
                if n == 4:
                    lax.fori_loop(SHARDS // 2, SHARDS, hand_soon, 0)

        return work

    def hand_g():
        @pl.when(core == 0)
        def _():
            right_copy(final + 1, gbuf, final * TOK + tail, TOK - tail).start()

    chunks(final, [final_slot(n) for n in range(CHUNKS * SPLIT)], hand_g)

    @pl.when(core == 1)
    def _():
        right_copy(final + 1, dz, final * TOK + tail, TOK - tail).start()

    grad_tiles(final, (0, 1, 2, 3), False)

    def block_rows(y, x):
        return pl.ds(pl.multiple_of((y * SIDE + x) * BLOCK, BLOCK), BLOCK)

    left_half = pl.ds(0, HALF)
    right_half = pl.ds(HALF, HALF)

    def x_copy(d, y):
        to = (px + d) % SIDE
        return pltpu.make_async_remote_copy(
            src_ref=send_x.at[y, pl.ds(pl.multiple_of(to * BLOCK, BLOCK), BLOCK)],
            dst_ref=recv_x.at[d - 1, y],
            send_sem=x_send.at[d - 1, y],
            recv_sem=x_recv.at[d - 1, y],
            device_id=at(py, to, core),
            device_id_type=MESH,
        )

    def y_copy(d, x):
        rows = pl.ds(pl.multiple_of(x * BLOCK, BLOCK), BLOCK)
        return pltpu.make_async_remote_copy(
            src_ref=send_y.at[d - 1, rows],
            dst_ref=recv_y.at[d - 1, rows],
            send_sem=y_send.at[d - 1, x],
            recv_sem=y_recv.at[d - 1, x],
            device_id=at((py + d) % SIDE, px, core),
            device_id_type=MESH,
        )

    def c_copy(h, e, c, kind):
        there = (py + e) % SIDE if h == 0 else (px + e) % SIDE
        return pltpu.make_async_remote_copy(
            src_ref=send_c.at[h, e, c],
            dst_ref=recv_c.at[kind, h, e],
            send_sem=c_send.at[h, e, c],
            recv_sem=c_recv.at[kind, h, e],
            device_id=at(there, px, c) if h == 0 else at(py, there, c),
            device_id_type=MESH,
        )

    order = (2, 1, 3, 0)
    frows = micro_rows(final)
    left_copy(final, act).wait_recv()
    right_copy(final, dz, final * TOK, tail).wait_recv()
    right_copy(final + 1, dz, final * TOK + tail, TOK - tail).wait_recv()
    for d in order:
        y = (py + d) % SIDE
        cols = pl.ds(pl.multiple_of(y * TILE, TILE), TILE)
        total = acc[cols, :] + dot_tn(peer_l[frows, cols], peer_r[frows, :])
        acc[cols, :] = total
        send_x[y] = total[:, :HALF].astype(BF16)
        for dx in (2, 1, 3):
            x_copy(dx, y).start()
        if d != 0:
            send_y[d - 1] = total[:, HALF:].astype(BF16)
    for e in order:
        for d in (2, 1, 3):
            y_copy(d, (px + e) % SIDE).start()
    route(final)

    @pl.when(jnp.logical_not(first))
    def _():
        for m in range(MICRO - 1):
            route_copy(m, 1).wait_recv()
        soon_units()
        lax.fori_loop(1, SHARDS, hand_soon, 0)
        route_copy(final, 1).wait_recv()

    late_units()
    lax.fori_loop(1, SHARDS, hand_late, 0)

    wait_all(all_ids, ids_recv)
    own = sec * SHARDS + sh
    feature = own // (SECTIONS * SHARDS // ids.shape[1])
    heard = all_ids[:, :, feature, :].reshape(SHARDS * MICRO, ids.shape[2])
    place = lax.broadcasted_iota(jnp.int32, heard.shape, 1) * ROWS_OWN + (heard & (ROWS_OWN - 1))
    ours = heard >> 10 == own
    low = jnp.min(jnp.where(ours, place, 1 << 20), axis=1, keepdims=True) & (ROWS_OWN - 1)
    high = jnp.max(jnp.where(ours, place, -1), axis=1, keepdims=True) & (ROWS_OWN - 1)
    at_lane = lax.broadcasted_iota(jnp.int32, (SHARDS * MICRO, 128), 1)
    parts = jnp.where(
        at_lane == 0,
        low >> 5,
        jnp.where(at_lane == 1, low & 31, jnp.where(at_lane == 2, high >> 5, high & 31)),
    )
    half = lax.broadcasted_iota(jnp.int32, (TOK, SHARDS * MICRO), 0) >> 1
    pair = lax.broadcasted_iota(jnp.int32, (TOK, SHARDS * MICRO), 1)
    came, micro = pair >> 2, pair & (MICRO - 1)
    place_of = jnp.where(
        micro < final, came * (MICRO - 1) + micro, SHARDS * (MICRO - 1) + came
    )
    twice = jnp.where(half == place_of, 1.0, 0.0).astype(BF16)
    both = jnp.dot(twice, parts.astype(F32).astype(BF16), preferred_element_type=F32)
    odd = lax.broadcasted_iota(jnp.int32, (TOK, 1), 0) & 1
    row_of = jnp.where(
        odd == 0, both[:, 0:1] * 32.0 + both[:, 1:2], both[:, 2:3] * 32.0 + both[:, 3:4]
    )
    named[...] = jnp.broadcast_to(row_of.astype(jnp.int32), (TOK, 128))
    put_named = pltpu.make_async_copy(named, out_named, out_sem.at[0])
    put_named.start()

    wait_all(all_ids, ids_send)
    wait_all(soon, soon_send)

    @pl.when((sec == 1) | last)
    def _():
        pool_copy(sec).wait_send()

    @pl.when(sec == 2)
    def _():
        hop_copy(0).wait_send()
        hop_copy(1).wait_send()

    @pl.when(last)
    def _():
        pass_copy(0).wait_send()
        pass_copy(1).wait_send()

    @pl.when(jnp.logical_not(first))
    def _():
        def left(c, carry):
            relay_copy(c).wait_send()
            return carry

        lax.fori_loop(0, PIECES, left, 0)

    @pl.when(first)
    def _():
        for m in range(final):
            for p in range(1, SECTIONS):
                route_copy(m, p).wait_send()

    for m in range(MICRO):
        left_copy(m, act).wait_send()
    for m in range(final):
        right_copy(m, dz, m * TOK, TOK).wait_send()
    right_copy(final, dz, final * TOK, tail).wait_send()
    right_copy(final + 1, dz, final * TOK + tail, TOK - tail).wait_send()

    for e in order:
        y = (py + e) % SIDE
        x = (px + e) % SIDE
        for d in range(1, SIDE):
            x_copy(d, y).wait_recv()
            y_copy(d, x).wait_recv()
        total = acc[block_rows(y, px), left_half]
        other = acc[block_rows(py, x), right_half]
        for d in range(1, SIDE):
            total = total + recv_x[d - 1, y].astype(F32)
            xrows = pl.ds(pl.multiple_of(x * BLOCK, BLOCK), BLOCK)
            other = other + recv_y[d - 1, xrows, :].astype(F32)
        for h, part in ((0, total), (1, other)):
            for c in range(2):
                send_c[h, e, c] = part[c * SHARE : (c + 1) * SHARE, :].astype(BF16)
                if e == 0:

                    @pl.when(core == c)
                    def _(h=h, c=c, part=part):
                        own_c[h] = part[c * SHARE : (c + 1) * SHARE, :]

                    @pl.when(core != c)
                    def _(h=h, c=c):
                        c_copy(h, 0, c, core).start()
                else:
                    c_copy(h, e, c, core).start()

    wait_all(got_soon, soon_recv)
    to_rows(got_soon, 0, SOON)
    wait_all(got_late, late_recv)
    to_rows(got_late, SOON, PER_PLANE)
    put_rows = pltpu.make_async_copy(rows_buf, out_rows, out_sem.at[1])
    put_rows.start()
    wait_all(late, late_send)

    @pl.when(first)
    def _():
        for p in range(1, SECTIONS):
            route_copy(final, p).wait_send()

    for d in range(1, SIDE):
        for y in range(SIDE):
            x_copy(d, y).wait_send()
            y_copy(d, y).wait_send()

    put_grads = []
    for kind, out in ((0, out_in), (1, out_out)):
        for h, cols in ((0, left_half), (1, right_half)):

            @pl.when(core == kind)
            def _(h=h, cols=cols, kind=kind):
                grads[kind, :, cols] = own_c[h]

            @pl.when(core != kind)
            def _(h=h, cols=cols, kind=kind):
                c_copy(h, 0, 1 - kind, kind).wait_recv()
                grads[kind, :, cols] = recv_c[kind, h, 0].astype(F32)

            total = grads[kind, :, cols]
            for e in range(1, SIDE):
                c_copy(h, e, 0, kind).wait_recv()
                total = total + recv_c[kind, h, e].astype(F32)
            grads[kind, :, cols] = total
        put = pltpu.make_async_copy(grads.at[kind], out, out_sem.at[2 + kind])
        put.start()
        put_grads.append(put)

    for h in range(2):
        for d in range(1, SIDE):
            for c in range(2):
                c_copy(h, d, c, core).wait_send()
        c_copy(h, 0, 1 - core, core).wait_send()
    for put in (put_named, put_rows, *put_grads):
        put.wait()


def relay(holder, saved, pooled, grad_top, w_in, w_out, ids):
    vmem = pl.BlockSpec(memory_space=pltpu.VMEM)
    anywhere = pl.BlockSpec(memory_space=pl.ANY)
    dma = pltpu.SemaphoreType.DMA
    tokens = MICRO * TOK
    return pl.pallas_call(
        kernel,
        out_shape=(
            jax.ShapeDtypeStruct((SHARE, WIDTH), F32),
            jax.ShapeDtypeStruct((SHARE, WIDTH), F32),
            jax.ShapeDtypeStruct((TOK, WIDTH), BF16),
            jax.ShapeDtypeStruct((TOK, 128), jnp.int32),
        ),
        in_specs=[pl.BlockSpec(memory_space=pltpu.SMEM)] + [anywhere] * 5 + [vmem],
        out_specs=(anywhere, anywhere, anywhere, anywhere),
        scratch_shapes=[
            pltpu.VMEM((WIDTH, WIDTH), BF16),
            pltpu.VMEM((WIDTH, WIDTH), BF16),
            pltpu.VMEM((WIDTH, WIDTH), BF16),
            pltpu.VMEM((WIDTH, WIDTH), BF16),
            pltpu.VMEM((tokens, WIDTH), BF16),
            pltpu.VMEM((tokens, WIDTH), BF16),
            pltpu.VMEM((tokens, WIDTH), BF16),
            pltpu.VMEM((SECTIONS, TOK, WIDTH), BF16),
            pltpu.VMEM((tokens, WIDTH), BF16),
            pltpu.VMEM((2, TOK, WIDTH), F32),
            pltpu.VMEM((tokens, WIDTH), BF16),
            pltpu.VMEM((WIDTH, WIDTH), F32),
            pltpu.VMEM((MICRO, 1, TOK), F32),
            pltpu.VMEM((SHARDS,) + ids.shape, jnp.int32),
            pltpu.VMEM((MICRO, TOK, WIDTH), BF16),
            pltpu.VMEM((TOK, WIDTH), BF16),
            pltpu.VMEM((SHARDS, 16 * (MICRO - 1), 128), BF16),
            pltpu.VMEM((SHARDS, 16 * (MICRO - 1), 128), BF16),
            pltpu.VMEM((SHARDS, 16, 128), BF16),
            pltpu.VMEM((SHARDS, 16, 128), BF16),
            pltpu.VMEM((SOON * 8, 128), F32),
            pltpu.VMEM((TOK, 128), jnp.int32),
            pltpu.VMEM((TOK, WIDTH), BF16),
            pltpu.VMEM((2, SHARE, WIDTH), F32),
            pltpu.VMEM((TOK, WIDTH), BF16),
            pltpu.VMEM((tokens, WIDTH), BF16),
            pltpu.VMEM((tokens, WIDTH), BF16),
            pltpu.VMEM((SIDE, SIDE * BLOCK, HALF), BF16),
            pltpu.VMEM((SIDE - 1, SIDE, BLOCK, HALF), BF16),
            pltpu.VMEM((SIDE - 1, SIDE * BLOCK, HALF), BF16),
            pltpu.VMEM((SIDE - 1, SIDE * BLOCK, HALF), BF16),
            pltpu.VMEM((2, SHARE, HALF), F32),
            pltpu.VMEM((2, SIDE, 2, SHARE, HALF), BF16),
            pltpu.VMEM((2, 2, SIDE, SHARE, HALF), BF16),
            dma((3 + MICRO,)),
            dma((MICRO,)),
            dma,
            dma((SECTIONS,)),
            dma((PIECES,)),
            dma((PIECES,)),
            dma((MICRO, SECTIONS)),
            dma((MICRO,)),
            dma,
            dma,
            dma,
            dma,
            pltpu.SemaphoreType.REGULAR((2,)),
            dma((2,)),
            dma((2,)),
            dma((2,)),
            dma((2,)),
            dma((4,)),
            dma,
            dma,
            dma((MICRO,)),
            dma((MICRO,)),
            dma((MICRO + 1,)),
            dma((MICRO + 1,)),
            dma((SIDE - 1, SIDE)),
            dma((SIDE - 1, SIDE)),
            dma((SIDE - 1, SIDE)),
            dma((SIDE - 1, SIDE)),
            dma((2, SIDE, 2)),
            dma((2, 2, SIDE)),
        ],
        compiler_params=pltpu.CompilerParams(
            collective_id=0, has_side_effects=True, vmem_limit_bytes=56 * 1024 * 1024
        ),
        cost_estimate=pl.CostEstimate(
            flops=10 * tokens * WIDTH * WIDTH, bytes_accessed=9 * 2**20, transcendentals=tokens * WIDTH
        ),
        name="relay",
    )(holder, saved, pooled, grad_top, w_in, w_out, ids)


def table_kernel(named, rows, grad_in, grad_out, table, out_in, out_out):
    block = pl.program_id(0)
    lane = lax.broadcasted_iota(jnp.int32, (TOK, WIDE), 1) + block * WIDE
    hit = jnp.where(lane == named[:, 0:1], 1.0, 0.0).astype(BF16)
    table[...] = dot_tn(hit, rows[...])

    @pl.when(block == 0)
    def _():
        out_in[...] = grad_in[...]
        out_out[...] = grad_out[...]


def owner_sums(named, rows, grad_in, grad_out):
    def whole(array):
        return pl.BlockSpec(array.shape, lambda b: (0, 0))

    return pl.pallas_call(
        table_kernel,
        grid=(ROWS_OWN // WIDE,),
        out_shape=(
            jax.ShapeDtypeStruct((ROWS_OWN, WIDTH), F32),
            jax.ShapeDtypeStruct(grad_in.shape, F32),
            jax.ShapeDtypeStruct(grad_out.shape, F32),
        ),
        in_specs=[whole(named), whole(rows), whole(grad_in), whole(grad_out)],
        out_specs=(
            pl.BlockSpec((WIDE, WIDTH), lambda b: (b, 0)),
            whole(grad_in),
            whole(grad_out),
        ),
        compiler_params=pltpu.CompilerParams(vmem_limit_bytes=32 * 1024 * 1024),
        cost_estimate=pl.CostEstimate(
            flops=2 * ROWS_OWN * TOK * WIDTH, bytes_accessed=5 * 2**20, transcendentals=0
        ),
        name="owner_sums",
    )(named, rows, grad_in, grad_out)


def local(saved, pooled, grad_top, w_in, w_out, feature_ids, holder_order):
    tokens = MICRO * TOK
    out_in, out_out, rows, named = relay(
        holder_order,
        saved.reshape(tokens, WIDTH),
        pooled.reshape(TOK, WIDTH),
        grad_top.reshape(tokens, WIDTH),
        w_in[0],
        w_out[0],
        jnp.transpose(feature_ids, (0, 2, 1)),
    )
    table_grad, grad_in, grad_out = owner_sums(named, rows, out_in, out_out)
    return (grad_in[None], grad_out[None], table_grad)


def solution(mesh):
    return jax.shard_map(
        local,
        mesh=mesh,
        in_specs=(
            P("section", None, "shard", None, None),
            P("section", "shard", None, None),
            P(None, "shard", None, None),
            P("section", None, None),
            P("section", None, None),
            P(None, "shard", None),
            P(),
        ),
        out_specs=(
            P("section", "shard", None),
            P("section", "shard", None),
            P(("section", "shard"), None),
        ),
        check_vma=False,
    )
```

```python
import jax
import jax.numpy as jnp
from jax import lax
from jax.experimental import pallas as pl
from jax.experimental.pallas import tpu as pltpu
from jax.sharding import PartitionSpec as P

ROWS_OWN = 1024
MESH = pl.DeviceIdType.MESH
F32 = jnp.float32
BF16 = jnp.bfloat16

SECTIONS = 4
SHARDS = 32
SIDE = 4
MICRO = 4
TOK = 256
CHUNK = 64
PIECE = 32
WIDTH = 1024
SHARE = WIDTH // SHARDS
PER_PLANE = TOK // SECTIONS
TILE = 256
WIDE = 512
CHUNKS = TOK // CHUNK
SPLIT = CHUNK // PIECE
PIECES = MICRO * TOK // PIECE
SOON = (MICRO - 1) * PER_PLANE
HALF = WIDTH // 2
BLOCK = 2 * SHARE


def dot_tn(a, b):
    return lax.dot_general(a, b, (((0,), (0,)), ((), ())), preferred_element_type=F32)


def kernel(
    holder,
    saved,
    pooled,
    grad_top,
    w_in,
    w_out,
    ids,
    out_parts,
    out_rows,
    out_named,
    win,
    wout,
    win_t,
    wout_t,
    xbuf,
    gbuf,
    nbuf,
    pbuf,
    act,
    slope,
    dz,
    acc,
    rank,
    all_ids,
    sorted_rows,
    routed,
    soon,
    got_soon,
    late,
    got_late,
    flat,
    named,
    rows_buf,
    transit,
    peer_l,
    peer_r,
    send_x,
    recv_x,
    send_y,
    recv_y,
    send_c,
    load_sem,
    top_sem,
    pool_send,
    pool_recv,
    relay_send,
    relay_recv,
    route_send,
    route_recv,
    soon_send,
    soon_recv,
    late_send,
    late_recv,
    ready,
    hop_send,
    hop_recv,
    pass_send,
    pass_recv,
    out_sem,
    ids_send,
    ids_recv,
    l_send,
    l_recv,
    r_send,
    r_recv,
    x_send,
    x_recv,
    y_send,
    y_recv,
    c_send,
    c_recv,
):
    sec = lax.axis_index("section")
    sh = lax.axis_index("shard")
    core = sh % 2
    px = (sh // 2) % SIDE
    py = sh // (2 * SIDE)
    first = sec == 0
    last = sec == SECTIONS - 1

    def at(y, x, c):
        return (sec, (y * SIDE + x) * 2 + c)

    def micro_rows(m):
        return pl.ds(pl.multiple_of(m * TOK, TOK), TOK)

    def token_rows(start, size):
        return pl.ds(pl.multiple_of(start, size), size)

    def load_x(m):
        rows = micro_rows(m)
        return pltpu.make_async_copy(saved.at[rows], xbuf.at[rows], load_sem.at[2 + m])

    def load_top(m):
        rows = micro_rows(m)
        return pltpu.make_async_copy(grad_top.at[rows], gbuf.at[rows], top_sem.at[m])

    load_win = pltpu.make_async_copy(w_in, win, load_sem.at[0])
    load_wout = pltpu.make_async_copy(w_out, wout, load_sem.at[1])
    load_pool = pltpu.make_async_copy(pooled, pbuf.at[0], load_sem.at[2 + MICRO])

    load_win.start()
    load_x(0).start()
    load_wout.start()

    @pl.when(last)
    def _():
        load_top(0).start()

    @pl.when(first)
    def _():
        load_pool.start()

    barrier = pltpu.get_barrier_semaphore()

    def greet(y, x, c):
        pl.semaphore_signal(barrier, inc=1, device_id=at(y, x, c), device_id_type=MESH)

    for k in range(1, SECTIONS):
        pl.semaphore_signal(
            barrier, inc=1, device_id=((sec + k) % SECTIONS, sh), device_id_type=MESH
        )
    for k in range(1, SIDE):
        greet(py, (px + k) % SIDE, core)
        greet((py + k) % SIDE, px, core)
    greet(py, px, 1 - core)

    def tell_row():
        for k in range(1, SIDE):
            to = at(py, (px + k) % SIDE, core)
            pl.semaphore_signal(ready.at[0], inc=1, device_id=to, device_id_type=MESH)

    def tell_plane():
        pl.semaphore_wait(ready.at[0], SIDE - 1)
        for k in range(1, SIDE):
            to = at((py + k) % SIDE, px, core)
            pl.semaphore_signal(ready.at[1], inc=1, device_id=to, device_id_type=MESH)

    def tell_ids(m, n):
        if n == 0:

            @pl.when(m == 0)
            def _():
                tell_plane()

        if n == 1:

            @pl.when(m == 0)
            def _():
                pl.semaphore_wait(ready.at[1], SIDE - 1)

        @pl.when((m > 0) | (n > 0))
        def _():
            ids_copy((sh + m * SPLIT * CHUNKS + n) % SHARDS, sh).start()

    def pool_copy(s):
        return pltpu.make_async_remote_copy(
            src_ref=pooled,
            dst_ref=pbuf.at[s],
            send_sem=pool_send,
            recv_sem=pool_recv.at[s],
            device_id=(0, sh),
            device_id_type=MESH,
        )

    def pool_rows(h):
        return pl.ds(h * (TOK // 2), TOK // 2)

    def hop_copy(h):
        return pltpu.make_async_remote_copy(
            src_ref=pooled.at[pool_rows(h)],
            dst_ref=transit.at[pool_rows(h)],
            send_sem=hop_send.at[h],
            recv_sem=hop_recv.at[h],
            device_id=(SECTIONS - 1, sh),
            device_id_type=MESH,
        )

    def pass_copy(h):
        return pltpu.make_async_remote_copy(
            src_ref=transit.at[pool_rows(h)],
            dst_ref=pbuf.at[2, pool_rows(h)],
            send_sem=pass_send.at[h],
            recv_sem=pass_recv.at[h],
            device_id=(0, sh),
            device_id_type=MESH,
        )

    def pass_pool(h):
        hop_copy(h).wait_recv()
        pass_copy(h).start()

    def relay_copy(c):
        rows = token_rows(c * PIECE, PIECE)
        return pltpu.make_async_remote_copy(
            src_ref=nbuf.at[rows],
            dst_ref=gbuf.at[rows],
            send_sem=relay_send.at[c],
            recv_sem=relay_recv.at[c],
            device_id=(jnp.maximum(sec - 1, 0), sh),
            device_id_type=MESH,
        )

    def route_copy(m, p):
        return pltpu.make_async_remote_copy(
            src_ref=sorted_rows.at[m, pl.ds(p * PER_PLANE, PER_PLANE)],
            dst_ref=routed.at[pl.ds(pl.multiple_of(m * PER_PLANE, PER_PLANE), PER_PLANE)],
            send_sem=route_send.at[m, p],
            recv_sem=route_recv.at[m],
            device_id=(p, sh),
            device_id_type=MESH,
        )

    def ids_copy(to, came):
        return pltpu.make_async_remote_copy(
            src_ref=ids,
            dst_ref=all_ids.at[came],
            send_sem=ids_send,
            recv_sem=ids_recv,
            device_id=(sec, to),
            device_id_type=MESH,
        )

    def left_copy(m, source):
        rows = micro_rows(m)
        return pltpu.make_async_remote_copy(
            src_ref=source.at[rows],
            dst_ref=peer_l.at[rows],
            send_sem=l_send.at[m],
            recv_sem=l_recv.at[m],
            device_id=at(py, px, 1 - core),
            device_id_type=MESH,
        )

    def right_copy(n, source, start, size):
        rows = pl.ds(pl.multiple_of(start, 64), size)
        return pltpu.make_async_remote_copy(
            src_ref=source.at[rows],
            dst_ref=peer_r.at[rows],
            send_sem=r_send.at[n],
            recv_sem=r_recv.at[n],
            device_id=at(py, px, 1 - core),
            device_id_type=MESH,
        )

    def send_left(m):
        @pl.when(core == 0)
        def _():
            left_copy(m, act).start()

        @pl.when(core == 1)
        def _():
            left_copy(m, xbuf).start()

    def send_right(n, start, size):
        @pl.when(core == 0)
        def _():
            right_copy(n, gbuf, start, size).start()

        @pl.when(core == 1)
        def _():
            right_copy(n, dz, start, size).start()

    def forward_open(m):
        rows = micro_rows(m)
        load_x(m).wait()

        @pl.when(first)
        def _():
            slot = 0
            for j in range(1, MICRO):
                slot = jnp.where(holder[j] == m, j, slot)
            extra = pbuf[slot]
            xbuf[rows, :] = (xbuf[rows, :].astype(F32) + extra.astype(F32)).astype(BF16)

    def forward_tile(m, j):
        rows = micro_rows(m)
        cols = pl.ds(j * TILE, TILE)
        z = jnp.dot(xbuf[rows, :], win[:, cols], preferred_element_type=F32)
        sig = jax.nn.sigmoid(z)
        act[rows, cols] = (z * sig).astype(BF16)
        slope[m % 2, :, cols] = sig * (1.0 + z * (1.0 - sig))

    def forward(m):
        forward_open(m)
        for j in range(WIDTH // TILE):
            forward_tile(m, j)

    def backward(m, start, size):
        crows = token_rows(m * TOK + start, size)
        krows = pl.ds(start, size)
        for j in range(WIDTH // WIDE):
            cols = pl.ds(j * WIDE, WIDE)
            ga = jnp.dot(gbuf[crows, :], wout_t[:, cols], preferred_element_type=F32)
            dz[crows, cols] = (ga * slope[m % 2, krows, cols]).astype(BF16)
        for j in range(WIDTH // WIDE):
            cols = pl.ds(j * WIDE, WIDE)
            back = jnp.dot(dz[crows, :], win_t[:, cols], preferred_element_type=F32)
            nbuf[crows, cols] = (gbuf[crows, cols].astype(F32) + back).astype(BF16)

    def grad_tiles(m, tiles, and_peer):
        rows = micro_rows(m)
        for kind, left, right in ((0, xbuf, dz), (1, act, gbuf)):

            @pl.when(core == kind)
            def _(left=left, right=right):
                for i in tiles:
                    cols = pl.ds(i * TILE, TILE)
                    total = acc[cols, :] + dot_tn(left[rows, cols], right[rows, :])
                    if and_peer:
                        total = total + dot_tn(peer_l[rows, cols], peer_r[rows, :])
                    acc[cols, :] = total

    def hear_peer(m):
        left_copy(m, act).wait_recv()
        right_copy(m, dz, m * TOK, TOK).wait_recv()

    load_win.wait()
    for j in range(WIDTH // TILE):
        cols = pl.ds(j * TILE, TILE)
        win_t[:, cols] = win[cols, :].T

    @pl.when(jnp.logical_not(first))
    def _():
        forward(0)

    load_wout.wait()
    for j in range(WIDTH // TILE):
        cols = pl.ds(j * TILE, TILE)
        wout_t[:, cols] = wout[cols, :].T

    pl.semaphore_wait(barrier, SECTIONS - 1 + 2 * (SIDE - 1) + 1)
    tell_row()

    @pl.when((sec == 1) | last)
    def _():
        pool_copy(sec).start()

    @pl.when(sec == 2)
    def _():
        hop_copy(0).start()
        hop_copy(1).start()

    @pl.when(last)
    def _():
        load_top(0).wait()
        for i in range(SPLIT):
            backward(0, i * PIECE, PIECE)
            relay_copy(i).start()
        for k in range(1, CHUNKS):
            backward(0, k * CHUNK, CHUNK)
            for i in range(SPLIT):
                relay_copy(k * SPLIT + i).start()
        for m in range(1, MICRO):
            load_top(m).start()

    for m in range(1, MICRO):
        load_x(m).start()

    def clear(i, carry):
        rows = pl.ds(pl.multiple_of(i * 64, 64), 64)
        acc[rows, :] = jnp.zeros((64, WIDTH), F32)
        return carry

    @pl.when(first)
    def _():
        lax.fori_loop(0, WIDTH // 64, clear, 0)
        row = lax.broadcasted_iota(jnp.int32, (TOK, TOK), 0)
        col = lax.broadcasted_iota(jnp.int32, (TOK, TOK), 1)
        feat = ids.shape[1]
        lane = lax.broadcasted_iota(jnp.int32, (ids.shape[2], TOK), 1)
        lead = lax.broadcasted_iota(jnp.int32, (ids.shape[2], TOK), 0)
        widen = jnp.where(lane >> 3 == lead, 1.0, 0.0).astype(BF16)
        for m in range(MICRO):
            owner = (ids[m] >> 10).astype(F32).astype(BF16)
            wide = jnp.dot(owner, widen, preferred_element_type=F32)
            inner = lax.broadcasted_iota(jnp.int32, (feat, TOK), 1) & 7
            outer = lax.broadcasted_iota(jnp.int32, (feat, TOK), 0)
            across = jnp.sum(jnp.where(inner == outer, wide, 0.0), axis=0, keepdims=True)
            down = jnp.sum(jnp.where(row == col, across, 0.0), axis=1, keepdims=True)
            earlier = jnp.where((down == across) & (row < col), 1.0, 0.0)
            rank[m] = 2.0 * across + jnp.sum(earlier, axis=0, keepdims=True)
        load_pool.wait()
        for s in (1, SECTIONS - 1):
            pool_copy(s).wait_recv()
        for h in range(2):
            pass_copy(h).wait_recv()
        forward(0)

    @pl.when(jnp.logical_not(first))
    def _():
        lax.fori_loop(0, WIDTH // 64, clear, 0)

    @pl.when(last)
    def _():
        pass_pool(0)

    all_ids[sh] = ids[...]
    send_left(0)

    def step(m, start, size, hook=None):
        pieces = [(m * TOK + start) // PIECE + i for i in range(size // PIECE)]

        @pl.when(jnp.logical_not(last))
        def _():
            for c in pieces:
                relay_copy(c).wait_recv()

        if hook is not None:
            hook()
        backward(m, start, size)

        @pl.when(jnp.logical_not(first))
        def _():
            for c in pieces:
                relay_copy(c).start()

    inner = jnp.logical_not(first | last)

    def chunks(m, slots, hook=None):
        for k in range(CHUNKS):
            fine = hook is not None and k == CHUNKS - 1
            for i in range(SPLIT):

                def piece(k=k, i=i):
                    at_last = hook if fine and i == SPLIT - 1 else None
                    step(m, k * CHUNK + i * PIECE, PIECE, at_last)

                if fine:
                    piece()
                else:
                    pl.when(inner)(piece)
                if not fine and i == SPLIT - 1:

                    @pl.when(first | (last & (m > 0)))
                    def _(k=k):
                        step(m, k * CHUNK, CHUNK)

                slots[k * SPLIT + i]()
                tell_ids(m, k * SPLIT + i)

    def route(m):
        rows = micro_rows(m)

        @pl.when(first)
        def _():
            target = lax.broadcasted_iota(jnp.int32, (TOK, TOK), 0).astype(F32)
            pick = jnp.where(target == rank[m], 1.0, 0.0).astype(BF16)
            ordered = jnp.dot(pick, nbuf[rows, :], preferred_element_type=F32).astype(BF16)
            sorted_rows[m] = ordered
            for p in range(1, SECTIONS):
                route_copy(m, p).start()
            routed[pl.ds(pl.multiple_of(m * PER_PLANE, PER_PLANE), PER_PLANE), :] = ordered[
                :PER_PLANE, :
            ]

    def micro_step(m, carry):
        @pl.when(last & (m == 2))
        def _():
            pass_pool(1)

        @pl.when(last & (m > 0))
        def _():
            load_top(m).wait()

        def forward_slot(j):
            def work():
                if j == 0:
                    forward_open(m + 1)
                forward_tile(m + 1, j)
                if j == WIDTH // TILE - 1:
                    send_left(m + 1)

            return work

        def grad_slot(i):
            def work():
                @pl.when(m > 0)
                def _():
                    if i == 0:
                        hear_peer(m - 1)
                    grad_tiles(m - 1, (i,), True)

            return work

        tiles = range(WIDTH // TILE)
        chunks(m, [forward_slot(j) for j in tiles] + [grad_slot(i) for i in tiles])
        send_right(m, m * TOK, TOK)
        route(m)
        return carry

    lax.fori_loop(0, MICRO - 1, micro_step, 0)

    final = MICRO - 1
    tail = TOK - CHUNK

    def unit_copy(source, target, send, recv, to, came):
        return pltpu.make_async_remote_copy(
            src_ref=source.at[to],
            dst_ref=target.at[came],
            send_sem=send,
            recv_sem=recv,
            device_id=(sec, to),
            device_id_type=MESH,
        )

    def hand_soon(k, carry):
        to = (sh + k) % SHARDS
        unit_copy(soon, got_soon, soon_send, soon_recv, to, sh).start()
        return carry

    def hand_late(k, carry):
        to = (sh + k) % SHARDS
        unit_copy(late, got_late, late_send, late_recv, to, sh).start()
        return carry

    def wait_all(ref, semaphore):
        others = ref.at[pl.ds(0, SHARDS - 1)]
        pltpu.make_async_copy(others, others, semaphore).wait()

    def soon_units():
        row = lax.broadcasted_iota(jnp.int32, (SOON, SOON), 0)
        col = lax.broadcasted_iota(jnp.int32, (SOON, SOON), 1)
        target = ((col >> 1) & (SHARDS - 1)) * (2 * (MICRO - 1)) + (col >> 6) * 2 + (col & 1)
        regroup = jnp.where(row == target, 1.0, 0.0).astype(BF16)
        by_owner = jnp.dot(regroup, routed[pl.ds(0, SOON), :], preferred_element_type=F32)
        for b in range(8):
            flat[pl.ds(b, SOON, stride=8), :] = by_owner[:, b * 128 : (b + 1) * 128]
        soon[...] = flat[...].reshape(soon.shape).astype(BF16)
        got_soon[sh] = soon[sh]

    def late_units():
        by_owner = routed[pl.ds(SOON, PER_PLANE), :].astype(F32)
        for b in range(8):
            flat[pl.ds(b, PER_PLANE, stride=8), :] = by_owner[:, b * 128 : (b + 1) * 128]
        late[...] = flat[pl.ds(0, PER_PLANE * 8), :].reshape(late.shape).astype(BF16)
        got_late[sh] = late[sh]

    def to_rows(got, start, count):
        flat[pl.ds(0, count * 8), :] = got[...].astype(F32).reshape(count * 8, 128)
        for b in range(8):
            rows_buf[pl.ds(start, count), pl.ds(b * 128, 128)] = flat[
                pl.ds(b, count, stride=8), :
            ].astype(BF16)

    @pl.when(last)
    def _():
        load_top(final).wait()

    def final_slot(n):
        def work():
            if n == 2:
                hear_peer(final - 1)
            if 2 <= n < 2 + WIDTH // TILE:
                grad_tiles(final - 1, (n - 2,), True)
            if n == 5:
                send_right(final, final * TOK, tail)

            @pl.when(first)
            def _():
                if n == 0:
                    soon_units()
                if n == 2:
                    lax.fori_loop(1, SHARDS // 2, hand_soon, 0)
                if n == 4:
                    lax.fori_loop(SHARDS // 2, SHARDS, hand_soon, 0)

        return work

    def hand_g():
        @pl.when(core == 0)
        def _():
            right_copy(final + 1, gbuf, final * TOK + tail, TOK - tail).start()

    chunks(final, [final_slot(n) for n in range(CHUNKS * SPLIT)], hand_g)

    @pl.when(core == 1)
    def _():
        right_copy(final + 1, dz, final * TOK + tail, TOK - tail).start()

    grad_tiles(final, (0, 1, 2, 3), False)

    def block_rows(y, x):
        return pl.ds(pl.multiple_of((y * SIDE + x) * BLOCK, BLOCK), BLOCK)

    left_half = pl.ds(0, HALF)
    right_half = pl.ds(HALF, HALF)

    def x_copy(d, y):
        to = (px + d) % SIDE
        return pltpu.make_async_remote_copy(
            src_ref=send_x.at[y, pl.ds(pl.multiple_of(to * BLOCK, BLOCK), BLOCK)],
            dst_ref=recv_x.at[d - 1, y],
            send_sem=x_send.at[d - 1, y],
            recv_sem=x_recv.at[d - 1, y],
            device_id=at(py, to, core),
            device_id_type=MESH,
        )

    def y_copy(d, x):
        rows = pl.ds(pl.multiple_of(x * BLOCK, BLOCK), BLOCK)
        return pltpu.make_async_remote_copy(
            src_ref=send_y.at[d - 1, rows],
            dst_ref=recv_y.at[d - 1, rows],
            send_sem=y_send.at[d - 1, x],
            recv_sem=y_recv.at[d - 1, x],
            device_id=at((py + d) % SIDE, px, core),
            device_id_type=MESH,
        )

    def c_copy(h, e, c, kind):
        there = (py + e) % SIDE if h == 0 else (px + e) % SIDE
        return pltpu.make_async_remote_copy(
            src_ref=send_c.at[h, e, c],
            dst_ref=out_parts.at[kind, h, e],
            send_sem=c_send.at[h, e, c],
            recv_sem=c_recv.at[kind, h, e],
            device_id=at(there, px, c) if h == 0 else at(py, there, c),
            device_id_type=MESH,
        )

    def own_part(h):
        return pltpu.make_async_copy(
            send_c.at[h, 0, core], out_parts.at[core, h, 0], out_sem.at[2 + h]
        )

    order = (2, 1, 3, 0)
    frows = micro_rows(final)
    left_copy(final, act).wait_recv()
    right_copy(final, dz, final * TOK, tail).wait_recv()
    right_copy(final + 1, dz, final * TOK + tail, TOK - tail).wait_recv()
    for d in order:
        y = (py + d) % SIDE
        cols = pl.ds(pl.multiple_of(y * TILE, TILE), TILE)
        total = acc[cols, :] + dot_tn(peer_l[frows, cols], peer_r[frows, :])
        acc[cols, :] = total
        send_x[y] = total[:, :HALF].astype(BF16)
        for dx in (2, 1, 3):
            x_copy(dx, y).start()
        if d != 0:
            send_y[d - 1] = total[:, HALF:].astype(BF16)
    for e in order:
        for d in (2, 1, 3):
            y_copy(d, (px + e) % SIDE).start()
    route(final)

    @pl.when(jnp.logical_not(first))
    def _():
        for m in range(MICRO - 1):
            route_copy(m, 1).wait_recv()
        soon_units()
        lax.fori_loop(1, SHARDS, hand_soon, 0)
        route_copy(final, 1).wait_recv()

    late_units()
    lax.fori_loop(1, SHARDS, hand_late, 0)

    wait_all(all_ids, ids_recv)
    own = sec * SHARDS + sh
    feature = own // (SECTIONS * SHARDS // ids.shape[1])
    heard = all_ids[:, :, feature, :].reshape(SHARDS * MICRO, ids.shape[2])
    place = lax.broadcasted_iota(jnp.int32, heard.shape, 1) * ROWS_OWN + (heard & (ROWS_OWN - 1))
    ours = heard >> 10 == own
    low = jnp.min(jnp.where(ours, place, 1 << 20), axis=1, keepdims=True) & (ROWS_OWN - 1)
    high = jnp.max(jnp.where(ours, place, -1), axis=1, keepdims=True) & (ROWS_OWN - 1)
    at_lane = lax.broadcasted_iota(jnp.int32, (SHARDS * MICRO, 128), 1)
    parts = jnp.where(
        at_lane == 0,
        low >> 5,
        jnp.where(at_lane == 1, low & 31, jnp.where(at_lane == 2, high >> 5, high & 31)),
    )
    half = lax.broadcasted_iota(jnp.int32, (TOK, SHARDS * MICRO), 0) >> 1
    pair = lax.broadcasted_iota(jnp.int32, (TOK, SHARDS * MICRO), 1)
    came, micro = pair >> 2, pair & (MICRO - 1)
    place_of = jnp.where(
        micro < final, came * (MICRO - 1) + micro, SHARDS * (MICRO - 1) + came
    )
    twice = jnp.where(half == place_of, 1.0, 0.0).astype(BF16)
    both = jnp.dot(twice, parts.astype(F32).astype(BF16), preferred_element_type=F32)
    odd = lax.broadcasted_iota(jnp.int32, (TOK, 1), 0) & 1
    row_of = jnp.where(
        odd == 0, both[:, 0:1] * 32.0 + both[:, 1:2], both[:, 2:3] * 32.0 + both[:, 3:4]
    )
    named[...] = jnp.broadcast_to(row_of.astype(jnp.int32), (TOK, 128))
    put_named = pltpu.make_async_copy(named, out_named, out_sem.at[0])
    put_named.start()

    wait_all(all_ids, ids_send)
    wait_all(soon, soon_send)

    @pl.when((sec == 1) | last)
    def _():
        pool_copy(sec).wait_send()

    @pl.when(sec == 2)
    def _():
        hop_copy(0).wait_send()
        hop_copy(1).wait_send()

    @pl.when(last)
    def _():
        pass_copy(0).wait_send()
        pass_copy(1).wait_send()

    @pl.when(jnp.logical_not(first))
    def _():
        def left(c, carry):
            relay_copy(c).wait_send()
            return carry

        lax.fori_loop(0, PIECES, left, 0)

    @pl.when(first)
    def _():
        for m in range(final):
            for p in range(1, SECTIONS):
                route_copy(m, p).wait_send()

    for m in range(MICRO):
        left_copy(m, act).wait_send()
    for m in range(final):
        right_copy(m, dz, m * TOK, TOK).wait_send()
    right_copy(final, dz, final * TOK, tail).wait_send()
    right_copy(final + 1, dz, final * TOK + tail, TOK - tail).wait_send()

    for e in order:
        y = (py + e) % SIDE
        x = (px + e) % SIDE
        for d in range(1, SIDE):
            x_copy(d, y).wait_recv()
            y_copy(d, x).wait_recv()
        total = acc[block_rows(y, px), left_half]
        other = acc[block_rows(py, x), right_half]
        for d in range(1, SIDE):
            total = total + recv_x[d - 1, y].astype(F32)
            xrows = pl.ds(pl.multiple_of(x * BLOCK, BLOCK), BLOCK)
            other = other + recv_y[d - 1, xrows, :].astype(F32)
        for h, part in ((0, total), (1, other)):
            for c in range(2):
                send_c[h, e, c] = part[c * SHARE : (c + 1) * SHARE, :].astype(BF16)
                if e == 0:

                    @pl.when(core == c)
                    def _(h=h, c=c):
                        own_part(h).start()

                    @pl.when(core != c)
                    def _(h=h, c=c):
                        c_copy(h, 0, c, core).start()
                else:
                    c_copy(h, e, c, core).start()

    wait_all(got_soon, soon_recv)
    to_rows(got_soon, 0, SOON)
    wait_all(got_late, late_recv)
    to_rows(got_late, SOON, PER_PLANE)
    put_rows = pltpu.make_async_copy(rows_buf, out_rows, out_sem.at[1])
    put_rows.start()
    wait_all(late, late_send)

    @pl.when(first)
    def _():
        for p in range(1, SECTIONS):
            route_copy(final, p).wait_send()

    for d in range(1, SIDE):
        for y in range(SIDE):
            x_copy(d, y).wait_send()
            y_copy(d, y).wait_send()

    for kind in range(2):
        for h in range(2):

            @pl.when(core != kind)
            def _(h=h, kind=kind):
                c_copy(h, 0, 1 - kind, kind).wait_recv()

            for e in range(1, SIDE):
                c_copy(h, e, 0, kind).wait_recv()

    for h in range(2):
        for d in range(1, SIDE):
            for c in range(2):
                c_copy(h, d, c, core).wait_send()
        c_copy(h, 0, 1 - core, core).wait_send()
    for put in (put_named, put_rows, own_part(0), own_part(1)):
        put.wait()


def relay(holder, saved, pooled, grad_top, w_in, w_out, ids):
    vmem = pl.BlockSpec(memory_space=pltpu.VMEM)
    anywhere = pl.BlockSpec(memory_space=pl.ANY)
    dma = pltpu.SemaphoreType.DMA
    tokens = MICRO * TOK
    return pl.pallas_call(
        kernel,
        out_shape=(
            jax.ShapeDtypeStruct((2, 2, SIDE, SHARE, HALF), BF16),
            jax.ShapeDtypeStruct((TOK, WIDTH), BF16),
            jax.ShapeDtypeStruct((TOK, 128), jnp.int32),
        ),
        in_specs=[pl.BlockSpec(memory_space=pltpu.SMEM)] + [anywhere] * 5 + [vmem],
        out_specs=(anywhere, anywhere, anywhere),
        scratch_shapes=[
            pltpu.VMEM((WIDTH, WIDTH), BF16),
            pltpu.VMEM((WIDTH, WIDTH), BF16),
            pltpu.VMEM((WIDTH, WIDTH), BF16),
            pltpu.VMEM((WIDTH, WIDTH), BF16),
            pltpu.VMEM((tokens, WIDTH), BF16),
            pltpu.VMEM((tokens, WIDTH), BF16),
            pltpu.VMEM((tokens, WIDTH), BF16),
            pltpu.VMEM((SECTIONS, TOK, WIDTH), BF16),
            pltpu.VMEM((tokens, WIDTH), BF16),
            pltpu.VMEM((2, TOK, WIDTH), F32),
            pltpu.VMEM((tokens, WIDTH), BF16),
            pltpu.VMEM((WIDTH, WIDTH), F32),
            pltpu.VMEM((MICRO, 1, TOK), F32),
            pltpu.VMEM((SHARDS,) + ids.shape, jnp.int32),
            pltpu.VMEM((MICRO, TOK, WIDTH), BF16),
            pltpu.VMEM((TOK, WIDTH), BF16),
            pltpu.VMEM((SHARDS, 16 * (MICRO - 1), 128), BF16),
            pltpu.VMEM((SHARDS, 16 * (MICRO - 1), 128), BF16),
            pltpu.VMEM((SHARDS, 16, 128), BF16),
            pltpu.VMEM((SHARDS, 16, 128), BF16),
            pltpu.VMEM((SOON * 8, 128), F32),
            pltpu.VMEM((TOK, 128), jnp.int32),
            pltpu.VMEM((TOK, WIDTH), BF16),
            pltpu.VMEM((TOK, WIDTH), BF16),
            pltpu.VMEM((tokens, WIDTH), BF16),
            pltpu.VMEM((tokens, WIDTH), BF16),
            pltpu.VMEM((SIDE, SIDE * BLOCK, HALF), BF16),
            pltpu.VMEM((SIDE - 1, SIDE, BLOCK, HALF), BF16),
            pltpu.VMEM((SIDE - 1, SIDE * BLOCK, HALF), BF16),
            pltpu.VMEM((SIDE - 1, SIDE * BLOCK, HALF), BF16),
            pltpu.VMEM((2, SIDE, 2, SHARE, HALF), BF16),
            dma((3 + MICRO,)),
            dma((MICRO,)),
            dma,
            dma((SECTIONS,)),
            dma((PIECES,)),
            dma((PIECES,)),
            dma((MICRO, SECTIONS)),
            dma((MICRO,)),
            dma,
            dma,
            dma,
            dma,
            pltpu.SemaphoreType.REGULAR((2,)),
            dma((2,)),
            dma((2,)),
            dma((2,)),
            dma((2,)),
            dma((4,)),
            dma,
            dma,
            dma((MICRO,)),
            dma((MICRO,)),
            dma((MICRO + 1,)),
            dma((MICRO + 1,)),
            dma((SIDE - 1, SIDE)),
            dma((SIDE - 1, SIDE)),
            dma((SIDE - 1, SIDE)),
            dma((SIDE - 1, SIDE)),
            dma((2, SIDE, 2)),
            dma((2, 2, SIDE)),
        ],
        compiler_params=pltpu.CompilerParams(
            collective_id=0, has_side_effects=True, vmem_limit_bytes=56 * 1024 * 1024
        ),
        cost_estimate=pl.CostEstimate(
            flops=10 * tokens * WIDTH * WIDTH, bytes_accessed=9 * 2**20, transcendentals=tokens * WIDTH
        ),
        name="relay",
    )(holder, saved, pooled, grad_top, w_in, w_out, ids)


def table_kernel(named, rows, parts, table, out_in, out_out):
    block = pl.program_id(0)
    lane = lax.broadcasted_iota(jnp.int32, (TOK, WIDE), 1) + block * WIDE
    hit = jnp.where(lane == named[:, 0:1], 1.0, 0.0).astype(BF16)
    table[...] = dot_tn(hit, rows[...])

    @pl.when(block == 0)
    def _():
        for kind, out in ((0, out_in), (1, out_out)):
            for h in range(2):
                total = parts[kind, h, 0].astype(F32)
                for e in range(1, SIDE):
                    total = total + parts[kind, h, e].astype(F32)
                out[:, h * HALF : (h + 1) * HALF] = total


def owner_sums(named, rows, parts):
    def whole(shape):
        return pl.BlockSpec(shape, lambda b: (0,) * len(shape))

    share = jax.ShapeDtypeStruct((SHARE, WIDTH), F32)
    return pl.pallas_call(
        table_kernel,
        grid=(ROWS_OWN // WIDE,),
        out_shape=(jax.ShapeDtypeStruct((ROWS_OWN, WIDTH), F32), share, share),
        in_specs=[whole(named.shape), whole(rows.shape), whole(parts.shape)],
        out_specs=(
            pl.BlockSpec((WIDE, WIDTH), lambda b: (b, 0)),
            whole(share.shape),
            whole(share.shape),
        ),
        compiler_params=pltpu.CompilerParams(vmem_limit_bytes=32 * 1024 * 1024),
        cost_estimate=pl.CostEstimate(
            flops=2 * ROWS_OWN * TOK * WIDTH, bytes_accessed=5 * 2**20, transcendentals=0
        ),
        name="owner_sums",
    )(named, rows, parts)


def local(saved, pooled, grad_top, w_in, w_out, feature_ids, holder_order):
    tokens = MICRO * TOK
    parts, rows, named = relay(
        holder_order,
        saved.reshape(tokens, WIDTH),
        pooled.reshape(TOK, WIDTH),
        grad_top.reshape(tokens, WIDTH),
        w_in[0],
        w_out[0],
        jnp.transpose(feature_ids, (0, 2, 1)),
    )
    table_grad, grad_in, grad_out = owner_sums(named, rows, parts)
    return (grad_in[None], grad_out[None], table_grad)


def solution(mesh):
    return jax.shard_map(
        local,
        mesh=mesh,
        in_specs=(
            P("section", None, "shard", None, None),
            P("section", "shard", None, None),
            P(None, "shard", None, None),
            P("section", None, None),
            P("section", None, None),
            P(None, "shard", None),
            P(),
        ),
        out_specs=(
            P("section", "shard", None),
            P("section", "shard", None),
            P(("section", "shard"), None),
        ),
        check_vma=False,
    )
```

```python
import jax
import jax.numpy as jnp
from jax import lax
from jax.experimental import pallas as pl
from jax.experimental.pallas import tpu as pltpu
from jax.sharding import PartitionSpec as P

ROWS_OWN = 1024
MESH = pl.DeviceIdType.MESH
F32 = jnp.float32
BF16 = jnp.bfloat16

SECTIONS = 4
SHARDS = 32
SIDE = 4
MICRO = 4
TOK = 256
CHUNK = 64
PIECE = 32
WIDTH = 1024
SHARE = WIDTH // SHARDS
PER_PLANE = TOK // SECTIONS
TILE = 256
WIDE = 512
CHUNKS = TOK // CHUNK
SPLIT = CHUNK // PIECE
DEPTH = 4
PIECES = MICRO * TOK // PIECE
SOON = (MICRO - 1) * PER_PLANE
HALF = WIDTH // 2
BLOCK = 2 * SHARE


def dot_tn(a, b):
    return lax.dot_general(a, b, (((0,), (0,)), ((), ())), preferred_element_type=F32)


def kernel(
    holder,
    saved,
    pooled,
    grad_top,
    w_in,
    w_out,
    ids,
    out_parts,
    out_rows,
    out_named,
    win,
    wout,
    win_t,
    wout_t,
    xbuf,
    gbuf,
    nbuf,
    pbuf,
    act,
    slope,
    dz,
    acc,
    rank,
    all_ids,
    sorted_rows,
    routed,
    soon,
    got_soon,
    late,
    got_late,
    flat,
    named,
    rows_buf,
    transit,
    peer_l,
    peer_r,
    send_x,
    recv_x,
    send_y,
    recv_y,
    send_c,
    load_sem,
    top_sem,
    pool_send,
    pool_recv,
    relay_send,
    relay_recv,
    route_send,
    route_recv,
    soon_send,
    soon_recv,
    late_send,
    late_recv,
    ready,
    hop_send,
    hop_recv,
    pass_send,
    pass_recv,
    out_sem,
    ids_send,
    ids_recv,
    l_send,
    l_recv,
    r_send,
    r_recv,
    x_send,
    x_recv,
    y_send,
    y_recv,
    c_send,
    c_recv,
):
    sec = lax.axis_index("section")
    sh = lax.axis_index("shard")
    core = sh % 2
    px = (sh // 2) % SIDE
    py = sh // (2 * SIDE)
    first = sec == 0
    last = sec == SECTIONS - 1

    def at(y, x, c):
        return (sec, (y * SIDE + x) * 2 + c)

    def micro_rows(m):
        return pl.ds(pl.multiple_of(m * TOK, TOK), TOK)

    def token_rows(start, size):
        return pl.ds(pl.multiple_of(start, size), size)

    def load_x(m):
        rows = micro_rows(m)
        return pltpu.make_async_copy(saved.at[rows], xbuf.at[rows], load_sem.at[2 + m])

    def load_top(m):
        rows = micro_rows(m)
        return pltpu.make_async_copy(grad_top.at[rows], gbuf.at[rows], top_sem.at[m])

    load_win = pltpu.make_async_copy(w_in, win, load_sem.at[0])
    load_wout = pltpu.make_async_copy(w_out, wout, load_sem.at[1])
    load_pool = pltpu.make_async_copy(pooled, pbuf.at[0], load_sem.at[2 + MICRO])

    load_win.start()
    load_x(0).start()
    load_wout.start()

    @pl.when(last)
    def _():
        load_top(0).start()

    @pl.when(first)
    def _():
        load_pool.start()

    barrier = pltpu.get_barrier_semaphore()

    def greet(y, x, c):
        pl.semaphore_signal(barrier, inc=1, device_id=at(y, x, c), device_id_type=MESH)

    for k in range(1, SECTIONS):
        pl.semaphore_signal(
            barrier, inc=1, device_id=((sec + k) % SECTIONS, sh), device_id_type=MESH
        )
    for k in range(1, SIDE):
        greet(py, (px + k) % SIDE, core)
        greet((py + k) % SIDE, px, core)
    greet(py, px, 1 - core)

    def tell_row():
        for k in range(1, SIDE):
            to = at(py, (px + k) % SIDE, core)
            pl.semaphore_signal(ready.at[0], inc=1, device_id=to, device_id_type=MESH)

    def tell_plane():
        pl.semaphore_wait(ready.at[0], SIDE - 1)
        for k in range(1, SIDE):
            to = at((py + k) % SIDE, px, core)
            pl.semaphore_signal(ready.at[1], inc=1, device_id=to, device_id_type=MESH)

    def tell_ids(m, n):
        if n == 0:

            @pl.when(m == 0)
            def _():
                tell_plane()

        if n == 1:

            @pl.when(m == 0)
            def _():
                pl.semaphore_wait(ready.at[1], SIDE - 1)

        @pl.when((m > 0) | (n > 0))
        def _():
            ids_copy((sh + m * SPLIT * CHUNKS + n) % SHARDS, sh).start()

    def pool_copy(s):
        return pltpu.make_async_remote_copy(
            src_ref=pooled,
            dst_ref=pbuf.at[s],
            send_sem=pool_send,
            recv_sem=pool_recv.at[s],
            device_id=(0, sh),
            device_id_type=MESH,
        )

    def pool_rows(h):
        return pl.ds(h * (TOK // 2), TOK // 2)

    def hop_copy(h):
        return pltpu.make_async_remote_copy(
            src_ref=pooled.at[pool_rows(h)],
            dst_ref=transit.at[pool_rows(h)],
            send_sem=hop_send.at[h],
            recv_sem=hop_recv.at[h],
            device_id=(SECTIONS - 1, sh),
            device_id_type=MESH,
        )

    def pass_copy(h):
        return pltpu.make_async_remote_copy(
            src_ref=transit.at[pool_rows(h)],
            dst_ref=pbuf.at[2, pool_rows(h)],
            send_sem=pass_send.at[h],
            recv_sem=pass_recv.at[h],
            device_id=(0, sh),
            device_id_type=MESH,
        )

    def pass_pool(h):
        hop_copy(h).wait_recv()
        pass_copy(h).start()

    def relay_copy(c):
        rows = token_rows(c * PIECE, PIECE)
        return pltpu.make_async_remote_copy(
            src_ref=nbuf.at[rows],
            dst_ref=gbuf.at[rows],
            send_sem=relay_send.at[c],
            recv_sem=relay_recv.at[c],
            device_id=(jnp.maximum(sec - 1, 0), sh),
            device_id_type=MESH,
        )

    def route_copy(m, p):
        return pltpu.make_async_remote_copy(
            src_ref=sorted_rows.at[m, pl.ds(p * PER_PLANE, PER_PLANE)],
            dst_ref=routed.at[pl.ds(pl.multiple_of(m * PER_PLANE, PER_PLANE), PER_PLANE)],
            send_sem=route_send.at[m, p],
            recv_sem=route_recv.at[m],
            device_id=(p, sh),
            device_id_type=MESH,
        )

    def ids_copy(to, came):
        return pltpu.make_async_remote_copy(
            src_ref=ids,
            dst_ref=all_ids.at[came],
            send_sem=ids_send,
            recv_sem=ids_recv,
            device_id=(sec, to),
            device_id_type=MESH,
        )

    def left_copy(m, source):
        rows = micro_rows(m)
        return pltpu.make_async_remote_copy(
            src_ref=source.at[rows],
            dst_ref=peer_l.at[rows],
            send_sem=l_send.at[m],
            recv_sem=l_recv.at[m],
            device_id=at(py, px, 1 - core),
            device_id_type=MESH,
        )

    def right_copy(n, source, start, size):
        rows = pl.ds(pl.multiple_of(start, 64), size)
        return pltpu.make_async_remote_copy(
            src_ref=source.at[rows],
            dst_ref=peer_r.at[rows],
            send_sem=r_send.at[n],
            recv_sem=r_recv.at[n],
            device_id=at(py, px, 1 - core),
            device_id_type=MESH,
        )

    def send_left(m):
        @pl.when(core == 0)
        def _():
            left_copy(m, act).start()

        @pl.when(core == 1)
        def _():
            left_copy(m, xbuf).start()

    def send_right(n, start, size):
        @pl.when(core == 0)
        def _():
            right_copy(n, gbuf, start, size).start()

        @pl.when(core == 1)
        def _():
            right_copy(n, dz, start, size).start()

    def forward_open(m):
        rows = micro_rows(m)
        load_x(m).wait()

        @pl.when(first)
        def _():
            slot = 0
            for j in range(1, MICRO):
                slot = jnp.where(holder[j] == m, j, slot)
            extra = pbuf[slot]
            xbuf[rows, :] = (xbuf[rows, :].astype(F32) + extra.astype(F32)).astype(BF16)

    def forward_tile(m, j):
        rows = micro_rows(m)
        cols = pl.ds(j * TILE, TILE)
        z = jnp.dot(xbuf[rows, :], win[:, cols], preferred_element_type=F32)
        sig = jax.nn.sigmoid(z)
        act[rows, cols] = (z * sig).astype(BF16)
        slope[m % 2, :, cols] = sig * (1.0 + z * (1.0 - sig))

    def forward(m):
        forward_open(m)
        for j in range(WIDTH // TILE):
            forward_tile(m, j)

    def backward(m, start, size):
        crows = token_rows(m * TOK + start, size)
        krows = pl.ds(start, size)
        for j in range(WIDTH // WIDE):
            cols = pl.ds(j * WIDE, WIDE)
            ga = jnp.dot(gbuf[crows, :], wout_t[:, cols], preferred_element_type=F32)
            dz[crows, cols] = (ga * slope[m % 2, krows, cols]).astype(BF16)
        for j in range(WIDTH // WIDE):
            cols = pl.ds(j * WIDE, WIDE)
            back = jnp.dot(dz[crows, :], win_t[:, cols], preferred_element_type=F32)
            nbuf[crows, cols] = (gbuf[crows, cols].astype(F32) + back).astype(BF16)

    def grad_tiles(m, tiles, and_peer):
        rows = micro_rows(m)
        for kind, left, right in ((0, xbuf, dz), (1, act, gbuf)):

            @pl.when(core == kind)
            def _(left=left, right=right):
                for i in tiles:
                    cols = pl.ds(i * TILE, TILE)
                    total = acc[cols, :] + dot_tn(left[rows, cols], right[rows, :])
                    if and_peer:
                        total = total + dot_tn(peer_l[rows, cols], peer_r[rows, :])
                    acc[cols, :] = total

    def hear_peer(m):
        left_copy(m, act).wait_recv()
        right_copy(m, dz, m * TOK, TOK).wait_recv()

    load_win.wait()
    for j in range(WIDTH // TILE):
        cols = pl.ds(j * TILE, TILE)
        win_t[:, cols] = win[cols, :].T

    @pl.when(jnp.logical_not(first))
    def _():
        forward(0)

    load_wout.wait()
    for j in range(WIDTH // TILE):
        cols = pl.ds(j * TILE, TILE)
        wout_t[:, cols] = wout[cols, :].T

    pl.semaphore_wait(barrier, SECTIONS - 1 + 2 * (SIDE - 1) + 1)
    tell_row()

    @pl.when((sec == 1) | last)
    def _():
        pool_copy(sec).start()

    @pl.when(sec == 2)
    def _():
        hop_copy(0).start()
        hop_copy(1).start()

    @pl.when(last)
    def _():
        load_top(0).wait()
        for i in range(SPLIT):
            backward(0, i * PIECE, PIECE)
            relay_copy(i).start()
        for k in range(1, CHUNKS):
            backward(0, k * CHUNK, CHUNK)
            for c in range(k * SPLIT, (k + 1) * SPLIT):
                if c >= DEPTH:
                    relay_copy(c - DEPTH).wait_send()
                relay_copy(c).start()
        for m in range(1, MICRO):
            load_top(m).start()

    for m in range(1, MICRO):
        load_x(m).start()

    def clear(i, carry):
        rows = pl.ds(pl.multiple_of(i * 64, 64), 64)
        acc[rows, :] = jnp.zeros((64, WIDTH), F32)
        return carry

    @pl.when(first)
    def _():
        lax.fori_loop(0, WIDTH // 64, clear, 0)
        row = lax.broadcasted_iota(jnp.int32, (TOK, TOK), 0)
        col = lax.broadcasted_iota(jnp.int32, (TOK, TOK), 1)
        feat = ids.shape[1]
        lane = lax.broadcasted_iota(jnp.int32, (ids.shape[2], TOK), 1)
        lead = lax.broadcasted_iota(jnp.int32, (ids.shape[2], TOK), 0)
        widen = jnp.where(lane >> 3 == lead, 1.0, 0.0).astype(BF16)
        for m in range(MICRO):
            owner = (ids[m] >> 10).astype(F32).astype(BF16)
            wide = jnp.dot(owner, widen, preferred_element_type=F32)
            inner = lax.broadcasted_iota(jnp.int32, (feat, TOK), 1) & 7
            outer = lax.broadcasted_iota(jnp.int32, (feat, TOK), 0)
            across = jnp.sum(jnp.where(inner == outer, wide, 0.0), axis=0, keepdims=True)
            down = jnp.sum(jnp.where(row == col, across, 0.0), axis=1, keepdims=True)
            earlier = jnp.where((down == across) & (row < col), 1.0, 0.0)
            rank[m] = 2.0 * across + jnp.sum(earlier, axis=0, keepdims=True)
        load_pool.wait()
        for s in (1, SECTIONS - 1):
            pool_copy(s).wait_recv()
        for h in range(2):
            pass_copy(h).wait_recv()
        forward(0)

    @pl.when(jnp.logical_not(first))
    def _():
        lax.fori_loop(0, WIDTH // 64, clear, 0)

    @pl.when(last)
    def _():
        pass_pool(0)

    all_ids[sh] = ids[...]
    send_left(0)

    def step(m, start, size, hook=None):
        pieces = [(m * TOK + start) // PIECE + i for i in range(size // PIECE)]

        @pl.when(jnp.logical_not(last))
        def _():
            for c in pieces:
                relay_copy(c).wait_recv()

        if hook is not None:
            hook()
        backward(m, start, size)

        @pl.when(jnp.logical_not(first))
        def _():
            for c in pieces:

                @pl.when(last)
                def _(c=c):
                    relay_copy(c - DEPTH).wait_send()

                relay_copy(c).start()

    inner = jnp.logical_not(first | last)

    def chunks(m, slots, hook=None):
        for k in range(CHUNKS):
            fine = hook is not None and k == CHUNKS - 1
            for i in range(SPLIT):

                def piece(k=k, i=i):
                    at_last = hook if fine and i == SPLIT - 1 else None
                    step(m, k * CHUNK + i * PIECE, PIECE, at_last)

                if fine:
                    piece()
                else:
                    pl.when(inner)(piece)
                if not fine and i == SPLIT - 1:

                    @pl.when(first | (last & (m > 0)))
                    def _(k=k):
                        step(m, k * CHUNK, CHUNK)

                slots[k * SPLIT + i]()
                tell_ids(m, k * SPLIT + i)

    def route(m):
        rows = micro_rows(m)

        @pl.when(first)
        def _():
            target = lax.broadcasted_iota(jnp.int32, (TOK, TOK), 0).astype(F32)
            pick = jnp.where(target == rank[m], 1.0, 0.0).astype(BF16)
            ordered = jnp.dot(pick, nbuf[rows, :], preferred_element_type=F32).astype(BF16)
            sorted_rows[m] = ordered
            route_copy(m, 1).start()
            route_copy(m, SECTIONS - 1).start()
            if isinstance(m, int):
                route_copy(m, 2).start()
            routed[pl.ds(pl.multiple_of(m * PER_PLANE, PER_PLANE), PER_PLANE), :] = ordered[
                :PER_PLANE, :
            ]

    def micro_step(m, carry):
        @pl.when(last & (m > 0))
        def _():
            load_top(m).wait()

        def forward_slot(j):
            def work():
                if j == 0:
                    forward_open(m + 1)
                forward_tile(m + 1, j)
                if j == WIDTH // TILE - 1:
                    send_left(m + 1)

            return work

        def grad_slot(i):
            def work():
                if i == 0:

                    @pl.when(last & (m == 1))
                    def _():
                        pass_pool(1)

                @pl.when(m > 0)
                def _():
                    if i == 0:
                        hear_peer(m - 1)
                    grad_tiles(m - 1, (i,), True)

            return work

        tiles = range(WIDTH // TILE)
        chunks(m, [forward_slot(j) for j in tiles] + [grad_slot(i) for i in tiles])
        send_right(m, m * TOK, TOK)
        route(m)
        return carry

    lax.fori_loop(0, MICRO - 1, micro_step, 0)

    final = MICRO - 1
    tail = TOK - CHUNK

    def unit_copy(source, target, send, recv, to, came):
        return pltpu.make_async_remote_copy(
            src_ref=source.at[to],
            dst_ref=target.at[came],
            send_sem=send,
            recv_sem=recv,
            device_id=(sec, to),
            device_id_type=MESH,
        )

    def hand_soon(k, carry):
        to = (sh + k) % SHARDS
        unit_copy(soon, got_soon, soon_send, soon_recv, to, sh).start()
        return carry

    def hand_late(k, carry):
        to = (sh + k) % SHARDS
        unit_copy(late, got_late, late_send, late_recv, to, sh).start()
        return carry

    def wait_all(ref, semaphore):
        others = ref.at[pl.ds(0, SHARDS - 1)]
        pltpu.make_async_copy(others, others, semaphore).wait()

    def soon_units():
        row = lax.broadcasted_iota(jnp.int32, (SOON, SOON), 0)
        col = lax.broadcasted_iota(jnp.int32, (SOON, SOON), 1)
        target = ((col >> 1) & (SHARDS - 1)) * (2 * (MICRO - 1)) + (col >> 6) * 2 + (col & 1)
        regroup = jnp.where(row == target, 1.0, 0.0).astype(BF16)
        by_owner = jnp.dot(regroup, routed[pl.ds(0, SOON), :], preferred_element_type=F32)
        for b in range(8):
            flat[pl.ds(b, SOON, stride=8), :] = by_owner[:, b * 128 : (b + 1) * 128]
        soon[...] = flat[...].reshape(soon.shape).astype(BF16)
        got_soon[sh] = soon[sh]

    def late_units():
        by_owner = routed[pl.ds(SOON, PER_PLANE), :].astype(F32)
        for b in range(8):
            flat[pl.ds(b, PER_PLANE, stride=8), :] = by_owner[:, b * 128 : (b + 1) * 128]
        late[...] = flat[pl.ds(0, PER_PLANE * 8), :].reshape(late.shape).astype(BF16)
        got_late[sh] = late[sh]

    def to_rows(got, start, count):
        flat[pl.ds(0, count * 8), :] = got[...].astype(F32).reshape(count * 8, 128)
        for b in range(8):
            rows_buf[pl.ds(start, count), pl.ds(b * 128, 128)] = flat[
                pl.ds(b, count, stride=8), :
            ].astype(BF16)

    @pl.when(last)
    def _():
        load_top(final).wait()

    def final_slot(n):
        def work():
            if n == 2:
                hear_peer(final - 1)
            if 2 <= n < 2 + WIDTH // TILE:
                grad_tiles(final - 1, (n - 2,), True)
            if n == 5:
                send_right(final, final * TOK, tail)

            @pl.when(first)
            def _():
                if n == 0:
                    soon_units()
                if n == 1:
                    for before in range(final):
                        route_copy(before, 2).start()
                if n == 2:
                    lax.fori_loop(1, SHARDS // 2, hand_soon, 0)
                if n == 4:
                    lax.fori_loop(SHARDS // 2, SHARDS, hand_soon, 0)

        return work

    def hand_g():
        @pl.when(core == 0)
        def _():
            right_copy(final + 1, gbuf, final * TOK + tail, TOK - tail).start()

    chunks(final, [final_slot(n) for n in range(CHUNKS * SPLIT)], hand_g)

    @pl.when(core == 1)
    def _():
        right_copy(final + 1, dz, final * TOK + tail, TOK - tail).start()

    grad_tiles(final, (0, 1, 2, 3), False)

    def block_rows(y, x):
        return pl.ds(pl.multiple_of((y * SIDE + x) * BLOCK, BLOCK), BLOCK)

    left_half = pl.ds(0, HALF)
    right_half = pl.ds(HALF, HALF)

    def x_copy(d, y):
        to = (px + d) % SIDE
        return pltpu.make_async_remote_copy(
            src_ref=send_x.at[y, pl.ds(pl.multiple_of(to * BLOCK, BLOCK), BLOCK)],
            dst_ref=recv_x.at[d - 1, y],
            send_sem=x_send.at[d - 1, y],
            recv_sem=x_recv.at[d - 1, y],
            device_id=at(py, to, core),
            device_id_type=MESH,
        )

    def y_copy(d, x):
        rows = pl.ds(pl.multiple_of(x * BLOCK, BLOCK), BLOCK)
        return pltpu.make_async_remote_copy(
            src_ref=send_y.at[d - 1, rows],
            dst_ref=recv_y.at[d - 1, rows],
            send_sem=y_send.at[d - 1, x],
            recv_sem=y_recv.at[d - 1, x],
            device_id=at((py + d) % SIDE, px, core),
            device_id_type=MESH,
        )

    def c_copy(h, e, c, kind):
        there = (py + e) % SIDE if h == 0 else (px + e) % SIDE
        return pltpu.make_async_remote_copy(
            src_ref=send_c.at[h, e, c],
            dst_ref=out_parts.at[kind, h, e],
            send_sem=c_send.at[h, e, c],
            recv_sem=c_recv.at[kind, h, e],
            device_id=at(there, px, c) if h == 0 else at(py, there, c),
            device_id_type=MESH,
        )

    def own_part(h):
        return pltpu.make_async_copy(
            send_c.at[h, 0, core], out_parts.at[core, h, 0], out_sem.at[2 + h]
        )

    order = (2, 1, 3, 0)
    frows = micro_rows(final)
    left_copy(final, act).wait_recv()
    right_copy(final, dz, final * TOK, tail).wait_recv()
    right_copy(final + 1, dz, final * TOK + tail, TOK - tail).wait_recv()
    for d in order:
        y = (py + d) % SIDE
        cols = pl.ds(pl.multiple_of(y * TILE, TILE), TILE)
        total = acc[cols, :] + dot_tn(peer_l[frows, cols], peer_r[frows, :])
        acc[cols, :] = total
        send_x[y] = total[:, :HALF].astype(BF16)
        for dx in (2, 1, 3):
            x_copy(dx, y).start()
        if d != 0:
            send_y[d - 1] = total[:, HALF:].astype(BF16)
    for e in order:
        for d in (2, 1, 3):
            y_copy(d, (px + e) % SIDE).start()
    route(final)

    @pl.when(jnp.logical_not(first))
    def _():
        for m in range(MICRO - 1):
            route_copy(m, 1).wait_recv()
        soon_units()
        lax.fori_loop(1, SHARDS, hand_soon, 0)
        route_copy(final, 1).wait_recv()

    late_units()
    lax.fori_loop(1, SHARDS, hand_late, 0)

    wait_all(all_ids, ids_recv)
    own = sec * SHARDS + sh
    feature = own // (SECTIONS * SHARDS // ids.shape[1])
    heard = all_ids[:, :, feature, :].reshape(SHARDS * MICRO, ids.shape[2])
    place = lax.broadcasted_iota(jnp.int32, heard.shape, 1) * ROWS_OWN + (heard & (ROWS_OWN - 1))
    ours = heard >> 10 == own
    low = jnp.min(jnp.where(ours, place, 1 << 20), axis=1, keepdims=True) & (ROWS_OWN - 1)
    high = jnp.max(jnp.where(ours, place, -1), axis=1, keepdims=True) & (ROWS_OWN - 1)
    at_lane = lax.broadcasted_iota(jnp.int32, (SHARDS * MICRO, 128), 1)
    parts = jnp.where(
        at_lane == 0,
        low >> 5,
        jnp.where(at_lane == 1, low & 31, jnp.where(at_lane == 2, high >> 5, high & 31)),
    )
    half = lax.broadcasted_iota(jnp.int32, (TOK, SHARDS * MICRO), 0) >> 1
    pair = lax.broadcasted_iota(jnp.int32, (TOK, SHARDS * MICRO), 1)
    came, micro = pair >> 2, pair & (MICRO - 1)
    place_of = jnp.where(
        micro < final, came * (MICRO - 1) + micro, SHARDS * (MICRO - 1) + came
    )
    twice = jnp.where(half == place_of, 1.0, 0.0).astype(BF16)
    both = jnp.dot(twice, parts.astype(F32).astype(BF16), preferred_element_type=F32)
    odd = lax.broadcasted_iota(jnp.int32, (TOK, 1), 0) & 1
    row_of = jnp.where(
        odd == 0, both[:, 0:1] * 32.0 + both[:, 1:2], both[:, 2:3] * 32.0 + both[:, 3:4]
    )
    named[...] = jnp.broadcast_to(row_of.astype(jnp.int32), (TOK, 128))
    put_named = pltpu.make_async_copy(named, out_named, out_sem.at[0])
    put_named.start()

    put_rows = pltpu.make_async_copy(rows_buf, out_rows, out_sem.at[1])

    def collect_rows():
        wait_all(got_soon, soon_recv)
        to_rows(got_soon, 0, SOON)
        wait_all(got_late, late_recv)
        to_rows(got_late, SOON, PER_PLANE)
        put_rows.start()

    pl.when(first)(collect_rows)

    for e in order:
        y = (py + e) % SIDE
        x = (px + e) % SIDE
        for d in range(1, SIDE):
            x_copy(d, y).wait_recv()
            y_copy(d, x).wait_recv()
        total = acc[block_rows(y, px), left_half]
        other = acc[block_rows(py, x), right_half]
        for d in range(1, SIDE):
            total = total + recv_x[d - 1, y].astype(F32)
            xrows = pl.ds(pl.multiple_of(x * BLOCK, BLOCK), BLOCK)
            other = other + recv_y[d - 1, xrows, :].astype(F32)
        for h, part in ((0, total), (1, other)):
            for c in range(2):
                send_c[h, e, c] = part[c * SHARE : (c + 1) * SHARE, :].astype(BF16)
                if e == 0:

                    @pl.when(core == c)
                    def _(h=h, c=c):
                        own_part(h).start()

                    @pl.when(core != c)
                    def _(h=h, c=c):
                        c_copy(h, 0, c, core).start()
                else:
                    c_copy(h, e, c, core).start()

    pl.when(jnp.logical_not(first))(collect_rows)

    wait_all(all_ids, ids_send)
    wait_all(soon, soon_send)

    @pl.when((sec == 1) | last)
    def _():
        pool_copy(sec).wait_send()

    @pl.when(sec == 2)
    def _():
        hop_copy(0).wait_send()
        hop_copy(1).wait_send()

    @pl.when(last)
    def _():
        pass_copy(0).wait_send()
        pass_copy(1).wait_send()

    @pl.when(jnp.logical_not(first))
    def _():
        def left(c, carry):
            relay_copy(c).wait_send()
            return carry

        lax.fori_loop(jnp.where(last, PIECES - DEPTH, 0), PIECES, left, 0)

    @pl.when(first)
    def _():
        for m in range(final):
            for p in range(1, SECTIONS):
                route_copy(m, p).wait_send()

    for m in range(MICRO):
        left_copy(m, act).wait_send()
    for m in range(final):
        right_copy(m, dz, m * TOK, TOK).wait_send()
    right_copy(final, dz, final * TOK, tail).wait_send()
    right_copy(final + 1, dz, final * TOK + tail, TOK - tail).wait_send()

    wait_all(late, late_send)

    @pl.when(first)
    def _():
        for p in range(1, SECTIONS):
            route_copy(final, p).wait_send()

    for d in range(1, SIDE):
        for y in range(SIDE):
            x_copy(d, y).wait_send()
            y_copy(d, y).wait_send()

    for kind in range(2):
        for h in range(2):

            @pl.when(core != kind)
            def _(h=h, kind=kind):
                c_copy(h, 0, 1 - kind, kind).wait_recv()

            for e in range(1, SIDE):
                c_copy(h, e, 0, kind).wait_recv()

    for h in range(2):
        for d in range(1, SIDE):
            for c in range(2):
                c_copy(h, d, c, core).wait_send()
        c_copy(h, 0, 1 - core, core).wait_send()
    for put in (put_named, put_rows, own_part(0), own_part(1)):
        put.wait()


def relay(holder, saved, pooled, grad_top, w_in, w_out, ids):
    vmem = pl.BlockSpec(memory_space=pltpu.VMEM)
    anywhere = pl.BlockSpec(memory_space=pl.ANY)
    dma = pltpu.SemaphoreType.DMA
    tokens = MICRO * TOK
    return pl.pallas_call(
        kernel,
        out_shape=(
            jax.ShapeDtypeStruct((2, 2, SIDE, SHARE, HALF), BF16),
            jax.ShapeDtypeStruct((TOK, WIDTH), BF16),
            jax.ShapeDtypeStruct((TOK, 128), jnp.int32),
        ),
        in_specs=[pl.BlockSpec(memory_space=pltpu.SMEM)] + [anywhere] * 5 + [vmem],
        out_specs=(anywhere, anywhere, anywhere),
        scratch_shapes=[
            pltpu.VMEM((WIDTH, WIDTH), BF16),
            pltpu.VMEM((WIDTH, WIDTH), BF16),
            pltpu.VMEM((WIDTH, WIDTH), BF16),
            pltpu.VMEM((WIDTH, WIDTH), BF16),
            pltpu.VMEM((tokens, WIDTH), BF16),
            pltpu.VMEM((tokens, WIDTH), BF16),
            pltpu.VMEM((tokens, WIDTH), BF16),
            pltpu.VMEM((SECTIONS, TOK, WIDTH), BF16),
            pltpu.VMEM((tokens, WIDTH), BF16),
            pltpu.VMEM((2, TOK, WIDTH), F32),
            pltpu.VMEM((tokens, WIDTH), BF16),
            pltpu.VMEM((WIDTH, WIDTH), F32),
            pltpu.VMEM((MICRO, 1, TOK), F32),
            pltpu.VMEM((SHARDS,) + ids.shape, jnp.int32),
            pltpu.VMEM((MICRO, TOK, WIDTH), BF16),
            pltpu.VMEM((TOK, WIDTH), BF16),
            pltpu.VMEM((SHARDS, 16 * (MICRO - 1), 128), BF16),
            pltpu.VMEM((SHARDS, 16 * (MICRO - 1), 128), BF16),
            pltpu.VMEM((SHARDS, 16, 128), BF16),
            pltpu.VMEM((SHARDS, 16, 128), BF16),
            pltpu.VMEM((SOON * 8, 128), F32),
            pltpu.VMEM((TOK, 128), jnp.int32),
            pltpu.VMEM((TOK, WIDTH), BF16),
            pltpu.VMEM((TOK, WIDTH), BF16),
            pltpu.VMEM((tokens, WIDTH), BF16),
            pltpu.VMEM((tokens, WIDTH), BF16),
            pltpu.VMEM((SIDE, SIDE * BLOCK, HALF), BF16),
            pltpu.VMEM((SIDE - 1, SIDE, BLOCK, HALF), BF16),
            pltpu.VMEM((SIDE - 1, SIDE * BLOCK, HALF), BF16),
            pltpu.VMEM((SIDE - 1, SIDE * BLOCK, HALF), BF16),
            pltpu.VMEM((2, SIDE, 2, SHARE, HALF), BF16),
            dma((3 + MICRO,)),
            dma((MICRO,)),
            dma,
            dma((SECTIONS,)),
            dma((PIECES,)),
            dma((PIECES,)),
            dma((MICRO, SECTIONS)),
            dma((MICRO,)),
            dma,
            dma,
            dma,
            dma,
            pltpu.SemaphoreType.REGULAR((2,)),
            dma((2,)),
            dma((2,)),
            dma((2,)),
            dma((2,)),
            dma((4,)),
            dma,
            dma,
            dma((MICRO,)),
            dma((MICRO,)),
            dma((MICRO + 1,)),
            dma((MICRO + 1,)),
            dma((SIDE - 1, SIDE)),
            dma((SIDE - 1, SIDE)),
            dma((SIDE - 1, SIDE)),
            dma((SIDE - 1, SIDE)),
            dma((2, SIDE, 2)),
            dma((2, 2, SIDE)),
        ],
        compiler_params=pltpu.CompilerParams(
            collective_id=0, has_side_effects=True, vmem_limit_bytes=56 * 1024 * 1024
        ),
        cost_estimate=pl.CostEstimate(
            flops=10 * tokens * WIDTH * WIDTH, bytes_accessed=9 * 2**20, transcendentals=tokens * WIDTH
        ),
        name="relay",
    )(holder, saved, pooled, grad_top, w_in, w_out, ids)


def table_kernel(named, rows, parts, table, out_in, out_out):
    block = pl.program_id(0)
    lane = lax.broadcasted_iota(jnp.int32, (TOK, WIDE), 1) + block * WIDE
    hit = jnp.where(lane == named[:, 0:1], 1.0, 0.0).astype(BF16)
    table[...] = dot_tn(hit, rows[...])

    @pl.when(block == 0)
    def _():
        for kind, out in ((0, out_in), (1, out_out)):
            for h in range(2):
                total = parts[kind, h, 0].astype(F32)
                for e in range(1, SIDE):
                    total = total + parts[kind, h, e].astype(F32)
                out[:, h * HALF : (h + 1) * HALF] = total


def owner_sums(named, rows, parts):
    def whole(shape):
        return pl.BlockSpec(shape, lambda b: (0,) * len(shape))

    share = jax.ShapeDtypeStruct((SHARE, WIDTH), F32)
    return pl.pallas_call(
        table_kernel,
        grid=(ROWS_OWN // WIDE,),
        out_shape=(jax.ShapeDtypeStruct((ROWS_OWN, WIDTH), F32), share, share),
        in_specs=[whole(named.shape), whole(rows.shape), whole(parts.shape)],
        out_specs=(
            pl.BlockSpec((WIDE, WIDTH), lambda b: (b, 0)),
            whole(share.shape),
            whole(share.shape),
        ),
        compiler_params=pltpu.CompilerParams(vmem_limit_bytes=32 * 1024 * 1024),
        cost_estimate=pl.CostEstimate(
            flops=2 * ROWS_OWN * TOK * WIDTH, bytes_accessed=5 * 2**20, transcendentals=0
        ),
        name="owner_sums",
    )(named, rows, parts)


def local(saved, pooled, grad_top, w_in, w_out, feature_ids, holder_order):
    tokens = MICRO * TOK
    parts, rows, named = relay(
        holder_order,
        saved.reshape(tokens, WIDTH),
        pooled.reshape(TOK, WIDTH),
        grad_top.reshape(tokens, WIDTH),
        w_in[0],
        w_out[0],
        jnp.transpose(feature_ids, (0, 2, 1)),
    )
    table_grad, grad_in, grad_out = owner_sums(named, rows, parts)
    return (grad_in[None], grad_out[None], table_grad)


def solution(mesh):
    return jax.shard_map(
        local,
        mesh=mesh,
        in_specs=(
            P("section", None, "shard", None, None),
            P("section", "shard", None, None),
            P(None, "shard", None, None),
            P("section", None, None),
            P("section", None, None),
            P(None, "shard", None),
            P(),
        ),
        out_specs=(
            P("section", "shard", None),
            P("section", "shard", None),
            P(("section", "shard"), None),
        ),
        check_vma=False,
    )
```

```python
import jax
import jax.numpy as jnp
from jax import lax
from jax.experimental import pallas as pl
from jax.experimental.pallas import tpu as pltpu
from jax.sharding import PartitionSpec as P

ROWS_OWN = 1024
MESH = pl.DeviceIdType.MESH
F32 = jnp.float32
BF16 = jnp.bfloat16

SECTIONS = 4
SHARDS = 32
SIDE = 4
MICRO = 4
TOK = 256
CHUNK = 64
PIECE = 32
WIDTH = 1024
SHARE = WIDTH // SHARDS
PER_PLANE = TOK // SECTIONS
TILE = 256
WIDE = 512
CHUNKS = TOK // CHUNK
SPLIT = CHUNK // PIECE
PIECES = MICRO * TOK // PIECE
SOON = (MICRO - 1) * PER_PLANE
HALF = WIDTH // 2
BLOCK = 2 * SHARE


def dot_tn(a, b):
    return lax.dot_general(a, b, (((0,), (0,)), ((), ())), preferred_element_type=F32)


def kernel(
    holder,
    saved,
    pooled,
    grad_top,
    w_in,
    w_out,
    ids,
    out_parts,
    out_rows,
    out_named,
    win,
    wout,
    win_t,
    wout_t,
    xbuf,
    gbuf,
    nbuf,
    pbuf,
    act,
    slope,
    dz,
    acc,
    rank,
    all_ids,
    sorted_rows,
    routed,
    soon,
    got_soon,
    late,
    got_late,
    flat,
    named,
    rows_buf,
    transit,
    peer_l,
    peer_r,
    send_x,
    recv_x,
    send_y,
    recv_y,
    send_c,
    load_sem,
    top_sem,
    pool_send,
    pool_recv,
    relay_send,
    relay_recv,
    route_send,
    route_recv,
    soon_send,
    soon_recv,
    late_send,
    late_recv,
    ready,
    hop_send,
    hop_recv,
    pass_send,
    pass_recv,
    out_sem,
    ids_send,
    ids_recv,
    l_send,
    l_recv,
    r_send,
    r_recv,
    x_send,
    x_recv,
    y_send,
    y_recv,
    c_send,
    c_recv,
):
    sec = lax.axis_index("section")
    sh = lax.axis_index("shard")
    core = sh % 2
    px = (sh // 2) % SIDE
    py = sh // (2 * SIDE)
    first = sec == 0
    last = sec == SECTIONS - 1

    def at(y, x, c):
        return (sec, (y * SIDE + x) * 2 + c)

    def micro_rows(m):
        return pl.ds(pl.multiple_of(m * TOK, TOK), TOK)

    def token_rows(start, size):
        return pl.ds(pl.multiple_of(start, size), size)

    def load_x(m):
        rows = micro_rows(m)
        return pltpu.make_async_copy(saved.at[rows], xbuf.at[rows], load_sem.at[2 + m])

    def load_top(m):
        rows = micro_rows(m)
        return pltpu.make_async_copy(grad_top.at[rows], gbuf.at[rows], top_sem.at[m])

    load_win = pltpu.make_async_copy(w_in, win, load_sem.at[0])
    load_wout = pltpu.make_async_copy(w_out, wout, load_sem.at[1])
    load_pool = pltpu.make_async_copy(pooled, pbuf.at[0], load_sem.at[2 + MICRO])

    load_win.start()
    load_x(0).start()
    load_wout.start()

    @pl.when(last)
    def _():
        load_top(0).start()

    @pl.when(first)
    def _():
        load_pool.start()

    barrier = pltpu.get_barrier_semaphore()

    def greet(y, x, c):
        pl.semaphore_signal(barrier, inc=1, device_id=at(y, x, c), device_id_type=MESH)

    for k in range(1, SECTIONS):
        pl.semaphore_signal(
            barrier, inc=1, device_id=((sec + k) % SECTIONS, sh), device_id_type=MESH
        )
    for k in range(1, SIDE):
        greet(py, (px + k) % SIDE, core)
        greet((py + k) % SIDE, px, core)
    greet(py, px, 1 - core)

    def tell_row():
        for k in range(1, SIDE):
            to = at(py, (px + k) % SIDE, core)
            pl.semaphore_signal(ready.at[0], inc=1, device_id=to, device_id_type=MESH)

    def tell_plane():
        pl.semaphore_wait(ready.at[0], SIDE - 1)
        for k in range(1, SIDE):
            to = at((py + k) % SIDE, px, core)
            pl.semaphore_signal(ready.at[1], inc=1, device_id=to, device_id_type=MESH)

    def tell_ids(m, n):
        start, total = SPLIT * CHUNKS // 2, SPLIT * CHUNKS

        def tell(k):
            ids_copy((sh + k) % SHARDS, sh).start()

        if n == 0:
            pl.when(m == 0)(tell_plane)
        if n == start:

            @pl.when(m == 0)
            def _():
                pl.semaphore_wait(ready.at[1], SIDE - 1)

        if n >= start:
            tell(m * total + n)
        else:

            @pl.when(m > 0)
            def _():
                tell(m * total + n)

        if 0 < n < start:

            @pl.when(m == 1)
            def _():
                tell(n)

    def pool_copy(s):
        return pltpu.make_async_remote_copy(
            src_ref=pooled,
            dst_ref=pbuf.at[s],
            send_sem=pool_send,
            recv_sem=pool_recv.at[s],
            device_id=(0, sh),
            device_id_type=MESH,
        )

    def pool_rows(h):
        return pl.ds(h * (TOK // 2), TOK // 2)

    def hop_copy(h):
        return pltpu.make_async_remote_copy(
            src_ref=pooled.at[pool_rows(h)],
            dst_ref=transit.at[pool_rows(h)],
            send_sem=hop_send.at[h],
            recv_sem=hop_recv.at[h],
            device_id=(SECTIONS - 1, sh),
            device_id_type=MESH,
        )

    def pass_copy(h):
        return pltpu.make_async_remote_copy(
            src_ref=transit.at[pool_rows(h)],
            dst_ref=pbuf.at[2, pool_rows(h)],
            send_sem=pass_send.at[h],
            recv_sem=pass_recv.at[h],
            device_id=(0, sh),
            device_id_type=MESH,
        )

    def pass_pool(h):
        hop_copy(h).wait_recv()
        pass_copy(h).start()

    def relay_copy(c):
        rows = token_rows(c * PIECE, PIECE)
        return pltpu.make_async_remote_copy(
            src_ref=nbuf.at[rows],
            dst_ref=gbuf.at[rows],
            send_sem=relay_send.at[c],
            recv_sem=relay_recv.at[c],
            device_id=(jnp.maximum(sec - 1, 0), sh),
            device_id_type=MESH,
        )

    def route_copy(m, p):
        return pltpu.make_async_remote_copy(
            src_ref=sorted_rows.at[m, pl.ds(p * PER_PLANE, PER_PLANE)],
            dst_ref=routed.at[pl.ds(pl.multiple_of(m * PER_PLANE, PER_PLANE), PER_PLANE)],
            send_sem=route_send.at[m, p],
            recv_sem=route_recv.at[m],
            device_id=(p, sh),
            device_id_type=MESH,
        )

    def ids_copy(to, came):
        return pltpu.make_async_remote_copy(
            src_ref=ids,
            dst_ref=all_ids.at[came],
            send_sem=ids_send,
            recv_sem=ids_recv,
            device_id=(sec, to),
            device_id_type=MESH,
        )

    def left_copy(m, source):
        rows = micro_rows(m)
        return pltpu.make_async_remote_copy(
            src_ref=source.at[rows],
            dst_ref=peer_l.at[rows],
            send_sem=l_send.at[m],
            recv_sem=l_recv.at[m],
            device_id=at(py, px, 1 - core),
            device_id_type=MESH,
        )

    def right_copy(n, source, start, size):
        rows = pl.ds(pl.multiple_of(start, 64), size)
        return pltpu.make_async_remote_copy(
            src_ref=source.at[rows],
            dst_ref=peer_r.at[rows],
            send_sem=r_send.at[n],
            recv_sem=r_recv.at[n],
            device_id=at(py, px, 1 - core),
            device_id_type=MESH,
        )

    def send_left(m):
        @pl.when(core == 0)
        def _():
            left_copy(m, act).start()

        @pl.when(core == 1)
        def _():
            left_copy(m, xbuf).start()

    def send_right(n, start, size):
        @pl.when(core == 0)
        def _():
            right_copy(n, gbuf, start, size).start()

        @pl.when(core == 1)
        def _():
            right_copy(n, dz, start, size).start()

    def forward_open(m):
        rows = micro_rows(m)
        load_x(m).wait()

        @pl.when(first)
        def _():
            slot = 0
            for j in range(1, MICRO):
                slot = jnp.where(holder[j] == m, j, slot)
            extra = pbuf[slot]
            xbuf[rows, :] = (xbuf[rows, :].astype(F32) + extra.astype(F32)).astype(BF16)

    def forward_tile(m, j):
        rows = micro_rows(m)
        cols = pl.ds(j * TILE, TILE)
        z = jnp.dot(xbuf[rows, :], win[:, cols], preferred_element_type=F32)
        sig = jax.nn.sigmoid(z)
        act[rows, cols] = (z * sig).astype(BF16)
        slope[m % 2, :, cols] = sig * (1.0 + z * (1.0 - sig))

    def forward(m):
        forward_open(m)
        for j in range(WIDTH // TILE):
            forward_tile(m, j)

    def backward(m, start, size):
        crows = token_rows(m * TOK + start, size)
        krows = pl.ds(start, size)
        for j in range(WIDTH // WIDE):
            cols = pl.ds(j * WIDE, WIDE)
            ga = jnp.dot(gbuf[crows, :], wout_t[:, cols], preferred_element_type=F32)
            dz[crows, cols] = (ga * slope[m % 2, krows, cols]).astype(BF16)
        for j in range(WIDTH // WIDE):
            cols = pl.ds(j * WIDE, WIDE)
            back = jnp.dot(dz[crows, :], win_t[:, cols], preferred_element_type=F32)
            nbuf[crows, cols] = (gbuf[crows, cols].astype(F32) + back).astype(BF16)

    def grad_tiles(m, tiles, and_peer):
        rows = micro_rows(m)
        for kind, left, right in ((0, xbuf, dz), (1, act, gbuf)):

            @pl.when(core == kind)
            def _(left=left, right=right):
                for i in tiles:
                    cols = pl.ds(i * TILE, TILE)
                    total = acc[cols, :] + dot_tn(left[rows, cols], right[rows, :])
                    if and_peer:
                        total = total + dot_tn(peer_l[rows, cols], peer_r[rows, :])
                    acc[cols, :] = total

    def hear_peer(m):
        left_copy(m, act).wait_recv()
        right_copy(m, dz, m * TOK, TOK).wait_recv()

    load_win.wait()
    for j in range(WIDTH // TILE):
        cols = pl.ds(j * TILE, TILE)
        win_t[:, cols] = win[cols, :].T

    @pl.when(jnp.logical_not(first))
    def _():
        forward(0)

    load_wout.wait()
    for j in range(WIDTH // TILE):
        cols = pl.ds(j * TILE, TILE)
        wout_t[:, cols] = wout[cols, :].T

    pl.semaphore_wait(barrier, SECTIONS - 1 + 2 * (SIDE - 1) + 1)
    tell_row()

    @pl.when((sec == 1) | last)
    def _():
        pool_copy(sec).start()

    @pl.when(sec == 2)
    def _():
        hop_copy(0).start()
        hop_copy(1).start()

    @pl.when(last)
    def _():
        load_top(0).wait()
        for i in range(SPLIT):
            backward(0, i * PIECE, PIECE)
            relay_copy(i).start()
        for k in range(1, CHUNKS):
            backward(0, k * CHUNK, CHUNK)
            for c in range(k * SPLIT, (k + 1) * SPLIT):
                relay_copy(c).start()
        for m in range(1, MICRO):
            load_top(m).start()

    for m in range(1, MICRO):
        load_x(m).start()

    def clear(i, carry):
        rows = pl.ds(pl.multiple_of(i * 64, 64), 64)
        acc[rows, :] = jnp.zeros((64, WIDTH), F32)
        return carry

    @pl.when(first)
    def _():
        lax.fori_loop(0, WIDTH // 64, clear, 0)
        row = lax.broadcasted_iota(jnp.int32, (TOK, TOK), 0)
        col = lax.broadcasted_iota(jnp.int32, (TOK, TOK), 1)
        feat = ids.shape[1]
        lane = lax.broadcasted_iota(jnp.int32, (ids.shape[2], TOK), 1)
        lead = lax.broadcasted_iota(jnp.int32, (ids.shape[2], TOK), 0)
        widen = jnp.where(lane >> 3 == lead, 1.0, 0.0).astype(BF16)
        for m in range(MICRO):
            owner = (ids[m] >> 10).astype(F32).astype(BF16)
            wide = jnp.dot(owner, widen, preferred_element_type=F32)
            inner = lax.broadcasted_iota(jnp.int32, (feat, TOK), 1) & 7
            outer = lax.broadcasted_iota(jnp.int32, (feat, TOK), 0)
            across = jnp.sum(jnp.where(inner == outer, wide, 0.0), axis=0, keepdims=True)
            down = jnp.sum(jnp.where(row == col, across, 0.0), axis=1, keepdims=True)
            earlier = jnp.where((down == across) & (row < col), 1.0, 0.0)
            rank[m] = 2.0 * across + jnp.sum(earlier, axis=0, keepdims=True)
        load_pool.wait()
        for s in (1, SECTIONS - 1):
            pool_copy(s).wait_recv()
        for h in range(2):
            pass_copy(h).wait_recv()
        forward(0)

    @pl.when(jnp.logical_not(first))
    def _():
        lax.fori_loop(0, WIDTH // 64, clear, 0)

    all_ids[sh] = ids[...]
    send_left(0)

    def step(m, start, size, hook=None):
        pieces = [(m * TOK + start) // PIECE + i for i in range(size // PIECE)]

        @pl.when(jnp.logical_not(last))
        def _():
            for c in pieces:
                relay_copy(c).wait_recv()

        if hook is not None:
            hook()
        backward(m, start, size)

        @pl.when(jnp.logical_not(first))
        def _():
            for c in pieces:
                relay_copy(c).start()

    inner = jnp.logical_not(first | last)

    def chunks(m, slots, hook=None):
        for k in range(CHUNKS):
            fine = hook is not None and k == CHUNKS - 1
            for i in range(SPLIT):

                def piece(k=k, i=i):
                    at_last = hook if fine and i == SPLIT - 1 else None
                    step(m, k * CHUNK + i * PIECE, PIECE, at_last)

                if fine:
                    piece()
                else:
                    pl.when(inner)(piece)
                if not fine and i == SPLIT - 1:

                    @pl.when(first | (last & (m > 0)))
                    def _(k=k):
                        step(m, k * CHUNK, CHUNK)

                slots[k * SPLIT + i]()
                tell_ids(m, k * SPLIT + i)

    def route(m):
        rows = micro_rows(m)

        @pl.when(first)
        def _():
            target = lax.broadcasted_iota(jnp.int32, (TOK, TOK), 0).astype(F32)
            pick = jnp.where(target == rank[m], 1.0, 0.0).astype(BF16)
            ordered = jnp.dot(pick, nbuf[rows, :], preferred_element_type=F32).astype(BF16)
            sorted_rows[m] = ordered
            route_copy(m, 1).start()
            route_copy(m, SECTIONS - 1).start()
            if isinstance(m, int):
                route_copy(m, 2).start()
            routed[pl.ds(pl.multiple_of(m * PER_PLANE, PER_PLANE), PER_PLANE), :] = ordered[
                :PER_PLANE, :
            ]

    def micro_step(m, carry):
        @pl.when(last & (m > 0))
        def _():
            load_top(m).wait()

        def forward_slot(j):
            def work():
                if j == 0:

                    @pl.when(last & (m == 1))
                    def _():
                        pass_pool(0)

                    forward_open(m + 1)
                forward_tile(m + 1, j)
                if j == WIDTH // TILE - 1:
                    send_left(m + 1)

            return work

        def grad_slot(i):
            def work():
                if i == 2:

                    @pl.when(last & (m == 1))
                    def _():
                        pass_pool(1)

                @pl.when(m > 0)
                def _():
                    if i == 0:
                        hear_peer(m - 1)
                    grad_tiles(m - 1, (i,), True)

            return work

        tiles = range(WIDTH // TILE)
        chunks(m, [forward_slot(j) for j in tiles] + [grad_slot(i) for i in tiles])
        send_right(m, m * TOK, TOK)
        route(m)
        return carry

    lax.fori_loop(0, MICRO - 1, micro_step, 0)

    final = MICRO - 1
    tail = TOK - CHUNK

    def unit_copy(source, target, send, recv, to, came):
        return pltpu.make_async_remote_copy(
            src_ref=source.at[to],
            dst_ref=target.at[came],
            send_sem=send,
            recv_sem=recv,
            device_id=(sec, to),
            device_id_type=MESH,
        )

    def hand_soon(k, carry):
        to = (sh + k) % SHARDS
        unit_copy(soon, got_soon, soon_send, soon_recv, to, sh).start()
        return carry

    def hand_late(k, carry):
        to = (sh + k) % SHARDS
        unit_copy(late, got_late, late_send, late_recv, to, sh).start()
        return carry

    def wait_all(ref, semaphore):
        others = ref.at[pl.ds(0, SHARDS - 1)]
        pltpu.make_async_copy(others, others, semaphore).wait()

    def soon_units():
        row = lax.broadcasted_iota(jnp.int32, (SOON, SOON), 0)
        col = lax.broadcasted_iota(jnp.int32, (SOON, SOON), 1)
        target = ((col >> 1) & (SHARDS - 1)) * (2 * (MICRO - 1)) + (col >> 6) * 2 + (col & 1)
        regroup = jnp.where(row == target, 1.0, 0.0).astype(BF16)
        by_owner = jnp.dot(regroup, routed[pl.ds(0, SOON), :], preferred_element_type=F32)
        for b in range(8):
            flat[pl.ds(b, SOON, stride=8), :] = by_owner[:, b * 128 : (b + 1) * 128]
        soon[...] = flat[...].reshape(soon.shape).astype(BF16)
        got_soon[sh] = soon[sh]

    def late_units():
        by_owner = routed[pl.ds(SOON, PER_PLANE), :].astype(F32)
        for b in range(8):
            flat[pl.ds(b, PER_PLANE, stride=8), :] = by_owner[:, b * 128 : (b + 1) * 128]
        late[...] = flat[pl.ds(0, PER_PLANE * 8), :].reshape(late.shape).astype(BF16)
        got_late[sh] = late[sh]

    def to_rows(got, start, count):
        flat[pl.ds(0, count * 8), :] = got[...].astype(F32).reshape(count * 8, 128)
        for b in range(8):
            rows_buf[pl.ds(start, count), pl.ds(b * 128, 128)] = flat[
                pl.ds(b, count, stride=8), :
            ].astype(BF16)

    @pl.when(last)
    def _():
        load_top(final).wait()

    def final_slot(n):
        def work():
            if n == 2:
                hear_peer(final - 1)
            if 2 <= n < 2 + WIDTH // TILE:
                grad_tiles(final - 1, (n - 2,), True)
            if n == 5:
                send_right(final, final * TOK, tail)

            @pl.when(first)
            def _():
                if n == 0:
                    soon_units()
                if n == 1:
                    for before in range(final):
                        route_copy(before, 2).start()
                if n == 2:
                    lax.fori_loop(1, SHARDS // 2, hand_soon, 0)
                if n == 4:
                    lax.fori_loop(SHARDS // 2, SHARDS, hand_soon, 0)

        return work

    def hand_g():
        @pl.when(core == 0)
        def _():
            right_copy(final + 1, gbuf, final * TOK + tail, TOK - tail).start()

    chunks(final, [final_slot(n) for n in range(CHUNKS * SPLIT)], hand_g)

    @pl.when(core == 1)
    def _():
        right_copy(final + 1, dz, final * TOK + tail, TOK - tail).start()

    grad_tiles(final, (0, 1, 2, 3), False)

    def block_rows(y, x):
        return pl.ds(pl.multiple_of((y * SIDE + x) * BLOCK, BLOCK), BLOCK)

    left_half = pl.ds(0, HALF)
    right_half = pl.ds(HALF, HALF)

    def x_copy(d, y):
        to = (px + d) % SIDE
        return pltpu.make_async_remote_copy(
            src_ref=send_x.at[y, pl.ds(pl.multiple_of(to * BLOCK, BLOCK), BLOCK)],
            dst_ref=recv_x.at[d - 1, y],
            send_sem=x_send.at[d - 1, y],
            recv_sem=x_recv.at[d - 1, y],
            device_id=at(py, to, core),
            device_id_type=MESH,
        )

    def y_copy(d, x):
        rows = pl.ds(pl.multiple_of(x * BLOCK, BLOCK), BLOCK)
        return pltpu.make_async_remote_copy(
            src_ref=send_y.at[d - 1, rows],
            dst_ref=recv_y.at[d - 1, rows],
            send_sem=y_send.at[d - 1, x],
            recv_sem=y_recv.at[d - 1, x],
            device_id=at((py + d) % SIDE, px, core),
            device_id_type=MESH,
        )

    def c_copy(h, e, c, kind):
        there = (py + e) % SIDE if h == 0 else (px + e) % SIDE
        return pltpu.make_async_remote_copy(
            src_ref=send_c.at[h, e, c],
            dst_ref=out_parts.at[kind, h, e],
            send_sem=c_send.at[h, e, c],
            recv_sem=c_recv.at[kind, h, e],
            device_id=at(there, px, c) if h == 0 else at(py, there, c),
            device_id_type=MESH,
        )

    def own_part(h):
        return pltpu.make_async_copy(
            send_c.at[h, 0, core], out_parts.at[core, h, 0], out_sem.at[2 + h]
        )

    order = (2, 1, 3, 0)
    frows = micro_rows(final)
    left_copy(final, act).wait_recv()
    right_copy(final, dz, final * TOK, tail).wait_recv()
    right_copy(final + 1, dz, final * TOK + tail, TOK - tail).wait_recv()
    for d in order:
        y = (py + d) % SIDE
        cols = pl.ds(pl.multiple_of(y * TILE, TILE), TILE)
        total = acc[cols, :] + dot_tn(peer_l[frows, cols], peer_r[frows, :])
        acc[cols, :] = total
        send_x[y] = total[:, :HALF].astype(BF16)
        for dx in (2, 1, 3):
            x_copy(dx, y).start()
        if d != 0:
            send_y[d - 1] = total[:, HALF:].astype(BF16)
    for e in order:
        for d in (2, 1, 3):
            y_copy(d, (px + e) % SIDE).start()
    route(final)

    @pl.when(jnp.logical_not(first))
    def _():
        for m in range(MICRO - 1):
            route_copy(m, 1).wait_recv()
        soon_units()
        lax.fori_loop(1, SHARDS, hand_soon, 0)
        route_copy(final, 1).wait_recv()

    late_units()
    lax.fori_loop(1, SHARDS, hand_late, 0)

    wait_all(all_ids, ids_recv)
    own = sec * SHARDS + sh
    feature = own // (SECTIONS * SHARDS // ids.shape[1])
    heard = all_ids[:, :, feature, :].reshape(SHARDS * MICRO, ids.shape[2])
    place = lax.broadcasted_iota(jnp.int32, heard.shape, 1) * ROWS_OWN + (heard & (ROWS_OWN - 1))
    ours = heard >> 10 == own
    low = jnp.min(jnp.where(ours, place, 1 << 20), axis=1, keepdims=True) & (ROWS_OWN - 1)
    high = jnp.max(jnp.where(ours, place, -1), axis=1, keepdims=True) & (ROWS_OWN - 1)
    at_lane = lax.broadcasted_iota(jnp.int32, (SHARDS * MICRO, 128), 1)
    parts = jnp.where(
        at_lane == 0,
        low >> 5,
        jnp.where(at_lane == 1, low & 31, jnp.where(at_lane == 2, high >> 5, high & 31)),
    )
    half = lax.broadcasted_iota(jnp.int32, (TOK, SHARDS * MICRO), 0) >> 1
    pair = lax.broadcasted_iota(jnp.int32, (TOK, SHARDS * MICRO), 1)
    came, micro = pair >> 2, pair & (MICRO - 1)
    place_of = jnp.where(
        micro < final, came * (MICRO - 1) + micro, SHARDS * (MICRO - 1) + came
    )
    twice = jnp.where(half == place_of, 1.0, 0.0).astype(BF16)
    both = jnp.dot(twice, parts.astype(F32).astype(BF16), preferred_element_type=F32)
    odd = lax.broadcasted_iota(jnp.int32, (TOK, 1), 0) & 1
    row_of = jnp.where(
        odd == 0, both[:, 0:1] * 32.0 + both[:, 1:2], both[:, 2:3] * 32.0 + both[:, 3:4]
    )
    named[...] = jnp.broadcast_to(row_of.astype(jnp.int32), (TOK, 128))
    put_named = pltpu.make_async_copy(named, out_named, out_sem.at[0])
    put_named.start()

    put_rows = pltpu.make_async_copy(rows_buf, out_rows, out_sem.at[1])

    def collect_rows():
        wait_all(got_soon, soon_recv)
        to_rows(got_soon, 0, SOON)
        wait_all(got_late, late_recv)
        to_rows(got_late, SOON, PER_PLANE)
        put_rows.start()

    pl.when(first)(collect_rows)

    for e in order:
        y = (py + e) % SIDE
        x = (px + e) % SIDE
        for d in range(1, SIDE):
            x_copy(d, y).wait_recv()
            y_copy(d, x).wait_recv()
        total = acc[block_rows(y, px), left_half]
        other = acc[block_rows(py, x), right_half]
        for d in range(1, SIDE):
            total = total + recv_x[d - 1, y].astype(F32)
            xrows = pl.ds(pl.multiple_of(x * BLOCK, BLOCK), BLOCK)
            other = other + recv_y[d - 1, xrows, :].astype(F32)
        for h, part in ((0, total), (1, other)):
            for c in range(2):
                send_c[h, e, c] = part[c * SHARE : (c + 1) * SHARE, :].astype(BF16)
                if e == 0:

                    @pl.when(core == c)
                    def _(h=h, c=c):
                        own_part(h).start()

                    @pl.when(core != c)
                    def _(h=h, c=c):
                        c_copy(h, 0, c, core).start()
                else:
                    c_copy(h, e, c, core).start()

    pl.when(jnp.logical_not(first))(collect_rows)

    wait_all(all_ids, ids_send)
    wait_all(soon, soon_send)

    @pl.when((sec == 1) | last)
    def _():
        pool_copy(sec).wait_send()

    @pl.when(sec == 2)
    def _():
        hop_copy(0).wait_send()
        hop_copy(1).wait_send()

    @pl.when(last)
    def _():
        pass_copy(0).wait_send()
        pass_copy(1).wait_send()

    @pl.when(jnp.logical_not(first))
    def _():
        def left(c, carry):
            relay_copy(c).wait_send()
            return carry

        lax.fori_loop(0, PIECES, left, 0)

    @pl.when(first)
    def _():
        for m in range(final):
            for p in range(1, SECTIONS):
                route_copy(m, p).wait_send()

    for m in range(MICRO):
        left_copy(m, act).wait_send()
    for m in range(final):
        right_copy(m, dz, m * TOK, TOK).wait_send()
    right_copy(final, dz, final * TOK, tail).wait_send()
    right_copy(final + 1, dz, final * TOK + tail, TOK - tail).wait_send()

    wait_all(late, late_send)

    @pl.when(first)
    def _():
        for p in range(1, SECTIONS):
            route_copy(final, p).wait_send()

    for d in range(1, SIDE):
        for y in range(SIDE):
            x_copy(d, y).wait_send()
            y_copy(d, y).wait_send()

    for kind in range(2):
        for h in range(2):

            @pl.when(core != kind)
            def _(h=h, kind=kind):
                c_copy(h, 0, 1 - kind, kind).wait_recv()

            for e in range(1, SIDE):
                c_copy(h, e, 0, kind).wait_recv()

    for h in range(2):
        for d in range(1, SIDE):
            for c in range(2):
                c_copy(h, d, c, core).wait_send()
        c_copy(h, 0, 1 - core, core).wait_send()
    for put in (put_named, put_rows, own_part(0), own_part(1)):
        put.wait()


def relay(holder, saved, pooled, grad_top, w_in, w_out, ids):
    vmem = pl.BlockSpec(memory_space=pltpu.VMEM)
    anywhere = pl.BlockSpec(memory_space=pl.ANY)
    dma = pltpu.SemaphoreType.DMA
    tokens = MICRO * TOK
    return pl.pallas_call(
        kernel,
        out_shape=(
            jax.ShapeDtypeStruct((2, 2, SIDE, SHARE, HALF), BF16),
            jax.ShapeDtypeStruct((TOK, WIDTH), BF16),
            jax.ShapeDtypeStruct((TOK, 128), jnp.int32),
        ),
        in_specs=[pl.BlockSpec(memory_space=pltpu.SMEM)] + [anywhere] * 5 + [vmem],
        out_specs=(anywhere, anywhere, anywhere),
        scratch_shapes=[
            pltpu.VMEM((WIDTH, WIDTH), BF16),
            pltpu.VMEM((WIDTH, WIDTH), BF16),
            pltpu.VMEM((WIDTH, WIDTH), BF16),
            pltpu.VMEM((WIDTH, WIDTH), BF16),
            pltpu.VMEM((tokens, WIDTH), BF16),
            pltpu.VMEM((tokens, WIDTH), BF16),
            pltpu.VMEM((tokens, WIDTH), BF16),
            pltpu.VMEM((SECTIONS, TOK, WIDTH), BF16),
            pltpu.VMEM((tokens, WIDTH), BF16),
            pltpu.VMEM((2, TOK, WIDTH), F32),
            pltpu.VMEM((tokens, WIDTH), BF16),
            pltpu.VMEM((WIDTH, WIDTH), F32),
            pltpu.VMEM((MICRO, 1, TOK), F32),
            pltpu.VMEM((SHARDS,) + ids.shape, jnp.int32),
            pltpu.VMEM((MICRO, TOK, WIDTH), BF16),
            pltpu.VMEM((TOK, WIDTH), BF16),
            pltpu.VMEM((SHARDS, 16 * (MICRO - 1), 128), BF16),
            pltpu.VMEM((SHARDS, 16 * (MICRO - 1), 128), BF16),
            pltpu.VMEM((SHARDS, 16, 128), BF16),
            pltpu.VMEM((SHARDS, 16, 128), BF16),
            pltpu.VMEM((SOON * 8, 128), F32),
            pltpu.VMEM((TOK, 128), jnp.int32),
            pltpu.VMEM((TOK, WIDTH), BF16),
            pltpu.VMEM((TOK, WIDTH), BF16),
            pltpu.VMEM((tokens, WIDTH), BF16),
            pltpu.VMEM((tokens, WIDTH), BF16),
            pltpu.VMEM((SIDE, SIDE * BLOCK, HALF), BF16),
            pltpu.VMEM((SIDE - 1, SIDE, BLOCK, HALF), BF16),
            pltpu.VMEM((SIDE - 1, SIDE * BLOCK, HALF), BF16),
            pltpu.VMEM((SIDE - 1, SIDE * BLOCK, HALF), BF16),
            pltpu.VMEM((2, SIDE, 2, SHARE, HALF), BF16),
            dma((3 + MICRO,)),
            dma((MICRO,)),
            dma,
            dma((SECTIONS,)),
            dma((PIECES,)),
            dma((PIECES,)),
            dma((MICRO, SECTIONS)),
            dma((MICRO,)),
            dma,
            dma,
            dma,
            dma,
            pltpu.SemaphoreType.REGULAR((2,)),
            dma((2,)),
            dma((2,)),
            dma((2,)),
            dma((2,)),
            dma((4,)),
            dma,
            dma,
            dma((MICRO,)),
            dma((MICRO,)),
            dma((MICRO + 1,)),
            dma((MICRO + 1,)),
            dma((SIDE - 1, SIDE)),
            dma((SIDE - 1, SIDE)),
            dma((SIDE - 1, SIDE)),
            dma((SIDE - 1, SIDE)),
            dma((2, SIDE, 2)),
            dma((2, 2, SIDE)),
        ],
        compiler_params=pltpu.CompilerParams(
            collective_id=0, has_side_effects=True, vmem_limit_bytes=56 * 1024 * 1024
        ),
        cost_estimate=pl.CostEstimate(
            flops=10 * tokens * WIDTH * WIDTH, bytes_accessed=9 * 2**20, transcendentals=tokens * WIDTH
        ),
        name="relay",
    )(holder, saved, pooled, grad_top, w_in, w_out, ids)


def table_kernel(named, rows, parts, table, out_in, out_out):
    block = pl.program_id(0)
    lane = lax.broadcasted_iota(jnp.int32, (TOK, WIDE), 1) + block * WIDE
    hit = jnp.where(lane == named[:, 0:1], 1.0, 0.0).astype(BF16)
    table[...] = dot_tn(hit, rows[...])

    @pl.when(block == 0)
    def _():
        for kind, out in ((0, out_in), (1, out_out)):
            for h in range(2):
                total = parts[kind, h, 0].astype(F32)
                for e in range(1, SIDE):
                    total = total + parts[kind, h, e].astype(F32)
                out[:, h * HALF : (h + 1) * HALF] = total


def owner_sums(named, rows, parts):
    def whole(shape):
        return pl.BlockSpec(shape, lambda b: (0,) * len(shape))

    share = jax.ShapeDtypeStruct((SHARE, WIDTH), F32)
    return pl.pallas_call(
        table_kernel,
        grid=(ROWS_OWN // WIDE,),
        out_shape=(jax.ShapeDtypeStruct((ROWS_OWN, WIDTH), F32), share, share),
        in_specs=[whole(named.shape), whole(rows.shape), whole(parts.shape)],
        out_specs=(
            pl.BlockSpec((WIDE, WIDTH), lambda b: (b, 0)),
            whole(share.shape),
            whole(share.shape),
        ),
        compiler_params=pltpu.CompilerParams(vmem_limit_bytes=32 * 1024 * 1024),
        cost_estimate=pl.CostEstimate(
            flops=2 * ROWS_OWN * TOK * WIDTH, bytes_accessed=5 * 2**20, transcendentals=0
        ),
        name="owner_sums",
    )(named, rows, parts)


def local(saved, pooled, grad_top, w_in, w_out, feature_ids, holder_order):
    tokens = MICRO * TOK
    parts, rows, named = relay(
        holder_order,
        saved.reshape(tokens, WIDTH),
        pooled.reshape(TOK, WIDTH),
        grad_top.reshape(tokens, WIDTH),
        w_in[0],
        w_out[0],
        jnp.transpose(feature_ids, (0, 2, 1)),
    )
    table_grad, grad_in, grad_out = owner_sums(named, rows, parts)
    return (grad_in[None], grad_out[None], table_grad)


def solution(mesh):
    return jax.shard_map(
        local,
        mesh=mesh,
        in_specs=(
            P("section", None, "shard", None, None),
            P("section", "shard", None, None),
            P(None, "shard", None, None),
            P("section", None, None),
            P("section", None, None),
            P(None, "shard", None),
            P(),
        ),
        out_specs=(
            P("section", "shard", None),
            P("section", "shard", None),
            P(("section", "shard"), None),
        ),
        check_vma=False,
    )
```

```python
import jax
import jax.numpy as jnp
from jax import lax
from jax.experimental import pallas as pl
from jax.experimental.pallas import tpu as pltpu
from jax.sharding import PartitionSpec as P

ROWS_OWN = 1024
MESH = pl.DeviceIdType.MESH
F32 = jnp.float32
BF16 = jnp.bfloat16

SECTIONS = 4
SHARDS = 32
SIDE = 4
MICRO = 4
TOK = 256
CHUNK = 64
PIECE = 32
WIDTH = 1024
SHARE = WIDTH // SHARDS
PER_PLANE = TOK // SECTIONS
TILE = 256
WIDE = 512
CHUNKS = TOK // CHUNK
SPLIT = CHUNK // PIECE
PIECES = MICRO * TOK // PIECE
SOON = (MICRO - 1) * PER_PLANE
HALF = WIDTH // 2
BLOCK = 2 * SHARE


def dot_tn(a, b):
    return lax.dot_general(a, b, (((0,), (0,)), ((), ())), preferred_element_type=F32)


def kernel(
    holder,
    saved,
    pooled,
    grad_top,
    w_in,
    w_out,
    ids,
    out_parts,
    out_rows,
    out_named,
    win,
    wout,
    win_t,
    wout_t,
    xbuf,
    gbuf,
    nbuf,
    pbuf,
    act,
    slope,
    dz,
    acc,
    rank,
    all_ids,
    sorted_rows,
    routed,
    soon,
    got_soon,
    late,
    got_late,
    flat,
    named,
    rows_buf,
    transit,
    peer_l,
    peer_r,
    send_x,
    recv_x,
    send_y,
    recv_y,
    send_c,
    load_sem,
    top_sem,
    pool_send,
    pool_recv,
    relay_send,
    relay_recv,
    route_send,
    route_recv,
    soon_send,
    soon_recv,
    late_send,
    late_recv,
    ready,
    hop_send,
    hop_recv,
    pass_send,
    pass_recv,
    out_sem,
    ids_send,
    ids_recv,
    l_send,
    l_recv,
    r_send,
    r_recv,
    x_send,
    x_recv,
    y_send,
    y_recv,
    c_send,
    c_recv,
):
    sec = lax.axis_index("section")
    sh = lax.axis_index("shard")
    core = sh % 2
    px = (sh // 2) % SIDE
    py = sh // (2 * SIDE)
    first = sec == 0
    last = sec == SECTIONS - 1

    def at(y, x, c):
        return (sec, (y * SIDE + x) * 2 + c)

    def micro_rows(m):
        return pl.ds(pl.multiple_of(m * TOK, TOK), TOK)

    def token_rows(start, size):
        return pl.ds(pl.multiple_of(start, size), size)

    def load_x(m):
        rows = micro_rows(m)
        return pltpu.make_async_copy(saved.at[rows], xbuf.at[rows], load_sem.at[2 + m])

    def load_top(m):
        rows = micro_rows(m)
        return pltpu.make_async_copy(grad_top.at[rows], gbuf.at[rows], top_sem.at[m])

    load_win = pltpu.make_async_copy(w_in, win, load_sem.at[0])
    load_wout = pltpu.make_async_copy(w_out, wout, load_sem.at[1])
    load_pool = pltpu.make_async_copy(pooled, pbuf.at[0], load_sem.at[2 + MICRO])

    load_win.start()
    load_x(0).start()
    load_wout.start()

    @pl.when(last)
    def _():
        load_top(0).start()

    @pl.when(first)
    def _():
        load_pool.start()

    barrier = pltpu.get_barrier_semaphore()

    def greet(y, x, c):
        pl.semaphore_signal(barrier, inc=1, device_id=at(y, x, c), device_id_type=MESH)

    for k in range(1, SECTIONS):
        pl.semaphore_signal(
            barrier, inc=1, device_id=((sec + k) % SECTIONS, sh), device_id_type=MESH
        )
    for k in range(1, SIDE):
        greet(py, (px + k) % SIDE, core)
        greet((py + k) % SIDE, px, core)
    greet(py, px, 1 - core)

    def tell_row():
        for k in range(1, SIDE):
            to = at(py, (px + k) % SIDE, core)
            pl.semaphore_signal(ready.at[0], inc=1, device_id=to, device_id_type=MESH)

    def tell_plane():
        pl.semaphore_wait(ready.at[0], SIDE - 1)
        for k in range(1, SIDE):
            to = at((py + k) % SIDE, px, core)
            pl.semaphore_signal(ready.at[1], inc=1, device_id=to, device_id_type=MESH)

    def tell_ids(m, n):
        start, total = SPLIT * CHUNKS // 2, SPLIT * CHUNKS

        def tell(k):
            ids_copy((sh + k) % SHARDS, sh).start()

        if n == 0:
            pl.when(m == 0)(tell_plane)
        if n == start:

            @pl.when(m == 0)
            def _():
                pl.semaphore_wait(ready.at[1], SIDE - 1)

        if n >= start:
            tell(m * total + n)
        else:

            @pl.when(m > 0)
            def _():
                tell(m * total + n)

        if 0 < n < start:

            @pl.when(m == 1)
            def _():
                tell(n)

    def pool_copy(s):
        return pltpu.make_async_remote_copy(
            src_ref=pooled,
            dst_ref=pbuf.at[s],
            send_sem=pool_send,
            recv_sem=pool_recv.at[s],
            device_id=(0, sh),
            device_id_type=MESH,
        )

    def pool_rows(h):
        return pl.ds(h * (TOK // 2), TOK // 2)

    def hop_copy(h):
        return pltpu.make_async_remote_copy(
            src_ref=pooled.at[pool_rows(h)],
            dst_ref=transit.at[pool_rows(h)],
            send_sem=hop_send.at[h],
            recv_sem=hop_recv.at[h],
            device_id=(SECTIONS - 1, sh),
            device_id_type=MESH,
        )

    def pass_copy(h):
        return pltpu.make_async_remote_copy(
            src_ref=transit.at[pool_rows(h)],
            dst_ref=pbuf.at[2, pool_rows(h)],
            send_sem=pass_send.at[h],
            recv_sem=pass_recv.at[h],
            device_id=(0, sh),
            device_id_type=MESH,
        )

    def pass_pool(h):
        hop_copy(h).wait_recv()
        pass_copy(h).start()

    def relay_copy(c):
        rows = token_rows(c * PIECE, PIECE)
        return pltpu.make_async_remote_copy(
            src_ref=nbuf.at[rows],
            dst_ref=gbuf.at[rows],
            send_sem=relay_send.at[c],
            recv_sem=relay_recv.at[c],
            device_id=(jnp.maximum(sec - 1, 0), sh),
            device_id_type=MESH,
        )

    def route_copy(m, p):
        return pltpu.make_async_remote_copy(
            src_ref=sorted_rows.at[m, pl.ds(p * PER_PLANE, PER_PLANE)],
            dst_ref=routed.at[pl.ds(pl.multiple_of(m * PER_PLANE, PER_PLANE), PER_PLANE)],
            send_sem=route_send.at[m, p],
            recv_sem=route_recv.at[m],
            device_id=(p, sh),
            device_id_type=MESH,
        )

    def ids_copy(to, came):
        return pltpu.make_async_remote_copy(
            src_ref=ids,
            dst_ref=all_ids.at[came],
            send_sem=ids_send,
            recv_sem=ids_recv,
            device_id=(sec, to),
            device_id_type=MESH,
        )

    def left_copy(m, source):
        rows = micro_rows(m)
        return pltpu.make_async_remote_copy(
            src_ref=source.at[rows],
            dst_ref=peer_l.at[rows],
            send_sem=l_send.at[m],
            recv_sem=l_recv.at[m],
            device_id=at(py, px, 1 - core),
            device_id_type=MESH,
        )

    def right_copy(n, source, start, size):
        rows = pl.ds(pl.multiple_of(start, 64), size)
        return pltpu.make_async_remote_copy(
            src_ref=source.at[rows],
            dst_ref=peer_r.at[rows],
            send_sem=r_send.at[n],
            recv_sem=r_recv.at[n],
            device_id=at(py, px, 1 - core),
            device_id_type=MESH,
        )

    def send_left(m):
        @pl.when(core == 0)
        def _():
            left_copy(m, act).start()

        @pl.when(core == 1)
        def _():
            left_copy(m, xbuf).start()

    def send_right(n, start, size):
        @pl.when(core == 0)
        def _():
            right_copy(n, gbuf, start, size).start()

        @pl.when(core == 1)
        def _():
            right_copy(n, dz, start, size).start()

    def forward_open(m):
        rows = micro_rows(m)
        load_x(m).wait()

        @pl.when(first)
        def _():
            slot = 0
            for j in range(1, MICRO):
                slot = jnp.where(holder[j] == m, j, slot)
            extra = pbuf[slot]
            xbuf[rows, :] = (xbuf[rows, :].astype(F32) + extra.astype(F32)).astype(BF16)

    def forward_tile(m, j):
        rows = micro_rows(m)
        cols = pl.ds(j * TILE, TILE)
        z = jnp.dot(xbuf[rows, :], win[:, cols], preferred_element_type=F32)
        sig = jax.nn.sigmoid(z)
        act[rows, cols] = (z * sig).astype(BF16)
        slope[m % 2, :, cols] = sig * (1.0 + z * (1.0 - sig))

    def forward(m):
        forward_open(m)
        for j in range(WIDTH // TILE):
            forward_tile(m, j)

    def backward(m, start, size):
        crows = token_rows(m * TOK + start, size)
        krows = pl.ds(start, size)
        for j in range(WIDTH // WIDE):
            cols = pl.ds(j * WIDE, WIDE)
            ga = jnp.dot(gbuf[crows, :], wout_t[:, cols], preferred_element_type=F32)
            dz[crows, cols] = (ga * slope[m % 2, krows, cols]).astype(BF16)
        for j in range(WIDTH // WIDE):
            cols = pl.ds(j * WIDE, WIDE)
            back = jnp.dot(dz[crows, :], win_t[:, cols], preferred_element_type=F32)
            nbuf[crows, cols] = (gbuf[crows, cols].astype(F32) + back).astype(BF16)

    def grad_tiles(m, tiles, and_peer):
        rows = micro_rows(m)
        for kind, left, right in ((0, xbuf, dz), (1, act, gbuf)):

            @pl.when(core == kind)
            def _(left=left, right=right):
                for i in tiles:
                    cols = pl.ds(i * TILE, TILE)
                    total = acc[cols, :] + dot_tn(left[rows, cols], right[rows, :])
                    if and_peer:
                        total = total + dot_tn(peer_l[rows, cols], peer_r[rows, :])
                    acc[cols, :] = total

    def hear_peer(m):
        left_copy(m, act).wait_recv()
        right_copy(m, dz, m * TOK, TOK).wait_recv()

    load_win.wait()
    for j in range(WIDTH // TILE):
        cols = pl.ds(j * TILE, TILE)
        win_t[:, cols] = win[cols, :].T

    @pl.when(jnp.logical_not(first))
    def _():
        forward(0)

    load_wout.wait()
    for j in range(WIDTH // TILE):
        cols = pl.ds(j * TILE, TILE)
        wout_t[:, cols] = wout[cols, :].T

    pl.semaphore_wait(barrier, SECTIONS - 1 + 2 * (SIDE - 1) + 1)
    tell_row()

    @pl.when((sec == 1) | last)
    def _():
        pool_copy(sec).start()

    @pl.when(sec == 2)
    def _():
        hop_copy(0).start()
        hop_copy(1).start()

    @pl.when(last)
    def _():
        load_top(0).wait()
        for i in range(SPLIT):
            backward(0, i * PIECE, PIECE)
            relay_copy(i).start()
        for k in range(1, CHUNKS):
            backward(0, k * CHUNK, CHUNK)
            for c in range(k * SPLIT, (k + 1) * SPLIT):
                relay_copy(c).start()
        for m in range(1, MICRO):
            load_top(m).start()

    for m in range(1, MICRO):
        load_x(m).start()

    def clear(i, carry):
        rows = pl.ds(pl.multiple_of(i * 64, 64), 64)
        acc[rows, :] = jnp.zeros((64, WIDTH), F32)
        return carry

    @pl.when(first)
    def _():
        lax.fori_loop(0, WIDTH // 64, clear, 0)
        row = lax.broadcasted_iota(jnp.int32, (TOK, TOK), 0)
        col = lax.broadcasted_iota(jnp.int32, (TOK, TOK), 1)
        feat = ids.shape[1]
        lane = lax.broadcasted_iota(jnp.int32, (ids.shape[2], TOK), 1)
        lead = lax.broadcasted_iota(jnp.int32, (ids.shape[2], TOK), 0)
        widen = jnp.where(lane >> 3 == lead, 1.0, 0.0).astype(BF16)
        for m in range(MICRO):
            owner = (ids[m] >> 10).astype(F32).astype(BF16)
            wide = jnp.dot(owner, widen, preferred_element_type=F32)
            inner = lax.broadcasted_iota(jnp.int32, (feat, TOK), 1) & 7
            outer = lax.broadcasted_iota(jnp.int32, (feat, TOK), 0)
            across = jnp.sum(jnp.where(inner == outer, wide, 0.0), axis=0, keepdims=True)
            down = jnp.sum(jnp.where(row == col, across, 0.0), axis=1, keepdims=True)
            earlier = jnp.where((down == across) & (row < col), 1.0, 0.0)
            rank[m] = 2.0 * across + jnp.sum(earlier, axis=0, keepdims=True)
        load_pool.wait()
        for s in (1, SECTIONS - 1):
            pool_copy(s).wait_recv()
        for h in range(2):
            pass_copy(h).wait_recv()
        forward(0)

    @pl.when(jnp.logical_not(first))
    def _():
        lax.fori_loop(0, WIDTH // 64, clear, 0)

    all_ids[sh] = ids[...]
    send_left(0)

    def step(m, start, size, hook=None):
        pieces = [(m * TOK + start) // PIECE + i for i in range(size // PIECE)]

        @pl.when(jnp.logical_not(last))
        def _():
            for c in pieces:
                relay_copy(c).wait_recv()

        if hook is not None:
            hook()
        backward(m, start, size)

        @pl.when(jnp.logical_not(first))
        def _():
            for c in pieces:
                relay_copy(c).start()

    inner = jnp.logical_not(first | last)

    def chunks(m, slots, hook=None):
        for k in range(CHUNKS):
            fine = hook is not None and k == CHUNKS - 1
            for i in range(SPLIT):

                def piece(k=k, i=i):
                    at_last = hook if fine and i == SPLIT - 1 else None
                    step(m, k * CHUNK + i * PIECE, PIECE, at_last)

                if fine:
                    piece()
                else:
                    pl.when(inner)(piece)
                if not fine and i == SPLIT - 1:

                    @pl.when(first | (last & (m > 0)))
                    def _(k=k):
                        step(m, k * CHUNK, CHUNK)

                slots[k * SPLIT + i]()
                tell_ids(m, k * SPLIT + i)

    def route(m):
        rows = micro_rows(m)

        @pl.when(first)
        def _():
            target = lax.broadcasted_iota(jnp.int32, (TOK, TOK), 0).astype(F32)
            pick = jnp.where(target == rank[m], 1.0, 0.0).astype(BF16)
            ordered = jnp.dot(pick, nbuf[rows, :], preferred_element_type=F32).astype(BF16)
            sorted_rows[m] = ordered
            route_copy(m, 1).start()
            route_copy(m, SECTIONS - 1).start()
            if isinstance(m, int):
                route_copy(m, 2).start()
            routed[pl.ds(pl.multiple_of(m * PER_PLANE, PER_PLANE), PER_PLANE), :] = ordered[
                :PER_PLANE, :
            ]

    def micro_step(m, carry):
        @pl.when(last & (m > 0))
        def _():
            load_top(m).wait()

        def forward_slot(j):
            def work():
                if j == 0:

                    @pl.when(last & (m == 1))
                    def _():
                        pass_pool(0)

                    forward_open(m + 1)
                forward_tile(m + 1, j)
                if j == WIDTH // TILE - 1:
                    send_left(m + 1)

            return work

        def grad_slot(i):
            def work():
                if i == 2:

                    @pl.when(last & (m == 1))
                    def _():
                        pass_pool(1)

                @pl.when(m > 0)
                def _():
                    if i == 0:
                        hear_peer(m - 1)
                    grad_tiles(m - 1, (i,), True)

            return work

        tiles = range(WIDTH // TILE)
        chunks(m, [forward_slot(j) for j in tiles] + [grad_slot(i) for i in tiles])
        send_right(m, m * TOK, TOK)
        route(m)
        return carry

    lax.fori_loop(0, MICRO - 1, micro_step, 0)

    final = MICRO - 1
    tail = TOK - CHUNK

    def unit_copy(source, target, send, recv, to, came):
        return pltpu.make_async_remote_copy(
            src_ref=source.at[to],
            dst_ref=target.at[came],
            send_sem=send,
            recv_sem=recv,
            device_id=(sec, to),
            device_id_type=MESH,
        )

    def hand_soon(k, carry):
        to = (sh + k) % SHARDS
        unit_copy(soon, got_soon, soon_send, soon_recv, to, sh).start()
        return carry

    def hand_late(k, carry):
        to = (sh + k) % SHARDS
        unit_copy(late, got_late, late_send, late_recv, to, sh).start()
        return carry

    def wait_all(ref, semaphore):
        others = ref.at[pl.ds(0, SHARDS - 1)]
        pltpu.make_async_copy(others, others, semaphore).wait()

    def soon_units():
        row = lax.broadcasted_iota(jnp.int32, (SOON, SOON), 0)
        col = lax.broadcasted_iota(jnp.int32, (SOON, SOON), 1)
        target = ((col >> 1) & (SHARDS - 1)) * (2 * (MICRO - 1)) + (col >> 6) * 2 + (col & 1)
        regroup = jnp.where(row == target, 1.0, 0.0).astype(BF16)
        by_owner = jnp.dot(regroup, routed[pl.ds(0, SOON), :], preferred_element_type=F32)
        for b in range(8):
            flat[pl.ds(b, SOON, stride=8), :] = by_owner[:, b * 128 : (b + 1) * 128]
        soon[...] = flat[...].reshape(soon.shape).astype(BF16)
        got_soon[sh] = soon[sh]

    def late_units():
        by_owner = routed[pl.ds(SOON, PER_PLANE), :].astype(F32)
        for b in range(8):
            flat[pl.ds(b, PER_PLANE, stride=8), :] = by_owner[:, b * 128 : (b + 1) * 128]
        late[...] = flat[pl.ds(0, PER_PLANE * 8), :].reshape(late.shape).astype(BF16)
        got_late[sh] = late[sh]

    def to_rows(got, start, count):
        flat[pl.ds(0, count * 8), :] = got[...].astype(F32).reshape(count * 8, 128)
        for b in range(8):
            rows_buf[pl.ds(start, count), pl.ds(b * 128, 128)] = flat[
                pl.ds(b, count, stride=8), :
            ].astype(BF16)

    @pl.when(last)
    def _():
        load_top(final).wait()

    def final_slot(n):
        def work():
            if n == 2:
                hear_peer(final - 1)
            if 2 <= n < 2 + WIDTH // TILE:
                grad_tiles(final - 1, (n - 2,), True)
            if n == 5:
                send_right(final, final * TOK, tail)

            @pl.when(first)
            def _():
                if n == 0:
                    soon_units()
                if n == 1:
                    for before in range(final):
                        route_copy(before, 2).start()
                if n == 2:
                    lax.fori_loop(1, SHARDS // 2, hand_soon, 0)
                if n == 4:
                    lax.fori_loop(SHARDS // 2, SHARDS, hand_soon, 0)

        return work

    def hand_g():
        @pl.when(core == 0)
        def _():
            right_copy(final + 1, gbuf, final * TOK + tail, TOK - tail).start()

    chunks(final, [final_slot(n) for n in range(CHUNKS * SPLIT)], hand_g)

    @pl.when(core == 1)
    def _():
        right_copy(final + 1, dz, final * TOK + tail, TOK - tail).start()

    grad_tiles(final, (0, 1, 2, 3), False)

    def block_rows(y, x):
        return pl.ds(pl.multiple_of((y * SIDE + x) * BLOCK, BLOCK), BLOCK)

    left_half = pl.ds(0, HALF)
    right_half = pl.ds(HALF, HALF)

    def x_copy(d, y):
        to = (px + d) % SIDE
        return pltpu.make_async_remote_copy(
            src_ref=send_x.at[y, pl.ds(pl.multiple_of(to * BLOCK, BLOCK), BLOCK)],
            dst_ref=recv_x.at[d - 1, y],
            send_sem=x_send.at[d - 1, y],
            recv_sem=x_recv.at[d - 1, y],
            device_id=at(py, to, core),
            device_id_type=MESH,
        )

    def y_copy(d, x):
        rows = pl.ds(pl.multiple_of(x * BLOCK, BLOCK), BLOCK)
        return pltpu.make_async_remote_copy(
            src_ref=send_y.at[d - 1, rows],
            dst_ref=recv_y.at[d - 1, rows],
            send_sem=y_send.at[d - 1, x],
            recv_sem=y_recv.at[d - 1, x],
            device_id=at((py + d) % SIDE, px, core),
            device_id_type=MESH,
        )

    def c_copy(h, e, c, kind):
        there = (py + e) % SIDE if h == 0 else (px + e) % SIDE
        return pltpu.make_async_remote_copy(
            src_ref=send_c.at[h, e, c],
            dst_ref=out_parts.at[kind, h, e],
            send_sem=c_send.at[h, e, c],
            recv_sem=c_recv.at[kind, h, e],
            device_id=at(there, px, c) if h == 0 else at(py, there, c),
            device_id_type=MESH,
        )

    def own_part(h):
        return pltpu.make_async_copy(
            send_c.at[h, 0, core], out_parts.at[core, h, 0], out_sem.at[2 + h]
        )

    order = (2, 1, 3, 0)
    frows = micro_rows(final)
    left_copy(final, act).wait_recv()
    right_copy(final, dz, final * TOK, tail).wait_recv()
    right_copy(final + 1, dz, final * TOK + tail, TOK - tail).wait_recv()
    for d in order:
        y = (py + d) % SIDE
        cols = pl.ds(pl.multiple_of(y * TILE, TILE), TILE)
        total = acc[cols, :] + dot_tn(peer_l[frows, cols], peer_r[frows, :])
        acc[cols, :] = total
        send_x[y] = total[:, :HALF].astype(BF16)
        for dx in (2, 1, 3):
            x_copy(dx, y).start()
        if d != 0:
            send_y[d - 1] = total[:, HALF:].astype(BF16)
    for e in order:
        for d in (2, 1, 3):
            y_copy(d, (px + e) % SIDE).start()
    route(final)

    @pl.when(jnp.logical_not(first))
    def _():
        for m in range(MICRO - 1):
            route_copy(m, 1).wait_recv()
        soon_units()
        lax.fori_loop(1, SHARDS, hand_soon, 0)
        route_copy(final, 1).wait_recv()

    late_units()
    lax.fori_loop(1, SHARDS, hand_late, 0)

    wait_all(all_ids, ids_recv)
    own = sec * SHARDS + sh
    feature = own // (SECTIONS * SHARDS // ids.shape[1])
    heard = all_ids[:, :, feature, :].reshape(SHARDS * MICRO, ids.shape[2])
    place = lax.broadcasted_iota(jnp.int32, heard.shape, 1) * ROWS_OWN + (heard & (ROWS_OWN - 1))
    ours = heard >> 10 == own
    low = jnp.min(jnp.where(ours, place, 1 << 20), axis=1, keepdims=True) & (ROWS_OWN - 1)
    high = jnp.max(jnp.where(ours, place, -1), axis=1, keepdims=True) & (ROWS_OWN - 1)
    at_lane = lax.broadcasted_iota(jnp.int32, (SHARDS * MICRO, 128), 1)
    parts = jnp.where(
        at_lane == 0,
        low >> 5,
        jnp.where(at_lane == 1, low & 31, jnp.where(at_lane == 2, high >> 5, high & 31)),
    )
    half = lax.broadcasted_iota(jnp.int32, (TOK, SHARDS * MICRO), 0) >> 1
    pair = lax.broadcasted_iota(jnp.int32, (TOK, SHARDS * MICRO), 1)
    came, micro = pair >> 2, pair & (MICRO - 1)
    place_of = jnp.where(
        micro < final, came * (MICRO - 1) + micro, SHARDS * (MICRO - 1) + came
    )
    twice = jnp.where(half == place_of, 1.0, 0.0).astype(BF16)
    both = jnp.dot(twice, parts.astype(F32).astype(BF16), preferred_element_type=F32)
    odd = lax.broadcasted_iota(jnp.int32, (TOK, 1), 0) & 1
    row_of = jnp.where(
        odd == 0, both[:, 0:1] * 32.0 + both[:, 1:2], both[:, 2:3] * 32.0 + both[:, 3:4]
    )
    named[...] = jnp.broadcast_to(row_of.astype(jnp.int32), (TOK, 128))
    put_named = pltpu.make_async_copy(named, out_named, out_sem.at[0])
    put_named.start()

    put_rows = pltpu.make_async_copy(rows_buf, out_rows, out_sem.at[1])

    def collect_soon():
        wait_all(got_soon, soon_recv)
        to_rows(got_soon, 0, SOON)

    pl.when(first)(collect_soon)

    for e in order:
        y = (py + e) % SIDE
        x = (px + e) % SIDE
        for d in range(1, SIDE):
            x_copy(d, y).wait_recv()
            y_copy(d, x).wait_recv()
        total = acc[block_rows(y, px), left_half]
        other = acc[block_rows(py, x), right_half]
        for d in range(1, SIDE):
            total = total + recv_x[d - 1, y].astype(F32)
            xrows = pl.ds(pl.multiple_of(x * BLOCK, BLOCK), BLOCK)
            other = other + recv_y[d - 1, xrows, :].astype(F32)
        for h, part in ((0, total), (1, other)):
            for c in range(2):
                send_c[h, e, c] = part[c * SHARE : (c + 1) * SHARE, :].astype(BF16)
                if e == 0:

                    @pl.when(core == c)
                    def _(h=h, c=c):
                        own_part(h).start()

                    @pl.when(core != c)
                    def _(h=h, c=c):
                        c_copy(h, 0, c, core).start()
                else:
                    c_copy(h, e, c, core).start()

    pl.when(jnp.logical_not(first))(collect_soon)
    wait_all(got_late, late_recv)
    to_rows(got_late, SOON, PER_PLANE)
    put_rows.start()

    wait_all(all_ids, ids_send)
    wait_all(soon, soon_send)

    @pl.when((sec == 1) | last)
    def _():
        pool_copy(sec).wait_send()

    @pl.when(sec == 2)
    def _():
        hop_copy(0).wait_send()
        hop_copy(1).wait_send()

    @pl.when(last)
    def _():
        pass_copy(0).wait_send()
        pass_copy(1).wait_send()

    @pl.when(jnp.logical_not(first))
    def _():
        def left(c, carry):
            relay_copy(c).wait_send()
            return carry

        lax.fori_loop(0, PIECES, left, 0)

    @pl.when(first)
    def _():
        for m in range(final):
            for p in range(1, SECTIONS):
                route_copy(m, p).wait_send()

    for m in range(MICRO):
        left_copy(m, act).wait_send()
    for m in range(final):
        right_copy(m, dz, m * TOK, TOK).wait_send()
    right_copy(final, dz, final * TOK, tail).wait_send()
    right_copy(final + 1, dz, final * TOK + tail, TOK - tail).wait_send()

    wait_all(late, late_send)

    @pl.when(first)
    def _():
        for p in range(1, SECTIONS):
            route_copy(final, p).wait_send()

    for d in range(1, SIDE):
        for y in range(SIDE):
            x_copy(d, y).wait_send()
            y_copy(d, y).wait_send()

    for kind in range(2):
        for h in range(2):

            @pl.when(core != kind)
            def _(h=h, kind=kind):
                c_copy(h, 0, 1 - kind, kind).wait_recv()

            for e in range(1, SIDE):
                c_copy(h, e, 0, kind).wait_recv()

    for h in range(2):
        for d in range(1, SIDE):
            for c in range(2):
                c_copy(h, d, c, core).wait_send()
        c_copy(h, 0, 1 - core, core).wait_send()
    for put in (put_named, put_rows, own_part(0), own_part(1)):
        put.wait()


def relay(holder, saved, pooled, grad_top, w_in, w_out, ids):
    vmem = pl.BlockSpec(memory_space=pltpu.VMEM)
    anywhere = pl.BlockSpec(memory_space=pl.ANY)
    dma = pltpu.SemaphoreType.DMA
    tokens = MICRO * TOK
    return pl.pallas_call(
        kernel,
        out_shape=(
            jax.ShapeDtypeStruct((2, 2, SIDE, SHARE, HALF), BF16),
            jax.ShapeDtypeStruct((TOK, WIDTH), BF16),
            jax.ShapeDtypeStruct((TOK, 128), jnp.int32),
        ),
        in_specs=[pl.BlockSpec(memory_space=pltpu.SMEM)] + [anywhere] * 5 + [vmem],
        out_specs=(anywhere, anywhere, anywhere),
        scratch_shapes=[
            pltpu.VMEM((WIDTH, WIDTH), BF16),
            pltpu.VMEM((WIDTH, WIDTH), BF16),
            pltpu.VMEM((WIDTH, WIDTH), BF16),
            pltpu.VMEM((WIDTH, WIDTH), BF16),
            pltpu.VMEM((tokens, WIDTH), BF16),
            pltpu.VMEM((tokens, WIDTH), BF16),
            pltpu.VMEM((tokens, WIDTH), BF16),
            pltpu.VMEM((SECTIONS, TOK, WIDTH), BF16),
            pltpu.VMEM((tokens, WIDTH), BF16),
            pltpu.VMEM((2, TOK, WIDTH), F32),
            pltpu.VMEM((tokens, WIDTH), BF16),
            pltpu.VMEM((WIDTH, WIDTH), F32),
            pltpu.VMEM((MICRO, 1, TOK), F32),
            pltpu.VMEM((SHARDS,) + ids.shape, jnp.int32),
            pltpu.VMEM((MICRO, TOK, WIDTH), BF16),
            pltpu.VMEM((TOK, WIDTH), BF16),
            pltpu.VMEM((SHARDS, 16 * (MICRO - 1), 128), BF16),
            pltpu.VMEM((SHARDS, 16 * (MICRO - 1), 128), BF16),
            pltpu.VMEM((SHARDS, 16, 128), BF16),
            pltpu.VMEM((SHARDS, 16, 128), BF16),
            pltpu.VMEM((SOON * 8, 128), F32),
            pltpu.VMEM((TOK, 128), jnp.int32),
            pltpu.VMEM((TOK, WIDTH), BF16),
            pltpu.VMEM((TOK, WIDTH), BF16),
            pltpu.VMEM((tokens, WIDTH), BF16),
            pltpu.VMEM((tokens, WIDTH), BF16),
            pltpu.VMEM((SIDE, SIDE * BLOCK, HALF), BF16),
            pltpu.VMEM((SIDE - 1, SIDE, BLOCK, HALF), BF16),
            pltpu.VMEM((SIDE - 1, SIDE * BLOCK, HALF), BF16),
            pltpu.VMEM((SIDE - 1, SIDE * BLOCK, HALF), BF16),
            pltpu.VMEM((2, SIDE, 2, SHARE, HALF), BF16),
            dma((3 + MICRO,)),
            dma((MICRO,)),
            dma,
            dma((SECTIONS,)),
            dma((PIECES,)),
            dma((PIECES,)),
            dma((MICRO, SECTIONS)),
            dma((MICRO,)),
            dma,
            dma,
            dma,
            dma,
            pltpu.SemaphoreType.REGULAR((2,)),
            dma((2,)),
            dma((2,)),
            dma((2,)),
            dma((2,)),
            dma((4,)),
            dma,
            dma,
            dma((MICRO,)),
            dma((MICRO,)),
            dma((MICRO + 1,)),
            dma((MICRO + 1,)),
            dma((SIDE - 1, SIDE)),
            dma((SIDE - 1, SIDE)),
            dma((SIDE - 1, SIDE)),
            dma((SIDE - 1, SIDE)),
            dma((2, SIDE, 2)),
            dma((2, 2, SIDE)),
        ],
        compiler_params=pltpu.CompilerParams(
            collective_id=0, has_side_effects=True, vmem_limit_bytes=56 * 1024 * 1024
        ),
        cost_estimate=pl.CostEstimate(
            flops=10 * tokens * WIDTH * WIDTH, bytes_accessed=9 * 2**20, transcendentals=tokens * WIDTH
        ),
        name="relay",
    )(holder, saved, pooled, grad_top, w_in, w_out, ids)


def table_kernel(named, rows, parts, table, out_in, out_out):
    block = pl.program_id(0)
    lane = lax.broadcasted_iota(jnp.int32, (TOK, WIDE), 1) + block * WIDE
    hit = jnp.where(lane == named[:, 0:1], 1.0, 0.0).astype(BF16)
    table[...] = dot_tn(hit, rows[...])

    @pl.when(block == 0)
    def _():
        for kind, out in ((0, out_in), (1, out_out)):
            for h in range(2):
                total = parts[kind, h, 0].astype(F32)
                for e in range(1, SIDE):
                    total = total + parts[kind, h, e].astype(F32)
                out[:, h * HALF : (h + 1) * HALF] = total


def owner_sums(named, rows, parts):
    def whole(shape):
        return pl.BlockSpec(shape, lambda b: (0,) * len(shape))

    share = jax.ShapeDtypeStruct((SHARE, WIDTH), F32)
    return pl.pallas_call(
        table_kernel,
        grid=(ROWS_OWN // WIDE,),
        out_shape=(jax.ShapeDtypeStruct((ROWS_OWN, WIDTH), F32), share, share),
        in_specs=[whole(named.shape), whole(rows.shape), whole(parts.shape)],
        out_specs=(
            pl.BlockSpec((WIDE, WIDTH), lambda b: (b, 0)),
            whole(share.shape),
            whole(share.shape),
        ),
        compiler_params=pltpu.CompilerParams(vmem_limit_bytes=32 * 1024 * 1024),
        cost_estimate=pl.CostEstimate(
            flops=2 * ROWS_OWN * TOK * WIDTH, bytes_accessed=5 * 2**20, transcendentals=0
        ),
        name="owner_sums",
    )(named, rows, parts)


def local(saved, pooled, grad_top, w_in, w_out, feature_ids, holder_order):
    tokens = MICRO * TOK
    parts, rows, named = relay(
        holder_order,
        saved.reshape(tokens, WIDTH),
        pooled.reshape(TOK, WIDTH),
        grad_top.reshape(tokens, WIDTH),
        w_in[0],
        w_out[0],
        jnp.transpose(feature_ids, (0, 2, 1)),
    )
    table_grad, grad_in, grad_out = owner_sums(named, rows, parts)
    return (grad_in[None], grad_out[None], table_grad)


def solution(mesh):
    return jax.shard_map(
        local,
        mesh=mesh,
        in_specs=(
            P("section", None, "shard", None, None),
            P("section", "shard", None, None),
            P(None, "shard", None, None),
            P("section", None, None),
            P("section", None, None),
            P(None, "shard", None),
            P(),
        ),
        out_specs=(
            P("section", "shard", None),
            P("section", "shard", None),
            P(("section", "shard"), None),
        ),
        check_vma=False,
    )
```

```python
import jax
import jax.numpy as jnp
from jax import lax
from jax.experimental import pallas as pl
from jax.experimental.pallas import tpu as pltpu
from jax.sharding import PartitionSpec as P

ROWS_OWN = 1024
MESH = pl.DeviceIdType.MESH
F32 = jnp.float32
BF16 = jnp.bfloat16

SECTIONS = 4
SHARDS = 32
SIDE = 4
MICRO = 4
TOK = 256
CHUNK = 64
PIECE = 32
WIDTH = 1024
SHARE = WIDTH // SHARDS
PER_PLANE = TOK // SECTIONS
TILE = 256
WIDE = 512
CHUNKS = TOK // CHUNK
SPLIT = CHUNK // PIECE
PIECES = MICRO * TOK // PIECE
SOON = (MICRO - 1) * PER_PLANE
HALF = WIDTH // 2
BLOCK = 2 * SHARE


def dot_tn(a, b):
    return lax.dot_general(a, b, (((0,), (0,)), ((), ())), preferred_element_type=F32)


def kernel(
    holder,
    saved,
    pooled,
    grad_top,
    w_in,
    w_out,
    ids,
    out_parts,
    out_rows,
    out_late,
    out_named,
    win,
    wout,
    win_t,
    wout_t,
    xbuf,
    gbuf,
    nbuf,
    pbuf,
    act,
    slope,
    dz,
    acc,
    rank,
    all_ids,
    sorted_rows,
    routed,
    soon,
    got_soon,
    late,
    flat,
    named,
    rows_buf,
    transit,
    peer_l,
    peer_r,
    send_x,
    recv_x,
    send_y,
    recv_y,
    send_c,
    load_sem,
    top_sem,
    pool_send,
    pool_recv,
    relay_send,
    relay_recv,
    route_send,
    route_recv,
    soon_send,
    soon_recv,
    late_send,
    late_recv,
    ready,
    hop_send,
    hop_recv,
    pass_send,
    pass_recv,
    out_sem,
    ids_send,
    ids_recv,
    l_send,
    l_recv,
    r_send,
    r_recv,
    x_send,
    x_recv,
    y_send,
    y_recv,
    c_send,
    c_recv,
):
    sec = lax.axis_index("section")
    sh = lax.axis_index("shard")
    core = sh % 2
    px = (sh // 2) % SIDE
    py = sh // (2 * SIDE)
    first = sec == 0
    last = sec == SECTIONS - 1

    def at(y, x, c):
        return (sec, (y * SIDE + x) * 2 + c)

    def micro_rows(m):
        return pl.ds(pl.multiple_of(m * TOK, TOK), TOK)

    def token_rows(start, size):
        return pl.ds(pl.multiple_of(start, size), size)

    def load_x(m):
        rows = micro_rows(m)
        return pltpu.make_async_copy(saved.at[rows], xbuf.at[rows], load_sem.at[2 + m])

    def load_top(m):
        rows = micro_rows(m)
        return pltpu.make_async_copy(grad_top.at[rows], gbuf.at[rows], top_sem.at[m])

    load_win = pltpu.make_async_copy(w_in, win, load_sem.at[0])
    load_wout = pltpu.make_async_copy(w_out, wout, load_sem.at[1])
    load_pool = pltpu.make_async_copy(pooled, pbuf.at[0], load_sem.at[2 + MICRO])

    load_win.start()
    load_x(0).start()
    load_wout.start()

    @pl.when(last)
    def _():
        load_top(0).start()

    @pl.when(first)
    def _():
        load_pool.start()

    barrier = pltpu.get_barrier_semaphore()

    def greet(y, x, c):
        pl.semaphore_signal(barrier, inc=1, device_id=at(y, x, c), device_id_type=MESH)

    for k in range(1, SECTIONS):
        pl.semaphore_signal(
            barrier, inc=1, device_id=((sec + k) % SECTIONS, sh), device_id_type=MESH
        )
    for k in range(1, SIDE):
        greet(py, (px + k) % SIDE, core)
        greet((py + k) % SIDE, px, core)
    greet(py, px, 1 - core)

    def tell_row():
        for k in range(1, SIDE):
            to = at(py, (px + k) % SIDE, core)
            pl.semaphore_signal(ready.at[0], inc=1, device_id=to, device_id_type=MESH)

    def tell_plane():
        pl.semaphore_wait(ready.at[0], SIDE - 1)
        for k in range(1, SIDE):
            to = at((py + k) % SIDE, px, core)
            pl.semaphore_signal(ready.at[1], inc=1, device_id=to, device_id_type=MESH)

    def tell_ids(m, n):
        start, total = SPLIT * CHUNKS // 2, SPLIT * CHUNKS

        def tell(k):
            ids_copy((sh + k) % SHARDS, sh).start()

        if n == 0:
            pl.when(m == 0)(tell_plane)
        if n == start:

            @pl.when(m == 0)
            def _():
                pl.semaphore_wait(ready.at[1], SIDE - 1)

        if n >= start:
            tell(m * total + n)
        else:

            @pl.when(m > 0)
            def _():
                tell(m * total + n)

        if 0 < n < start:

            @pl.when(m == 1)
            def _():
                tell(n)

    def pool_copy(s):
        return pltpu.make_async_remote_copy(
            src_ref=pooled,
            dst_ref=pbuf.at[s],
            send_sem=pool_send,
            recv_sem=pool_recv.at[s],
            device_id=(0, sh),
            device_id_type=MESH,
        )

    def pool_rows(h):
        return pl.ds(h * (TOK // 2), TOK // 2)

    def hop_copy(h):
        return pltpu.make_async_remote_copy(
            src_ref=pooled.at[pool_rows(h)],
            dst_ref=transit.at[pool_rows(h)],
            send_sem=hop_send.at[h],
            recv_sem=hop_recv.at[h],
            device_id=(SECTIONS - 1, sh),
            device_id_type=MESH,
        )

    def pass_copy(h):
        return pltpu.make_async_remote_copy(
            src_ref=transit.at[pool_rows(h)],
            dst_ref=pbuf.at[2, pool_rows(h)],
            send_sem=pass_send.at[h],
            recv_sem=pass_recv.at[h],
            device_id=(0, sh),
            device_id_type=MESH,
        )

    def pass_pool(h):
        hop_copy(h).wait_recv()
        pass_copy(h).start()

    def relay_copy(c):
        rows = token_rows(c * PIECE, PIECE)
        return pltpu.make_async_remote_copy(
            src_ref=nbuf.at[rows],
            dst_ref=gbuf.at[rows],
            send_sem=relay_send.at[c],
            recv_sem=relay_recv.at[c],
            device_id=(jnp.maximum(sec - 1, 0), sh),
            device_id_type=MESH,
        )

    def route_copy(m, p):
        return pltpu.make_async_remote_copy(
            src_ref=sorted_rows.at[m, pl.ds(p * PER_PLANE, PER_PLANE)],
            dst_ref=routed.at[pl.ds(pl.multiple_of(m * PER_PLANE, PER_PLANE), PER_PLANE)],
            send_sem=route_send.at[m, p],
            recv_sem=route_recv.at[m],
            device_id=(p, sh),
            device_id_type=MESH,
        )

    def ids_copy(to, came):
        return pltpu.make_async_remote_copy(
            src_ref=ids,
            dst_ref=all_ids.at[came],
            send_sem=ids_send,
            recv_sem=ids_recv,
            device_id=(sec, to),
            device_id_type=MESH,
        )

    def left_copy(m, source):
        rows = micro_rows(m)
        return pltpu.make_async_remote_copy(
            src_ref=source.at[rows],
            dst_ref=peer_l.at[rows],
            send_sem=l_send.at[m],
            recv_sem=l_recv.at[m],
            device_id=at(py, px, 1 - core),
            device_id_type=MESH,
        )

    def right_copy(n, source, start, size):
        rows = pl.ds(pl.multiple_of(start, 64), size)
        return pltpu.make_async_remote_copy(
            src_ref=source.at[rows],
            dst_ref=peer_r.at[rows],
            send_sem=r_send.at[n],
            recv_sem=r_recv.at[n],
            device_id=at(py, px, 1 - core),
            device_id_type=MESH,
        )

    def send_left(m):
        @pl.when(core == 0)
        def _():
            left_copy(m, act).start()

        @pl.when(core == 1)
        def _():
            left_copy(m, xbuf).start()

    def send_right(n, start, size):
        @pl.when(core == 0)
        def _():
            right_copy(n, gbuf, start, size).start()

        @pl.when(core == 1)
        def _():
            right_copy(n, dz, start, size).start()

    def forward_open(m):
        rows = micro_rows(m)
        load_x(m).wait()

        @pl.when(first)
        def _():
            slot = 0
            for j in range(1, MICRO):
                slot = jnp.where(holder[j] == m, j, slot)
            extra = pbuf[slot]
            xbuf[rows, :] = (xbuf[rows, :].astype(F32) + extra.astype(F32)).astype(BF16)

    def forward_tile(m, j):
        rows = micro_rows(m)
        cols = pl.ds(j * TILE, TILE)
        z = jnp.dot(xbuf[rows, :], win[:, cols], preferred_element_type=F32)
        sig = jax.nn.sigmoid(z)
        act[rows, cols] = (z * sig).astype(BF16)
        slope[m % 2, :, cols] = sig * (1.0 + z * (1.0 - sig))

    def forward(m):
        forward_open(m)
        for j in range(WIDTH // TILE):
            forward_tile(m, j)

    def backward(m, start, size):
        crows = token_rows(m * TOK + start, size)
        krows = pl.ds(start, size)
        for j in range(WIDTH // WIDE):
            cols = pl.ds(j * WIDE, WIDE)
            ga = jnp.dot(gbuf[crows, :], wout_t[:, cols], preferred_element_type=F32)
            dz[crows, cols] = (ga * slope[m % 2, krows, cols]).astype(BF16)
        for j in range(WIDTH // WIDE):
            cols = pl.ds(j * WIDE, WIDE)
            back = jnp.dot(dz[crows, :], win_t[:, cols], preferred_element_type=F32)
            nbuf[crows, cols] = (gbuf[crows, cols].astype(F32) + back).astype(BF16)

    def grad_tiles(m, tiles, and_peer):
        rows = micro_rows(m)
        for kind, left, right in ((0, xbuf, dz), (1, act, gbuf)):

            @pl.when(core == kind)
            def _(left=left, right=right):
                for i in tiles:
                    cols = pl.ds(i * TILE, TILE)
                    total = acc[cols, :] + dot_tn(left[rows, cols], right[rows, :])
                    if and_peer:
                        total = total + dot_tn(peer_l[rows, cols], peer_r[rows, :])
                    acc[cols, :] = total

    def hear_peer(m):
        left_copy(m, act).wait_recv()
        right_copy(m, dz, m * TOK, TOK).wait_recv()

    load_win.wait()
    for j in range(WIDTH // TILE):
        cols = pl.ds(j * TILE, TILE)
        win_t[:, cols] = win[cols, :].T

    @pl.when(jnp.logical_not(first))
    def _():
        forward(0)

    load_wout.wait()
    for j in range(WIDTH // TILE):
        cols = pl.ds(j * TILE, TILE)
        wout_t[:, cols] = wout[cols, :].T

    pl.semaphore_wait(barrier, SECTIONS - 1 + 2 * (SIDE - 1) + 1)
    tell_row()

    @pl.when((sec == 1) | last)
    def _():
        pool_copy(sec).start()

    @pl.when(sec == 2)
    def _():
        hop_copy(0).start()
        hop_copy(1).start()

    @pl.when(last)
    def _():
        load_top(0).wait()
        for i in range(SPLIT):
            backward(0, i * PIECE, PIECE)
            relay_copy(i).start()
        for k in range(1, CHUNKS):
            backward(0, k * CHUNK, CHUNK)
            for c in range(k * SPLIT, (k + 1) * SPLIT):
                relay_copy(c).start()
        for m in range(1, MICRO):
            load_top(m).start()

    for m in range(1, MICRO):
        load_x(m).start()

    def clear(i, carry):
        rows = pl.ds(pl.multiple_of(i * 64, 64), 64)
        acc[rows, :] = jnp.zeros((64, WIDTH), F32)
        return carry

    @pl.when(first)
    def _():
        lax.fori_loop(0, WIDTH // 64, clear, 0)
        row = lax.broadcasted_iota(jnp.int32, (TOK, TOK), 0)
        col = lax.broadcasted_iota(jnp.int32, (TOK, TOK), 1)
        feat = ids.shape[1]
        lane = lax.broadcasted_iota(jnp.int32, (ids.shape[2], TOK), 1)
        lead = lax.broadcasted_iota(jnp.int32, (ids.shape[2], TOK), 0)
        widen = jnp.where(lane >> 3 == lead, 1.0, 0.0).astype(BF16)
        for m in range(MICRO):
            owner = (ids[m] >> 10).astype(F32).astype(BF16)
            wide = jnp.dot(owner, widen, preferred_element_type=F32)
            inner = lax.broadcasted_iota(jnp.int32, (feat, TOK), 1) & 7
            outer = lax.broadcasted_iota(jnp.int32, (feat, TOK), 0)
            across = jnp.sum(jnp.where(inner == outer, wide, 0.0), axis=0, keepdims=True)
            down = jnp.sum(jnp.where(row == col, across, 0.0), axis=1, keepdims=True)
            earlier = jnp.where((down == across) & (row < col), 1.0, 0.0)
            rank[m] = 2.0 * across + jnp.sum(earlier, axis=0, keepdims=True)
        load_pool.wait()
        for s in (1, SECTIONS - 1):
            pool_copy(s).wait_recv()
        for h in range(2):
            pass_copy(h).wait_recv()
        forward(0)

    @pl.when(jnp.logical_not(first))
    def _():
        lax.fori_loop(0, WIDTH // 64, clear, 0)

    all_ids[sh] = ids[...]
    send_left(0)

    def step(m, start, size, hook=None):
        pieces = [(m * TOK + start) // PIECE + i for i in range(size // PIECE)]

        @pl.when(jnp.logical_not(last))
        def _():
            for c in pieces:
                relay_copy(c).wait_recv()

        if hook is not None:
            hook()
        backward(m, start, size)

        @pl.when(jnp.logical_not(first))
        def _():
            for c in pieces:
                relay_copy(c).start()

    inner = jnp.logical_not(first | last)

    def chunks(m, slots, hook=None):
        for k in range(CHUNKS):
            fine = hook is not None and k == CHUNKS - 1
            for i in range(SPLIT):

                def piece(k=k, i=i):
                    at_last = hook if fine and i == SPLIT - 1 else None
                    step(m, k * CHUNK + i * PIECE, PIECE, at_last)

                if fine:
                    piece()
                else:
                    pl.when(inner)(piece)
                if not fine and i == SPLIT - 1:

                    @pl.when(first | (last & (m > 0)))
                    def _(k=k):
                        step(m, k * CHUNK, CHUNK)

                slots[k * SPLIT + i]()
                tell_ids(m, k * SPLIT + i)

    def route(m):
        rows = micro_rows(m)

        @pl.when(first)
        def _():
            target = lax.broadcasted_iota(jnp.int32, (TOK, TOK), 0).astype(F32)
            pick = jnp.where(target == rank[m], 1.0, 0.0).astype(BF16)
            ordered = jnp.dot(pick, nbuf[rows, :], preferred_element_type=F32).astype(BF16)
            sorted_rows[m] = ordered
            route_copy(m, 1).start()
            route_copy(m, SECTIONS - 1).start()
            if isinstance(m, int):
                route_copy(m, 2).start()
            routed[pl.ds(pl.multiple_of(m * PER_PLANE, PER_PLANE), PER_PLANE), :] = ordered[
                :PER_PLANE, :
            ]

    def micro_step(m, carry):
        @pl.when(last & (m > 0))
        def _():
            load_top(m).wait()

        def forward_slot(j):
            def work():
                if j == 0:

                    @pl.when(last & (m == 1))
                    def _():
                        pass_pool(0)

                    forward_open(m + 1)
                forward_tile(m + 1, j)
                if j == WIDTH // TILE - 1:
                    send_left(m + 1)

            return work

        def grad_slot(i):
            def work():
                if i == 2:

                    @pl.when(last & (m == 1))
                    def _():
                        pass_pool(1)

                @pl.when(m > 0)
                def _():
                    if i == 0:
                        hear_peer(m - 1)
                    grad_tiles(m - 1, (i,), True)

            return work

        tiles = range(WIDTH // TILE)
        chunks(m, [forward_slot(j) for j in tiles] + [grad_slot(i) for i in tiles])
        send_right(m, m * TOK, TOK)
        route(m)
        return carry

    lax.fori_loop(0, MICRO - 1, micro_step, 0)

    final = MICRO - 1
    tail = TOK - CHUNK

    def unit_copy(source, target, send, recv, to, came):
        return pltpu.make_async_remote_copy(
            src_ref=source.at[to],
            dst_ref=target.at[came],
            send_sem=send,
            recv_sem=recv,
            device_id=(sec, to),
            device_id_type=MESH,
        )

    def hand_soon(k, carry):
        to = (sh + k) % SHARDS
        unit_copy(soon, got_soon, soon_send, soon_recv, to, sh).start()
        return carry

    def hand_late(k, carry):
        to = (sh + k) % SHARDS
        unit_copy(late, out_late, late_send, late_recv, to, sh).start()
        return carry

    def wait_all(ref, semaphore):
        others = ref.at[pl.ds(0, SHARDS - 1)]
        pltpu.make_async_copy(others, others, semaphore).wait()

    def soon_units():
        row = lax.broadcasted_iota(jnp.int32, (SOON, SOON), 0)
        col = lax.broadcasted_iota(jnp.int32, (SOON, SOON), 1)
        target = ((col >> 1) & (SHARDS - 1)) * (2 * (MICRO - 1)) + (col >> 6) * 2 + (col & 1)
        regroup = jnp.where(row == target, 1.0, 0.0).astype(BF16)
        by_owner = jnp.dot(regroup, routed[pl.ds(0, SOON), :], preferred_element_type=F32)
        for b in range(8):
            flat[pl.ds(b, SOON, stride=8), :] = by_owner[:, b * 128 : (b + 1) * 128]
        soon[...] = flat[...].reshape(soon.shape).astype(BF16)
        got_soon[sh] = soon[sh]

    def own_late():
        return pltpu.make_async_copy(late.at[sh], out_late.at[sh], out_sem.at[4])

    def late_units():
        by_owner = routed[pl.ds(SOON, PER_PLANE), :].astype(F32)
        for b in range(8):
            flat[pl.ds(b, PER_PLANE, stride=8), :] = by_owner[:, b * 128 : (b + 1) * 128]
        late[...] = flat[pl.ds(0, PER_PLANE * 8), :].reshape(late.shape).astype(BF16)
        own_late().start()

    def soon_rows():
        flat[...] = got_soon[...].astype(F32).reshape(SOON * 8, 128)
        for b in range(8):
            rows_buf[:, pl.ds(b * 128, 128)] = flat[pl.ds(b, SOON, stride=8), :].astype(BF16)

    @pl.when(last)
    def _():
        load_top(final).wait()

    def final_slot(n):
        def work():
            if n == 2:
                hear_peer(final - 1)
            if 2 <= n < 2 + WIDTH // TILE:
                grad_tiles(final - 1, (n - 2,), True)
            if n == 5:
                send_right(final, final * TOK, tail)

            @pl.when(first)
            def _():
                if n == 0:
                    soon_units()
                if n == 1:
                    for before in range(final):
                        route_copy(before, 2).start()
                if n == 2:
                    lax.fori_loop(1, SHARDS // 2, hand_soon, 0)
                if n == 4:
                    lax.fori_loop(SHARDS // 2, SHARDS, hand_soon, 0)

        return work

    def hand_g():
        @pl.when(core == 0)
        def _():
            right_copy(final + 1, gbuf, final * TOK + tail, TOK - tail).start()

    chunks(final, [final_slot(n) for n in range(CHUNKS * SPLIT)], hand_g)

    @pl.when(core == 1)
    def _():
        right_copy(final + 1, dz, final * TOK + tail, TOK - tail).start()

    grad_tiles(final, (0, 1, 2, 3), False)

    def block_rows(y, x):
        return pl.ds(pl.multiple_of((y * SIDE + x) * BLOCK, BLOCK), BLOCK)

    left_half = pl.ds(0, HALF)
    right_half = pl.ds(HALF, HALF)

    def x_copy(d, y):
        to = (px + d) % SIDE
        return pltpu.make_async_remote_copy(
            src_ref=send_x.at[y, pl.ds(pl.multiple_of(to * BLOCK, BLOCK), BLOCK)],
            dst_ref=recv_x.at[d - 1, y],
            send_sem=x_send.at[d - 1, y],
            recv_sem=x_recv.at[d - 1, y],
            device_id=at(py, to, core),
            device_id_type=MESH,
        )

    def y_copy(d, x):
        rows = pl.ds(pl.multiple_of(x * BLOCK, BLOCK), BLOCK)
        return pltpu.make_async_remote_copy(
            src_ref=send_y.at[d - 1, rows],
            dst_ref=recv_y.at[d - 1, rows],
            send_sem=y_send.at[d - 1, x],
            recv_sem=y_recv.at[d - 1, x],
            device_id=at((py + d) % SIDE, px, core),
            device_id_type=MESH,
        )

    def c_copy(h, e, c, kind):
        there = (py + e) % SIDE if h == 0 else (px + e) % SIDE
        return pltpu.make_async_remote_copy(
            src_ref=send_c.at[h, e, c],
            dst_ref=out_parts.at[kind, h, e],
            send_sem=c_send.at[h, e, c],
            recv_sem=c_recv.at[kind, h, e],
            device_id=at(there, px, c) if h == 0 else at(py, there, c),
            device_id_type=MESH,
        )

    def own_part(h):
        return pltpu.make_async_copy(
            send_c.at[h, 0, core], out_parts.at[core, h, 0], out_sem.at[2 + h]
        )

    order = (2, 1, 3, 0)
    frows = micro_rows(final)
    left_copy(final, act).wait_recv()
    right_copy(final, dz, final * TOK, tail).wait_recv()
    right_copy(final + 1, dz, final * TOK + tail, TOK - tail).wait_recv()
    for d in order:
        y = (py + d) % SIDE
        cols = pl.ds(pl.multiple_of(y * TILE, TILE), TILE)
        total = acc[cols, :] + dot_tn(peer_l[frows, cols], peer_r[frows, :])
        acc[cols, :] = total
        send_x[y] = total[:, :HALF].astype(BF16)
        for dx in (2, 1, 3):
            x_copy(dx, y).start()
        if d != 0:
            send_y[d - 1] = total[:, HALF:].astype(BF16)
    for e in order:
        for d in (2, 1, 3):
            y_copy(d, (px + e) % SIDE).start()
    route(final)

    @pl.when(jnp.logical_not(first))
    def _():
        for m in range(MICRO - 1):
            route_copy(m, 1).wait_recv()
        soon_units()
        lax.fori_loop(1, SHARDS, hand_soon, 0)
        route_copy(final, 1).wait_recv()

    late_units()
    lax.fori_loop(1, SHARDS, hand_late, 0)

    wait_all(all_ids, ids_recv)
    own = sec * SHARDS + sh
    feature = own // (SECTIONS * SHARDS // ids.shape[1])
    heard = all_ids[:, :, feature, :].reshape(SHARDS * MICRO, ids.shape[2])
    place = lax.broadcasted_iota(jnp.int32, heard.shape, 1) * ROWS_OWN + (heard & (ROWS_OWN - 1))
    ours = heard >> 10 == own
    low = jnp.min(jnp.where(ours, place, 1 << 20), axis=1, keepdims=True) & (ROWS_OWN - 1)
    high = jnp.max(jnp.where(ours, place, -1), axis=1, keepdims=True) & (ROWS_OWN - 1)
    at_lane = lax.broadcasted_iota(jnp.int32, (SHARDS * MICRO, 128), 1)
    parts = jnp.where(
        at_lane == 0,
        low >> 5,
        jnp.where(at_lane == 1, low & 31, jnp.where(at_lane == 2, high >> 5, high & 31)),
    )
    half = lax.broadcasted_iota(jnp.int32, (TOK, SHARDS * MICRO), 0) >> 1
    pair = lax.broadcasted_iota(jnp.int32, (TOK, SHARDS * MICRO), 1)
    came, micro = pair >> 2, pair & (MICRO - 1)
    place_of = jnp.where(
        micro < final, came * (MICRO - 1) + micro, SHARDS * (MICRO - 1) + came
    )
    twice = jnp.where(half == place_of, 1.0, 0.0).astype(BF16)
    both = jnp.dot(twice, parts.astype(F32).astype(BF16), preferred_element_type=F32)
    odd = lax.broadcasted_iota(jnp.int32, (TOK, 1), 0) & 1
    row_of = jnp.where(
        odd == 0, both[:, 0:1] * 32.0 + both[:, 1:2], both[:, 2:3] * 32.0 + both[:, 3:4]
    )
    named[...] = jnp.broadcast_to(row_of.astype(jnp.int32), (TOK, 128))
    put_named = pltpu.make_async_copy(named, out_named, out_sem.at[0])
    put_named.start()

    put_rows = pltpu.make_async_copy(rows_buf, out_rows, out_sem.at[1])

    def collect_soon():
        wait_all(got_soon, soon_recv)
        soon_rows()
        put_rows.start()

    pl.when(first)(collect_soon)

    for e in order:
        y = (py + e) % SIDE
        x = (px + e) % SIDE
        for d in range(1, SIDE):
            x_copy(d, y).wait_recv()
            y_copy(d, x).wait_recv()
        total = acc[block_rows(y, px), left_half]
        other = acc[block_rows(py, x), right_half]
        for d in range(1, SIDE):
            total = total + recv_x[d - 1, y].astype(F32)
            xrows = pl.ds(pl.multiple_of(x * BLOCK, BLOCK), BLOCK)
            other = other + recv_y[d - 1, xrows, :].astype(F32)
        for h, part in ((0, total), (1, other)):
            for c in range(2):
                send_c[h, e, c] = part[c * SHARE : (c + 1) * SHARE, :].astype(BF16)
                if e == 0:

                    @pl.when(core == c)
                    def _(h=h, c=c):
                        own_part(h).start()

                    @pl.when(core != c)
                    def _(h=h, c=c):
                        c_copy(h, 0, c, core).start()
                else:
                    c_copy(h, e, c, core).start()

    pl.when(jnp.logical_not(first))(collect_soon)
    wait_all(all_ids, ids_send)
    wait_all(soon, soon_send)

    @pl.when((sec == 1) | last)
    def _():
        pool_copy(sec).wait_send()

    @pl.when(sec == 2)
    def _():
        hop_copy(0).wait_send()
        hop_copy(1).wait_send()

    @pl.when(last)
    def _():
        pass_copy(0).wait_send()
        pass_copy(1).wait_send()

    @pl.when(jnp.logical_not(first))
    def _():
        def left(c, carry):
            relay_copy(c).wait_send()
            return carry

        lax.fori_loop(0, PIECES, left, 0)

    @pl.when(first)
    def _():
        for m in range(final):
            for p in range(1, SECTIONS):
                route_copy(m, p).wait_send()

    for m in range(MICRO):
        left_copy(m, act).wait_send()
    for m in range(final):
        right_copy(m, dz, m * TOK, TOK).wait_send()
    right_copy(final, dz, final * TOK, tail).wait_send()
    right_copy(final + 1, dz, final * TOK + tail, TOK - tail).wait_send()

    wait_all(late, late_send)

    @pl.when(first)
    def _():
        for p in range(1, SECTIONS):
            route_copy(final, p).wait_send()

    for d in range(1, SIDE):
        for y in range(SIDE):
            x_copy(d, y).wait_send()
            y_copy(d, y).wait_send()

    for kind in range(2):
        for h in range(2):

            @pl.when(core != kind)
            def _(h=h, kind=kind):
                c_copy(h, 0, 1 - kind, kind).wait_recv()

            for e in range(1, SIDE):
                c_copy(h, e, 0, kind).wait_recv()

    for h in range(2):
        for d in range(1, SIDE):
            for c in range(2):
                c_copy(h, d, c, core).wait_send()
        c_copy(h, 0, 1 - core, core).wait_send()
    wait_all(out_late, late_recv)
    for put in (put_named, put_rows, own_late(), own_part(0), own_part(1)):
        put.wait()


def relay(holder, saved, pooled, grad_top, w_in, w_out, ids):
    vmem = pl.BlockSpec(memory_space=pltpu.VMEM)
    anywhere = pl.BlockSpec(memory_space=pl.ANY)
    dma = pltpu.SemaphoreType.DMA
    tokens = MICRO * TOK
    return pl.pallas_call(
        kernel,
        out_shape=(
            jax.ShapeDtypeStruct((2, 2, SIDE, SHARE, HALF), BF16),
            jax.ShapeDtypeStruct((SOON, WIDTH), BF16),
            jax.ShapeDtypeStruct((SHARDS, 16, 128), BF16),
            jax.ShapeDtypeStruct((TOK, 128), jnp.int32),
        ),
        in_specs=[pl.BlockSpec(memory_space=pltpu.SMEM)] + [anywhere] * 5 + [vmem],
        out_specs=(anywhere, anywhere, anywhere, anywhere),
        scratch_shapes=[
            pltpu.VMEM((WIDTH, WIDTH), BF16),
            pltpu.VMEM((WIDTH, WIDTH), BF16),
            pltpu.VMEM((WIDTH, WIDTH), BF16),
            pltpu.VMEM((WIDTH, WIDTH), BF16),
            pltpu.VMEM((tokens, WIDTH), BF16),
            pltpu.VMEM((tokens, WIDTH), BF16),
            pltpu.VMEM((tokens, WIDTH), BF16),
            pltpu.VMEM((SECTIONS, TOK, WIDTH), BF16),
            pltpu.VMEM((tokens, WIDTH), BF16),
            pltpu.VMEM((2, TOK, WIDTH), F32),
            pltpu.VMEM((tokens, WIDTH), BF16),
            pltpu.VMEM((WIDTH, WIDTH), F32),
            pltpu.VMEM((MICRO, 1, TOK), F32),
            pltpu.VMEM((SHARDS,) + ids.shape, jnp.int32),
            pltpu.VMEM((MICRO, TOK, WIDTH), BF16),
            pltpu.VMEM((TOK, WIDTH), BF16),
            pltpu.VMEM((SHARDS, 16 * (MICRO - 1), 128), BF16),
            pltpu.VMEM((SHARDS, 16 * (MICRO - 1), 128), BF16),
            pltpu.VMEM((SHARDS, 16, 128), BF16),
            pltpu.VMEM((SOON * 8, 128), F32),
            pltpu.VMEM((TOK, 128), jnp.int32),
            pltpu.VMEM((SOON, WIDTH), BF16),
            pltpu.VMEM((TOK, WIDTH), BF16),
            pltpu.VMEM((tokens, WIDTH), BF16),
            pltpu.VMEM((tokens, WIDTH), BF16),
            pltpu.VMEM((SIDE, SIDE * BLOCK, HALF), BF16),
            pltpu.VMEM((SIDE - 1, SIDE, BLOCK, HALF), BF16),
            pltpu.VMEM((SIDE - 1, SIDE * BLOCK, HALF), BF16),
            pltpu.VMEM((SIDE - 1, SIDE * BLOCK, HALF), BF16),
            pltpu.VMEM((2, SIDE, 2, SHARE, HALF), BF16),
            dma((3 + MICRO,)),
            dma((MICRO,)),
            dma,
            dma((SECTIONS,)),
            dma((PIECES,)),
            dma((PIECES,)),
            dma((MICRO, SECTIONS)),
            dma((MICRO,)),
            dma,
            dma,
            dma,
            dma,
            pltpu.SemaphoreType.REGULAR((2,)),
            dma((2,)),
            dma((2,)),
            dma((2,)),
            dma((2,)),
            dma((5,)),
            dma,
            dma,
            dma((MICRO,)),
            dma((MICRO,)),
            dma((MICRO + 1,)),
            dma((MICRO + 1,)),
            dma((SIDE - 1, SIDE)),
            dma((SIDE - 1, SIDE)),
            dma((SIDE - 1, SIDE)),
            dma((SIDE - 1, SIDE)),
            dma((2, SIDE, 2)),
            dma((2, 2, SIDE)),
        ],
        compiler_params=pltpu.CompilerParams(
            collective_id=0, has_side_effects=True, vmem_limit_bytes=56 * 1024 * 1024
        ),
        cost_estimate=pl.CostEstimate(
            flops=10 * tokens * WIDTH * WIDTH, bytes_accessed=9 * 2**20, transcendentals=tokens * WIDTH
        ),
        name="relay",
    )(holder, saved, pooled, grad_top, w_in, w_out, ids)


def table_kernel(named, soon, late, parts, table, out_in, out_out, rows, flat):
    block = pl.program_id(0)

    @pl.when(block == 0)
    def _():
        rows[pl.ds(0, SOON), :] = soon[...]
        flat[...] = late[...].astype(F32).reshape(PER_PLANE * 8, 128)
        for b in range(8):
            rows[pl.ds(SOON, PER_PLANE), pl.ds(b * 128, 128)] = flat[
                pl.ds(b, PER_PLANE, stride=8), :
            ].astype(BF16)

    lane = lax.broadcasted_iota(jnp.int32, (TOK, WIDE), 1) + block * WIDE
    hit = jnp.where(lane == named[:, 0:1], 1.0, 0.0).astype(BF16)
    table[...] = dot_tn(hit, rows[...])

    @pl.when(block == 0)
    def _():
        for kind, out in ((0, out_in), (1, out_out)):
            for h in range(2):
                total = parts[kind, h, 0].astype(F32)
                for e in range(1, SIDE):
                    total = total + parts[kind, h, e].astype(F32)
                out[:, h * HALF : (h + 1) * HALF] = total


def owner_sums(named, soon, late, parts):
    def whole(shape):
        return pl.BlockSpec(shape, lambda b: (0,) * len(shape))

    share = jax.ShapeDtypeStruct((SHARE, WIDTH), F32)
    return pl.pallas_call(
        table_kernel,
        grid=(ROWS_OWN // WIDE,),
        out_shape=(jax.ShapeDtypeStruct((ROWS_OWN, WIDTH), F32), share, share),
        in_specs=[whole(array.shape) for array in (named, soon, late, parts)],
        out_specs=(
            pl.BlockSpec((WIDE, WIDTH), lambda b: (b, 0)),
            whole(share.shape),
            whole(share.shape),
        ),
        scratch_shapes=[
            pltpu.VMEM((TOK, WIDTH), BF16),
            pltpu.VMEM((PER_PLANE * 8, 128), F32),
        ],
        compiler_params=pltpu.CompilerParams(vmem_limit_bytes=32 * 1024 * 1024),
        cost_estimate=pl.CostEstimate(
            flops=2 * ROWS_OWN * TOK * WIDTH, bytes_accessed=5 * 2**20, transcendentals=0
        ),
        name="owner_sums",
    )(named, soon, late, parts)


def local(saved, pooled, grad_top, w_in, w_out, feature_ids, holder_order):
    tokens = MICRO * TOK
    parts, soon, late, named = relay(
        holder_order,
        saved.reshape(tokens, WIDTH),
        pooled.reshape(TOK, WIDTH),
        grad_top.reshape(tokens, WIDTH),
        w_in[0],
        w_out[0],
        jnp.transpose(feature_ids, (0, 2, 1)),
    )
    table_grad, grad_in, grad_out = owner_sums(named, soon, late, parts)
    return (grad_in[None], grad_out[None], table_grad)


def solution(mesh):
    return jax.shard_map(
        local,
        mesh=mesh,
        in_specs=(
            P("section", None, "shard", None, None),
            P("section", "shard", None, None),
            P(None, "shard", None, None),
            P("section", None, None),
            P("section", None, None),
            P(None, "shard", None),
            P(),
        ),
        out_specs=(
            P("section", "shard", None),
            P("section", "shard", None),
            P(("section", "shard"), None),
        ),
        check_vma=False,
    )
```

```python
import jax
import jax.numpy as jnp
from jax import lax
from jax.experimental import pallas as pl
from jax.experimental.pallas import tpu as pltpu
from jax.sharding import PartitionSpec as P

ROWS_OWN = 1024
MESH = pl.DeviceIdType.MESH
F32 = jnp.float32
BF16 = jnp.bfloat16

SECTIONS = 4
SHARDS = 32
SIDE = 4
MICRO = 4
TOK = 256
CHUNK = 64
PIECE = 32
WIDTH = 1024
SHARE = WIDTH // SHARDS
PER_PLANE = TOK // SECTIONS
TILE = 256
WIDE = 512
CHUNKS = TOK // CHUNK
SPLIT = CHUNK // PIECE
PIECES = MICRO * TOK // PIECE
SOON = (MICRO - 1) * PER_PLANE
HALF = WIDTH // 2
BLOCK = 2 * SHARE


def dot_tn(a, b):
    return lax.dot_general(a, b, (((0,), (0,)), ((), ())), preferred_element_type=F32)


def kernel(
    holder,
    saved,
    pooled,
    grad_top,
    w_in,
    w_out,
    ids,
    out_parts,
    out_rows,
    out_named,
    win,
    wout,
    win_t,
    wout_t,
    xbuf,
    gbuf,
    nbuf,
    pbuf,
    act,
    slope,
    dz,
    acc,
    rank,
    all_ids,
    sorted_rows,
    routed,
    soon,
    got_soon,
    late,
    got_late,
    flat,
    named,
    rows_buf,
    transit,
    peer_l,
    peer_r,
    send_x,
    recv_x,
    send_y,
    recv_y,
    send_c,
    load_sem,
    top_sem,
    pool_send,
    pool_recv,
    relay_send,
    relay_recv,
    route_send,
    route_recv,
    soon_send,
    soon_recv,
    late_send,
    late_recv,
    ready,
    hop_send,
    hop_recv,
    pass_send,
    pass_recv,
    out_sem,
    ids_send,
    ids_recv,
    l_send,
    l_recv,
    r_send,
    r_recv,
    x_send,
    x_recv,
    y_send,
    y_recv,
    c_send,
    c_recv,
):
    sec = lax.axis_index("section")
    sh = lax.axis_index("shard")
    core = sh % 2
    px = (sh // 2) % SIDE
    py = sh // (2 * SIDE)
    first = sec == 0
    last = sec == SECTIONS - 1

    def at(y, x, c):
        return (sec, (y * SIDE + x) * 2 + c)

    def micro_rows(m):
        return pl.ds(pl.multiple_of(m * TOK, TOK), TOK)

    def token_rows(start, size):
        return pl.ds(pl.multiple_of(start, size), size)

    def load_x(m):
        rows = micro_rows(m)
        return pltpu.make_async_copy(saved.at[rows], xbuf.at[rows], load_sem.at[2 + m])

    def load_top(m):
        rows = micro_rows(m)
        return pltpu.make_async_copy(grad_top.at[rows], gbuf.at[rows], top_sem.at[m])

    load_win = pltpu.make_async_copy(w_in, win, load_sem.at[0])
    load_wout = pltpu.make_async_copy(w_out, wout, load_sem.at[1])
    load_pool = pltpu.make_async_copy(pooled, pbuf.at[0], load_sem.at[2 + MICRO])

    load_win.start()
    load_x(0).start()
    load_wout.start()

    @pl.when(last)
    def _():
        load_top(0).start()

    @pl.when(first)
    def _():
        load_pool.start()

    barrier = pltpu.get_barrier_semaphore()

    def greet(y, x, c):
        pl.semaphore_signal(barrier, inc=1, device_id=at(y, x, c), device_id_type=MESH)

    for k in range(1, SECTIONS):
        pl.semaphore_signal(
            barrier, inc=1, device_id=((sec + k) % SECTIONS, sh), device_id_type=MESH
        )
    for k in range(1, SIDE):
        greet(py, (px + k) % SIDE, core)
        greet((py + k) % SIDE, px, core)
    greet(py, px, 1 - core)

    def tell_row():
        for k in range(1, SIDE):
            to = at(py, (px + k) % SIDE, core)
            pl.semaphore_signal(ready.at[0], inc=1, device_id=to, device_id_type=MESH)

    def tell_plane():
        pl.semaphore_wait(ready.at[0], SIDE - 1)
        for k in range(1, SIDE):
            to = at((py + k) % SIDE, px, core)
            pl.semaphore_signal(ready.at[1], inc=1, device_id=to, device_id_type=MESH)

    def tell_ids(m, n):
        start, total = SPLIT * CHUNKS // 2, SPLIT * CHUNKS

        def tell(k):
            ids_copy((sh + k) % SHARDS, sh).start()

        if n == 0:
            pl.when(m == 0)(tell_plane)
        if n == start:

            @pl.when(m == 0)
            def _():
                pl.semaphore_wait(ready.at[1], SIDE - 1)

        if n >= start:
            tell(m * total + n)
        else:

            @pl.when(m > 0)
            def _():
                tell(m * total + n)

        if 0 < n < start:

            @pl.when(m == 1)
            def _():
                tell(n)

    def pool_copy(s):
        return pltpu.make_async_remote_copy(
            src_ref=pooled,
            dst_ref=pbuf.at[s],
            send_sem=pool_send,
            recv_sem=pool_recv.at[s],
            device_id=(0, sh),
            device_id_type=MESH,
        )

    def pool_rows(h):
        return pl.ds(h * (TOK // 2), TOK // 2)

    def hop_copy(h):
        return pltpu.make_async_remote_copy(
            src_ref=pooled.at[pool_rows(h)],
            dst_ref=transit.at[pool_rows(h)],
            send_sem=hop_send.at[h],
            recv_sem=hop_recv.at[h],
            device_id=(SECTIONS - 1, sh),
            device_id_type=MESH,
        )

    def pass_copy(h):
        return pltpu.make_async_remote_copy(
            src_ref=transit.at[pool_rows(h)],
            dst_ref=pbuf.at[2, pool_rows(h)],
            send_sem=pass_send.at[h],
            recv_sem=pass_recv.at[h],
            device_id=(0, sh),
            device_id_type=MESH,
        )

    def pass_pool(h):
        hop_copy(h).wait_recv()
        pass_copy(h).start()

    def relay_copy(c):
        rows = token_rows(c * PIECE, PIECE)
        return pltpu.make_async_remote_copy(
            src_ref=nbuf.at[rows],
            dst_ref=gbuf.at[rows],
            send_sem=relay_send.at[c],
            recv_sem=relay_recv.at[c],
            device_id=(jnp.maximum(sec - 1, 0), sh),
            device_id_type=MESH,
        )

    def route_copy(m, p):
        return pltpu.make_async_remote_copy(
            src_ref=sorted_rows.at[m, pl.ds(p * PER_PLANE, PER_PLANE)],
            dst_ref=routed.at[pl.ds(pl.multiple_of(m * PER_PLANE, PER_PLANE), PER_PLANE)],
            send_sem=route_send.at[m, p],
            recv_sem=route_recv.at[m],
            device_id=(p, sh),
            device_id_type=MESH,
        )

    def ids_copy(to, came):
        return pltpu.make_async_remote_copy(
            src_ref=ids,
            dst_ref=all_ids.at[came],
            send_sem=ids_send,
            recv_sem=ids_recv,
            device_id=(sec, to),
            device_id_type=MESH,
        )

    def left_copy(m, source):
        rows = micro_rows(m)
        return pltpu.make_async_remote_copy(
            src_ref=source.at[rows],
            dst_ref=peer_l.at[rows],
            send_sem=l_send.at[m],
            recv_sem=l_recv.at[m],
            device_id=at(py, px, 1 - core),
            device_id_type=MESH,
        )

    def right_copy(n, source, start, size):
        rows = pl.ds(pl.multiple_of(start, 64), size)
        return pltpu.make_async_remote_copy(
            src_ref=source.at[rows],
            dst_ref=peer_r.at[rows],
            send_sem=r_send.at[n],
            recv_sem=r_recv.at[n],
            device_id=at(py, px, 1 - core),
            device_id_type=MESH,
        )

    def send_left(m):
        @pl.when(core == 0)
        def _():
            left_copy(m, act).start()

        @pl.when(core == 1)
        def _():
            left_copy(m, xbuf).start()

    def send_right(n, start, size):
        @pl.when(core == 0)
        def _():
            right_copy(n, gbuf, start, size).start()

        @pl.when(core == 1)
        def _():
            right_copy(n, dz, start, size).start()

    def forward_open(m):
        rows = micro_rows(m)
        load_x(m).wait()

        @pl.when(first)
        def _():
            slot = 0
            for j in range(1, MICRO):
                slot = jnp.where(holder[j] == m, j, slot)
            extra = pbuf[slot]
            xbuf[rows, :] = (xbuf[rows, :].astype(F32) + extra.astype(F32)).astype(BF16)

    def forward_tile(m, j):
        rows = micro_rows(m)
        cols = pl.ds(j * TILE, TILE)
        z = jnp.dot(xbuf[rows, :], win[:, cols], preferred_element_type=F32)
        sig = jax.nn.sigmoid(z)
        act[rows, cols] = (z * sig).astype(BF16)
        slope[m % 2, :, cols] = sig * (1.0 + z * (1.0 - sig))

    def forward(m):
        forward_open(m)
        for j in range(WIDTH // TILE):
            forward_tile(m, j)

    def backward(m, start, size):
        crows = token_rows(m * TOK + start, size)
        krows = pl.ds(start, size)
        for j in range(WIDTH // WIDE):
            cols = pl.ds(j * WIDE, WIDE)
            ga = jnp.dot(gbuf[crows, :], wout_t[:, cols], preferred_element_type=F32)
            dz[crows, cols] = (ga * slope[m % 2, krows, cols]).astype(BF16)
        for j in range(WIDTH // WIDE):
            cols = pl.ds(j * WIDE, WIDE)
            back = jnp.dot(dz[crows, :], win_t[:, cols], preferred_element_type=F32)
            nbuf[crows, cols] = (gbuf[crows, cols].astype(F32) + back).astype(BF16)

    def grad_tiles(m, tiles, and_peer):
        rows = micro_rows(m)
        for kind, left, right in ((0, xbuf, dz), (1, act, gbuf)):

            @pl.when(core == kind)
            def _(left=left, right=right):
                for i in tiles:
                    cols = pl.ds(i * TILE, TILE)
                    total = acc[cols, :] + dot_tn(left[rows, cols], right[rows, :])
                    if and_peer:
                        total = total + dot_tn(peer_l[rows, cols], peer_r[rows, :])
                    acc[cols, :] = total

    def hear_peer(m):
        left_copy(m, act).wait_recv()
        right_copy(m, dz, m * TOK, TOK).wait_recv()

    load_win.wait()
    for j in range(WIDTH // TILE):
        cols = pl.ds(j * TILE, TILE)
        win_t[:, cols] = win[cols, :].T

    @pl.when(jnp.logical_not(first))
    def _():
        forward(0)

    load_wout.wait()
    for j in range(WIDTH // TILE):
        cols = pl.ds(j * TILE, TILE)
        wout_t[:, cols] = wout[cols, :].T

    pl.semaphore_wait(barrier, SECTIONS - 1 + 2 * (SIDE - 1) + 1)
    tell_row()

    @pl.when((sec == 1) | last)
    def _():
        pool_copy(sec).start()

    @pl.when(sec == 2)
    def _():
        hop_copy(0).start()
        hop_copy(1).start()

    @pl.when(last)
    def _():
        load_top(0).wait()
        for i in range(SPLIT):
            backward(0, i * PIECE, PIECE)
            relay_copy(i).start()
        for k in range(1, CHUNKS):
            backward(0, k * CHUNK, CHUNK)
            for c in range(k * SPLIT, (k + 1) * SPLIT):
                relay_copy(c).start()
        for m in range(1, MICRO):
            load_top(m).start()

    for m in range(1, MICRO):
        load_x(m).start()

    def clear(i, carry):
        rows = pl.ds(pl.multiple_of(i * 64, 64), 64)
        acc[rows, :] = jnp.zeros((64, WIDTH), F32)
        return carry

    @pl.when(first)
    def _():
        lax.fori_loop(0, WIDTH // 64, clear, 0)
        row = lax.broadcasted_iota(jnp.int32, (TOK, TOK), 0)
        col = lax.broadcasted_iota(jnp.int32, (TOK, TOK), 1)
        feat = ids.shape[1]
        lane = lax.broadcasted_iota(jnp.int32, (ids.shape[2], TOK), 1)
        lead = lax.broadcasted_iota(jnp.int32, (ids.shape[2], TOK), 0)
        widen = jnp.where(lane >> 3 == lead, 1.0, 0.0).astype(BF16)
        for m in range(MICRO):
            owner = (ids[m] >> 10).astype(F32).astype(BF16)
            wide = jnp.dot(owner, widen, preferred_element_type=F32)
            inner = lax.broadcasted_iota(jnp.int32, (feat, TOK), 1) & 7
            outer = lax.broadcasted_iota(jnp.int32, (feat, TOK), 0)
            across = jnp.sum(jnp.where(inner == outer, wide, 0.0), axis=0, keepdims=True)
            down = jnp.sum(jnp.where(row == col, across, 0.0), axis=1, keepdims=True)
            earlier = jnp.where((down == across) & (row < col), 1.0, 0.0)
            rank[m] = 2.0 * across + jnp.sum(earlier, axis=0, keepdims=True)
        load_pool.wait()
        for s in (1, SECTIONS - 1):
            pool_copy(s).wait_recv()
        for h in range(2):
            pass_copy(h).wait_recv()
        forward(0)

    @pl.when(jnp.logical_not(first))
    def _():
        lax.fori_loop(0, WIDTH // 64, clear, 0)

    all_ids[sh] = ids[...]
    send_left(0)

    def step(m, start, size, hook=None):
        pieces = [(m * TOK + start) // PIECE + i for i in range(size // PIECE)]

        @pl.when(jnp.logical_not(last))
        def _():
            for c in pieces:
                relay_copy(c).wait_recv()

        if hook is not None:
            hook()
        backward(m, start, size)

        @pl.when(jnp.logical_not(first))
        def _():
            for c in pieces:
                relay_copy(c).start()

    inner = jnp.logical_not(first | last)

    def chunks(m, slots, hook=None):
        for k in range(CHUNKS):
            fine = hook is not None and k == CHUNKS - 1
            for i in range(SPLIT):

                def piece(k=k, i=i):
                    at_last = hook if fine and i == SPLIT - 1 else None
                    step(m, k * CHUNK + i * PIECE, PIECE, at_last)

                if fine:
                    piece()
                else:
                    pl.when(inner)(piece)
                if not fine and i == SPLIT - 1:

                    @pl.when(first | (last & (m > 0)))
                    def _(k=k):
                        step(m, k * CHUNK, CHUNK)

                slots[k * SPLIT + i]()
                tell_ids(m, k * SPLIT + i)

    def route(m):
        rows = micro_rows(m)

        @pl.when(first)
        def _():
            target = lax.broadcasted_iota(jnp.int32, (TOK, TOK), 0).astype(F32)
            pick = jnp.where(target == rank[m], 1.0, 0.0).astype(BF16)
            ordered = jnp.dot(pick, nbuf[rows, :], preferred_element_type=F32).astype(BF16)
            sorted_rows[m] = ordered
            route_copy(m, 1).start()
            route_copy(m, SECTIONS - 1).start()
            if isinstance(m, int):
                route_copy(m, 2).start()
            routed[pl.ds(pl.multiple_of(m * PER_PLANE, PER_PLANE), PER_PLANE), :] = ordered[
                :PER_PLANE, :
            ]

    def micro_step(m, carry):
        @pl.when(last & (m > 0))
        def _():
            load_top(m).wait()

        def forward_slot(j):
            def work():
                if j == 0:

                    @pl.when(last & (m == 1))
                    def _():
                        pass_pool(0)

                    forward_open(m + 1)
                forward_tile(m + 1, j)
                if j == WIDTH // TILE - 1:
                    send_left(m + 1)

            return work

        def grad_slot(i):
            def work():
                if i == 2:

                    @pl.when(last & (m == 1))
                    def _():
                        pass_pool(1)

                @pl.when(m > 0)
                def _():
                    if i == 0:
                        hear_peer(m - 1)
                    grad_tiles(m - 1, (i,), True)

            return work

        tiles = range(WIDTH // TILE)
        chunks(m, [forward_slot(j) for j in tiles] + [grad_slot(i) for i in tiles])
        send_right(m, m * TOK, TOK)
        route(m)
        return carry

    lax.fori_loop(0, MICRO - 1, micro_step, 0)

    final = MICRO - 1
    tail = TOK - CHUNK

    def unit_copy(source, target, send, recv, to, came):
        return pltpu.make_async_remote_copy(
            src_ref=source.at[to],
            dst_ref=target.at[came],
            send_sem=send,
            recv_sem=recv,
            device_id=(sec, to),
            device_id_type=MESH,
        )

    def hand_soon(k, carry):
        to = (sh + k) % SHARDS
        unit_copy(soon, got_soon, soon_send, soon_recv, to, sh).start()
        return carry

    def hand_late(k, carry):
        to = (sh + k) % SHARDS
        unit_copy(late, got_late, late_send, late_recv, to, sh).start()
        return carry

    def wait_all(ref, semaphore):
        others = ref.at[pl.ds(0, SHARDS - 1)]
        pltpu.make_async_copy(others, others, semaphore).wait()

    def soon_units():
        row = lax.broadcasted_iota(jnp.int32, (SOON, SOON), 0)
        col = lax.broadcasted_iota(jnp.int32, (SOON, SOON), 1)
        target = ((col >> 1) & (SHARDS - 1)) * (2 * (MICRO - 1)) + (col >> 6) * 2 + (col & 1)
        regroup = jnp.where(row == target, 1.0, 0.0).astype(BF16)
        by_owner = jnp.dot(regroup, routed[pl.ds(0, SOON), :], preferred_element_type=F32)
        for b in range(8):
            flat[pl.ds(b, SOON, stride=8), :] = by_owner[:, b * 128 : (b + 1) * 128]
        soon[...] = flat[...].reshape(soon.shape).astype(BF16)
        got_soon[sh] = soon[sh]

    def late_units():
        by_owner = routed[pl.ds(SOON, PER_PLANE), :].astype(F32)
        for b in range(8):
            flat[pl.ds(b, PER_PLANE, stride=8), :] = by_owner[:, b * 128 : (b + 1) * 128]
        late[...] = flat[pl.ds(0, PER_PLANE * 8), :].reshape(late.shape).astype(BF16)
        got_late[sh] = late[sh]

    def to_rows(got, start, count):
        flat[pl.ds(0, count * 8), :] = got[...].astype(F32).reshape(count * 8, 128)
        for b in range(8):
            rows_buf[pl.ds(start, count), pl.ds(b * 128, 128)] = flat[
                pl.ds(b, count, stride=8), :
            ].astype(BF16)

    @pl.when(last)
    def _():
        load_top(final).wait()

    def final_slot(n):
        def work():
            if n == 2:
                hear_peer(final - 1)
            if 2 <= n < 2 + WIDTH // TILE:
                grad_tiles(final - 1, (n - 2,), True)
            if n == 5:
                send_right(final, final * TOK, tail)

            @pl.when(first)
            def _():
                if n == 0:
                    soon_units()
                if n == 1:
                    for before in range(final):
                        route_copy(before, 2).start()
                if n == 2:
                    lax.fori_loop(1, SHARDS // 2, hand_soon, 0)
                if n == 4:
                    lax.fori_loop(SHARDS // 2, SHARDS, hand_soon, 0)

        return work

    def hand_g():
        @pl.when(core == 0)
        def _():
            right_copy(final + 1, gbuf, final * TOK + tail, TOK - tail).start()

    chunks(final, [final_slot(n) for n in range(CHUNKS * SPLIT)], hand_g)

    @pl.when(core == 1)
    def _():
        right_copy(final + 1, dz, final * TOK + tail, TOK - tail).start()

    grad_tiles(final, (0, 1, 2, 3), False)

    def block_rows(y, x):
        return pl.ds(pl.multiple_of((y * SIDE + x) * BLOCK, BLOCK), BLOCK)

    left_half = pl.ds(0, HALF)
    right_half = pl.ds(HALF, HALF)

    def x_copy(d, y):
        to = (px + d) % SIDE
        return pltpu.make_async_remote_copy(
            src_ref=send_x.at[y, pl.ds(pl.multiple_of(to * BLOCK, BLOCK), BLOCK)],
            dst_ref=recv_x.at[d - 1, y],
            send_sem=x_send.at[d - 1, y],
            recv_sem=x_recv.at[d - 1, y],
            device_id=at(py, to, core),
            device_id_type=MESH,
        )

    def y_copy(d, x):
        rows = pl.ds(pl.multiple_of(x * BLOCK, BLOCK), BLOCK)
        return pltpu.make_async_remote_copy(
            src_ref=send_y.at[d - 1, rows],
            dst_ref=recv_y.at[d - 1, rows],
            send_sem=y_send.at[d - 1, x],
            recv_sem=y_recv.at[d - 1, x],
            device_id=at((py + d) % SIDE, px, core),
            device_id_type=MESH,
        )

    def c_copy(h, e, c, kind):
        there = (py + e) % SIDE if h == 0 else (px + e) % SIDE
        return pltpu.make_async_remote_copy(
            src_ref=send_c.at[h, e, c],
            dst_ref=out_parts.at[kind, h, e],
            send_sem=c_send.at[h, e, c],
            recv_sem=c_recv.at[kind, h, e],
            device_id=at(there, px, c) if h == 0 else at(py, there, c),
            device_id_type=MESH,
        )

    def own_part(h):
        return pltpu.make_async_copy(
            send_c.at[h, 0, core], out_parts.at[core, h, 0], out_sem.at[2 + h]
        )

    order = (2, 1, 3, 0)
    frows = micro_rows(final)
    left_copy(final, act).wait_recv()
    right_copy(final, dz, final * TOK, tail).wait_recv()
    right_copy(final + 1, dz, final * TOK + tail, TOK - tail).wait_recv()
    for d in order:
        y = (py + d) % SIDE
        cols = pl.ds(pl.multiple_of(y * TILE, TILE), TILE)
        total = acc[cols, :] + dot_tn(peer_l[frows, cols], peer_r[frows, :])
        acc[cols, :] = total
        send_x[y] = total[:, :HALF].astype(BF16)
        for dx in (2, 1, 3):
            x_copy(dx, y).start()
        if d != 0:
            send_y[d - 1] = total[:, HALF:].astype(BF16)
            for e in order:
                y_copy(d, (px + e) % SIDE).start()
    route(final)

    @pl.when(jnp.logical_not(first))
    def _():
        for m in range(MICRO - 1):
            route_copy(m, 1).wait_recv()
        soon_units()
        lax.fori_loop(1, SHARDS, hand_soon, 0)
        route_copy(final, 1).wait_recv()

    late_units()
    lax.fori_loop(1, SHARDS, hand_late, 0)

    wait_all(all_ids, ids_recv)
    own = sec * SHARDS + sh
    feature = own // (SECTIONS * SHARDS // ids.shape[1])
    heard = all_ids[:, :, feature, :].reshape(SHARDS * MICRO, ids.shape[2])
    place = lax.broadcasted_iota(jnp.int32, heard.shape, 1) * ROWS_OWN + (heard & (ROWS_OWN - 1))
    ours = heard >> 10 == own
    low = jnp.min(jnp.where(ours, place, 1 << 20), axis=1, keepdims=True) & (ROWS_OWN - 1)
    high = jnp.max(jnp.where(ours, place, -1), axis=1, keepdims=True) & (ROWS_OWN - 1)
    at_lane = lax.broadcasted_iota(jnp.int32, (SHARDS * MICRO, 128), 1)
    parts = jnp.where(
        at_lane == 0,
        low >> 5,
        jnp.where(at_lane == 1, low & 31, jnp.where(at_lane == 2, high >> 5, high & 31)),
    )
    half = lax.broadcasted_iota(jnp.int32, (TOK, SHARDS * MICRO), 0) >> 1
    pair = lax.broadcasted_iota(jnp.int32, (TOK, SHARDS * MICRO), 1)
    came, micro = pair >> 2, pair & (MICRO - 1)
    place_of = jnp.where(
        micro < final, came * (MICRO - 1) + micro, SHARDS * (MICRO - 1) + came
    )
    twice = jnp.where(half == place_of, 1.0, 0.0).astype(BF16)
    both = jnp.dot(twice, parts.astype(F32).astype(BF16), preferred_element_type=F32)
    odd = lax.broadcasted_iota(jnp.int32, (TOK, 1), 0) & 1
    row_of = jnp.where(
        odd == 0, both[:, 0:1] * 32.0 + both[:, 1:2], both[:, 2:3] * 32.0 + both[:, 3:4]
    )
    named[...] = jnp.broadcast_to(row_of.astype(jnp.int32), (TOK, 128))
    put_named = pltpu.make_async_copy(named, out_named, out_sem.at[0])
    put_named.start()

    put_rows = pltpu.make_async_copy(rows_buf, out_rows, out_sem.at[1])

    def collect_soon():
        wait_all(got_soon, soon_recv)
        to_rows(got_soon, 0, SOON)

    pl.when(first)(collect_soon)

    for e in order:
        y = (py + e) % SIDE
        x = (px + e) % SIDE
        for d in range(1, SIDE):
            x_copy(d, y).wait_recv()
            y_copy(d, x).wait_recv()
        total = acc[block_rows(y, px), left_half]
        other = acc[block_rows(py, x), right_half]
        for d in range(1, SIDE):
            total = total + recv_x[d - 1, y].astype(F32)
            xrows = pl.ds(pl.multiple_of(x * BLOCK, BLOCK), BLOCK)
            other = other + recv_y[d - 1, xrows, :].astype(F32)
        for h, part in ((0, total), (1, other)):
            for c in range(2):
                send_c[h, e, c] = part[c * SHARE : (c + 1) * SHARE, :].astype(BF16)
                if e == 0:

                    @pl.when(core == c)
                    def _(h=h, c=c):
                        own_part(h).start()

                    @pl.when(core != c)
                    def _(h=h, c=c):
                        c_copy(h, 0, c, core).start()
                else:
                    c_copy(h, e, c, core).start()

    pl.when(jnp.logical_not(first))(collect_soon)
    wait_all(got_late, late_recv)
    to_rows(got_late, SOON, PER_PLANE)
    put_rows.start()

    wait_all(all_ids, ids_send)
    wait_all(soon, soon_send)

    @pl.when((sec == 1) | last)
    def _():
        pool_copy(sec).wait_send()

    @pl.when(sec == 2)
    def _():
        hop_copy(0).wait_send()
        hop_copy(1).wait_send()

    @pl.when(last)
    def _():
        pass_copy(0).wait_send()
        pass_copy(1).wait_send()

    @pl.when(jnp.logical_not(first))
    def _():
        def left(c, carry):
            relay_copy(c).wait_send()
            return carry

        lax.fori_loop(0, PIECES, left, 0)

    @pl.when(first)
    def _():
        for m in range(final):
            for p in range(1, SECTIONS):
                route_copy(m, p).wait_send()

    for m in range(MICRO):
        left_copy(m, act).wait_send()
    for m in range(final):
        right_copy(m, dz, m * TOK, TOK).wait_send()
    right_copy(final, dz, final * TOK, tail).wait_send()
    right_copy(final + 1, dz, final * TOK + tail, TOK - tail).wait_send()

    wait_all(late, late_send)

    @pl.when(first)
    def _():
        for p in range(1, SECTIONS):
            route_copy(final, p).wait_send()

    for d in range(1, SIDE):
        for y in range(SIDE):
            x_copy(d, y).wait_send()
            y_copy(d, y).wait_send()

    for kind in range(2):
        for h in range(2):

            @pl.when(core != kind)
            def _(h=h, kind=kind):
                c_copy(h, 0, 1 - kind, kind).wait_recv()

            for e in range(1, SIDE):
                c_copy(h, e, 0, kind).wait_recv()

    for h in range(2):
        for d in range(1, SIDE):
            for c in range(2):
                c_copy(h, d, c, core).wait_send()
        c_copy(h, 0, 1 - core, core).wait_send()
    for put in (put_named, put_rows, own_part(0), own_part(1)):
        put.wait()


def relay(holder, saved, pooled, grad_top, w_in, w_out, ids):
    vmem = pl.BlockSpec(memory_space=pltpu.VMEM)
    anywhere = pl.BlockSpec(memory_space=pl.ANY)
    dma = pltpu.SemaphoreType.DMA
    tokens = MICRO * TOK
    return pl.pallas_call(
        kernel,
        out_shape=(
            jax.ShapeDtypeStruct((2, 2, SIDE, SHARE, HALF), BF16),
            jax.ShapeDtypeStruct((TOK, WIDTH), BF16),
            jax.ShapeDtypeStruct((TOK, 128), jnp.int32),
        ),
        in_specs=[pl.BlockSpec(memory_space=pltpu.SMEM)] + [anywhere] * 5 + [vmem],
        out_specs=(anywhere, anywhere, anywhere),
        scratch_shapes=[
            pltpu.VMEM((WIDTH, WIDTH), BF16),
            pltpu.VMEM((WIDTH, WIDTH), BF16),
            pltpu.VMEM((WIDTH, WIDTH), BF16),
            pltpu.VMEM((WIDTH, WIDTH), BF16),
            pltpu.VMEM((tokens, WIDTH), BF16),
            pltpu.VMEM((tokens, WIDTH), BF16),
            pltpu.VMEM((tokens, WIDTH), BF16),
            pltpu.VMEM((SECTIONS, TOK, WIDTH), BF16),
            pltpu.VMEM((tokens, WIDTH), BF16),
            pltpu.VMEM((2, TOK, WIDTH), F32),
            pltpu.VMEM((tokens, WIDTH), BF16),
            pltpu.VMEM((WIDTH, WIDTH), F32),
            pltpu.VMEM((MICRO, 1, TOK), F32),
            pltpu.VMEM((SHARDS,) + ids.shape, jnp.int32),
            pltpu.VMEM((MICRO, TOK, WIDTH), BF16),
            pltpu.VMEM((TOK, WIDTH), BF16),
            pltpu.VMEM((SHARDS, 16 * (MICRO - 1), 128), BF16),
            pltpu.VMEM((SHARDS, 16 * (MICRO - 1), 128), BF16),
            pltpu.VMEM((SHARDS, 16, 128), BF16),
            pltpu.VMEM((SHARDS, 16, 128), BF16),
            pltpu.VMEM((SOON * 8, 128), F32),
            pltpu.VMEM((TOK, 128), jnp.int32),
            pltpu.VMEM((TOK, WIDTH), BF16),
            pltpu.VMEM((TOK, WIDTH), BF16),
            pltpu.VMEM((tokens, WIDTH), BF16),
            pltpu.VMEM((tokens, WIDTH), BF16),
            pltpu.VMEM((SIDE, SIDE * BLOCK, HALF), BF16),
            pltpu.VMEM((SIDE - 1, SIDE, BLOCK, HALF), BF16),
            pltpu.VMEM((SIDE - 1, SIDE * BLOCK, HALF), BF16),
            pltpu.VMEM((SIDE - 1, SIDE * BLOCK, HALF), BF16),
            pltpu.VMEM((2, SIDE, 2, SHARE, HALF), BF16),
            dma((3 + MICRO,)),
            dma((MICRO,)),
            dma,
            dma((SECTIONS,)),
            dma((PIECES,)),
            dma((PIECES,)),
            dma((MICRO, SECTIONS)),
            dma((MICRO,)),
            dma,
            dma,
            dma,
            dma,
            pltpu.SemaphoreType.REGULAR((2,)),
            dma((2,)),
            dma((2,)),
            dma((2,)),
            dma((2,)),
            dma((4,)),
            dma,
            dma,
            dma((MICRO,)),
            dma((MICRO,)),
            dma((MICRO + 1,)),
            dma((MICRO + 1,)),
            dma((SIDE - 1, SIDE)),
            dma((SIDE - 1, SIDE)),
            dma((SIDE - 1, SIDE)),
            dma((SIDE - 1, SIDE)),
            dma((2, SIDE, 2)),
            dma((2, 2, SIDE)),
        ],
        compiler_params=pltpu.CompilerParams(
            collective_id=0, has_side_effects=True, vmem_limit_bytes=56 * 1024 * 1024
        ),
        cost_estimate=pl.CostEstimate(
            flops=10 * tokens * WIDTH * WIDTH, bytes_accessed=9 * 2**20, transcendentals=tokens * WIDTH
        ),
        name="relay",
    )(holder, saved, pooled, grad_top, w_in, w_out, ids)


def table_kernel(named, rows, parts, table, out_in, out_out):
    block = pl.program_id(0)
    lane = lax.broadcasted_iota(jnp.int32, (TOK, WIDE), 1) + block * WIDE
    hit = jnp.where(lane == named[:, 0:1], 1.0, 0.0).astype(BF16)
    table[...] = dot_tn(hit, rows[...])

    @pl.when(block == 0)
    def _():
        for kind, out in ((0, out_in), (1, out_out)):
            for h in range(2):
                total = parts[kind, h, 0].astype(F32)
                for e in range(1, SIDE):
                    total = total + parts[kind, h, e].astype(F32)
                out[:, h * HALF : (h + 1) * HALF] = total


def owner_sums(named, rows, parts):
    def whole(shape):
        return pl.BlockSpec(shape, lambda b: (0,) * len(shape))

    share = jax.ShapeDtypeStruct((SHARE, WIDTH), F32)
    return pl.pallas_call(
        table_kernel,
        grid=(ROWS_OWN // WIDE,),
        out_shape=(jax.ShapeDtypeStruct((ROWS_OWN, WIDTH), F32), share, share),
        in_specs=[whole(named.shape), whole(rows.shape), whole(parts.shape)],
        out_specs=(
            pl.BlockSpec((WIDE, WIDTH), lambda b: (b, 0)),
            whole(share.shape),
            whole(share.shape),
        ),
        compiler_params=pltpu.CompilerParams(vmem_limit_bytes=32 * 1024 * 1024),
        cost_estimate=pl.CostEstimate(
            flops=2 * ROWS_OWN * TOK * WIDTH, bytes_accessed=5 * 2**20, transcendentals=0
        ),
        name="owner_sums",
    )(named, rows, parts)


def local(saved, pooled, grad_top, w_in, w_out, feature_ids, holder_order):
    tokens = MICRO * TOK
    parts, rows, named = relay(
        holder_order,
        saved.reshape(tokens, WIDTH),
        pooled.reshape(TOK, WIDTH),
        grad_top.reshape(tokens, WIDTH),
        w_in[0],
        w_out[0],
        jnp.transpose(feature_ids, (0, 2, 1)),
    )
    table_grad, grad_in, grad_out = owner_sums(named, rows, parts)
    return (grad_in[None], grad_out[None], table_grad)


def solution(mesh):
    return jax.shard_map(
        local,
        mesh=mesh,
        in_specs=(
            P("section", None, "shard", None, None),
            P("section", "shard", None, None),
            P(None, "shard", None, None),
            P("section", None, None),
            P("section", None, None),
            P(None, "shard", None),
            P(),
        ),
        out_specs=(
            P("section", "shard", None),
            P("section", "shard", None),
            P(("section", "shard"), None),
        ),
        check_vma=False,
    )
```
